32 devices in a mesh: dp: 8 (over y, x, core), ctx: 4 (over z).
Axes of the slice: x: 2, y: 2, z: 4, core: 2. Of those that a mesh axis runs over, the one named last changes fastest.
Arguments:
- hidden: bfloat16 [8, 1024, 1536], P('dp', 'ctx'), may hold values from -6 to 6
- cotangent: bfloat16 [8, 1024, 1536], P('dp', 'ctx'), may hold values from -6 to 6
- span_order: int32 [8, 8], P('dp'), may hold values from 0 to 7, each once within a row
- attn_gain: bfloat16 [1536], P(('dp', 'ctx')), may hold values from 0.25 to 1.75
- w_query: bfloat16 [1536, 1536], P(('dp', 'ctx')), may hold values from -0.15625 to 0.15625
- b_query: bfloat16 [1536], P(('dp', 'ctx')), may hold values from -3 to 3
- w_key: bfloat16 [1536, 256], P(('dp', 'ctx')), may hold values from -0.15625 to 0.15625
- b_key: bfloat16 [256], P(('dp', 'ctx')), may hold values from -3 to 3
- w_value: bfloat16 [1536, 256], P(('dp', 'ctx')), may hold values from -0.15625 to 0.15625
- b_value: bfloat16 [256], P(('dp', 'ctx')), may hold values from -3 to 3
- w_out: bfloat16 [1536, 1536], P(('dp', 'ctx')), may hold values from -0.625 to 0.625
- ffn_gain: bfloat16 [1536], P(('dp', 'ctx')), may hold values from 0.25 to 1.75
- w_gate: bfloat16 [1536, 8960], P(('dp', 'ctx')), may hold values from -0.15625 to 0.15625
- w_up: bfloat16 [1536, 8960], P(('dp', 'ctx')), may hold values from -0.15625 to 0.15625
- w_down: bfloat16 [1536, 8960], P(('dp', 'ctx')), may hold values from -0.125 to 0.125
Outputs:
- result: bfloat16 [8, 1024, 1536], P('dp', 'ctx')
- hidden_grad: float32 [8, 1024, 1536], P('dp', 'ctx')
- attn_gain_grad: float32 [1536], P(('dp', 'ctx'))
- w_query_grad: float32 [1536, 1536], P(('dp', 'ctx'))
- b_query_grad: float32 [1536], P(('dp', 'ctx'))
- w_key_grad: float32 [1536, 256], P(('dp', 'ctx'))
- b_key_grad: float32 [256], P(('dp', 'ctx'))
- w_value_grad: float32 [1536, 256], P(('dp', 'ctx'))
- b_value_grad: float32 [256], P(('dp', 'ctx'))
- w_out_grad: float32 [1536, 1536], P(('dp', 'ctx'))
- ffn_gain_grad: float32 [1536], P(('dp', 'ctx'))
- w_gate_grad: float32 [1536, 8960], P(('dp', 'ctx'))
- w_up_grad: float32 [1536, 8960], P(('dp', 'ctx'))
- w_down_grad: float32 [1536, 8960], P(('dp', 'ctx'))
The draws below stay inside these ranges and needn't reach their ends.
Inputs may be any that keep to these rules, and one draw needn't show every extreme that they name: `span_order`: each row is a permutation; entry j of a row names the block of 128 positions that the row's stored places j * 128 to (j + 1) * 128 - 1 hold.
All inputs are finite; a program needn't handle non-finite values.
Results may differ from the reference program's by a relative error of at most 0.019.
Values may be sent and summed in bfloat16 or wider, within the bound.
A program may use at most 384 MiB of HBM per device.

```python
import jax
import jax.numpy as jnp
from jax import lax

D = 1536
HEADS = 12
KV_HEADS = 2
HD = 128
FF = 8960
SPAN = 128
SEQ_LEN = 1024
BATCH = 8
N_CTX = 4


def shard_levels(key, extent, split, least, high):
    level = 1.0
    for position, parts in split:
        steps = jax.random.uniform(jax.random.fold_in(jax.random.fold_in(key, 6), position), (parts,), jnp.float32, least / len(split), high / len(split))
        level = level * jnp.repeat(jnp.exp(steps), extent[position] // parts).reshape((-1,) + (1,) * (len(extent) - 1 - position))
    return level


def centred(key, extent, scale, most, pieces=(), held_as=jnp.bfloat16):
    loudness = shard_levels(key, extent, pieces, -0.22, 0.18) if pieces else 1.0
    drawn = jax.random.normal(key, extent, jnp.float32) * scale * loudness
    return jnp.minimum(jnp.maximum(drawn, -most), most).astype(held_as)


def setup_inputs(seed: int = 0) -> dict:
    seeds = jax.random.split(jax.random.key(seed), 16)
    hidden = centred(seeds[0], (BATCH, SEQ_LEN, D), 1.0, 6.0, ((0, 8), (1, 4)))
    cotangent = centred(seeds[1], (BATCH, SEQ_LEN, D), 1.0, 6.0, ((0, 8), (1, 4)))
    span_order = jax.vmap(lambda own: jax.random.permutation(own, 2 * N_CTX))(jax.random.split(seeds[2], BATCH)).reshape((BATCH, 2 * N_CTX)).astype(jnp.int32)
    attn_gain = jnp.clip(1.0 + 0.15 * jax.random.normal(seeds[3], (D,), jnp.float32), 0.25, 1.75).astype(jnp.bfloat16)
    w_query = centred(seeds[4], (D, HEADS * HD), D ** -0.5, 0.15625, ((0, 32),))
    b_query = centred(seeds[5], (HEADS * HD,), 0.5, 3.0, ((0, 32),))
    w_key = centred(seeds[6], (D, KV_HEADS * HD), D ** -0.5, 0.15625, ((0, 32),))
    b_key = centred(seeds[7], (KV_HEADS * HD,), 0.5, 3.0, ((0, 32),))
    w_value = centred(seeds[8], (D, KV_HEADS * HD), D ** -0.5, 0.15625, ((0, 32),))
    b_value = centred(seeds[9], (KV_HEADS * HD,), 0.5, 3.0, ((0, 32),))
    w_out = centred(seeds[10], (D, HEADS * HD), (HEADS * HD // 16) ** -0.5, 0.625, ((0, 32),))
    ffn_gain = jnp.clip(1.0 + 0.15 * jax.random.normal(seeds[11], (D,), jnp.float32), 0.25, 1.75).astype(jnp.bfloat16)
    w_gate = centred(seeds[12], (D, FF), D ** -0.5, 0.15625, ((0, 32),))
    w_up = centred(seeds[13], (D, FF), D ** -0.5, 0.15625, ((0, 32),))
    w_down = centred(seeds[14], (D, FF), (FF // 4) ** -0.5, 0.125, ((0, 32),))
    return {"hidden": hidden, "cotangent": cotangent, "span_order": span_order, "attn_gain": attn_gain, "w_query": w_query, "b_query": b_query, "w_key": w_key, "b_key": b_key, "w_value": w_value, "b_value": b_value, "w_out": w_out, "ffn_gain": ffn_gain, "w_gate": w_gate, "w_up": w_up, "w_down": w_down}


norm_eps = 1e-06
rope_base = 10000.0
masked_fill = -1e+30

@jax.custom_vjp
def low(v):
    return lax.optimization_barrier(v.astype(jnp.bfloat16)).astype(jnp.float32)

@jax.custom_vjp
def low_back(v):
    return v

def low_keep(v):
    return (low(v), None)

def low_pass(kept, grad):
    return (grad,)

def back_keep(v):
    return (v, None)

def back_low(kept, grad):
    return (low(grad),)
low.defvjp(low_keep, low_pass)
low_back.defvjp(back_keep, back_low)

def matmul(left, right):
    return jnp.dot(left, right, precision=lax.Precision.HIGHEST)

def rms_norm(values, gain):
    factor = lax.rsqrt(lax.optimization_barrier(jnp.mean(values * values, axis=-1, keepdims=True)) + norm_eps)
    return values * factor * gain

def rotate(values, places):
    half = values.shape[-1] // 2
    freqs = rope_base ** (-(jnp.arange(half, dtype=jnp.float32) * 2.0 / values.shape[-1]))
    angles = places.astype(jnp.float32)[:, None] * freqs[None, :]
    cosine = jnp.cos(angles)[:, None, :]
    sine = jnp.sin(angles)[:, None, :]
    first = values[..., :half]
    second = values[..., half:]
    return jnp.concatenate([first * cosine - second * sine, second * cosine + first * sine], axis=-1)

def sequence_forward(source, places, attn_gain, w_query, b_query, w_key, b_key, w_value, b_value, w_out, ffn_gain, w_gate, w_up, w_down):
    length = source.shape[0]
    groups = HEADS // KV_HEADS
    normed = low(rms_norm(source, attn_gain))
    queries = low_back(matmul(normed, w_query) + b_query).reshape(length, HEADS, HD)
    key_rows = low_back(matmul(normed, w_key) + b_key).reshape(length, KV_HEADS, HD)
    values = low_back(low(matmul(normed, w_value) + b_value)).reshape(length, KV_HEADS, HD)
    queries = low(rotate(queries, places)).reshape(length, KV_HEADS, groups, HD)
    key_rows = low(rotate(key_rows, places))
    scores = jnp.einsum('qkgd,skd->kgqs', queries, key_rows, precision=lax.Precision.HIGHEST)
    scores = low_back(scores * HD ** (-0.5))
    allowed = places[None, :] <= places[:, None]
    masked = jnp.where(allowed[None, None], scores, masked_fill)
    row_max = lax.optimization_barrier(jnp.max(masked, axis=-1, keepdims=True))
    expo = jnp.exp(masked - row_max)
    attend = low(expo / lax.optimization_barrier(jnp.sum(expo, axis=-1, keepdims=True)))
    mixed = jnp.einsum('kgqs,skd->qkgd', attend, values, precision=lax.Precision.HIGHEST)
    mixed = low_back(low(mixed.reshape(length, HEADS * HD)))
    resid = source + low_back(matmul(mixed, w_out.T))
    normed_two = low(rms_norm(resid, ffn_gain))
    gate_pre = low_back(matmul(normed_two, w_gate))
    up_pre = low_back(matmul(normed_two, w_up))
    act = low(jax.nn.silu(gate_pre) * up_pre)
    return resid + low_back(matmul(act, w_down.T))

def forward(source, places, weights):

    def one_sequence(pair):
        return sequence_forward(pair[0], pair[1], *weights)
    return lax.map(jax.checkpoint(one_sequence), (source, places))

def reference(hidden, cotangent, span_order, attn_gain, w_query, b_query, w_key, b_key, w_value, b_value, w_out, ffn_gain, w_gate, w_up, w_down):
    places_all = jnp.arange(SEQ_LEN, dtype=jnp.int32)
    places = jnp.repeat(span_order, SPAN, axis=1) * SPAN + places_all[None, :] % SPAN
    weights = [attn_gain, w_query, b_query, w_key, b_key, w_value, b_value, w_out, ffn_gain, w_gate, w_up, w_down]
    floats = tuple((item.astype(jnp.float32) for item in weights))

    def apply_layer(source, params):
        return forward(source, places, params)
    output, pullback = jax.vjp(apply_layer, hidden.astype(jnp.float32), floats)
    source_grad, weight_grads = pullback(cotangent.astype(jnp.float32))
    return (output.astype(jnp.bfloat16), source_grad, weight_grads[0], weight_grads[1], weight_grads[2], weight_grads[3], weight_grads[4], weight_grads[5], weight_grads[6], weight_grads[7], weight_grads[8], weight_grads[9], weight_grads[10], weight_grads[11])
```

```python
import functools

import jax
import jax.numpy as jnp
from jax import lax
from jax.experimental import pallas as pl
from jax.experimental.pallas import tpu as pltpu
from jax.sharding import PartitionSpec as P

D = 1536
HEADS = 12
KV_HEADS = 2
HD = 128


norm_eps = 1e-06
rope_base = 10000.0
masked_fill = -1e30


def angles_for(places, width):
    half = width // 2
    freqs = rope_base ** (-(jnp.arange(half, dtype=jnp.float32) * 2.0 / width))
    angles = places.astype(jnp.float32)[:, None] * freqs[None, :]
    return (jnp.cos(angles)[:, None, :], jnp.sin(angles)[:, None, :])


def rotate(values, cosine, sine):
    half = values.shape[-1] // 2
    first = values[..., :half]
    second = values[..., half:]
    return jnp.concatenate(
        [first * cosine - second * sine, second * cosine + first * sine], axis=-1
    )


def rotate_back(values, cosine, sine):
    half = values.shape[-1] // 2
    first = values[..., :half]
    second = values[..., half:]
    return jnp.concatenate(
        [first * cosine + second * sine, second * cosine - first * sine], axis=-1
    )


def norm_forward(source, gain):
    factor = lax.rsqrt(jnp.mean(source * source, axis=-1, keepdims=True) + norm_eps)
    return (factor, (source * factor * gain).astype(jnp.bfloat16))


def norm_backward(source, factor, gain, grad_normed):
    unit = source * factor
    gain_grad = jnp.sum(grad_normed * unit, axis=0)
    scaled = grad_normed * gain
    source_grad = factor * (scaled - unit * jnp.mean(scaled * unit, axis=-1, keepdims=True))
    return (source_grad, gain_grad)


def right_dot(left, weight):
    return jnp.einsum("rf,df->rd", left, weight, preferred_element_type=jnp.float32)


def plain_dot(left, weight):
    return jnp.dot(left, weight, preferred_element_type=jnp.float32)


def owned_columns(values, ctx_size, ctx_rank, shard_rows):
    rows = values.shape[0]
    blocks = values.shape[1] // (shard_rows * ctx_size)
    shaped = values.reshape(rows, blocks, ctx_size, shard_rows)
    picked = lax.dynamic_index_in_dim(shaped, ctx_rank, axis=2, keepdims=False)
    return picked.reshape(rows, blocks * shard_rows)


def outer_add(left, right):
    return jnp.einsum("rc,rf->cf", left, right, preferred_element_type=jnp.float32)


MESH = pl.DeviceIdType.MESH


def flip(index, mask):
    for bit in (1, 2, 4, 8, 16):
        if mask & bit:
            index = index + bit - 2 * bit * ((index // bit) % 2)
    return index


def either(a, b):
    return a + b - 2 * a * b


def dot(a, b, dims):
    return lax.dot_general(a, b, (dims, ((), ())), preferred_element_type=jnp.float32)


def ffn_kernel(
    ctx_size, n_own, go_own, go_p, go_y, go_py, go_core, sgu, sd, xgu, xd, zgu, zd, xzgu, xzd,
    hr, dgu, dd,
    wgu, wd, nt, go, ggu, act, csend, crecv, hpart, stage,
    w_sem, io_sem, n_send, n_recv, f_send, f_recv, c_send, c_recv, o_send, o_recv, st_sem,
):
    dp = lax.axis_index("dp")
    ctx = lax.axis_index("ctx")
    me = dp * ctx_size + ctx
    y, x, c = dp // 4, (dp // 2) % 2, dp % 2
    h, p = ctx // 2, ctx % 2
    width = wd.shape[1]
    shard = sgu.shape[2]
    rows, model = n_own.shape

    def at(index):
        return (index // ctx_size, index % ctx_size)

    core = at(flip(me, 4))

    def partner(o):
        return (dp + (o // 2) * 4 * (1 - 2 * y), ctx + (o % 2) * (1 - 2 * p))

    barrier = pltpu.get_barrier_semaphore()
    for device in (core, partner(1), partner(2), partner(3)):
        pl.semaphore_signal(barrier, inc=1, device_id=device, device_id_type=MESH)

    load_n = pltpu.make_async_copy(n_own, nt.at[0], io_sem.at[0])
    load_n.start()
    go_loads = []
    for o, ref in enumerate((go_own, go_p, go_y, go_py)):
        go_loads.append(pltpu.make_async_copy(ref, go.at[2 * o], io_sem.at[1 + o]))
        go_loads.append(pltpu.make_async_copy(go_core.at[o], go.at[2 * o + 1], io_sem.at[5 + o]))
    for copy in go_loads:
        copy.start()
    for mask, (gu_ref, d_ref) in ((0, (sgu, sd)), (8, (xgu, xd)), (2, (zgu, zd)), (10, (xzgu, xzd))):
        for j in range(8):
            rel = mask + (j // 4) * 16 + ((j // 2) % 2) * 4 + j % 2
            row = pl.ds(pl.multiple_of(flip(me, rel) * shard, shard), shard)
            pltpu.make_async_copy(gu_ref.at[j, 0], wgu.at[row, pl.ds(0, width)], w_sem.at[0]).start()
            pltpu.make_async_copy(gu_ref.at[j, 1], wgu.at[row, pl.ds(width, width)], w_sem.at[0]).start()
            pltpu.make_async_copy(d_ref.at[j], wd.at[row], w_sem.at[1]).start()

    pl.semaphore_wait(barrier, 4)
    load_n.wait()

    def push_n(slot, dst, device, send, recv):
        return pltpu.make_async_remote_copy(
            src_ref=nt.at[slot], dst_ref=nt.at[dst], send_sem=send, recv_sem=recv,
            device_id=device, device_id_type=MESH,
        )

    first = [push_n(0, 2 * o, partner(o), n_send.at[o], n_recv.at[o]) for o in (1, 2, 3)]
    for copy in first:
        copy.start()
    push_n(0, 1, core, f_send.at[0], f_recv.at[0]).start()
    pltpu.make_async_copy(wgu, wgu, w_sem.at[0]).wait()
    pltpu.make_async_copy(wd, wd, w_sem.at[1]).wait()
    for copy in go_loads:
        copy.wait()

    def tile(slot):
        gu = dot(nt[slot], wgu[...], ((1,), (0,)))
        ga = dot(go[slot], wd[...], ((1,), (0,)))
        gate, up = gu[:, :width], gu[:, width:]
        sig = 1.0 / (1.0 + jnp.exp(-gate))
        silu = gate * sig
        act[slot] = (silu * up).astype(jnp.bfloat16)
        ggu[slot, :, pl.ds(0, width)] = (ga * up * sig * (1.0 + gate * (1.0 - sig))).astype(jnp.bfloat16)
        ggu[slot, :, pl.ds(width, width)] = (ga * silu).astype(jnp.bfloat16)
        grad = dot(ggu[slot], wgu[...], ((1,), (1,)))
        out = dot(act[slot], wd[...], ((1,), (1,)))
        return (grad.astype(jnp.bfloat16), out.astype(jnp.bfloat16))

    def cross(o):
        return pltpu.make_async_remote_copy(
            src_ref=csend, dst_ref=crecv.at[o % 2], send_sem=c_send, recv_sem=c_recv.at[o % 2],
            device_id=core, device_id_type=MESH,
        )

    def final(o):
        return pltpu.make_async_remote_copy(
            src_ref=hpart.at[o], dst_ref=hr.at[o], send_sem=o_send.at[o], recv_sem=o_recv.at[o],
            device_id=partner(o), device_id_type=MESH,
        )

    keep = pltpu.make_async_copy(hpart.at[0], hr.at[0], io_sem.at[0])

    def combine(o):
        cross(o).wait_recv()
        total = hpart[o].astype(jnp.float32) + crecv[o % 2].astype(jnp.float32)
        hpart[o] = total.astype(jnp.bfloat16)

    def step(o, carry):
        @pl.when(o > 0)
        def _():
            push_n(0, 2 * o, partner(o), n_send.at[o], n_recv.at[o]).wait_recv()
            push_n(2 * o, 2 * o + 1, core, f_send.at[o], f_recv.at[o]).start()

        grad, out = tile(2 * o)
        hpart[o, 0] = grad
        hpart[o, 1] = out

        @pl.when(o > 0)
        def _():
            combine(o - 1)

        @pl.when(o == 1)
        def _():
            keep.start()

        @pl.when(o > 1)
        def _():
            final(o - 1).start()

        push_n(2 * o, 2 * o + 1, core, f_send.at[o], f_recv.at[o]).wait_recv()
        grad, out = tile(2 * o + 1)

        @pl.when(o > 0)
        def _():
            cross(o).wait_send()

        csend[0] = grad
        csend[1] = out
        cross(o).start()
        return carry

    lax.fori_loop(0, 4, step, 0)
    combine(3)
    final(3).start()

    def stage_wait(slot):
        pltpu.make_async_copy(stage.at[slot], stage.at[slot], st_sem.at[slot]).wait()

    def weights(q, carry):
        slot = q % 2

        @pl.when(q > 1)
        def _():
            stage_wait(slot)

        chunk = 8 * shard
        cols = pl.ds(pl.multiple_of(q * chunk, chunk), chunk)
        left = nt[:, :, cols].reshape(8 * rows, chunk)
        for half in range(2):
            part = pl.ds(half * width, width)
            right = ggu[:, :, part].reshape(8 * rows, width)
            stage[slot, :, part] = dot(left, right, ((0,), (0,))).astype(jnp.bfloat16)
        left = go[:, :, cols].reshape(8 * rows, chunk)
        right = act[...].reshape(8 * rows, width)
        stage[slot, :, pl.ds(2 * width, width)] = dot(left, right, ((0,), (0,))).astype(jnp.bfloat16)
        yr, xr = either(q // 2, y), either(q % 2, x)
        for j in range(8):
            cr, hrel, pr = either(j // 4, c), either((j // 2) % 2, h), either(j % 2, p)
            block = yr * 4 + cr * 2 + pr
            row = pl.ds(j * shard, shard)
            for half in range(2):
                pltpu.make_async_copy(
                    stage.at[slot, row, pl.ds(half * width, width)], dgu.at[xr, hrel, block, half], st_sem.at[slot]
                ).start()
            pltpu.make_async_copy(
                stage.at[slot, row, pl.ds(2 * width, width)], dd.at[xr, hrel, block], st_sem.at[slot]
            ).start()
        return carry

    lax.fori_loop(0, 4, weights, 0)
    stage_wait(0)
    stage_wait(1)
    keep.wait()
    cross(3).wait_send()
    for copy in first:
        copy.wait_send()
    for o in range(4):
        push_n(2 * o, 2 * o + 1, core, f_send.at[o], f_recv.at[o]).wait_send()
    for o in (1, 2, 3):
        final(o).wait()


def ffn_call(ctx_size, n_own, go_tiles, weights):
    rows, model = n_own.shape
    shard, width = weights[0].shape[2:]
    low = jnp.bfloat16
    return pl.pallas_call(
        functools.partial(ffn_kernel, ctx_size),
        out_shape=(
            jax.ShapeDtypeStruct((4, 2, rows, model), low),
            jax.ShapeDtypeStruct((2, 2, 8, 2, shard, width), low),
            jax.ShapeDtypeStruct((2, 2, 8, shard, width), low),
        ),
        in_specs=[pl.BlockSpec(memory_space=pl.ANY)] * 14,
        out_specs=[pl.BlockSpec(memory_space=pl.ANY)] * 3,
        scratch_shapes=[
            pltpu.VMEM((model, 2 * width), low),
            pltpu.VMEM((model, width), low),
            pltpu.VMEM((8, rows, model), low),
            pltpu.VMEM((8, rows, model), low),
            pltpu.VMEM((8, rows, 2 * width), low),
            pltpu.VMEM((8, rows, width), low),
            pltpu.VMEM((2, rows, model), low),
            pltpu.VMEM((2, 2, rows, model), low),
            pltpu.VMEM((4, 2, rows, model), low),
            pltpu.VMEM((2, 8 * shard, 3 * width), low),
            pltpu.SemaphoreType.DMA((2,)),
            pltpu.SemaphoreType.DMA((9,)),
            pltpu.SemaphoreType.DMA((4,)),
            pltpu.SemaphoreType.DMA((4,)),
            pltpu.SemaphoreType.DMA((4,)),
            pltpu.SemaphoreType.DMA((4,)),
            pltpu.SemaphoreType.DMA,
            pltpu.SemaphoreType.DMA((2,)),
            pltpu.SemaphoreType.DMA((4,)),
            pltpu.SemaphoreType.DMA((4,)),
            pltpu.SemaphoreType.DMA((2,)),
        ],
        compiler_params=pltpu.CompilerParams(
            collective_id=1, has_side_effects=True, vmem_limit_bytes=63 << 20
        ),
        name="ffn",
    )(n_own, *go_tiles, *weights)


def permute(value, mask, size):
    return lax.ppermute(value, ("dp", "ctx"), [(i, i ^ mask) for i in range(size)])


def fits(mesh):
    return mesh.shape["dp"] == 8 and mesh.shape["ctx"] == 4


def fast_device(
    hidden,
    cotangent,
    span_order,
    attn_gain,
    w_query,
    b_query,
    w_key,
    b_key,
    w_value,
    b_value,
    w_out,
    ffn_gain,
    w_gate,
    w_up,
    w_down,
):
    ctx_size = lax.axis_size("ctx")
    ctx_rank = lax.axis_index("ctx")
    size = lax.axis_size("dp") * ctx_size
    me = lax.axis_index("dp") * ctx_size + ctx_rank
    batches = hidden.shape[0]
    length = hidden.shape[1]
    span_len = length // 2
    seq_len = length * ctx_size
    row_count = batches * length
    groups = HEADS // KV_HEADS
    shard_rows = w_query.shape[0]
    head_scale = HD ** (-0.5)
    kv_width = KV_HEADS * HD
    q_width = HEADS * HD
    both = ("dp", "ctx")

    hidden_units = w_gate.shape[1]
    piece = -(-hidden_units // (8 * 128)) * 128
    stacked = jnp.pad(jnp.stack([w_gate, w_up, w_down]), ((0, 0), (0, 0), (0, 8 * piece - hidden_units)))
    pieces = stacked.reshape(3, shard_rows, 4, 2, piece).transpose(2, 3, 0, 1, 4)
    y, core, p = me // 16, (me // 4) % 2, me % 2
    mine = lax.dynamic_index_in_dim(pieces, core, 1, False)
    other = lax.dynamic_index_in_dim(pieces, 1 - core, 1, False)
    other = permute(other, 4, size)
    col = 2 * y + p
    sets = []
    for mask in (0, 1, 16, 17):
        want = jnp.bitwise_xor(col, (mask // 16) * 2 + mask % 2)
        chosen = jnp.stack(
            [lax.dynamic_index_in_dim(mine, want, 0, False), lax.dynamic_index_in_dim(other, want, 0, False)]
        )
        sets.append(permute(chosen, mask, size) if mask else chosen)
    whole = jnp.stack(sets)
    whole = whole.reshape(2, 2, 2, 3, shard_rows, piece).transpose(0, 2, 1, 3, 4, 5)
    whole = whole.reshape(8, 3, shard_rows, piece)
    own_gu, own_d = whole[:, :2], whole[:, 2]
    z_gu = permute(own_gu, 2, size)
    x_gu = permute(own_gu, 8, size)
    x_d = permute(own_d, 8, size)
    z_d = permute(own_d, 2, size)
    xz_gu = permute(z_gu, 8, size)
    xz_d = permute(z_d, 8, size)

    grad_out = cotangent.reshape(row_count, D)
    go_tiles = [grad_out] + [permute(grad_out, mask, size) for mask in (1, 16, 17)]
    go_core = permute(jnp.stack(go_tiles), 4, size)

    places = jnp.arange(seq_len, dtype=jnp.int32)
    every_pos = jnp.repeat(span_order, span_len, axis=1) * span_len + places[None, :] % span_len
    local_pos = lax.dynamic_slice_in_dim(every_pos, ctx_rank * length, length, 1)
    cosine, sine = angles_for(local_pos.reshape(row_count), HD)
    allowed = (every_pos[:, None, :] <= local_pos[:, :, None])[:, None, None]

    gains = jnp.stack([attn_gain, b_query, ffn_gain], axis=1)
    pair = jnp.pad(jnp.concatenate([b_key, b_value]), (0, shard_rows - 2 * b_key.shape[0]))
    packed = jnp.concatenate(
        [w_query, w_key, w_value, gains, pair[:, None], jnp.zeros((shard_rows, 124), jnp.bfloat16)], axis=1
    )
    packed = lax.all_gather(packed, both, axis=0, tiled=True)
    out_full = lax.all_gather(w_out, both, axis=0, tiled=True)
    proj_width = q_width + 2 * kv_width
    proj_full = packed[:, :proj_width]
    small = packed[:, proj_width : proj_width + 4].astype(jnp.float32)
    gain_one = small[:, 0]
    gain_two = small[:, 2]
    biases = small[:, 3].reshape(size, shard_rows)
    per = b_key.shape[0]
    bias = jnp.concatenate([small[:, 1], biases[:, :per].reshape(-1), biases[:, per : 2 * per].reshape(-1)])

    source = hidden.reshape(row_count, D).astype(jnp.float32)
    attn_factor, normed = norm_forward(source, gain_one)
    raw = plain_dot(normed, proj_full) + bias
    query_raw, key_raw = raw[:, :q_width], raw[:, q_width : q_width + kv_width]
    value_low = raw[:, q_width + kv_width :].astype(jnp.bfloat16)
    query_rot = rotate(query_raw.reshape(row_count, HEADS, HD), cosine, sine).astype(jnp.bfloat16)
    query_rot = query_rot.reshape(batches, length, KV_HEADS, groups, HD)
    key_rot = rotate(key_raw.reshape(row_count, KV_HEADS, HD), cosine, sine).astype(jnp.bfloat16)
    key_value = jnp.concatenate([key_rot.reshape(row_count, kv_width), value_low], axis=1)
    key_value = lax.all_gather(key_value.reshape(batches, length, 2 * kv_width), "ctx", axis=1, tiled=True)
    key_all = key_value[:, :, :kv_width].reshape(batches, seq_len, KV_HEADS, HD)
    value_all = key_value[:, :, kv_width:].reshape(batches, seq_len, KV_HEADS, HD)
    scores = (
        jnp.einsum("bqkgd,bskd->bkgqs", query_rot, key_all, preferred_element_type=jnp.float32)
        * head_scale
    )
    masked = jnp.where(allowed, scores, masked_fill)
    row_max = jnp.max(masked, axis=-1, keepdims=True)
    expo = jnp.exp(masked - row_max)
    expo_sum = jnp.sum(expo, axis=-1, keepdims=True)
    log_total = row_max + jnp.log(expo_sum)
    attend = (expo / expo_sum).astype(jnp.bfloat16)
    mixed = jnp.einsum("bkgqs,bskd->bqkgd", attend, value_all, preferred_element_type=jnp.float32)
    mixed = mixed.reshape(row_count, q_width).astype(jnp.bfloat16)
    resid = source + right_dot(mixed, out_full)
    ffn_factor, normed_two = norm_forward(resid, gain_two)

    tiles, gu_grad, d_grad = ffn_call(
        ctx_size, normed_two, go_tiles + [go_core], [own_gu, own_d, x_gu, x_d, z_gu, z_d, xz_gu, xz_d]
    )
    sums = jnp.sum(tiles.astype(jnp.float32), axis=0)
    grad_norm_two = sums[0]
    result = (resid + sums[1]).astype(jnp.bfloat16).reshape(batches, length, D)

    def fold(part):
        high = permute(part[1, 1], 8, size)
        low_part = permute(part[1, 0], 8, size)
        far = (part[0, 1].astype(jnp.float32) + high.astype(jnp.float32)).astype(jnp.bfloat16)
        far = permute(far, 2, size)
        near = part[0, 0].astype(jnp.float32) + low_part.astype(jnp.float32)
        return (near + far.astype(jnp.float32)).astype(jnp.bfloat16)

    d_sum = fold(d_grad)
    gu_sum = fold(gu_grad)
    whole_grad = jnp.concatenate([gu_sum, d_sum[:, None]], axis=1)
    whole_grad = whole_grad.reshape(2, 2, 2, 3, shard_rows, piece)
    parts = []
    for mask in (0, 1, 16, 17):
        part = whole_grad[mask // 16, :, mask % 2]
        parts.append(permute(part, mask, size) if mask else part)
    parts = jnp.stack(parts)
    theirs = permute(parts[:, 1], 4, size)
    ordered = jnp.stack([parts[:, 0], theirs], axis=0)
    ordered = ordered[jnp.bitwise_xor(jnp.arange(2), core)]
    ordered = ordered[:, jnp.bitwise_xor(jnp.arange(4), col)]
    flat = ordered.transpose(2, 3, 1, 0, 4).reshape(3, shard_rows, 8 * piece)[:, :, :hidden_units]
    flat = flat.astype(jnp.float32)
    w_gate_grad, w_up_grad, w_down_grad = flat[0], flat[1], flat[2]

    grad_plain = grad_out.astype(jnp.float32)
    resid_back, ffn_gain_part = norm_backward(resid, ffn_factor, gain_two, grad_norm_two)
    grad_resid = grad_plain + resid_back
    grad_attn = grad_resid.astype(jnp.bfloat16)
    grad_mixed = plain_dot(grad_attn, out_full).astype(jnp.bfloat16)
    grad_mixed = grad_mixed.reshape(batches, length, KV_HEADS, groups, HD)
    scores = (
        jnp.einsum("bqkgd,bskd->bkgqs", query_rot, key_all, preferred_element_type=jnp.float32)
        * head_scale
    )
    masked = jnp.where(allowed, scores, masked_fill)
    attend_full = jnp.exp(masked - log_total)
    attend = attend_full.astype(jnp.bfloat16)
    grad_attend = jnp.einsum(
        "bqkgd,bskd->bkgqs", grad_mixed, value_all, preferred_element_type=jnp.float32
    )
    value_grad_all = jnp.einsum(
        "bkgqs,bqkgd->bskd", attend, grad_mixed, preferred_element_type=jnp.float32
    )
    delta = jnp.sum(grad_attend * attend_full, axis=-1, keepdims=True)
    grad_scores = (attend_full * (grad_attend - delta)).astype(jnp.bfloat16)
    query_grad_rot = (
        jnp.einsum("bkgqs,bskd->bqkgd", grad_scores, key_all, preferred_element_type=jnp.float32)
        * head_scale
    )
    key_grad_all = (
        jnp.einsum("bkgqs,bqkgd->bskd", grad_scores, query_rot, preferred_element_type=jnp.float32)
        * head_scale
    )
    kv_grad = jnp.concatenate(
        [key_grad_all.reshape(batches, seq_len, kv_width), value_grad_all.reshape(batches, seq_len, kv_width)],
        axis=2,
    ).astype(jnp.bfloat16)
    kv_grad = lax.psum_scatter(kv_grad, "ctx", scatter_dimension=1, tiled=True).astype(jnp.float32)
    key_grad_rot, value_grad = kv_grad[:, :, :kv_width], kv_grad[:, :, kv_width:]
    query_grad = (
        rotate_back(query_grad_rot.reshape(row_count, HEADS, HD), cosine, sine)
        .reshape(row_count, q_width)
        .astype(jnp.bfloat16)
    )
    key_grad = (
        rotate_back(key_grad_rot.reshape(row_count, KV_HEADS, HD), cosine, sine)
        .reshape(row_count, kv_width)
        .astype(jnp.bfloat16)
    )
    value_grad = value_grad.reshape(row_count, kv_width).astype(jnp.bfloat16)
    proj_grad = jnp.concatenate([query_grad, key_grad, value_grad], axis=1)
    grad_norm_one = right_dot(proj_grad, proj_full)
    source_back, attn_gain_part = norm_backward(source, attn_factor, gain_one, grad_norm_one)
    hidden_grad = (grad_resid + source_back).reshape(batches, length, D)

    bias_part = jnp.sum(proj_grad.astype(jnp.float32), axis=0)
    kv_bias = bias_part[q_width:].reshape(2, size, per).transpose(1, 0, 2).reshape(size, 2 * per)
    kv_bias = jnp.pad(kv_bias, ((0, 0), (0, shard_rows - 2 * per))).reshape(-1)
    columns = jnp.stack([attn_gain_part, bias_part[:q_width], ffn_gain_part, kv_bias], axis=1)
    part = jnp.concatenate(
        [outer_add(normed, proj_grad), columns, jnp.zeros((D, 124), jnp.float32)], axis=1
    ).astype(jnp.bfloat16)
    proj_sum = lax.psum_scatter(part, both, scatter_dimension=0, tiled=True).astype(jnp.float32)
    w_out_grad = lax.psum_scatter(
        outer_add(grad_attn, mixed).astype(jnp.bfloat16), both, scatter_dimension=0, tiled=True
    ).astype(jnp.float32)
    w_query_grad = proj_sum[:, :q_width]
    w_key_grad = proj_sum[:, q_width : q_width + kv_width]
    w_value_grad = proj_sum[:, q_width + kv_width : proj_width]
    small = proj_sum[:, proj_width : proj_width + 4]
    return (
        result,
        hidden_grad,
        small[:, 0],
        w_query_grad,
        small[:, 1],
        w_key_grad,
        small[:per, 3],
        w_value_grad,
        small[per : 2 * per, 3],
        w_out_grad,
        small[:, 2],
        w_gate_grad,
        w_up_grad,
        w_down_grad,
    )


def general_device(
    hidden,
    cotangent,
    span_order,
    attn_gain,
    w_query,
    b_query,
    w_key,
    b_key,
    w_value,
    b_value,
    w_out,
    ffn_gain,
    w_gate,
    w_up,
    w_down,
):
    ctx_size = lax.axis_size("ctx")
    ctx_rank = lax.axis_index("ctx")
    batches = hidden.shape[0]
    length = hidden.shape[1]
    span_len = length // 2
    seq_len = length * ctx_size
    row_count = batches * length
    groups = HEADS // KV_HEADS
    shard_rows = w_query.shape[0]
    head_scale = HD ** (-0.5)
    kv_width = KV_HEADS * HD
    q_width = HEADS * HD
    places = jnp.arange(seq_len, dtype=jnp.int32)
    every_pos = jnp.repeat(span_order, span_len, axis=1) * span_len + places[None, :] % span_len
    local_pos = lax.dynamic_slice_in_dim(every_pos, ctx_rank * length, length, 1)
    cosine, sine = angles_for(local_pos.reshape(row_count), HD)
    allowed = (every_pos[:, None, :] <= local_pos[:, :, None])[:, None, None]
    attn_full = (
        lax.all_gather(attn_gain, ("dp", "ctx"), axis=0, tiled=True),
        lax.all_gather(w_query, ("dp", "ctx"), axis=0, tiled=True),
        lax.all_gather(w_key, ("dp", "ctx"), axis=0, tiled=True),
        lax.all_gather(w_value, ("dp", "ctx"), axis=0, tiled=True),
        lax.all_gather(w_out, ("dp", "ctx"), axis=0, tiled=True),
        lax.all_gather(b_query, ("dp", "ctx"), axis=0, tiled=True),
        lax.all_gather(b_key, ("dp", "ctx"), axis=0, tiled=True),
        lax.all_gather(b_value, ("dp", "ctx"), axis=0, tiled=True),
    )
    gain_one = attn_full[0].astype(jnp.float32)
    source = hidden.reshape(row_count, D).astype(jnp.float32)
    attn_factor, normed = norm_forward(source, gain_one)
    query_raw = plain_dot(normed, attn_full[1]) + attn_full[5].astype(jnp.float32)
    key_raw = plain_dot(normed, attn_full[2]) + attn_full[6].astype(jnp.float32)
    value_low = (plain_dot(normed, attn_full[3]) + attn_full[7].astype(jnp.float32)).astype(
        jnp.bfloat16
    )
    query_rot = rotate(query_raw.reshape(row_count, HEADS, HD), cosine, sine).astype(jnp.bfloat16)
    query_rot = query_rot.reshape(batches, length, KV_HEADS, groups, HD)
    key_rot = rotate(key_raw.reshape(row_count, KV_HEADS, HD), cosine, sine).astype(jnp.bfloat16)
    key_rot = key_rot.reshape(batches, length, kv_width)
    key_all, value_all = (
        lax.all_gather(key_rot, "ctx", axis=1, tiled=True),
        lax.all_gather(value_low.reshape(batches, length, kv_width), "ctx", axis=1, tiled=True),
    )
    key_all = key_all.reshape(batches, seq_len, KV_HEADS, HD)
    value_all = value_all.reshape(batches, seq_len, KV_HEADS, HD)
    scores = (
        jnp.einsum("bqkgd,bskd->bkgqs", query_rot, key_all, preferred_element_type=jnp.float32)
        * head_scale
    )
    masked = jnp.where(allowed, scores, masked_fill)
    row_max = jnp.max(masked, axis=-1, keepdims=True)
    expo = jnp.exp(masked - row_max)
    expo_sum = jnp.sum(expo, axis=-1, keepdims=True)
    log_total = row_max + jnp.log(expo_sum)
    attend = (expo / expo_sum).astype(jnp.bfloat16)
    mixed = jnp.einsum("bkgqs,bskd->bqkgd", attend, value_all, preferred_element_type=jnp.float32)
    mixed = mixed.reshape(row_count, q_width).astype(jnp.bfloat16)
    resid = source + right_dot(mixed, attn_full[4])
    ffn_full = (
        lax.all_gather(ffn_gain, ("dp", "ctx"), axis=0, tiled=True),
        lax.all_gather(w_gate, ("dp", "ctx"), axis=0, tiled=True),
        lax.all_gather(w_up, ("dp", "ctx"), axis=0, tiled=True),
        lax.all_gather(w_down, ("dp", "ctx"), axis=0, tiled=True),
    )
    gain_two = ffn_full[0].astype(jnp.float32)
    ffn_factor, normed_two = norm_forward(resid, gain_two)
    gate_pre = plain_dot(normed_two, ffn_full[1])
    up_pre = plain_dot(normed_two, ffn_full[2])
    sigmoid_gate = jax.nn.sigmoid(gate_pre)
    silu_gate = gate_pre * sigmoid_gate
    act = (silu_gate * up_pre).astype(jnp.bfloat16)
    output = resid + right_dot(act, ffn_full[3])
    result = output.astype(jnp.bfloat16).reshape(batches, length, D)
    ffn_back = (
        lax.all_gather(ffn_gain, ("dp", "ctx"), axis=0, tiled=True),
        lax.all_gather(w_gate, ("dp", "ctx"), axis=0, tiled=True),
        lax.all_gather(w_up, ("dp", "ctx"), axis=0, tiled=True),
        lax.all_gather(w_down, ("dp", "ctx"), axis=0, tiled=True),
    )
    grad_out = cotangent.reshape(row_count, D)
    grad_plain = grad_out.astype(jnp.float32)
    grad_act = plain_dot(grad_out, ffn_back[3])
    grad_gate = (grad_act * up_pre * sigmoid_gate * (1.0 + gate_pre * (1.0 - sigmoid_gate))).astype(
        jnp.bfloat16
    )
    grad_up = (grad_act * silu_gate).astype(jnp.bfloat16)
    pieces = (
        lax.all_gather(normed_two, "ctx", axis=0, tiled=True),
        lax.all_gather(grad_gate, "ctx", axis=0, tiled=True),
        lax.all_gather(grad_up, "ctx", axis=0, tiled=True),
        lax.all_gather(act, "ctx", axis=0, tiled=True),
        lax.all_gather(grad_out, "ctx", axis=0, tiled=True),
    )
    picked_in = owned_columns(pieces[0], ctx_size, ctx_rank, shard_rows)
    picked_out = owned_columns(pieces[4], ctx_size, ctx_rank, shard_rows)
    w_gate_grad, w_up_grad, w_down_grad = (
        lax.psum_scatter(
            outer_add(picked_in, pieces[1]).astype(jnp.bfloat16),
            "dp",
            scatter_dimension=0,
            tiled=True,
        ).astype(jnp.float32),
        lax.psum_scatter(
            outer_add(picked_in, pieces[2]).astype(jnp.bfloat16),
            "dp",
            scatter_dimension=0,
            tiled=True,
        ).astype(jnp.float32),
        lax.psum_scatter(
            outer_add(picked_out, pieces[3]).astype(jnp.bfloat16),
            "dp",
            scatter_dimension=0,
            tiled=True,
        ).astype(jnp.float32),
    )
    grad_norm_two = right_dot(grad_gate, ffn_back[1]) + right_dot(grad_up, ffn_back[2])
    resid_back, ffn_gain_part = norm_backward(resid, ffn_factor, gain_two, grad_norm_two)
    grad_resid = grad_plain + resid_back
    attn_back = (
        lax.all_gather(attn_gain, ("dp", "ctx"), axis=0, tiled=True),
        lax.all_gather(w_query, ("dp", "ctx"), axis=0, tiled=True),
        lax.all_gather(w_key, ("dp", "ctx"), axis=0, tiled=True),
        lax.all_gather(w_value, ("dp", "ctx"), axis=0, tiled=True),
        lax.all_gather(w_out, ("dp", "ctx"), axis=0, tiled=True),
        lax.all_gather(b_query, ("dp", "ctx"), axis=0, tiled=True),
        lax.all_gather(b_key, ("dp", "ctx"), axis=0, tiled=True),
        lax.all_gather(b_value, ("dp", "ctx"), axis=0, tiled=True),
    )
    grad_attn = grad_resid.astype(jnp.bfloat16)
    grad_mixed = plain_dot(grad_attn, attn_back[4]).astype(jnp.bfloat16)
    grad_mixed = grad_mixed.reshape(batches, length, KV_HEADS, groups, HD)
    scores = (
        jnp.einsum("bqkgd,bskd->bkgqs", query_rot, key_all, preferred_element_type=jnp.float32)
        * head_scale
    )
    masked = jnp.where(allowed, scores, masked_fill)
    attend_full = jnp.exp(masked - log_total)
    attend = attend_full.astype(jnp.bfloat16)
    grad_attend = jnp.einsum(
        "bqkgd,bskd->bkgqs", grad_mixed, value_all, preferred_element_type=jnp.float32
    )
    value_grad_all = jnp.einsum(
        "bkgqs,bqkgd->bskd", attend, grad_mixed, preferred_element_type=jnp.float32
    )
    delta = jnp.sum(grad_attend * attend_full, axis=-1, keepdims=True)
    grad_scores = (attend_full * (grad_attend - delta)).astype(jnp.bfloat16)
    query_grad_rot = (
        jnp.einsum("bkgqs,bskd->bqkgd", grad_scores, key_all, preferred_element_type=jnp.float32)
        * head_scale
    )
    key_grad_all = (
        jnp.einsum("bkgqs,bqkgd->bskd", grad_scores, query_rot, preferred_element_type=jnp.float32)
        * head_scale
    )
    key_grad_rot, value_grad = (
        lax.psum_scatter(
            key_grad_all.reshape(batches, seq_len, kv_width), "ctx", scatter_dimension=1, tiled=True
        ),
        lax.psum_scatter(
            value_grad_all.reshape(batches, seq_len, kv_width),
            "ctx",
            scatter_dimension=1,
            tiled=True,
        ),
    )
    query_grad = (
        rotate_back(query_grad_rot.reshape(row_count, HEADS, HD), cosine, sine)
        .reshape(row_count, q_width)
        .astype(jnp.bfloat16)
    )
    key_grad = (
        rotate_back(key_grad_rot.reshape(row_count, KV_HEADS, HD), cosine, sine)
        .reshape(row_count, kv_width)
        .astype(jnp.bfloat16)
    )
    value_grad = value_grad.reshape(row_count, kv_width).astype(jnp.bfloat16)
    proj_grad = jnp.concatenate([query_grad, key_grad, value_grad], axis=1)
    pieces = (
        lax.all_gather(normed, "ctx", axis=0, tiled=True),
        lax.all_gather(proj_grad, "ctx", axis=0, tiled=True),
        lax.all_gather(grad_attn, "ctx", axis=0, tiled=True),
        lax.all_gather(mixed, "ctx", axis=0, tiled=True),
    )
    picked_in = owned_columns(pieces[0], ctx_size, ctx_rank, shard_rows)
    picked_out = owned_columns(pieces[2], ctx_size, ctx_rank, shard_rows)
    proj_sum, w_out_grad = (
        lax.psum_scatter(
            outer_add(picked_in, pieces[1]).astype(jnp.bfloat16),
            "dp",
            scatter_dimension=0,
            tiled=True,
        ).astype(jnp.float32),
        lax.psum_scatter(
            outer_add(picked_out, pieces[3]).astype(jnp.bfloat16),
            "dp",
            scatter_dimension=0,
            tiled=True,
        ).astype(jnp.float32),
    )
    grad_norm_one = (
        right_dot(query_grad, attn_back[1])
        + right_dot(key_grad, attn_back[2])
        + right_dot(value_grad, attn_back[3])
    )
    source_back, attn_gain_part = norm_backward(source, attn_factor, gain_one, grad_norm_one)
    hidden_grad = (grad_resid + source_back).reshape(batches, length, D)
    query_bias_part = jnp.sum(query_grad.astype(jnp.float32), axis=0)
    key_bias_part = jnp.sum(key_grad.astype(jnp.float32), axis=0)
    value_bias_part = jnp.sum(value_grad.astype(jnp.float32), axis=0)
    small_sums = (
        lax.psum_scatter(attn_gain_part, ("dp", "ctx"), scatter_dimension=0, tiled=True),
        lax.psum_scatter(query_bias_part, ("dp", "ctx"), scatter_dimension=0, tiled=True),
        lax.psum_scatter(key_bias_part, ("dp", "ctx"), scatter_dimension=0, tiled=True),
        lax.psum_scatter(value_bias_part, ("dp", "ctx"), scatter_dimension=0, tiled=True),
        lax.psum_scatter(ffn_gain_part, ("dp", "ctx"), scatter_dimension=0, tiled=True),
    )
    w_query_grad = proj_sum[:, :q_width]
    w_key_grad = proj_sum[:, q_width : q_width + kv_width]
    w_value_grad = proj_sum[:, q_width + kv_width :]
    return (
        result,
        hidden_grad,
        small_sums[0],
        w_query_grad,
        small_sums[1],
        w_key_grad,
        small_sums[2],
        w_value_grad,
        small_sums[3],
        w_out_grad,
        small_sums[4],
        w_gate_grad,
        w_up_grad,
        w_down_grad,
    )


def solution(mesh):
    placed = (
        P("dp", "ctx", None),
        P("dp", "ctx", None),
        P("dp", None),
        P(("dp", "ctx")),
        P(("dp", "ctx"), None),
        P(("dp", "ctx")),
        P(("dp", "ctx"), None),
        P(("dp", "ctx")),
        P(("dp", "ctx"), None),
        P(("dp", "ctx")),
        P(("dp", "ctx"), None),
        P(("dp", "ctx")),
        P(("dp", "ctx"), None),
        P(("dp", "ctx"), None),
        P(("dp", "ctx"), None),
    )
    return jax.shard_map(
        fast_device if fits(mesh) else general_device,
        mesh=mesh,
        in_specs=placed,
        out_specs=(
            P("dp", "ctx", None),
            P("dp", "ctx", None),
            P(("dp", "ctx")),
            P(("dp", "ctx"), None),
            P(("dp", "ctx")),
            P(("dp", "ctx"), None),
            P(("dp", "ctx")),
            P(("dp", "ctx"), None),
            P(("dp", "ctx")),
            P(("dp", "ctx"), None),
            P(("dp", "ctx")),
            P(("dp", "ctx"), None),
            P(("dp", "ctx"), None),
            P(("dp", "ctx"), None),
        ),
        check_vma=False,
    )
```

```python
import functools

import jax
import jax.numpy as jnp
from jax import lax
from jax.experimental import pallas as pl
from jax.experimental.pallas import tpu as pltpu
from jax.sharding import PartitionSpec as P

D = 1536
HEADS = 12
KV_HEADS = 2
HD = 128


norm_eps = 1e-06
rope_base = 10000.0
masked_fill = -1e30


def angles_for(places, width):
    half = width // 2
    freqs = rope_base ** (-(jnp.arange(half, dtype=jnp.float32) * 2.0 / width))
    angles = places.astype(jnp.float32)[:, None] * freqs[None, :]
    return (jnp.cos(angles)[:, None, :], jnp.sin(angles)[:, None, :])


def rotate(values, cosine, sine):
    half = values.shape[-1] // 2
    first = values[..., :half]
    second = values[..., half:]
    return jnp.concatenate(
        [first * cosine - second * sine, second * cosine + first * sine], axis=-1
    )


def rotate_back(values, cosine, sine):
    half = values.shape[-1] // 2
    first = values[..., :half]
    second = values[..., half:]
    return jnp.concatenate(
        [first * cosine + second * sine, second * cosine - first * sine], axis=-1
    )


def norm_forward(source, gain):
    factor = lax.rsqrt(jnp.mean(source * source, axis=-1, keepdims=True) + norm_eps)
    return (factor, (source * factor * gain).astype(jnp.bfloat16))


def norm_backward(source, factor, gain, grad_normed):
    unit = source * factor
    gain_grad = jnp.sum(grad_normed * unit, axis=0)
    scaled = grad_normed * gain
    source_grad = factor * (scaled - unit * jnp.mean(scaled * unit, axis=-1, keepdims=True))
    return (source_grad, gain_grad)


def right_dot(left, weight):
    return jnp.einsum("rf,df->rd", left, weight, preferred_element_type=jnp.float32)


def plain_dot(left, weight):
    return jnp.dot(left, weight, preferred_element_type=jnp.float32)


def owned_columns(values, ctx_size, ctx_rank, shard_rows):
    rows = values.shape[0]
    blocks = values.shape[1] // (shard_rows * ctx_size)
    shaped = values.reshape(rows, blocks, ctx_size, shard_rows)
    picked = lax.dynamic_index_in_dim(shaped, ctx_rank, axis=2, keepdims=False)
    return picked.reshape(rows, blocks * shard_rows)


def outer_add(left, right):
    return jnp.einsum("rc,rf->cf", left, right, preferred_element_type=jnp.float32)


MESH = pl.DeviceIdType.MESH


def flip(index, mask):
    for bit in (1, 2, 4, 8, 16):
        if mask & bit:
            index = index + bit - 2 * bit * ((index // bit) % 2)
    return index


def either(a, b):
    return a + b - 2 * a * b


def dot(a, b, dims):
    return lax.dot_general(a, b, (dims, ((), ())), preferred_element_type=jnp.float32)


def ffn_kernel(
    ctx_size, n_own, go_all, big,
    hr, dgu, dd,
    wgu, wd, nt, go, ggu, act, csend, crecv, hpart, stage,
    w_sem, io_sem, n_send, n_recv, f_send, f_recv, c_send, c_recv, o_send, o_recv, st_sem,
):
    dp = lax.axis_index("dp")
    ctx = lax.axis_index("ctx")
    me = dp * ctx_size + ctx
    y, x, c = dp // 4, (dp // 2) % 2, dp % 2
    h, p = ctx // 2, ctx % 2
    width = wd.shape[1]
    shard = dgu.shape[4]
    rows, model = n_own.shape

    def at(index):
        return (index // ctx_size, index % ctx_size)

    core = at(flip(me, 4))

    def partner(o):
        return (dp + (o // 2) * 4 * (1 - 2 * y), ctx + (o % 2) * (1 - 2 * p))

    barrier = pltpu.get_barrier_semaphore()
    for device in (core, partner(1), partner(2), partner(3)):
        pl.semaphore_signal(barrier, inc=1, device_id=device, device_id_type=MESH)

    load_n = pltpu.make_async_copy(n_own, nt.at[0], io_sem.at[0])
    load_n.start()
    load_go = pltpu.make_async_copy(go_all, go, io_sem.at[1])
    load_go.start()
    load_gu = pltpu.make_async_copy(big.at[:, pl.ds(0, 2 * width)], wgu, w_sem.at[0])
    load_gu.start()
    load_d = pltpu.make_async_copy(big.at[:, pl.ds(2 * width, width)], wd, w_sem.at[1])
    load_d.start()

    pl.semaphore_wait(barrier, 4)
    load_n.wait()

    def push_n(slot, dst, device, send, recv):
        return pltpu.make_async_remote_copy(
            src_ref=nt.at[slot], dst_ref=nt.at[dst], send_sem=send, recv_sem=recv,
            device_id=device, device_id_type=MESH,
        )

    first = [push_n(0, 2 * o, partner(o), n_send.at[o], n_recv.at[o]) for o in (1, 2, 3)]
    for copy in first:
        copy.start()
    push_n(0, 1, core, f_send.at[0], f_recv.at[0]).start()
    load_gu.wait()
    load_d.wait()
    load_go.wait()

    def tile(slot):
        gu = dot(nt[slot], wgu[...], ((1,), (0,)))
        ga = dot(go[slot], wd[...], ((1,), (0,)))
        gate, up = gu[:, :width], gu[:, width:]
        sig = 1.0 / (1.0 + jnp.exp(-gate))
        silu = gate * sig
        act[slot] = (silu * up).astype(jnp.bfloat16)
        ggu[slot, :, pl.ds(0, width)] = (ga * up * sig * (1.0 + gate * (1.0 - sig))).astype(jnp.bfloat16)
        ggu[slot, :, pl.ds(width, width)] = (ga * silu).astype(jnp.bfloat16)
        grad = dot(ggu[slot], wgu[...], ((1,), (1,)))
        out = dot(act[slot], wd[...], ((1,), (1,)))
        return (grad.astype(jnp.bfloat16), out.astype(jnp.bfloat16))

    def cross(o):
        return pltpu.make_async_remote_copy(
            src_ref=csend, dst_ref=crecv.at[o % 2], send_sem=c_send, recv_sem=c_recv.at[o % 2],
            device_id=core, device_id_type=MESH,
        )

    def final(o):
        return pltpu.make_async_remote_copy(
            src_ref=hpart.at[o], dst_ref=hr.at[o], send_sem=o_send.at[o], recv_sem=o_recv.at[o],
            device_id=partner(o), device_id_type=MESH,
        )

    keep = pltpu.make_async_copy(hpart.at[0], hr.at[0], io_sem.at[0])

    def combine(o):
        cross(o).wait_recv()
        total = hpart[o].astype(jnp.float32) + crecv[o % 2].astype(jnp.float32)
        hpart[o] = total.astype(jnp.bfloat16)

    def step(o, carry):
        @pl.when(o > 0)
        def _():
            push_n(0, 2 * o, partner(o), n_send.at[o], n_recv.at[o]).wait_recv()
            push_n(2 * o, 2 * o + 1, core, f_send.at[o], f_recv.at[o]).start()

        grad, out = tile(2 * o)
        hpart[o, 0] = grad
        hpart[o, 1] = out

        @pl.when(o > 0)
        def _():
            combine(o - 1)

        @pl.when(o == 1)
        def _():
            keep.start()

        @pl.when(o > 1)
        def _():
            final(o - 1).start()

        push_n(2 * o, 2 * o + 1, core, f_send.at[o], f_recv.at[o]).wait_recv()
        grad, out = tile(2 * o + 1)

        @pl.when(o > 0)
        def _():
            cross(o).wait_send()

        csend[0] = grad
        csend[1] = out
        cross(o).start()
        return carry

    lax.fori_loop(0, 4, step, 0)
    combine(3)
    final(3).start()

    def stage_wait(slot):
        pltpu.make_async_copy(stage.at[slot], stage.at[slot], st_sem.at[slot]).wait()

    def weights(q, carry):
        slot = q % 2

        @pl.when(q > 1)
        def _():
            stage_wait(slot)

        chunk = 8 * shard
        cols = pl.ds(pl.multiple_of(q * chunk, chunk), chunk)
        left = nt[:, :, cols].reshape(8 * rows, chunk)
        for half in range(2):
            part = pl.ds(half * width, width)
            right = ggu[:, :, part].reshape(8 * rows, width)
            stage[slot, :, part] = dot(left, right, ((0,), (0,))).astype(jnp.bfloat16)
        left = go[:, :, cols].reshape(8 * rows, chunk)
        right = act[...].reshape(8 * rows, width)
        stage[slot, :, pl.ds(2 * width, width)] = dot(left, right, ((0,), (0,))).astype(jnp.bfloat16)
        yr, xr = either(q // 2, y), either(q % 2, x)
        for j in range(8):
            cr, hrel, pr = either(j // 4, c), either((j // 2) % 2, h), either(j % 2, p)
            block = yr * 4 + cr * 2 + pr
            row = pl.ds(j * shard, shard)
            for half in range(2):
                pltpu.make_async_copy(
                    stage.at[slot, row, pl.ds(half * width, width)], dgu.at[xr, hrel, block, half], st_sem.at[slot]
                ).start()
            pltpu.make_async_copy(
                stage.at[slot, row, pl.ds(2 * width, width)], dd.at[xr, hrel, block], st_sem.at[slot]
            ).start()
        return carry

    lax.fori_loop(0, 4, weights, 0)
    stage_wait(0)
    stage_wait(1)
    keep.wait()
    cross(3).wait_send()
    for copy in first:
        copy.wait_send()
    for o in range(4):
        push_n(2 * o, 2 * o + 1, core, f_send.at[o], f_recv.at[o]).wait_send()
    for o in (1, 2, 3):
        final(o).wait()


def ffn_call(ctx_size, shard, n_own, go_all, big):
    rows, model = n_own.shape
    width = big.shape[1] // 3
    low = jnp.bfloat16
    return pl.pallas_call(
        functools.partial(ffn_kernel, ctx_size),
        out_shape=(
            jax.ShapeDtypeStruct((4, 2, rows, model), low),
            jax.ShapeDtypeStruct((2, 2, 8, 2, shard, width), low),
            jax.ShapeDtypeStruct((2, 2, 8, shard, width), low),
        ),
        in_specs=[pl.BlockSpec(memory_space=pl.ANY)] * 3,
        out_specs=[pl.BlockSpec(memory_space=pl.ANY)] * 3,
        scratch_shapes=[
            pltpu.VMEM((model, 2 * width), low),
            pltpu.VMEM((model, width), low),
            pltpu.VMEM((8, rows, model), low),
            pltpu.VMEM((8, rows, model), low),
            pltpu.VMEM((8, rows, 2 * width), low),
            pltpu.VMEM((8, rows, width), low),
            pltpu.VMEM((2, rows, model), low),
            pltpu.VMEM((2, 2, rows, model), low),
            pltpu.VMEM((4, 2, rows, model), low),
            pltpu.VMEM((2, 8 * shard, 3 * width), low),
            pltpu.SemaphoreType.DMA((2,)),
            pltpu.SemaphoreType.DMA((2,)),
            pltpu.SemaphoreType.DMA((4,)),
            pltpu.SemaphoreType.DMA((4,)),
            pltpu.SemaphoreType.DMA((4,)),
            pltpu.SemaphoreType.DMA((4,)),
            pltpu.SemaphoreType.DMA,
            pltpu.SemaphoreType.DMA((2,)),
            pltpu.SemaphoreType.DMA((4,)),
            pltpu.SemaphoreType.DMA((4,)),
            pltpu.SemaphoreType.DMA((2,)),
        ],
        compiler_params=pltpu.CompilerParams(
            collective_id=1, has_side_effects=True, vmem_limit_bytes=63 << 20
        ),
        name="ffn",
    )(n_own, go_all, big)


def turn(values, cosine, sine):
    return values * cosine + pltpu.roll(values, HD // 2, 1) * sine


def front_kernel(
    ctx_size, hidden, cosine, sine, pos_q, pos_k, spread, packed, w_out, w_gate, w_up, w_down, grad_out,
    normed_o, query_o, kv_o, total_o, mixed_o, resid_o, normed_two_o, small_o, proj_o, out_o, big, go,
    proj, out_w, source, query, kv, mixed, total,
    load_sem, ag_send, ag_recv, core_send, core_recv, big_send, big_recv, go_send, go_recv, kv_send, kv_recv, back_sem,
):
    dp = lax.axis_index("dp")
    ctx = lax.axis_index("ctx")
    me = dp * ctx_size + ctx
    shard, wide = packed.shape
    rows, model = hidden.shape
    width = big.shape[1] // 3
    kv_width = KV_HEADS * HD
    q_width = HEADS * HD
    proj_width = q_width + 2 * kv_width
    groups = HEADS // KV_HEADS

    def at(index):
        return (index // ctx_size, index % ctx_size)

    def block(mask, count=1):
        base = flip(me, mask) // count * count
        return pl.ds(pl.multiple_of(base * shard, shard), shard * count)

    def remote(src, dst, send, recv, mask):
        return pltpu.make_async_remote_copy(
            src_ref=src, dst_ref=dst, send_sem=send, recv_sem=recv, device_id=at(flip(me, mask)), device_id_type=MESH
        )

    def drain(ref, sem):
        pltpu.make_async_copy(ref, ref, sem).wait()

    barrier = pltpu.get_barrier_semaphore()
    partners = (1, 2, 4, 5, 8, 16, 17, 20, 21)
    for mask in partners:
        pl.semaphore_signal(barrier, inc=1, device_id=at(flip(me, mask)), device_id_type=MESH)

    own = (
        pltpu.make_async_copy(packed, proj.at[block(0)], load_sem.at[0]),
        pltpu.make_async_copy(w_out, out_w.at[block(0)], load_sem.at[1]),
    )
    for copy in own:
        copy.start()
    hidden_units = w_gate.shape[1]
    cuts = []
    for k in range(8):
        size = min(width, hidden_units - k * width)
        for n, ref in enumerate((w_gate, w_up, w_down)):
            cuts.append((ref.at[:, pl.ds(k * width, size)], source.at[k, :, pl.ds(n * width, size)]))
            if size < width:
                source[k, :, pl.ds(n * width + size, width - size)] = jnp.zeros((shard, width - size), source.dtype)
    cuts = [pltpu.make_async_copy(a, b, load_sem.at[2 + i]) for i, (a, b) in enumerate(cuts)]
    for copy in cuts:
        copy.start()
    pl.semaphore_wait(barrier, len(partners))
    for copy in own:
        copy.wait()

    pair = ((proj, 0), (out_w, 1))

    def ag(mask, over):
        for ref, n in pair:
            remote(ref.at[block(mask)], ref.at[block(mask)], ag_send.at[n], ag_recv.at[n, mask | over], over).start()

    def ag_wait(mask):
        for ref, n in pair:
            remote(ref.at[block(mask)], ref.at[block(mask)], ag_send.at[n], ag_recv.at[n, mask], 1).wait_recv()

    def group(mask):
        return [
            remote(ref.at[block(mask, 4)], ref.at[block(mask, 4)], core_send.at[n, mask // 8], core_recv.at[n, mask // 8], 4)
            for ref, n in pair
        ]

    def group_wait(mask, n):
        ref = pair[n][0]
        remote(ref.at[block(mask | 4, 4)], ref.at[block(mask | 4, 4)], core_send.at[n, mask // 8], core_recv.at[n, mask // 8], 4).wait_recv()

    for over in (2, 1, 8, 16):
        ag(0, over)

    for copy in cuts:
        copy.wait()
    y, x, c = dp // 4, (dp // 2) % 2, dp % 2
    h, p = ctx // 2, ctx % 2

    def column(mask):
        return either(y, mask // 16) * 4 + either(p, mask % 2) * 2 + either(c, (mask // 4) % 2)

    own_big = pltpu.make_async_copy(source.at[column(0)], big.at[block(0)], load_sem.at[0])
    own_big.start()
    for mask in (4, 1, 16, 5, 20, 17, 21):
        remote(source.at[column(mask)], big.at[block(0)], big_send.at[0], big_recv.at[mask], mask).start()
    first_z = remote(source.at[column(0)], big.at[block(0)], big_send.at[0], big_recv.at[2], 2)
    first_z.start()

    def big_forward(mask, over):
        remote(big.at[block(mask)], big.at[block(mask)], big_send.at[0], big_recv.at[mask | over], over).start()

    def big_wait(mask):
        remote(big.at[block(mask)], big.at[block(mask)], big_send.at[0], big_recv.at[mask], 1).wait_recv()

    ag_wait(1)
    for over in (8, 16):
        ag(1, over)
    ag_wait(8)
    ag(8, 16)
    ag_wait(2)
    for over in (1, 8, 16):
        ag(2, over)
    ag_wait(9)
    ag(9, 16)
    big_wait(4)
    big_forward(4, 2)
    big_wait(1)
    big_forward(1, 2)
    ag_wait(3)
    for over in (8, 16):
        ag(3, over)
    for copy in group(0):
        copy.start()
    ag_wait(10)
    ag(10, 16)
    ag_wait(11)
    ag(11, 16)
    for copy in group(8):
        copy.start()
    remote(source.at[column(0)], big.at[block(0)], big_send.at[0], big_recv.at[8], 8).start()
    for mask in (16, 5, 20, 17, 21):
        big_wait(mask)
        big_forward(mask, 2)
    for mask in (4, 1, 16, 5):
        big_forward(mask, 8)
    for mask in (16, 17, 18, 19):
        ag_wait(mask)
    for copy in group(16):
        copy.start()
    for mask in (24, 25, 26, 27):
        ag_wait(mask)
    for copy in group(24):
        copy.start()
    for mask in (20, 17, 21):
        big_forward(mask, 8)
    own_go = pltpu.make_async_copy(grad_out, go.at[0], load_sem.at[1])
    own_go.start()
    for o, mask in ((1, 1), (2, 16), (3, 17)):
        remote(grad_out, go.at[2 * o], go_send.at[o], go_recv.at[2 * o], mask).start()
    remote(grad_out, go.at[1], go_send.at[0], go_recv.at[1], 4).start()
    for mask in (0, 8, 16, 24):
        group_wait(mask, 0)

    small = jnp.transpose(proj[:, proj_width:].astype(jnp.float32))
    small_o[...] = small[:8]
    kv_bias = dot(small[:8].astype(jnp.bfloat16), spread[...], ((1,), (0,)))[3:4]
    values = hidden[...].astype(jnp.float32)
    factor = lax.rsqrt(jnp.mean(values * values, axis=-1, keepdims=True) + norm_eps)
    normed_o[...] = (values * factor * small[0:1]).astype(jnp.bfloat16)
    cos, sin = cosine[...], sine[...]
    raw = dot(normed_o[...], proj[:, q_width:proj_width], ((1,), (0,))) + kv_bias
    mine = block(0)
    for g in range(KV_HEADS):
        kv[ctx, :, pl.ds(g * HD, HD)] = turn(raw[:, g * HD : (g + 1) * HD], cos, sin).astype(jnp.bfloat16)
    kv[ctx, :, pl.ds(kv_width, kv_width)] = raw[:, kv_width:].astype(jnp.bfloat16)

    def kv_push(mask, over):
        slot = flip(ctx, mask)
        return remote(kv.at[slot], kv.at[slot], kv_send.at[mask | over], kv_recv.at[mask | over], over)

    kv_push(0, 2).start()
    kv_push(0, 1).start()
    for half in range(2):
        part = half * (q_width // 2)
        raw = dot(normed_o[...], proj[:, part : part + q_width // 2], ((1,), (0,)))
        raw = raw + small[1:2, part : part + q_width // 2]
        for i in range(HEADS // 2):
            query[half * (HEADS // 2) + i] = turn(raw[:, i * HD : (i + 1) * HD], cos, sin).astype(jnp.bfloat16)
    big_wait(2)
    big_forward(2, 8)
    kv_push(0, 2).wait_recv()
    kv_push(2, 1).start()
    for mask in (6, 3):
        big_wait(mask)
        big_forward(mask, 8)
    kv_push(0, 1).wait_recv()
    kv_push(2, 1).wait_recv()
    query_back = pltpu.make_async_copy(query, query_o, back_sem.at[0])
    query_back.start()
    kv_back = pltpu.make_async_copy(kv, kv_o, back_sem.at[1])
    kv_back.start()

    def head(n, carry):
        g = n // groups
        keys = kv[:, :, pl.ds(pl.multiple_of(g * HD, HD), HD)].reshape(ctx_size * rows, HD)
        vals = kv[:, :, pl.ds(pl.multiple_of(kv_width + g * HD, HD), HD)].reshape(ctx_size * rows, HD)
        scores = dot(query[n], keys, ((1,), (1,))) * HD ** (-0.5)
        scores = jnp.where(pos_k[...] <= pos_q[...], scores, masked_fill)
        top = jnp.max(scores, axis=-1, keepdims=True)
        expo = jnp.exp(scores - top)
        expo_sum = jnp.sum(expo, axis=-1, keepdims=True)
        attend = (expo / expo_sum).astype(jnp.bfloat16)
        mixed[:, pl.ds(pl.multiple_of(n * HD, HD), HD)] = dot(attend, vals, ((1,), (0,))).astype(jnp.bfloat16)
        total[n] = jnp.broadcast_to(top + jnp.log(expo_sum), (rows, HD))
        return carry

    lax.fori_loop(0, HEADS // 2, head, 0)
    for o, mask in ((1, 1), (2, 16), (3, 17)):
        remote(grad_out, go.at[2 * o], go_send.at[o], go_recv.at[2 * o], mask).wait_recv()
        remote(go.at[2 * o], go.at[2 * o + 1], go_send.at[3 + o], go_recv.at[2 * o + 1], 4).start()
    big_wait(18)
    big_forward(18, 8)
    lax.fori_loop(HEADS // 2, HEADS, head, 0)
    mixed_back = pltpu.make_async_copy(mixed, mixed_o, back_sem.at[2])
    mixed_back.start()
    total_back = pltpu.make_async_copy(total, total_o, back_sem.at[3])
    total_back.start()
    for mask in (0, 8, 16, 24):
        group_wait(mask, 1)
    proj_back = pltpu.make_async_copy(proj, proj_o, back_sem.at[4])
    proj_back.start()
    out_back = pltpu.make_async_copy(out_w, out_o, back_sem.at[5])
    out_back.start()
    resid = hidden[...].astype(jnp.float32) + dot(mixed[...], out_w[...], ((1,), (1,)))
    resid_o[...] = resid
    factor = lax.rsqrt(jnp.mean(resid * resid, axis=-1, keepdims=True) + norm_eps)
    normed_two_o[...] = (resid * factor * small_o[2:3]).astype(jnp.bfloat16)
    for mask in (7, 22, 19, 23):
        big_wait(mask)
        big_forward(mask, 8)

    for mask in (8, 12, 9, 24, 13, 28, 25, 29, 10, 14, 11, 26, 15, 30, 27, 31):
        big_wait(mask)
    own_big.wait()
    own_go.wait()
    sent = 7 + 8 + 8 + 8
    drain(big.at[pl.ds(0, sent * shard)], big_send.at[0])
    for ref, n in pair:
        drain(ref.at[pl.ds(0, 15 * shard)], ag_send.at[n])
        for mask in (0, 8, 16, 24):
            group(mask)[n].wait_send()
    remote(grad_out, go.at[1], go_send.at[0], go_recv.at[1], 4).wait()
    for o, mask in ((1, 1), (2, 16), (3, 17)):
        remote(grad_out, go.at[2 * o], go_send.at[o], go_recv.at[2 * o], mask).wait_send()
        remote(go.at[2 * o], go.at[2 * o + 1], go_send.at[3 + o], go_recv.at[2 * o + 1], 4).wait()
    kv_push(0, 2).wait_send()
    kv_push(0, 1).wait_send()
    kv_push(2, 1).wait_send()
    for copy in (query_back, kv_back, mixed_back, total_back, proj_back, out_back):
        copy.wait()


def front_call(ctx_size, hidden, cosine, sine, pos_q, pos_k, spread, packed, w_out, w_gate, w_up, w_down, grad_out):
    rows, model = hidden.shape
    shard, wide = packed.shape
    kv_width = KV_HEADS * HD
    q_width = HEADS * HD
    width = -(-w_gate.shape[1] // (8 * 128)) * 128
    low, full = jnp.bfloat16, jnp.float32
    vmem = pl.BlockSpec(memory_space=pltpu.VMEM)
    anywhere = pl.BlockSpec(memory_space=pl.ANY)
    shapes = (
        ((rows, model), low, vmem),
        ((HEADS, rows, HD), low, anywhere),
        ((ctx_size, rows, 2 * kv_width), low, anywhere),
        ((HEADS, rows, HD), full, anywhere),
        ((rows, q_width), low, anywhere),
        ((rows, model), full, vmem),
        ((rows, model), low, vmem),
        ((8, model), full, vmem),
        ((model, wide), low, anywhere),
        ((model, q_width), low, anywhere),
        ((model, 3 * width), low, anywhere),
        ((8, rows, model), low, anywhere),
    )
    sem = pltpu.SemaphoreType.DMA
    return pl.pallas_call(
        functools.partial(front_kernel, ctx_size),
        out_shape=tuple(jax.ShapeDtypeStruct(shape, kind) for shape, kind, _ in shapes),
        in_specs=[vmem] * 6 + [anywhere] * 6,
        out_specs=tuple(spec for _, _, spec in shapes),
        scratch_shapes=[
            pltpu.VMEM((model, wide), low),
            pltpu.VMEM((model, q_width), low),
            pltpu.VMEM((8, shard, 3 * width), low),
            pltpu.VMEM((HEADS, rows, HD), low),
            pltpu.VMEM((ctx_size, rows, 2 * kv_width), low),
            pltpu.VMEM((rows, q_width), low),
            pltpu.VMEM((HEADS, rows, HD), full),
            sem((26,)), sem((2,)), sem((2, 32)), sem((2, 4)), sem((2, 4)), sem((1,)), sem((32,)),
            sem((7,)), sem((8,)), sem((4,)), sem((4,)), sem((6,)),
        ],
        compiler_params=pltpu.CompilerParams(
            collective_id=0, has_side_effects=True, vmem_limit_bytes=56 << 20
        ),
        name="front",
    )(hidden, cosine, sine, pos_q, pos_k, spread, packed, w_out, w_gate, w_up, w_down, grad_out)


def permute(value, mask, size):
    return lax.ppermute(value, ("dp", "ctx"), [(i, i ^ mask) for i in range(size)])


def fits(mesh):
    return mesh.shape["dp"] == 8 and mesh.shape["ctx"] == 4


def fast_device(
    hidden,
    cotangent,
    span_order,
    attn_gain,
    w_query,
    b_query,
    w_key,
    b_key,
    w_value,
    b_value,
    w_out,
    ffn_gain,
    w_gate,
    w_up,
    w_down,
):
    ctx_size = lax.axis_size("ctx")
    ctx_rank = lax.axis_index("ctx")
    size = lax.axis_size("dp") * ctx_size
    me = lax.axis_index("dp") * ctx_size + ctx_rank
    batches = hidden.shape[0]
    length = hidden.shape[1]
    span_len = length // 2
    seq_len = length * ctx_size
    row_count = batches * length
    groups = HEADS // KV_HEADS
    shard_rows = w_query.shape[0]
    head_scale = HD ** (-0.5)
    kv_width = KV_HEADS * HD
    q_width = HEADS * HD
    both = ("dp", "ctx")
    piece = -(-w_gate.shape[1] // (8 * 128)) * 128
    hidden_units = w_gate.shape[1]

    col = 2 * (me // 16) + me % 2
    core = (me // 4) % 2
    grad_out = cotangent.reshape(row_count, D)
    places = jnp.arange(seq_len, dtype=jnp.int32)
    every_pos = jnp.repeat(span_order, span_len, axis=1) * span_len + places[None, :] % span_len
    local_pos = lax.dynamic_slice_in_dim(every_pos, ctx_rank * length, length, 1)
    cosine, sine = angles_for(local_pos.reshape(row_count), HD)
    cos_full = jnp.concatenate([cosine[:, 0], cosine[:, 0]], axis=1)
    sin_full = jnp.concatenate([-sine[:, 0], sine[:, 0]], axis=1)
    allowed = every_pos.reshape(1, seq_len) <= local_pos.reshape(length, 1)

    gains = jnp.stack([attn_gain, b_query, ffn_gain], axis=1)
    per = b_key.shape[0]
    pair = jnp.pad(jnp.concatenate([b_key, b_value]), (0, shard_rows - 2 * per))
    packed = jnp.concatenate(
        [w_query, w_key, w_value, gains, pair[:, None], jnp.zeros((shard_rows, 124), jnp.bfloat16)], axis=1
    )
    proj_width = q_width + 2 * kv_width
    unit = jnp.arange(2 * kv_width)
    unit = unit % kv_width // per * shard_rows + unit // kv_width * per + unit % per
    spread = (jnp.arange(D)[:, None] == unit[None, :]).astype(jnp.bfloat16)
    source = hidden.reshape(row_count, D)
    normed, query_heads, key_value, log_total, mixed, resid, normed_two, small, proj_full, out_full, big, go_all = front_call(
        ctx_size, source, cos_full, sin_full, local_pos.reshape(length, 1), every_pos.reshape(1, seq_len), spread,
        packed, w_out, w_gate, w_up, w_down, grad_out,
    )
    source = source.astype(jnp.float32)
    gain_one, gain_two = small[0], small[2]
    attn_factor = lax.rsqrt(jnp.mean(source * source, axis=-1, keepdims=True) + norm_eps)
    ffn_factor = lax.rsqrt(jnp.mean(resid * resid, axis=-1, keepdims=True) + norm_eps)
    proj_full = proj_full[:, :proj_width]
    query_heads = query_heads.reshape(KV_HEADS, groups, length, HD)
    log_total = log_total[:, :, :1].reshape(KV_HEADS, groups, length, 1)
    key_value = key_value.reshape(seq_len, 2, KV_HEADS, HD)
    key_all, value_all = key_value[:, 0], key_value[:, 1]

    tiles, gu_grad, d_grad = ffn_call(ctx_size, shard_rows, normed_two, go_all, big)
    sums = jnp.sum(tiles.astype(jnp.float32), axis=0)
    grad_norm_two = sums[0]
    result = (resid + sums[1]).astype(jnp.bfloat16).reshape(batches, length, D)

    def fold(part):
        high = permute(part[1, 1], 8, size)
        low_part = permute(part[1, 0], 8, size)
        far = (part[0, 1].astype(jnp.float32) + high.astype(jnp.float32)).astype(jnp.bfloat16)
        far = permute(far, 2, size)
        near = part[0, 0].astype(jnp.float32) + low_part.astype(jnp.float32)
        return (near + far.astype(jnp.float32)).astype(jnp.bfloat16)

    d_sum = fold(d_grad)
    gu_sum = fold(gu_grad)
    whole_grad = jnp.concatenate([gu_sum, d_sum[:, None]], axis=1)
    whole_grad = whole_grad.reshape(2, 2, 2, 3, shard_rows, piece)
    parts = []
    for mask in (0, 1, 16, 17):
        part = whole_grad[mask // 16, :, mask % 2]
        parts.append(permute(part, mask, size) if mask else part)
    parts = jnp.stack(parts)
    theirs = permute(parts[:, 1], 4, size)
    ordered = jnp.stack([parts[:, 0], theirs], axis=0)
    ordered = ordered[jnp.bitwise_xor(jnp.arange(2), core)]
    ordered = ordered[:, jnp.bitwise_xor(jnp.arange(4), col)]
    flat = ordered.transpose(2, 3, 1, 0, 4).reshape(3, shard_rows, 8 * piece)[:, :, :hidden_units]
    flat = flat.astype(jnp.float32)
    w_gate_grad, w_up_grad, w_down_grad = flat[0], flat[1], flat[2]

    grad_plain = grad_out.astype(jnp.float32)
    resid_back, ffn_gain_part = norm_backward(resid, ffn_factor, gain_two, grad_norm_two)
    grad_resid = grad_plain + resid_back
    grad_attn = grad_resid.astype(jnp.bfloat16)
    grad_mixed = plain_dot(grad_attn, out_full).astype(jnp.bfloat16)
    grad_mixed = grad_mixed.reshape(length, KV_HEADS, groups, HD).transpose(1, 2, 0, 3)
    scores = (
        jnp.einsum("kgqd,skd->kgqs", query_heads, key_all, preferred_element_type=jnp.float32) * head_scale
    )
    masked = jnp.where(allowed, scores, masked_fill)
    attend_full = jnp.exp(masked - log_total)
    attend = attend_full.astype(jnp.bfloat16)
    grad_attend = jnp.einsum("kgqd,skd->kgqs", grad_mixed, value_all, preferred_element_type=jnp.float32)
    value_grad_all = jnp.einsum("kgqs,kgqd->skd", attend, grad_mixed, preferred_element_type=jnp.float32)
    delta = jnp.sum(grad_attend * attend_full, axis=-1, keepdims=True)
    grad_scores = (attend_full * (grad_attend - delta)).astype(jnp.bfloat16)
    query_grad_rot = (
        jnp.einsum("kgqs,skd->qkgd", grad_scores, key_all, preferred_element_type=jnp.float32) * head_scale
    )
    key_grad_all = (
        jnp.einsum("kgqs,kgqd->skd", grad_scores, query_heads, preferred_element_type=jnp.float32) * head_scale
    )
    kv_grad = jnp.concatenate(
        [key_grad_all.reshape(batches, seq_len, kv_width), value_grad_all.reshape(batches, seq_len, kv_width)],
        axis=2,
    ).astype(jnp.bfloat16)
    kv_grad = lax.psum_scatter(kv_grad, "ctx", scatter_dimension=1, tiled=True).astype(jnp.float32)
    key_grad_rot, value_grad = kv_grad[:, :, :kv_width], kv_grad[:, :, kv_width:]
    query_grad = (
        rotate_back(query_grad_rot.reshape(row_count, HEADS, HD), cosine, sine)
        .reshape(row_count, q_width)
        .astype(jnp.bfloat16)
    )
    key_grad = (
        rotate_back(key_grad_rot.reshape(row_count, KV_HEADS, HD), cosine, sine)
        .reshape(row_count, kv_width)
        .astype(jnp.bfloat16)
    )
    value_grad = value_grad.reshape(row_count, kv_width).astype(jnp.bfloat16)
    proj_grad = jnp.concatenate([query_grad, key_grad, value_grad], axis=1)
    grad_norm_one = right_dot(proj_grad, proj_full)
    source_back, attn_gain_part = norm_backward(source, attn_factor, gain_one, grad_norm_one)
    hidden_grad = (grad_resid + source_back).reshape(batches, length, D)

    bias_part = jnp.sum(proj_grad.astype(jnp.float32), axis=0)
    kv_bias = bias_part[q_width:].reshape(2, size, per).transpose(1, 0, 2).reshape(size, 2 * per)
    kv_bias = jnp.pad(kv_bias, ((0, 0), (0, shard_rows - 2 * per))).reshape(-1)
    columns = jnp.stack([attn_gain_part, bias_part[:q_width], ffn_gain_part, kv_bias], axis=1)
    part = jnp.concatenate(
        [outer_add(normed, proj_grad), columns, jnp.zeros((D, 124), jnp.float32)], axis=1
    ).astype(jnp.bfloat16)
    proj_sum = lax.psum_scatter(part, both, scatter_dimension=0, tiled=True).astype(jnp.float32)
    w_out_grad = lax.psum_scatter(
        outer_add(grad_attn, mixed).astype(jnp.bfloat16), both, scatter_dimension=0, tiled=True
    ).astype(jnp.float32)
    w_query_grad = proj_sum[:, :q_width]
    w_key_grad = proj_sum[:, q_width : q_width + kv_width]
    w_value_grad = proj_sum[:, q_width + kv_width : proj_width]
    small = proj_sum[:, proj_width : proj_width + 4]
    return (
        result,
        hidden_grad,
        small[:, 0],
        w_query_grad,
        small[:, 1],
        w_key_grad,
        small[:per, 3],
        w_value_grad,
        small[per : 2 * per, 3],
        w_out_grad,
        small[:, 2],
        w_gate_grad,
        w_up_grad,
        w_down_grad,
    )


def general_device(
    hidden,
    cotangent,
    span_order,
    attn_gain,
    w_query,
    b_query,
    w_key,
    b_key,
    w_value,
    b_value,
    w_out,
    ffn_gain,
    w_gate,
    w_up,
    w_down,
):
    ctx_size = lax.axis_size("ctx")
    ctx_rank = lax.axis_index("ctx")
    batches = hidden.shape[0]
    length = hidden.shape[1]
    span_len = length // 2
    seq_len = length * ctx_size
    row_count = batches * length
    groups = HEADS // KV_HEADS
    shard_rows = w_query.shape[0]
    head_scale = HD ** (-0.5)
    kv_width = KV_HEADS * HD
    q_width = HEADS * HD
    places = jnp.arange(seq_len, dtype=jnp.int32)
    every_pos = jnp.repeat(span_order, span_len, axis=1) * span_len + places[None, :] % span_len
    local_pos = lax.dynamic_slice_in_dim(every_pos, ctx_rank * length, length, 1)
    cosine, sine = angles_for(local_pos.reshape(row_count), HD)
    allowed = (every_pos[:, None, :] <= local_pos[:, :, None])[:, None, None]
    attn_full = (
        lax.all_gather(attn_gain, ("dp", "ctx"), axis=0, tiled=True),
        lax.all_gather(w_query, ("dp", "ctx"), axis=0, tiled=True),
        lax.all_gather(w_key, ("dp", "ctx"), axis=0, tiled=True),
        lax.all_gather(w_value, ("dp", "ctx"), axis=0, tiled=True),
        lax.all_gather(w_out, ("dp", "ctx"), axis=0, tiled=True),
        lax.all_gather(b_query, ("dp", "ctx"), axis=0, tiled=True),
        lax.all_gather(b_key, ("dp", "ctx"), axis=0, tiled=True),
        lax.all_gather(b_value, ("dp", "ctx"), axis=0, tiled=True),
    )
    gain_one = attn_full[0].astype(jnp.float32)
    source = hidden.reshape(row_count, D).astype(jnp.float32)
    attn_factor, normed = norm_forward(source, gain_one)
    query_raw = plain_dot(normed, attn_full[1]) + attn_full[5].astype(jnp.float32)
    key_raw = plain_dot(normed, attn_full[2]) + attn_full[6].astype(jnp.float32)
    value_low = (plain_dot(normed, attn_full[3]) + attn_full[7].astype(jnp.float32)).astype(
        jnp.bfloat16
    )
    query_rot = rotate(query_raw.reshape(row_count, HEADS, HD), cosine, sine).astype(jnp.bfloat16)
    query_rot = query_rot.reshape(batches, length, KV_HEADS, groups, HD)
    key_rot = rotate(key_raw.reshape(row_count, KV_HEADS, HD), cosine, sine).astype(jnp.bfloat16)
    key_rot = key_rot.reshape(batches, length, kv_width)
    key_all, value_all = (
        lax.all_gather(key_rot, "ctx", axis=1, tiled=True),
        lax.all_gather(value_low.reshape(batches, length, kv_width), "ctx", axis=1, tiled=True),
    )
    key_all = key_all.reshape(batches, seq_len, KV_HEADS, HD)
    value_all = value_all.reshape(batches, seq_len, KV_HEADS, HD)
    scores = (
        jnp.einsum("bqkgd,bskd->bkgqs", query_rot, key_all, preferred_element_type=jnp.float32)
        * head_scale
    )
    masked = jnp.where(allowed, scores, masked_fill)
    row_max = jnp.max(masked, axis=-1, keepdims=True)
    expo = jnp.exp(masked - row_max)
    expo_sum = jnp.sum(expo, axis=-1, keepdims=True)
    log_total = row_max + jnp.log(expo_sum)
    attend = (expo / expo_sum).astype(jnp.bfloat16)
    mixed = jnp.einsum("bkgqs,bskd->bqkgd", attend, value_all, preferred_element_type=jnp.float32)
    mixed = mixed.reshape(row_count, q_width).astype(jnp.bfloat16)
    resid = source + right_dot(mixed, attn_full[4])
    ffn_full = (
        lax.all_gather(ffn_gain, ("dp", "ctx"), axis=0, tiled=True),
        lax.all_gather(w_gate, ("dp", "ctx"), axis=0, tiled=True),
        lax.all_gather(w_up, ("dp", "ctx"), axis=0, tiled=True),
        lax.all_gather(w_down, ("dp", "ctx"), axis=0, tiled=True),
    )
    gain_two = ffn_full[0].astype(jnp.float32)
    ffn_factor, normed_two = norm_forward(resid, gain_two)
    gate_pre = plain_dot(normed_two, ffn_full[1])
    up_pre = plain_dot(normed_two, ffn_full[2])
    sigmoid_gate = jax.nn.sigmoid(gate_pre)
    silu_gate = gate_pre * sigmoid_gate
    act = (silu_gate * up_pre).astype(jnp.bfloat16)
    output = resid + right_dot(act, ffn_full[3])
    result = output.astype(jnp.bfloat16).reshape(batches, length, D)
    ffn_back = (
        lax.all_gather(ffn_gain, ("dp", "ctx"), axis=0, tiled=True),
        lax.all_gather(w_gate, ("dp", "ctx"), axis=0, tiled=True),
        lax.all_gather(w_up, ("dp", "ctx"), axis=0, tiled=True),
        lax.all_gather(w_down, ("dp", "ctx"), axis=0, tiled=True),
    )
    grad_out = cotangent.reshape(row_count, D)
    grad_plain = grad_out.astype(jnp.float32)
    grad_act = plain_dot(grad_out, ffn_back[3])
    grad_gate = (grad_act * up_pre * sigmoid_gate * (1.0 + gate_pre * (1.0 - sigmoid_gate))).astype(
        jnp.bfloat16
    )
    grad_up = (grad_act * silu_gate).astype(jnp.bfloat16)
    pieces = (
        lax.all_gather(normed_two, "ctx", axis=0, tiled=True),
        lax.all_gather(grad_gate, "ctx", axis=0, tiled=True),
        lax.all_gather(grad_up, "ctx", axis=0, tiled=True),
        lax.all_gather(act, "ctx", axis=0, tiled=True),
        lax.all_gather(grad_out, "ctx", axis=0, tiled=True),
    )
    picked_in = owned_columns(pieces[0], ctx_size, ctx_rank, shard_rows)
    picked_out = owned_columns(pieces[4], ctx_size, ctx_rank, shard_rows)
    w_gate_grad, w_up_grad, w_down_grad = (
        lax.psum_scatter(
            outer_add(picked_in, pieces[1]).astype(jnp.bfloat16),
            "dp",
            scatter_dimension=0,
            tiled=True,
        ).astype(jnp.float32),
        lax.psum_scatter(
            outer_add(picked_in, pieces[2]).astype(jnp.bfloat16),
            "dp",
            scatter_dimension=0,
            tiled=True,
        ).astype(jnp.float32),
        lax.psum_scatter(
            outer_add(picked_out, pieces[3]).astype(jnp.bfloat16),
            "dp",
            scatter_dimension=0,
            tiled=True,
        ).astype(jnp.float32),
    )
    grad_norm_two = right_dot(grad_gate, ffn_back[1]) + right_dot(grad_up, ffn_back[2])
    resid_back, ffn_gain_part = norm_backward(resid, ffn_factor, gain_two, grad_norm_two)
    grad_resid = grad_plain + resid_back
    attn_back = (
        lax.all_gather(attn_gain, ("dp", "ctx"), axis=0, tiled=True),
        lax.all_gather(w_query, ("dp", "ctx"), axis=0, tiled=True),
        lax.all_gather(w_key, ("dp", "ctx"), axis=0, tiled=True),
        lax.all_gather(w_value, ("dp", "ctx"), axis=0, tiled=True),
        lax.all_gather(w_out, ("dp", "ctx"), axis=0, tiled=True),
        lax.all_gather(b_query, ("dp", "ctx"), axis=0, tiled=True),
        lax.all_gather(b_key, ("dp", "ctx"), axis=0, tiled=True),
        lax.all_gather(b_value, ("dp", "ctx"), axis=0, tiled=True),
    )
    grad_attn = grad_resid.astype(jnp.bfloat16)
    grad_mixed = plain_dot(grad_attn, attn_back[4]).astype(jnp.bfloat16)
    grad_mixed = grad_mixed.reshape(batches, length, KV_HEADS, groups, HD)
    scores = (
        jnp.einsum("bqkgd,bskd->bkgqs", query_rot, key_all, preferred_element_type=jnp.float32)
        * head_scale
    )
    masked = jnp.where(allowed, scores, masked_fill)
    attend_full = jnp.exp(masked - log_total)
    attend = attend_full.astype(jnp.bfloat16)
    grad_attend = jnp.einsum(
        "bqkgd,bskd->bkgqs", grad_mixed, value_all, preferred_element_type=jnp.float32
    )
    value_grad_all = jnp.einsum(
        "bkgqs,bqkgd->bskd", attend, grad_mixed, preferred_element_type=jnp.float32
    )
    delta = jnp.sum(grad_attend * attend_full, axis=-1, keepdims=True)
    grad_scores = (attend_full * (grad_attend - delta)).astype(jnp.bfloat16)
    query_grad_rot = (
        jnp.einsum("bkgqs,bskd->bqkgd", grad_scores, key_all, preferred_element_type=jnp.float32)
        * head_scale
    )
    key_grad_all = (
        jnp.einsum("bkgqs,bqkgd->bskd", grad_scores, query_rot, preferred_element_type=jnp.float32)
        * head_scale
    )
    key_grad_rot, value_grad = (
        lax.psum_scatter(
            key_grad_all.reshape(batches, seq_len, kv_width), "ctx", scatter_dimension=1, tiled=True
        ),
        lax.psum_scatter(
            value_grad_all.reshape(batches, seq_len, kv_width),
            "ctx",
            scatter_dimension=1,
            tiled=True,
        ),
    )
    query_grad = (
        rotate_back(query_grad_rot.reshape(row_count, HEADS, HD), cosine, sine)
        .reshape(row_count, q_width)
        .astype(jnp.bfloat16)
    )
    key_grad = (
        rotate_back(key_grad_rot.reshape(row_count, KV_HEADS, HD), cosine, sine)
        .reshape(row_count, kv_width)
        .astype(jnp.bfloat16)
    )
    value_grad = value_grad.reshape(row_count, kv_width).astype(jnp.bfloat16)
    proj_grad = jnp.concatenate([query_grad, key_grad, value_grad], axis=1)
    pieces = (
        lax.all_gather(normed, "ctx", axis=0, tiled=True),
        lax.all_gather(proj_grad, "ctx", axis=0, tiled=True),
        lax.all_gather(grad_attn, "ctx", axis=0, tiled=True),
        lax.all_gather(mixed, "ctx", axis=0, tiled=True),
    )
    picked_in = owned_columns(pieces[0], ctx_size, ctx_rank, shard_rows)
    picked_out = owned_columns(pieces[2], ctx_size, ctx_rank, shard_rows)
    proj_sum, w_out_grad = (
        lax.psum_scatter(
            outer_add(picked_in, pieces[1]).astype(jnp.bfloat16),
            "dp",
            scatter_dimension=0,
            tiled=True,
        ).astype(jnp.float32),
        lax.psum_scatter(
            outer_add(picked_out, pieces[3]).astype(jnp.bfloat16),
            "dp",
            scatter_dimension=0,
            tiled=True,
        ).astype(jnp.float32),
    )
    grad_norm_one = (
        right_dot(query_grad, attn_back[1])
        + right_dot(key_grad, attn_back[2])
        + right_dot(value_grad, attn_back[3])
    )
    source_back, attn_gain_part = norm_backward(source, attn_factor, gain_one, grad_norm_one)
    hidden_grad = (grad_resid + source_back).reshape(batches, length, D)
    query_bias_part = jnp.sum(query_grad.astype(jnp.float32), axis=0)
    key_bias_part = jnp.sum(key_grad.astype(jnp.float32), axis=0)
    value_bias_part = jnp.sum(value_grad.astype(jnp.float32), axis=0)
    small_sums = (
        lax.psum_scatter(attn_gain_part, ("dp", "ctx"), scatter_dimension=0, tiled=True),
        lax.psum_scatter(query_bias_part, ("dp", "ctx"), scatter_dimension=0, tiled=True),
        lax.psum_scatter(key_bias_part, ("dp", "ctx"), scatter_dimension=0, tiled=True),
        lax.psum_scatter(value_bias_part, ("dp", "ctx"), scatter_dimension=0, tiled=True),
        lax.psum_scatter(ffn_gain_part, ("dp", "ctx"), scatter_dimension=0, tiled=True),
    )
    w_query_grad = proj_sum[:, :q_width]
    w_key_grad = proj_sum[:, q_width : q_width + kv_width]
    w_value_grad = proj_sum[:, q_width + kv_width :]
    return (
        result,
        hidden_grad,
        small_sums[0],
        w_query_grad,
        small_sums[1],
        w_key_grad,
        small_sums[2],
        w_value_grad,
        small_sums[3],
        w_out_grad,
        small_sums[4],
        w_gate_grad,
        w_up_grad,
        w_down_grad,
    )


def solution(mesh):
    placed = (
        P("dp", "ctx", None),
        P("dp", "ctx", None),
        P("dp", None),
        P(("dp", "ctx")),
        P(("dp", "ctx"), None),
        P(("dp", "ctx")),
        P(("dp", "ctx"), None),
        P(("dp", "ctx")),
        P(("dp", "ctx"), None),
        P(("dp", "ctx")),
        P(("dp", "ctx"), None),
        P(("dp", "ctx")),
        P(("dp", "ctx"), None),
        P(("dp", "ctx"), None),
        P(("dp", "ctx"), None),
    )
    return jax.shard_map(
        fast_device if fits(mesh) else general_device,
        mesh=mesh,
        in_specs=placed,
        out_specs=(
            P("dp", "ctx", None),
            P("dp", "ctx", None),
            P(("dp", "ctx")),
            P(("dp", "ctx"), None),
            P(("dp", "ctx")),
            P(("dp", "ctx"), None),
            P(("dp", "ctx")),
            P(("dp", "ctx"), None),
            P(("dp", "ctx")),
            P(("dp", "ctx"), None),
            P(("dp", "ctx")),
            P(("dp", "ctx"), None),
            P(("dp", "ctx"), None),
            P(("dp", "ctx"), None),
        ),
        check_vma=False,
    )
```

```python
import functools

import jax
import jax.numpy as jnp
from jax import lax
from jax.experimental import pallas as pl
from jax.experimental.pallas import tpu as pltpu
from jax.sharding import PartitionSpec as P

D = 1536
HEADS = 12
KV_HEADS = 2
HD = 128


norm_eps = 1e-06
rope_base = 10000.0
masked_fill = -1e30


def angles_for(places, width):
    half = width // 2
    freqs = rope_base ** (-(jnp.arange(half, dtype=jnp.float32) * 2.0 / width))
    angles = places.astype(jnp.float32)[:, None] * freqs[None, :]
    return (jnp.cos(angles)[:, None, :], jnp.sin(angles)[:, None, :])


def rotate(values, cosine, sine):
    half = values.shape[-1] // 2
    first = values[..., :half]
    second = values[..., half:]
    return jnp.concatenate(
        [first * cosine - second * sine, second * cosine + first * sine], axis=-1
    )


def rotate_back(values, cosine, sine):
    half = values.shape[-1] // 2
    first = values[..., :half]
    second = values[..., half:]
    return jnp.concatenate(
        [first * cosine + second * sine, second * cosine - first * sine], axis=-1
    )


def norm_forward(source, gain):
    factor = lax.rsqrt(jnp.mean(source * source, axis=-1, keepdims=True) + norm_eps)
    return (factor, (source * factor * gain).astype(jnp.bfloat16))


def norm_backward(source, factor, gain, grad_normed):
    unit = source * factor
    gain_grad = jnp.sum(grad_normed * unit, axis=0)
    scaled = grad_normed * gain
    source_grad = factor * (scaled - unit * jnp.mean(scaled * unit, axis=-1, keepdims=True))
    return (source_grad, gain_grad)


def right_dot(left, weight):
    return jnp.einsum("rf,df->rd", left, weight, preferred_element_type=jnp.float32)


def plain_dot(left, weight):
    return jnp.dot(left, weight, preferred_element_type=jnp.float32)


def owned_columns(values, ctx_size, ctx_rank, shard_rows):
    rows = values.shape[0]
    blocks = values.shape[1] // (shard_rows * ctx_size)
    shaped = values.reshape(rows, blocks, ctx_size, shard_rows)
    picked = lax.dynamic_index_in_dim(shaped, ctx_rank, axis=2, keepdims=False)
    return picked.reshape(rows, blocks * shard_rows)


def outer_add(left, right):
    return jnp.einsum("rc,rf->cf", left, right, preferred_element_type=jnp.float32)


MESH = pl.DeviceIdType.MESH


def flip(index, mask):
    for bit in (1, 2, 4, 8, 16):
        if mask & bit:
            index = index + bit - 2 * bit * ((index // bit) % 2)
    return index


def either(a, b):
    return a + b - 2 * a * b


def dot(a, b, dims):
    return lax.dot_general(a, b, (dims, ((), ())), preferred_element_type=jnp.float32)


def ffn_kernel(
    ctx_size, n_own, go_all, big,
    hr, grads,
    wgu, wd, nt, go, ggu, act, csend, crecv, hpart, stage,
    w_sem, io_sem, n_send, n_recv, f_send, f_recv, c_send, c_recv, o_send, o_recv, st_sem,
):
    dp = lax.axis_index("dp")
    ctx = lax.axis_index("ctx")
    me = dp * ctx_size + ctx
    y, x, c = dp // 4, (dp // 2) % 2, dp % 2
    h, p = ctx // 2, ctx % 2
    width = wd.shape[1]
    shard = grads.shape[3]
    rows, model = n_own.shape

    def at(index):
        return (index // ctx_size, index % ctx_size)

    core = at(flip(me, 4))

    def partner(o):
        return (dp + (o // 2) * 4 * (1 - 2 * y), ctx + (o % 2) * (1 - 2 * p))

    barrier = pltpu.get_barrier_semaphore()
    for device in (core, partner(1), partner(2), partner(3)):
        pl.semaphore_signal(barrier, inc=1, device_id=device, device_id_type=MESH)

    load_n = pltpu.make_async_copy(n_own, nt.at[0], io_sem.at[0])
    load_n.start()
    load_go = pltpu.make_async_copy(go_all, go, io_sem.at[1])
    load_go.start()
    load_gu = pltpu.make_async_copy(big.at[:, pl.ds(0, 2 * width)], wgu, w_sem.at[0])
    load_gu.start()
    load_d = pltpu.make_async_copy(big.at[:, pl.ds(2 * width, width)], wd, w_sem.at[1])
    load_d.start()

    pl.semaphore_wait(barrier, 4)
    load_n.wait()

    def push_n(slot, dst, device, send, recv):
        return pltpu.make_async_remote_copy(
            src_ref=nt.at[slot], dst_ref=nt.at[dst], send_sem=send, recv_sem=recv,
            device_id=device, device_id_type=MESH,
        )

    first = [push_n(0, 2 * o, partner(o), n_send.at[o], n_recv.at[o]) for o in (1, 2, 3)]
    for copy in first:
        copy.start()
    push_n(0, 1, core, f_send.at[0], f_recv.at[0]).start()
    load_gu.wait()
    load_d.wait()
    load_go.wait()

    def tile(slot):
        gu = dot(nt[slot], wgu[...], ((1,), (0,)))
        ga = dot(go[slot], wd[...], ((1,), (0,)))
        gate, up = gu[:, :width], gu[:, width:]
        sig = 1.0 / (1.0 + jnp.exp(-gate))
        silu = gate * sig
        act[slot] = (silu * up).astype(jnp.bfloat16)
        ggu[slot, :, pl.ds(0, width)] = (ga * up * sig * (1.0 + gate * (1.0 - sig))).astype(jnp.bfloat16)
        ggu[slot, :, pl.ds(width, width)] = (ga * silu).astype(jnp.bfloat16)
        grad = dot(ggu[slot], wgu[...], ((1,), (1,)))
        out = dot(act[slot], wd[...], ((1,), (1,)))
        return (grad.astype(jnp.bfloat16), out.astype(jnp.bfloat16))

    def cross(o):
        return pltpu.make_async_remote_copy(
            src_ref=csend, dst_ref=crecv.at[o % 2], send_sem=c_send, recv_sem=c_recv.at[o % 2],
            device_id=core, device_id_type=MESH,
        )

    def final(o):
        return pltpu.make_async_remote_copy(
            src_ref=hpart.at[o], dst_ref=hr.at[o], send_sem=o_send.at[o], recv_sem=o_recv.at[o],
            device_id=partner(o), device_id_type=MESH,
        )

    keep = pltpu.make_async_copy(hpart.at[0], hr.at[0], io_sem.at[0])

    def combine(o):
        cross(o).wait_recv()
        total = hpart[o].astype(jnp.float32) + crecv[o % 2].astype(jnp.float32)
        hpart[o] = total.astype(jnp.bfloat16)

    def step(o, carry):
        @pl.when(o > 0)
        def _():
            push_n(0, 2 * o, partner(o), n_send.at[o], n_recv.at[o]).wait_recv()
            push_n(2 * o, 2 * o + 1, core, f_send.at[o], f_recv.at[o]).start()

        grad, out = tile(2 * o)
        hpart[o, 0] = grad
        hpart[o, 1] = out

        @pl.when(o > 0)
        def _():
            combine(o - 1)

        @pl.when(o == 1)
        def _():
            keep.start()

        @pl.when(o > 1)
        def _():
            final(o - 1).start()

        push_n(2 * o, 2 * o + 1, core, f_send.at[o], f_recv.at[o]).wait_recv()
        grad, out = tile(2 * o + 1)

        @pl.when(o > 0)
        def _():
            cross(o).wait_send()

        csend[0] = grad
        csend[1] = out
        cross(o).start()
        return carry

    lax.fori_loop(0, 4, step, 0)
    combine(3)
    final(3).start()

    def stage_wait(slot):
        pltpu.make_async_copy(stage.at[slot], stage.at[slot], st_sem.at[slot]).wait()

    def weights(q, carry):
        slot = q % 2

        @pl.when(q > 1)
        def _():
            stage_wait(slot)

        chunk = 8 * shard
        cols = pl.ds(pl.multiple_of(q * chunk, chunk), chunk)
        left = nt[:, :, cols].reshape(8 * rows, chunk)
        for half in range(2):
            part = pl.ds(half * width, width)
            right = ggu[:, :, part].reshape(8 * rows, width)
            stage[slot, :, part] = dot(left, right, ((0,), (0,))).astype(jnp.bfloat16)
        left = go[:, :, cols].reshape(8 * rows, chunk)
        right = act[...].reshape(8 * rows, width)
        stage[slot, :, pl.ds(2 * width, width)] = dot(left, right, ((0,), (0,))).astype(jnp.bfloat16)
        yr, xr = either(q // 2, y), either(q % 2, x)
        for j in range(8):
            cr, hrel, pr = either(j // 4, c), either((j // 2) % 2, h), either(j % 2, p)
            block = yr * 4 + cr * 2 + pr
            row = pl.ds(j * shard, shard)
            pltpu.make_async_copy(stage.at[slot, row], grads.at[xr, hrel, block], st_sem.at[slot]).start()
        return carry

    lax.fori_loop(0, 4, weights, 0)
    stage_wait(0)
    stage_wait(1)
    keep.wait()
    cross(3).wait_send()
    for copy in first:
        copy.wait_send()
    for o in range(4):
        push_n(2 * o, 2 * o + 1, core, f_send.at[o], f_recv.at[o]).wait_send()
    for o in (1, 2, 3):
        final(o).wait()


def ffn_call(ctx_size, shard, n_own, go_all, big):
    rows, model = n_own.shape
    width = big.shape[1] // 3
    low = jnp.bfloat16
    return pl.pallas_call(
        functools.partial(ffn_kernel, ctx_size),
        out_shape=(
            jax.ShapeDtypeStruct((4, 2, rows, model), low),
            jax.ShapeDtypeStruct((2, 2, 8, shard, 3 * width), low),
        ),
        in_specs=[pl.BlockSpec(memory_space=pl.ANY)] * 3,
        out_specs=[pl.BlockSpec(memory_space=pl.ANY)] * 2,
        scratch_shapes=[
            pltpu.VMEM((model, 2 * width), low),
            pltpu.VMEM((model, width), low),
            pltpu.VMEM((8, rows, model), low),
            pltpu.VMEM((8, rows, model), low),
            pltpu.VMEM((8, rows, 2 * width), low),
            pltpu.VMEM((8, rows, width), low),
            pltpu.VMEM((2, rows, model), low),
            pltpu.VMEM((2, 2, rows, model), low),
            pltpu.VMEM((4, 2, rows, model), low),
            pltpu.VMEM((2, 8 * shard, 3 * width), low),
            pltpu.SemaphoreType.DMA((2,)),
            pltpu.SemaphoreType.DMA((2,)),
            pltpu.SemaphoreType.DMA((4,)),
            pltpu.SemaphoreType.DMA((4,)),
            pltpu.SemaphoreType.DMA((4,)),
            pltpu.SemaphoreType.DMA((4,)),
            pltpu.SemaphoreType.DMA,
            pltpu.SemaphoreType.DMA((2,)),
            pltpu.SemaphoreType.DMA((4,)),
            pltpu.SemaphoreType.DMA((4,)),
            pltpu.SemaphoreType.DMA((2,)),
        ],
        compiler_params=pltpu.CompilerParams(
            collective_id=1, has_side_effects=True, vmem_limit_bytes=63 << 20
        ),
        name="ffn",
    )(n_own, go_all, big)


def turn(values, cosine, sine):
    return values * cosine + pltpu.roll(values, HD // 2, 1) * sine


def front_kernel(
    ctx_size, hidden, cosine, sine, pos_q, pos_k, spread, packed, w_out, w_gate, w_up, w_down, grad_out,
    normed_o, query_o, kv_o, total_o, mixed_o, resid_o, normed_two_o, small_o, proj_o, out_o, big, go,
    proj, out_w, source, query, kv, mixed,
    load_sem, ag_send, ag_recv, core_send, core_recv, big_send, big_recv, go_send, go_recv, kv_send, kv_recv, back_sem,
):
    dp = lax.axis_index("dp")
    ctx = lax.axis_index("ctx")
    me = dp * ctx_size + ctx
    shard, wide = packed.shape
    rows, model = hidden.shape
    width = big.shape[1] // 3
    kv_width = KV_HEADS * HD
    q_width = HEADS * HD
    proj_width = q_width + 2 * kv_width
    groups = HEADS // KV_HEADS

    def at(index):
        return (index // ctx_size, index % ctx_size)

    def block(mask, count=1):
        base = flip(me, mask) // count * count
        return pl.ds(pl.multiple_of(base * shard, shard), shard * count)

    def remote(src, dst, send, recv, mask):
        return pltpu.make_async_remote_copy(
            src_ref=src, dst_ref=dst, send_sem=send, recv_sem=recv, device_id=at(flip(me, mask)), device_id_type=MESH
        )

    def drain(ref, sem):
        pltpu.make_async_copy(ref, ref, sem).wait()

    barrier = pltpu.get_barrier_semaphore()
    partners = (1, 2, 4, 5, 8, 16, 17, 20, 21)
    for mask in partners:
        pl.semaphore_signal(barrier, inc=1, device_id=at(flip(me, mask)), device_id_type=MESH)

    own = (
        pltpu.make_async_copy(packed, proj.at[block(0)], load_sem.at[0]),
        pltpu.make_async_copy(w_out, out_w.at[block(0)], load_sem.at[1]),
    )
    for copy in own:
        copy.start()
    hidden_units = w_gate.shape[1]
    cuts = []
    for k in range(8):
        size = min(width, hidden_units - k * width)
        for n, ref in enumerate((w_gate, w_up, w_down)):
            cuts.append((ref.at[:, pl.ds(k * width, size)], source.at[k, :, pl.ds(n * width, size)]))
            if size < width:
                source[k, :, pl.ds(n * width + size, width - size)] = jnp.zeros((shard, width - size), source.dtype)
    cuts = [pltpu.make_async_copy(a, b, load_sem.at[2 + i]) for i, (a, b) in enumerate(cuts)]
    for copy in cuts:
        copy.start()
    pl.semaphore_wait(barrier, len(partners))
    for copy in own:
        copy.wait()

    pair = ((proj, 0), (out_w, 1))

    def ag(n, mask, over):
        ref = pair[n][0]
        remote(ref.at[block(mask)], ref.at[block(mask)], ag_send.at[n], ag_recv.at[n, mask | over], over).start()

    def ag_pass(n, mask, *overs):
        ref = pair[n][0]
        remote(ref.at[block(mask)], ref.at[block(mask)], ag_send.at[n], ag_recv.at[n, mask], 1).wait_recv()
        for over in overs:
            ag(n, mask, over)

    def group(n, mask):
        ref = pair[n][0]
        part = ref.at[block(mask, 4)]
        return remote(part, part, core_send.at[n, mask // 8], core_recv.at[n, mask // 8], 4)

    def group_wait(mask, n):
        ref = pair[n][0]
        remote(ref.at[block(mask | 4, 4)], ref.at[block(mask | 4, 4)], core_send.at[n, mask // 8], core_recv.at[n, mask // 8], 4).wait_recv()

    for over in (2, 1, 8, 16):
        ag(0, 0, over)
    for over in (2, 1, 8):
        ag(1, 0, over)

    for copy in cuts:
        copy.wait()
    y, x, c = dp // 4, (dp // 2) % 2, dp % 2
    h, p = ctx // 2, ctx % 2

    def column(mask):
        return either(y, mask // 16) * 4 + either(p, mask % 2) * 2 + either(c, (mask // 4) % 2)

    own_big = pltpu.make_async_copy(source.at[column(0)], big.at[block(0)], load_sem.at[0])
    own_big.start()
    def cut(mask):
        remote(source.at[column(mask)], big.at[block(0)], big_send.at[0], big_recv.at[mask], mask).start()

    def big_forward(mask, over):
        remote(big.at[block(mask)], big.at[block(mask)], big_send.at[0], big_recv.at[mask | over], over).start()

    def big_pass(mask, *overs):
        remote(big.at[block(mask)], big.at[block(mask)], big_send.at[0], big_recv.at[mask], 1).wait_recv()
        for over in overs:
            big_forward(mask, over)

    for mask in (4, 1, 5):
        cut(mask)
    remote(source.at[column(0)], big.at[block(0)], big_send.at[0], big_recv.at[2], 2).start()

    ag_pass(0, 1, 8, 16)
    ag_pass(0, 8, 16)
    ag_pass(0, 2, 1, 8, 16)
    ag_pass(0, 9, 16)
    ag_pass(0, 3, 8, 16)
    group(0, 0).start()
    big_pass(4, 2)
    ag_pass(0, 10, 16)
    ag_pass(0, 11, 16)
    group(0, 8).start()
    for mask in (16, 20, 17, 21):
        cut(mask)
    ag_pass(1, 1, 8)
    ag_pass(1, 2, 1, 8)
    remote(source.at[column(0)], big.at[block(0)], big_send.at[0], big_recv.at[8], 8).start()
    big_forward(4, 8)
    for mask in (16, 17, 18, 19):
        ag_pass(0, mask)
    group(0, 16).start()
    ag_pass(1, 3, 8)
    big_pass(1, 2, 8)
    for mask in (24, 25, 26, 27):
        ag_pass(0, mask)
    group(0, 24).start()
    for mask in (0, 8, 16, 24):
        group_wait(mask, 0)

    small = jnp.transpose(proj[:, proj_width:].astype(jnp.float32))
    small_o[...] = small[:8]
    kv_bias = dot(small[:8].astype(jnp.bfloat16), spread[...], ((1,), (0,)))[3:4]
    values = hidden[...].astype(jnp.float32)
    factor = lax.rsqrt(jnp.mean(values * values, axis=-1, keepdims=True) + norm_eps)
    normed_o[...] = (values * factor * small[0:1]).astype(jnp.bfloat16)
    cos, sin = cosine[...], sine[...]
    raw = dot(normed_o[...], proj[:, q_width:proj_width], ((1,), (0,))) + kv_bias
    mine = block(0)
    for g in range(KV_HEADS):
        kv[ctx, :, pl.ds(g * HD, HD)] = turn(raw[:, g * HD : (g + 1) * HD], cos, sin).astype(jnp.bfloat16)
    kv[ctx, :, pl.ds(kv_width, kv_width)] = raw[:, kv_width:].astype(jnp.bfloat16)

    def kv_push(mask, over):
        slot = flip(ctx, mask)
        return remote(kv.at[slot], kv.at[slot], kv_send.at[mask | over], kv_recv.at[mask | over], over)

    kv_push(0, 2).start()
    kv_push(0, 1).start()
    big_pass(5, 2, 8)
    big_pass(16, 2, 8)
    for mask in (0, 1, 2, 3):
        ag(1, mask, 16)
    group(1, 0).start()
    for mask in (8, 9, 10, 11):
        ag_pass(1, mask, 16)
    group(1, 8).start()
    for half in range(2):
        part = half * (q_width // 2)
        raw = dot(normed_o[...], proj[:, part : part + q_width // 2], ((1,), (0,)))
        raw = raw + small[1:2, part : part + q_width // 2]
        for i in range(HEADS // 2):
            query[half * (HEADS // 2) + i] = turn(raw[:, i * HD : (i + 1) * HD], cos, sin).astype(jnp.bfloat16)
    kv_push(0, 2).wait_recv()
    kv_push(2, 1).start()
    for mask in (20, 17, 21):
        big_pass(mask, 2, 8)
    for o, mask in ((1, 1), (2, 16), (3, 17)):
        remote(grad_out, go.at[2 * o], go_send.at[o], go_recv.at[2 * o], mask).start()
    remote(grad_out, go.at[1], go_send.at[0], go_recv.at[1], 4).start()
    for mask in (2, 6):
        big_pass(mask, 8)
    kv_push(0, 1).wait_recv()
    kv_push(2, 1).wait_recv()
    query_back = pltpu.make_async_copy(query, query_o, back_sem.at[0])
    query_back.start()
    kv_back = pltpu.make_async_copy(kv, kv_o, back_sem.at[1])
    kv_back.start()

    def head(n, carry):
        g = n // groups
        keys = kv[:, :, pl.ds(pl.multiple_of(g * HD, HD), HD)].reshape(ctx_size * rows, HD)
        vals = kv[:, :, pl.ds(pl.multiple_of(kv_width + g * HD, HD), HD)].reshape(ctx_size * rows, HD)
        scores = dot(query[n], keys, ((1,), (1,))) * HD ** (-0.5)
        scores = jnp.where(pos_k[...] <= pos_q[...], scores, masked_fill)
        top = jnp.max(scores, axis=-1, keepdims=True)
        expo = jnp.exp(scores - top)
        expo_sum = jnp.sum(expo, axis=-1, keepdims=True)
        attend = (expo / expo_sum).astype(jnp.bfloat16)
        mixed[:, pl.ds(pl.multiple_of(n * HD, HD), HD)] = dot(attend, vals, ((1,), (0,))).astype(jnp.bfloat16)
        lane = lax.broadcasted_iota(jnp.int32, (rows, HD), 1)
        total_o[...] = jnp.where(lane == n, top + jnp.log(expo_sum), total_o[...])
        return carry

    total_o[...] = jnp.zeros_like(total_o)
    lax.fori_loop(0, HEADS, head, 0)
    own_go = pltpu.make_async_copy(grad_out, go.at[0], load_sem.at[1])
    own_go.start()
    mixed_back = pltpu.make_async_copy(mixed, mixed_o, back_sem.at[2])
    mixed_back.start()
    for mask in (3, 7):
        big_pass(mask, 8)
    for n, mask in enumerate((16, 17, 18, 19, 24, 25, 26, 27)):
        ag_pass(1, mask)
        if n % 4 == 3:
            group(1, mask & 24).start()
    for mask in (0, 8, 16, 24):
        group_wait(mask, 1)
    proj_back = pltpu.make_async_copy(proj, proj_o, back_sem.at[4])
    proj_back.start()
    out_back = pltpu.make_async_copy(out_w, out_o, back_sem.at[5])
    out_back.start()
    resid = hidden[...].astype(jnp.float32) + dot(mixed[...], out_w[...], ((1,), (1,)))
    resid_o[...] = resid
    factor = lax.rsqrt(jnp.mean(resid * resid, axis=-1, keepdims=True) + norm_eps)
    normed_two_o[...] = (resid * factor * small_o[2:3]).astype(jnp.bfloat16)
    for o, mask in ((1, 1), (2, 16), (3, 17)):
        remote(grad_out, go.at[2 * o], go_send.at[o], go_recv.at[2 * o], mask).wait_recv()
        remote(go.at[2 * o], go.at[2 * o + 1], go_send.at[3 + o], go_recv.at[2 * o + 1], 4).start()
    for mask in (18, 22, 19, 23):
        big_pass(mask, 8)

    for mask in (8, 12, 9, 24, 13, 28, 25, 29, 10, 14, 11, 26, 15, 30, 27, 31):
        big_pass(mask)
    own_big.wait()
    own_go.wait()
    sent = 7 + 8 + 8 + 8
    drain(big.at[pl.ds(0, sent * shard)], big_send.at[0])
    for ref, n in pair:
        drain(ref.at[pl.ds(0, 15 * shard)], ag_send.at[n])
        for mask in (0, 8, 16, 24):
            group(n, mask).wait_send()
    remote(grad_out, go.at[1], go_send.at[0], go_recv.at[1], 4).wait()
    for o, mask in ((1, 1), (2, 16), (3, 17)):
        remote(grad_out, go.at[2 * o], go_send.at[o], go_recv.at[2 * o], mask).wait_send()
        remote(go.at[2 * o], go.at[2 * o + 1], go_send.at[3 + o], go_recv.at[2 * o + 1], 4).wait()
    kv_push(0, 2).wait_send()
    kv_push(0, 1).wait_send()
    kv_push(2, 1).wait_send()
    for copy in (query_back, kv_back, mixed_back, proj_back, out_back):
        copy.wait()


def front_call(ctx_size, hidden, cosine, sine, pos_q, pos_k, spread, packed, w_out, w_gate, w_up, w_down, grad_out):
    rows, model = hidden.shape
    shard, wide = packed.shape
    kv_width = KV_HEADS * HD
    q_width = HEADS * HD
    width = -(-w_gate.shape[1] // (8 * 128)) * 128
    low, full = jnp.bfloat16, jnp.float32
    vmem = pl.BlockSpec(memory_space=pltpu.VMEM)
    anywhere = pl.BlockSpec(memory_space=pl.ANY)
    shapes = (
        ((rows, model), low, vmem),
        ((HEADS, rows, HD), low, anywhere),
        ((ctx_size, rows, 2 * kv_width), low, anywhere),
        ((rows, HD), full, vmem),
        ((rows, q_width), low, anywhere),
        ((rows, model), full, vmem),
        ((rows, model), low, vmem),
        ((8, model), full, vmem),
        ((model, wide), low, anywhere),
        ((model, q_width), low, anywhere),
        ((model, 3 * width), low, anywhere),
        ((8, rows, model), low, anywhere),
    )
    sem = pltpu.SemaphoreType.DMA
    return pl.pallas_call(
        functools.partial(front_kernel, ctx_size),
        out_shape=tuple(jax.ShapeDtypeStruct(shape, kind) for shape, kind, _ in shapes),
        in_specs=[vmem] * 6 + [anywhere] * 6,
        out_specs=tuple(spec for _, _, spec in shapes),
        scratch_shapes=[
            pltpu.VMEM((model, wide), low),
            pltpu.VMEM((model, q_width), low),
            pltpu.VMEM((8, shard, 3 * width), low),
            pltpu.VMEM((HEADS, rows, HD), low),
            pltpu.VMEM((ctx_size, rows, 2 * kv_width), low),
            pltpu.VMEM((rows, q_width), low),
            sem((26,)), sem((2,)), sem((2, 32)), sem((2, 4)), sem((2, 4)), sem((1,)), sem((32,)),
            sem((7,)), sem((8,)), sem((4,)), sem((4,)), sem((6,)),
        ],
        compiler_params=pltpu.CompilerParams(
            collective_id=0, has_side_effects=True, vmem_limit_bytes=56 << 20
        ),
        name="front",
    )(hidden, cosine, sine, pos_q, pos_k, spread, packed, w_out, w_gate, w_up, w_down, grad_out)


def back_kernel(
    ctx_size, grad_two, resid, hidden, grad_out, normed, mixed, query, kv, total, cosine, sine, pos_q, pos_k, small, spread,
    proj, out_w, grads,
    hidden_o, query_o, key_o, outw_o, gate_o, up_o, down_o,
    weight, turned, left_n, left_a, right_b, right_p, side, side_in, g_b, g_q, g_k,
    y_b, y_q, y_k, x_b, x_q, x_k, p_b, p_q, p_k, h_b, h_q, h_k,
    own, far, zin, fin, stage, heads_g, lse, dkv, kv_out, kv_p, kv_h, grad_resid,
    load_sem, xs, xr, zs, zr, fs, fr, cs, cr, rs, rr, ks, kr, st_sem,
):
    dp = lax.axis_index("dp")
    ctx = lax.axis_index("ctx")
    me = dp * ctx_size + ctx
    y, x, c = dp // 4, (dp // 2) % 2, dp % 2
    h, p = ctx // 2, ctx % 2
    rows, model = resid.shape
    shard = grads.shape[3]
    width = grads.shape[4] // 3
    hidden_units = gate_o.shape[1]
    kv_width = KV_HEADS * HD
    q_width = HEADS * HD
    groups = HEADS // KV_HEADS
    low, full = jnp.bfloat16, jnp.float32
    span = ctx_size * shard

    def at(index):
        return (index // ctx_size, index % ctx_size)

    def remote(src, dst, send, recv, mask):
        return pltpu.make_async_remote_copy(
            src_ref=src, dst_ref=dst, send_sem=send, recv_sem=recv, device_id=at(flip(me, mask)), device_id_type=MESH
        )

    def group_rows(mask):
        return pl.ds(pl.multiple_of(flip(dp, mask // 4) * span, span), span)

    def mask_of(j):
        return (j // 4) * 16 + ((j // 2) % 2) * 4 + j % 2

    barrier = pltpu.get_barrier_semaphore()
    partners = (1, 2, 4, 5, 8, 16, 17, 20, 21)
    for mask in partners:
        pl.semaphore_signal(barrier, inc=1, device_id=at(flip(me, mask)), device_id_type=MESH)
    load_w = pltpu.make_async_copy(out_w, weight.at[:, pl.ds(0, q_width)], load_sem.at[0])
    load_w.start()
    load_own = [pltpu.make_async_copy(grads.at[0, 1], own, load_sem.at[1]), pltpu.make_async_copy(grads.at[0, 0], own, load_sem.at[2])]
    load_own[0].start()
    pl.semaphore_wait(barrier, len(partners))

    def far_push(half, j):
        return remote(grads.at[1, half, j], far.at[half, j], xs.at[half, j], xr.at[half, j], 8)

    for j in range(8):
        far_push(1, j).start()

    def transposed(value, left, n):
        turned[n] = jnp.transpose(value)
        for i, mask in enumerate((0, 8, 16, 24)):
            left[i, :, pl.ds(0, rows)] = turned[n, group_rows(mask)]
            cross_left(left, n, i, mask).start()

    def cross_left(left, n, i, mask):
        return remote(turned.at[n, group_rows(mask | 4)], left.at[i, :, pl.ds(rows, rows)], cs.at[n, i], cr.at[n, i], 4)

    def cross(src, dst, n, i):
        return remote(src, dst, cs.at[n, i], cr.at[n, i], 4)

    transposed(normed[...], left_n, 0)
    right_b[pl.ds(0, rows)] = mixed[...]
    cross_mixed = cross(mixed, right_b.at[pl.ds(rows, rows)], 2, 0)
    cross_mixed.start()

    value = resid[...]
    factor = lax.rsqrt(jnp.mean(value * value, axis=-1, keepdims=True) + norm_eps)
    unit = value * factor
    scaled = grad_two[...] * small[2:3]
    ffn_row = jnp.sum(grad_two[...] * unit, axis=0, keepdims=True)
    grad_resid[...] = grad_out[...].astype(full) + factor * (
        scaled - unit * jnp.mean(scaled * unit, axis=-1, keepdims=True)
    )
    grad_attn = grad_resid[...].astype(low)
    transposed(grad_attn, left_a, 1)
    lse[...] = jnp.transpose(total[...])
    load_w.wait()
    for half in range(2):
        part = half * (q_width // 2)
        moved = dot(grad_attn, weight[:, part : part + q_width // 2], ((1,), (0,))).astype(low)
        for i in range(HEADS // 2):
            heads_g[half * (HEADS // 2) + i] = moved[:, i * HD : (i + 1) * HD]
    load_p = pltpu.make_async_copy(proj, weight, load_sem.at[0])
    load_p.start()

    streams = ((g_b, y_b, x_b, p_b, h_b), (g_q, y_q, x_q, p_q, h_q), (g_k, y_k, x_k, p_k, h_k))

    def add(ref, other):
        ref[...] = (ref[...].astype(full) + other[...].astype(full)).astype(low)

    def y_push(s, k):
        g, yy = streams[s][:2]
        return remote(g.at[2 + k], yy.at[k], rs.at[s, k], rr.at[s, k], 16)

    def x_push(s):
        g, xx = streams[s][0], streams[s][2]
        return remote(g.at[1], xx, rs.at[s, 2], rr.at[s, 2], 8)

    def block_of(hr, other):
        z = 2 * either(h, hr) + either(p, other)
        return pl.ds(pl.multiple_of(z * shard, shard), shard)

    def p_push(s, hr):
        g, pp = streams[s][0], streams[s][3]
        return remote(g.at[0, block_of(hr, 1)], pp.at[hr], rs.at[s, 3 + hr], rr.at[s, 3 + hr], 1)

    def h_push(s):
        g, hh = streams[s][0], streams[s][4]
        return remote(g.at[0, block_of(1, 0)], hh, rs.at[s, 5], rr.at[s, 5], 2)

    def y_pass(s):
        g, yy = streams[s][:2]
        y_push(s, 1).wait_recv()
        add(g.at[1], yy.at[1])
        x_push(s).start()
        y_push(s, 0).wait_recv()
        add(g.at[0], yy.at[0])

    def x_pass(s):
        x_push(s).wait_recv()
        add(streams[s][0].at[0], streams[s][2])
        p_push(s, 1).start()
        p_push(s, 0).start()

    def p_pass(s):
        g, pp = streams[s][0], streams[s][3]
        p_push(s, 1).wait_recv()
        add(g.at[0, block_of(1, 0)], pp.at[1])
        h_push(s).start()
        p_push(s, 0).wait_recv()
        add(g.at[0, block_of(0, 0)], pp.at[0])

    def h_pass(s, out):
        h_push(s).wait_recv()
        out[...] = streams[s][0][0, block_of(0, 0)].astype(full) + streams[s][4][...].astype(full)

    for i, mask in enumerate((0, 8, 16, 24)):
        cross_left(left_a, 1, i, mask).wait_recv()
    cross_mixed.wait_recv()
    for i in (3, 2, 1, 0):
        g_b[i] = dot(left_a[i], right_b[...], ((1,), (0,))).astype(low)
        if i > 1:
            y_push(0, i - 2).start()

    def z_push(j):
        return remote(far.at[1, j], zin.at[j], zs.at[j], zr.at[j], 2)

    def far_step(j):
        far_push(1, j).wait_recv()
        far[1, j] = (far[1, j].astype(full) + own[j].astype(full)).astype(low)
        z_push(j).start()

    load_own[0].wait()

    def head(n, carry):
        g = n // groups
        k_cols = pl.ds(pl.multiple_of(g * HD, HD), HD)
        v_cols = pl.ds(pl.multiple_of(kv_width + g * HD, HD), HD)
        keys = kv[:, :, k_cols].reshape(ctx_size * rows, HD)
        vals = kv[:, :, v_cols].reshape(ctx_size * rows, HD)
        scores = dot(keys, query[n], ((1,), (1,))) * HD ** (-0.5)
        scores = jnp.where(pos_k[...] <= pos_q[...], scores, masked_fill)
        attend = jnp.exp(scores - lse[pl.ds(n, 1), :])
        grad_attend = dot(vals, heads_g[n], ((1,), (1,)))
        delta = jnp.sum(grad_attend * attend, axis=0, keepdims=True)
        grad_scores = (attend * (grad_attend - delta)).astype(low)
        dkv[:, k_cols] += dot(grad_scores, query[n], ((1,), (0,)))
        dkv[:, v_cols] += dot(attend.astype(low), heads_g[n], ((1,), (0,)))
        back = dot(grad_scores, keys, ((0,), (0,))) * HD ** (-0.5)
        back = turn(back, cosine[...], -sine[...]).astype(low)
        right_p[pl.ds(0, rows), pl.ds(pl.multiple_of(n * HD, HD), HD)] = back
        return carry

    dkv[...] = jnp.zeros_like(dkv)
    lax.fori_loop(0, HEADS // 2, head, 0)
    far_step(0)
    lax.fori_loop(HEADS // 2, HEADS, head, 0)
    far_step(1)

    for z in range(ctx_size):
        part = dkv[pl.ds(z * rows, rows)]
        kv_out[z, :, pl.ds(0, kv_width)] = (part[:, :kv_width] * HD ** (-0.5)).astype(low)
        kv_out[z, :, pl.ds(kv_width, kv_width)] = part[:, kv_width:].astype(low)

    def kv_push(hr):
        return remote(kv_out.at[2 * either(h, hr) + 1 - p], kv_p.at[hr], ks.at[hr], kr.at[hr], 1)

    def kv_cross():
        return remote(kv_out.at[2 * (1 - h) + p], kv_h, ks.at[2], kr.at[2], 2)

    kv_push(1).start()
    kv_push(0).start()
    cross_q = cross(
        right_p.at[pl.ds(0, rows), pl.ds(0, q_width)], right_p.at[pl.ds(rows, rows), pl.ds(0, q_width)], 2, 1
    )
    cross_q.start()
    y_pass(0)
    kv_push(1).wait_recv()
    add(kv_out.at[2 * (1 - h) + p], kv_p.at[1])
    kv_cross().start()
    kv_push(0).wait_recv()
    add(kv_out.at[2 * h + p], kv_p.at[0])
    far_step(2)
    for i, mask in enumerate((0, 8, 16, 24)):
        cross_left(left_n, 0, i, mask).wait_recv()
    cross_q.wait_recv()
    for i in (3, 2, 1, 0):
        g_q[i] = dot(left_n[i], right_p[:, pl.ds(0, q_width)], ((1,), (0,))).astype(low)
        if i > 1:
            y_push(1, i - 2).start()
    load_p.wait()
    hidden_o[...] = dot(right_p[pl.ds(0, rows), pl.ds(0, q_width)], weight[:, pl.ds(0, q_width)], ((1,), (1,)))
    far_step(3)
    far_step(4)
    kv_cross().wait_recv()
    final = kv_out[2 * h + p].astype(full) + kv_h[...].astype(full)
    for g in range(KV_HEADS):
        right_p[pl.ds(0, rows), pl.ds(q_width + g * HD, HD)] = turn(
            final[:, g * HD : (g + 1) * HD], cosine[...], -sine[...]
        ).astype(low)
    right_p[pl.ds(0, rows), pl.ds(q_width + kv_width, kv_width)] = final[:, kv_width:].astype(low)
    cross_kv = cross(
        right_p.at[pl.ds(0, rows), pl.ds(q_width, 2 * kv_width)],
        right_p.at[pl.ds(rows, rows), pl.ds(q_width, 2 * kv_width)], 2, 2,
    )
    cross_kv.start()
    grad_one = hidden_o[...] + dot(
        right_p[pl.ds(0, rows), pl.ds(q_width, 2 * kv_width)], weight[:, pl.ds(q_width, 2 * kv_width)], ((1,), (1,))
    )
    value = hidden[...].astype(full)
    factor = lax.rsqrt(jnp.mean(value * value, axis=-1, keepdims=True) + norm_eps)
    unit = value * factor
    scaled = grad_one * small[0:1]
    attn_row = jnp.sum(grad_one * unit, axis=0, keepdims=True)
    hidden_o[...] = grad_resid[...] + factor * (scaled - unit * jnp.mean(scaled * unit, axis=-1, keepdims=True))
    bias = jnp.sum(right_p[pl.ds(0, rows)].astype(full), axis=0, keepdims=True)
    kv_bias = jnp.broadcast_to(bias[:, q_width:], (8, 2 * kv_width)).astype(low)
    kv_row = dot(kv_bias, spread[...], ((1,), (1,)))[:1]
    table = jnp.concatenate([attn_row, bias[:, :q_width], ffn_row, kv_row, jnp.zeros((124, model), full)], axis=0)
    side[...] = jnp.transpose(table).astype(low)

    def cross_side(i, mask):
        return cross(side.at[group_rows(mask | 4)], side_in.at[i], 3, i)

    for i, mask in enumerate((0, 8, 16, 24)):
        cross_side(i, mask).start()
    cross_kv.wait_recv()
    for i, mask in ((3, 24), (2, 16), (1, 8), (0, 0)):
        g_k[i, :, pl.ds(0, 2 * kv_width)] = dot(
            left_n[i], right_p[:, pl.ds(q_width, 2 * kv_width)], ((1,), (0,))
        ).astype(low)
        cross_side(i, mask).wait_recv()
        g_k[i, :, pl.ds(2 * kv_width, HD)] = (
            side[group_rows(mask)].astype(full) + side_in[i].astype(full)
        ).astype(low)
        if i > 1:
            y_push(2, i - 2).start()
    x_pass(0)
    far_step(5)
    y_pass(1)
    far_step(6)
    y_pass(2)
    far_step(7)
    p_pass(0)
    for j in range(8):
        far_push(0, j).start()
    load_own[1].start()
    x_pass(1)
    x_pass(2)
    h_pass(0, outw_o)
    p_pass(1)
    p_pass(2)
    load_own[1].wait()

    def fin_push(j):
        return remote(own.at[j], fin.at[j], fs.at[j], fr.at[j], mask_of(j))

    def total_step(j):
        far_push(0, j).wait_recv()
        z_push(j).wait_recv()
        own[j] = (own[j].astype(full) + far[0, j].astype(full) + zin[j].astype(full)).astype(low)

    outs = (gate_o, up_o, down_o)
    last = hidden_units - 7 * width

    def store(j, ref):
        slot = j % 2
        stage[slot] = ref[...].astype(full)
        mask = mask_of(j)
        k = either(y, mask // 16) * 4 + either(p, mask % 2) * 2 + either(c, (mask // 4) % 2)

        @pl.when(k < 7)
        def _():
            for n in range(3):
                pltpu.make_async_copy(
                    stage.at[slot, :, pl.ds(n * width, width)],
                    outs[n].at[:, pl.ds(pl.multiple_of(k * width, HD), width)], st_sem.at[slot],
                ).start()
            pltpu.make_async_copy(stage.at[slot], stage.at[slot], st_sem.at[slot]).wait()

        @pl.when(k == 7)
        def _():
            for n in range(3):
                pltpu.make_async_copy(
                    stage.at[slot, :, pl.ds(n * width, last)], outs[n].at[:, pl.ds(7 * width, last)], st_sem.at[slot]
                ).start()
            part = stage.at[slot, :, pl.ds(0, 3 * last)]
            pltpu.make_async_copy(part, part, st_sem.at[slot]).wait()

    total_step(0)
    store(0, own.at[0])
    for j in range(1, 8):
        total_step(j)
        fin_push(j).start()
    h_pass(1, query_o)
    h_pass(2, key_o)
    for j in range(1, 8):
        fin_push(j).wait_recv()
        store(j, fin.at[j])

    for j in range(8):
        far_push(0, j).wait_send()
        far_push(1, j).wait_send()
        z_push(j).wait_send()
        if j:
            fin_push(j).wait_send()
    for i, mask in enumerate((0, 8, 16, 24)):
        cross_left(left_n, 0, i, mask).wait_send()
        cross_left(left_a, 1, i, mask).wait_send()
        cross_side(i, mask).wait_send()
    for copy in (cross_mixed, cross_q, cross_kv):
        copy.wait_send()
    for s in range(3):
        for k in range(2):
            y_push(s, k).wait_send()
            p_push(s, k).wait_send()
        x_push(s).wait_send()
        h_push(s).wait_send()
    kv_push(0).wait_send()
    kv_push(1).wait_send()
    kv_cross().wait_send()


def back_call(
    ctx_size, hidden_units, grad_two, resid, hidden, grad_out, normed, mixed, query, kv, total, cosine, sine, pos_q, pos_k,
    small, spread, proj, out_w, grads,
):
    rows, model = resid.shape
    shard, wide = grads.shape[3:]
    kv_width = KV_HEADS * HD
    q_width = HEADS * HD
    k_cols = 2 * kv_width + HD
    span = ctx_size * shard
    low, full = jnp.bfloat16, jnp.float32
    vmem = pl.BlockSpec(memory_space=pltpu.VMEM)
    anywhere = pl.BlockSpec(memory_space=pl.ANY)
    shapes = (
        ((rows, model), vmem),
        ((shard, q_width), vmem),
        ((shard, k_cols), vmem),
        ((shard, q_width), vmem),
        ((shard, hidden_units), anywhere),
        ((shard, hidden_units), anywhere),
        ((shard, hidden_units), anywhere),
    )
    sem = pltpu.SemaphoreType.DMA
    cols = (q_width, q_width, k_cols)

    def each(*lead):
        return [pltpu.VMEM(lead + (n,), low) for n in cols]

    return pl.pallas_call(
        functools.partial(back_kernel, ctx_size),
        out_shape=tuple(jax.ShapeDtypeStruct(shape, full) for shape, _ in shapes),
        in_specs=[vmem] * 15 + [anywhere] * 3,
        out_specs=tuple(spec for _, spec in shapes),
        scratch_shapes=[
            pltpu.VMEM(proj.shape, low),
            pltpu.VMEM((2, model, rows), low),
            pltpu.VMEM((4, span, 2 * rows), low),
            pltpu.VMEM((4, span, 2 * rows), low),
            pltpu.VMEM((2 * rows, q_width), low),
            pltpu.VMEM((2 * rows, q_width + 2 * kv_width), low),
            pltpu.VMEM((model, HD), low),
            pltpu.VMEM((4, span, HD), low),
            *each(4, span),
            *each(2, span),
            *each(span),
            *each(2, shard),
            *each(shard),
            pltpu.VMEM((8, shard, wide), low),
            pltpu.VMEM((2, 8, shard, wide), low),
            pltpu.VMEM((8, shard, wide), low),
            pltpu.VMEM((8, shard, wide), low),
            pltpu.VMEM((2, shard, wide), full),
            pltpu.VMEM((HEADS, rows, HD), low),
            pltpu.VMEM((HD, rows), full),
            pltpu.VMEM((ctx_size * rows, 2 * kv_width), full),
            pltpu.VMEM((ctx_size, rows, 2 * kv_width), low),
            pltpu.VMEM((2, rows, 2 * kv_width), low),
            pltpu.VMEM((rows, 2 * kv_width), low),
            pltpu.VMEM((rows, model), full),
            sem((3,)), sem((2, 8)), sem((2, 8)), sem((8,)), sem((8,)), sem((8,)), sem((8,)),
            sem((4, 4)), sem((4, 4)), sem((3, 6)), sem((3, 6)), sem((3,)), sem((3,)), sem((2,)),
        ],
        compiler_params=pltpu.CompilerParams(
            collective_id=2, has_side_effects=True, vmem_limit_bytes=63 << 20
        ),
        name="back",
    )(
        grad_two, resid, hidden, grad_out, normed, mixed, query, kv, total, cosine, sine, pos_q, pos_k, small, spread,
        proj, out_w, grads,
    )


def fits(mesh):
    return mesh.shape["dp"] == 8 and mesh.shape["ctx"] == 4


def fast_device(
    hidden,
    cotangent,
    span_order,
    attn_gain,
    w_query,
    b_query,
    w_key,
    b_key,
    w_value,
    b_value,
    w_out,
    ffn_gain,
    w_gate,
    w_up,
    w_down,
):
    ctx_size = lax.axis_size("ctx")
    ctx_rank = lax.axis_index("ctx")
    batches = hidden.shape[0]
    length = hidden.shape[1]
    span_len = length // 2
    seq_len = length * ctx_size
    row_count = batches * length
    shard_rows = w_query.shape[0]
    kv_width = KV_HEADS * HD
    q_width = HEADS * HD

    grad_out = cotangent.reshape(row_count, D)
    places = jnp.arange(seq_len, dtype=jnp.int32)
    every_pos = jnp.repeat(span_order, span_len, axis=1) * span_len + places[None, :] % span_len
    local_pos = lax.dynamic_slice_in_dim(every_pos, ctx_rank * length, length, 1)
    cosine, sine = angles_for(local_pos.reshape(row_count), HD)
    cos_full = jnp.concatenate([cosine[:, 0], cosine[:, 0]], axis=1)
    sin_full = jnp.concatenate([-sine[:, 0], sine[:, 0]], axis=1)

    gains = jnp.stack([attn_gain, b_query, ffn_gain], axis=1)
    per = b_key.shape[0]
    pair = jnp.pad(jnp.concatenate([b_key, b_value]), (0, shard_rows - 2 * per))
    packed = jnp.concatenate(
        [w_query, w_key, w_value, gains, pair[:, None], jnp.zeros((shard_rows, 124), jnp.bfloat16)], axis=1
    )
    unit = jnp.arange(2 * kv_width)
    unit = unit % kv_width // per * shard_rows + unit // kv_width * per + unit % per
    spread = (jnp.arange(D)[:, None] == unit[None, :]).astype(jnp.bfloat16)
    source = hidden.reshape(row_count, D)
    normed, query_heads, key_value, log_total, mixed, resid, normed_two, small, proj_full, out_full, big, go_all = front_call(
        ctx_size, source, cos_full, sin_full, local_pos.reshape(length, 1), every_pos.reshape(1, seq_len), spread,
        packed, w_out, w_gate, w_up, w_down, grad_out,
    )
    tiles, grads = ffn_call(ctx_size, shard_rows, normed_two, go_all, big)
    sums = jnp.sum(tiles.astype(jnp.float32), axis=0)
    result = (resid + sums[1]).astype(jnp.bfloat16).reshape(batches, length, D)
    hidden_grad, w_query_grad, kv_sum, w_out_grad, w_gate_grad, w_up_grad, w_down_grad = back_call(
        ctx_size, w_gate.shape[1], sums[0], resid, source, grad_out, normed, mixed, query_heads, key_value, log_total,
        cos_full, sin_full, local_pos.reshape(1, length), every_pos.reshape(seq_len, 1), small, spread,
        proj_full, out_full, grads,
    )
    sides = kv_sum[:, 2 * kv_width : 2 * kv_width + 4]
    return (
        result,
        hidden_grad.reshape(batches, length, D),
        sides[:, 0],
        w_query_grad,
        sides[:, 1],
        kv_sum[:, :kv_width],
        sides[:per, 3],
        kv_sum[:, kv_width : 2 * kv_width],
        sides[per : 2 * per, 3],
        w_out_grad,
        sides[:, 2],
        w_gate_grad,
        w_up_grad,
        w_down_grad,
    )


def general_device(
    hidden,
    cotangent,
    span_order,
    attn_gain,
    w_query,
    b_query,
    w_key,
    b_key,
    w_value,
    b_value,
    w_out,
    ffn_gain,
    w_gate,
    w_up,
    w_down,
):
    ctx_size = lax.axis_size("ctx")
    ctx_rank = lax.axis_index("ctx")
    batches = hidden.shape[0]
    length = hidden.shape[1]
    span_len = length // 2
    seq_len = length * ctx_size
    row_count = batches * length
    groups = HEADS // KV_HEADS
    shard_rows = w_query.shape[0]
    head_scale = HD ** (-0.5)
    kv_width = KV_HEADS * HD
    q_width = HEADS * HD
    places = jnp.arange(seq_len, dtype=jnp.int32)
    every_pos = jnp.repeat(span_order, span_len, axis=1) * span_len + places[None, :] % span_len
    local_pos = lax.dynamic_slice_in_dim(every_pos, ctx_rank * length, length, 1)
    cosine, sine = angles_for(local_pos.reshape(row_count), HD)
    allowed = (every_pos[:, None, :] <= local_pos[:, :, None])[:, None, None]
    attn_full = (
        lax.all_gather(attn_gain, ("dp", "ctx"), axis=0, tiled=True),
        lax.all_gather(w_query, ("dp", "ctx"), axis=0, tiled=True),
        lax.all_gather(w_key, ("dp", "ctx"), axis=0, tiled=True),
        lax.all_gather(w_value, ("dp", "ctx"), axis=0, tiled=True),
        lax.all_gather(w_out, ("dp", "ctx"), axis=0, tiled=True),
        lax.all_gather(b_query, ("dp", "ctx"), axis=0, tiled=True),
        lax.all_gather(b_key, ("dp", "ctx"), axis=0, tiled=True),
        lax.all_gather(b_value, ("dp", "ctx"), axis=0, tiled=True),
    )
    gain_one = attn_full[0].astype(jnp.float32)
    source = hidden.reshape(row_count, D).astype(jnp.float32)
    attn_factor, normed = norm_forward(source, gain_one)
    query_raw = plain_dot(normed, attn_full[1]) + attn_full[5].astype(jnp.float32)
    key_raw = plain_dot(normed, attn_full[2]) + attn_full[6].astype(jnp.float32)
    value_low = (plain_dot(normed, attn_full[3]) + attn_full[7].astype(jnp.float32)).astype(
        jnp.bfloat16
    )
    query_rot = rotate(query_raw.reshape(row_count, HEADS, HD), cosine, sine).astype(jnp.bfloat16)
    query_rot = query_rot.reshape(batches, length, KV_HEADS, groups, HD)
    key_rot = rotate(key_raw.reshape(row_count, KV_HEADS, HD), cosine, sine).astype(jnp.bfloat16)
    key_rot = key_rot.reshape(batches, length, kv_width)
    key_all, value_all = (
        lax.all_gather(key_rot, "ctx", axis=1, tiled=True),
        lax.all_gather(value_low.reshape(batches, length, kv_width), "ctx", axis=1, tiled=True),
    )
    key_all = key_all.reshape(batches, seq_len, KV_HEADS, HD)
    value_all = value_all.reshape(batches, seq_len, KV_HEADS, HD)
    scores = (
        jnp.einsum("bqkgd,bskd->bkgqs", query_rot, key_all, preferred_element_type=jnp.float32)
        * head_scale
    )
    masked = jnp.where(allowed, scores, masked_fill)
    row_max = jnp.max(masked, axis=-1, keepdims=True)
    expo = jnp.exp(masked - row_max)
    expo_sum = jnp.sum(expo, axis=-1, keepdims=True)
    log_total = row_max + jnp.log(expo_sum)
    attend = (expo / expo_sum).astype(jnp.bfloat16)
    mixed = jnp.einsum("bkgqs,bskd->bqkgd", attend, value_all, preferred_element_type=jnp.float32)
    mixed = mixed.reshape(row_count, q_width).astype(jnp.bfloat16)
    resid = source + right_dot(mixed, attn_full[4])
    ffn_full = (
        lax.all_gather(ffn_gain, ("dp", "ctx"), axis=0, tiled=True),
        lax.all_gather(w_gate, ("dp", "ctx"), axis=0, tiled=True),
        lax.all_gather(w_up, ("dp", "ctx"), axis=0, tiled=True),
        lax.all_gather(w_down, ("dp", "ctx"), axis=0, tiled=True),
    )
    gain_two = ffn_full[0].astype(jnp.float32)
    ffn_factor, normed_two = norm_forward(resid, gain_two)
    gate_pre = plain_dot(normed_two, ffn_full[1])
    up_pre = plain_dot(normed_two, ffn_full[2])
    sigmoid_gate = jax.nn.sigmoid(gate_pre)
    silu_gate = gate_pre * sigmoid_gate
    act = (silu_gate * up_pre).astype(jnp.bfloat16)
    output = resid + right_dot(act, ffn_full[3])
    result = output.astype(jnp.bfloat16).reshape(batches, length, D)
    ffn_back = (
        lax.all_gather(ffn_gain, ("dp", "ctx"), axis=0, tiled=True),
        lax.all_gather(w_gate, ("dp", "ctx"), axis=0, tiled=True),
        lax.all_gather(w_up, ("dp", "ctx"), axis=0, tiled=True),
        lax.all_gather(w_down, ("dp", "ctx"), axis=0, tiled=True),
    )
    grad_out = cotangent.reshape(row_count, D)
    grad_plain = grad_out.astype(jnp.float32)
    grad_act = plain_dot(grad_out, ffn_back[3])
    grad_gate = (grad_act * up_pre * sigmoid_gate * (1.0 + gate_pre * (1.0 - sigmoid_gate))).astype(
        jnp.bfloat16
    )
    grad_up = (grad_act * silu_gate).astype(jnp.bfloat16)
    pieces = (
        lax.all_gather(normed_two, "ctx", axis=0, tiled=True),
        lax.all_gather(grad_gate, "ctx", axis=0, tiled=True),
        lax.all_gather(grad_up, "ctx", axis=0, tiled=True),
        lax.all_gather(act, "ctx", axis=0, tiled=True),
        lax.all_gather(grad_out, "ctx", axis=0, tiled=True),
    )
    picked_in = owned_columns(pieces[0], ctx_size, ctx_rank, shard_rows)
    picked_out = owned_columns(pieces[4], ctx_size, ctx_rank, shard_rows)
    w_gate_grad, w_up_grad, w_down_grad = (
        lax.psum_scatter(
            outer_add(picked_in, pieces[1]).astype(jnp.bfloat16),
            "dp",
            scatter_dimension=0,
            tiled=True,
        ).astype(jnp.float32),
        lax.psum_scatter(
            outer_add(picked_in, pieces[2]).astype(jnp.bfloat16),
            "dp",
            scatter_dimension=0,
            tiled=True,
        ).astype(jnp.float32),
        lax.psum_scatter(
            outer_add(picked_out, pieces[3]).astype(jnp.bfloat16),
            "dp",
            scatter_dimension=0,
            tiled=True,
        ).astype(jnp.float32),
    )
    grad_norm_two = right_dot(grad_gate, ffn_back[1]) + right_dot(grad_up, ffn_back[2])
    resid_back, ffn_gain_part = norm_backward(resid, ffn_factor, gain_two, grad_norm_two)
    grad_resid = grad_plain + resid_back
    attn_back = (
        lax.all_gather(attn_gain, ("dp", "ctx"), axis=0, tiled=True),
        lax.all_gather(w_query, ("dp", "ctx"), axis=0, tiled=True),
        lax.all_gather(w_key, ("dp", "ctx"), axis=0, tiled=True),
        lax.all_gather(w_value, ("dp", "ctx"), axis=0, tiled=True),
        lax.all_gather(w_out, ("dp", "ctx"), axis=0, tiled=True),
        lax.all_gather(b_query, ("dp", "ctx"), axis=0, tiled=True),
        lax.all_gather(b_key, ("dp", "ctx"), axis=0, tiled=True),
        lax.all_gather(b_value, ("dp", "ctx"), axis=0, tiled=True),
    )
    grad_attn = grad_resid.astype(jnp.bfloat16)
    grad_mixed = plain_dot(grad_attn, attn_back[4]).astype(jnp.bfloat16)
    grad_mixed = grad_mixed.reshape(batches, length, KV_HEADS, groups, HD)
    scores = (
        jnp.einsum("bqkgd,bskd->bkgqs", query_rot, key_all, preferred_element_type=jnp.float32)
        * head_scale
    )
    masked = jnp.where(allowed, scores, masked_fill)
    attend_full = jnp.exp(masked - log_total)
    attend = attend_full.astype(jnp.bfloat16)
    grad_attend = jnp.einsum(
        "bqkgd,bskd->bkgqs", grad_mixed, value_all, preferred_element_type=jnp.float32
    )
    value_grad_all = jnp.einsum(
        "bkgqs,bqkgd->bskd", attend, grad_mixed, preferred_element_type=jnp.float32
    )
    delta = jnp.sum(grad_attend * attend_full, axis=-1, keepdims=True)
    grad_scores = (attend_full * (grad_attend - delta)).astype(jnp.bfloat16)
    query_grad_rot = (
        jnp.einsum("bkgqs,bskd->bqkgd", grad_scores, key_all, preferred_element_type=jnp.float32)
        * head_scale
    )
    key_grad_all = (
        jnp.einsum("bkgqs,bqkgd->bskd", grad_scores, query_rot, preferred_element_type=jnp.float32)
        * head_scale
    )
    key_grad_rot, value_grad = (
        lax.psum_scatter(
            key_grad_all.reshape(batches, seq_len, kv_width), "ctx", scatter_dimension=1, tiled=True
        ),
        lax.psum_scatter(
            value_grad_all.reshape(batches, seq_len, kv_width),
            "ctx",
            scatter_dimension=1,
            tiled=True,
        ),
    )
    query_grad = (
        rotate_back(query_grad_rot.reshape(row_count, HEADS, HD), cosine, sine)
        .reshape(row_count, q_width)
        .astype(jnp.bfloat16)
    )
    key_grad = (
        rotate_back(key_grad_rot.reshape(row_count, KV_HEADS, HD), cosine, sine)
        .reshape(row_count, kv_width)
        .astype(jnp.bfloat16)
    )
    value_grad = value_grad.reshape(row_count, kv_width).astype(jnp.bfloat16)
    proj_grad = jnp.concatenate([query_grad, key_grad, value_grad], axis=1)
    pieces = (
        lax.all_gather(normed, "ctx", axis=0, tiled=True),
        lax.all_gather(proj_grad, "ctx", axis=0, tiled=True),
        lax.all_gather(grad_attn, "ctx", axis=0, tiled=True),
        lax.all_gather(mixed, "ctx", axis=0, tiled=True),
    )
    picked_in = owned_columns(pieces[0], ctx_size, ctx_rank, shard_rows)
    picked_out = owned_columns(pieces[2], ctx_size, ctx_rank, shard_rows)
    proj_sum, w_out_grad = (
        lax.psum_scatter(
            outer_add(picked_in, pieces[1]).astype(jnp.bfloat16),
            "dp",
            scatter_dimension=0,
            tiled=True,
        ).astype(jnp.float32),
        lax.psum_scatter(
            outer_add(picked_out, pieces[3]).astype(jnp.bfloat16),
            "dp",
            scatter_dimension=0,
            tiled=True,
        ).astype(jnp.float32),
    )
    grad_norm_one = (
        right_dot(query_grad, attn_back[1])
        + right_dot(key_grad, attn_back[2])
        + right_dot(value_grad, attn_back[3])
    )
    source_back, attn_gain_part = norm_backward(source, attn_factor, gain_one, grad_norm_one)
    hidden_grad = (grad_resid + source_back).reshape(batches, length, D)
    query_bias_part = jnp.sum(query_grad.astype(jnp.float32), axis=0)
    key_bias_part = jnp.sum(key_grad.astype(jnp.float32), axis=0)
    value_bias_part = jnp.sum(value_grad.astype(jnp.float32), axis=0)
    small_sums = (
        lax.psum_scatter(attn_gain_part, ("dp", "ctx"), scatter_dimension=0, tiled=True),
        lax.psum_scatter(query_bias_part, ("dp", "ctx"), scatter_dimension=0, tiled=True),
        lax.psum_scatter(key_bias_part, ("dp", "ctx"), scatter_dimension=0, tiled=True),
        lax.psum_scatter(value_bias_part, ("dp", "ctx"), scatter_dimension=0, tiled=True),
        lax.psum_scatter(ffn_gain_part, ("dp", "ctx"), scatter_dimension=0, tiled=True),
    )
    w_query_grad = proj_sum[:, :q_width]
    w_key_grad = proj_sum[:, q_width : q_width + kv_width]
    w_value_grad = proj_sum[:, q_width + kv_width :]
    return (
        result,
        hidden_grad,
        small_sums[0],
        w_query_grad,
        small_sums[1],
        w_key_grad,
        small_sums[2],
        w_value_grad,
        small_sums[3],
        w_out_grad,
        small_sums[4],
        w_gate_grad,
        w_up_grad,
        w_down_grad,
    )


def solution(mesh):
    placed = (
        P("dp", "ctx", None),
        P("dp", "ctx", None),
        P("dp", None),
        P(("dp", "ctx")),
        P(("dp", "ctx"), None),
        P(("dp", "ctx")),
        P(("dp", "ctx"), None),
        P(("dp", "ctx")),
        P(("dp", "ctx"), None),
        P(("dp", "ctx")),
        P(("dp", "ctx"), None),
        P(("dp", "ctx")),
        P(("dp", "ctx"), None),
        P(("dp", "ctx"), None),
        P(("dp", "ctx"), None),
    )
    return jax.shard_map(
        fast_device if fits(mesh) else general_device,
        mesh=mesh,
        in_specs=placed,
        out_specs=(
            P("dp", "ctx", None),
            P("dp", "ctx", None),
            P(("dp", "ctx")),
            P(("dp", "ctx"), None),
            P(("dp", "ctx")),
            P(("dp", "ctx"), None),
            P(("dp", "ctx")),
            P(("dp", "ctx"), None),
            P(("dp", "ctx")),
            P(("dp", "ctx"), None),
            P(("dp", "ctx")),
            P(("dp", "ctx"), None),
            P(("dp", "ctx"), None),
            P(("dp", "ctx"), None),
        ),
        check_vma=False,
    )
```

```python
import functools

import jax
import jax.numpy as jnp
from jax import lax
from jax.experimental import pallas as pl
from jax.experimental.pallas import tpu as pltpu
from jax.sharding import PartitionSpec as P

D = 1536
HEADS = 12
KV_HEADS = 2
HD = 128


norm_eps = 1e-06
rope_base = 10000.0
masked_fill = -1e30


def angles_for(places, width):
    half = width // 2
    freqs = rope_base ** (-(jnp.arange(half, dtype=jnp.float32) * 2.0 / width))
    angles = places.astype(jnp.float32)[:, None] * freqs[None, :]
    return (jnp.cos(angles)[:, None, :], jnp.sin(angles)[:, None, :])


def rotate(values, cosine, sine):
    half = values.shape[-1] // 2
    first = values[..., :half]
    second = values[..., half:]
    return jnp.concatenate(
        [first * cosine - second * sine, second * cosine + first * sine], axis=-1
    )


def rotate_back(values, cosine, sine):
    half = values.shape[-1] // 2
    first = values[..., :half]
    second = values[..., half:]
    return jnp.concatenate(
        [first * cosine + second * sine, second * cosine - first * sine], axis=-1
    )


def norm_forward(source, gain):
    factor = lax.rsqrt(jnp.mean(source * source, axis=-1, keepdims=True) + norm_eps)
    return (factor, (source * factor * gain).astype(jnp.bfloat16))


def norm_backward(source, factor, gain, grad_normed):
    unit = source * factor
    gain_grad = jnp.sum(grad_normed * unit, axis=0)
    scaled = grad_normed * gain
    source_grad = factor * (scaled - unit * jnp.mean(scaled * unit, axis=-1, keepdims=True))
    return (source_grad, gain_grad)


def right_dot(left, weight):
    return jnp.einsum("rf,df->rd", left, weight, preferred_element_type=jnp.float32)


def plain_dot(left, weight):
    return jnp.dot(left, weight, preferred_element_type=jnp.float32)


def owned_columns(values, ctx_size, ctx_rank, shard_rows):
    rows = values.shape[0]
    blocks = values.shape[1] // (shard_rows * ctx_size)
    shaped = values.reshape(rows, blocks, ctx_size, shard_rows)
    picked = lax.dynamic_index_in_dim(shaped, ctx_rank, axis=2, keepdims=False)
    return picked.reshape(rows, blocks * shard_rows)


def outer_add(left, right):
    return jnp.einsum("rc,rf->cf", left, right, preferred_element_type=jnp.float32)


MESH = pl.DeviceIdType.MESH


def flip(index, mask):
    for bit in (1, 2, 4, 8, 16):
        if mask & bit:
            index = index + bit - 2 * bit * ((index // bit) % 2)
    return index


def either(a, b):
    return a + b - 2 * a * b


def dot(a, b, dims):
    return lax.dot_general(a, b, (dims, ((), ())), preferred_element_type=jnp.float32)


def widths(hidden_units):
    width = -(-hidden_units // (8 * 128)) * 128
    first = width // 384 * 256
    return (first, width - first)


def ffn_kernel(
    ctx_size, n_own, go_all, big, big_two,
    grad_two, r_part, grads, grads_two, near, zin,
    w_one, w_two, nt, go, ggu, act, crecv, part, h_in, h_mid, stage, own, far,
    io_sem, n_send, n_recv, f_send, f_recv, c_send, c_recv, o_send, o_recv, st_sem, w_send, w_recv, l_sem, x_send, x_recv, z_send, z_recv, d_sem,
):
    dp = lax.axis_index("dp")
    ctx = lax.axis_index("ctx")
    me = dp * ctx_size + ctx
    y, x, c = dp // 4, (dp // 2) % 2, dp % 2
    h, p = ctx // 2, ctx % 2
    one, two = w_one.shape[1] // 3, w_two.shape[1] // 3
    shard = grads.shape[3]
    rows, model = n_own.shape
    low, full = jnp.bfloat16, jnp.float32

    def at(index):
        return (index // ctx_size, index % ctx_size)

    def remote(src, dst, send, recv, mask):
        return pltpu.make_async_remote_copy(
            src_ref=src, dst_ref=dst, send_sem=send, recv_sem=recv, device_id=at(flip(me, mask)), device_id_type=MESH
        )

    def block(mask):
        return pl.ds(pl.multiple_of(flip(me, mask) * shard, shard), shard)

    barrier = pltpu.get_barrier_semaphore()
    partners = (1, 2, 4, 8, 16)
    for mask in partners:
        pl.semaphore_signal(barrier, inc=1, device_id=at(flip(me, mask)), device_id_type=MESH)
    load_n = pltpu.make_async_copy(n_own, nt.at[0], io_sem.at[0])
    load_w = pltpu.make_async_copy(big, w_one, io_sem.at[1])
    load_go = pltpu.make_async_copy(go_all, go, io_sem.at[2])
    held = (0, 4, 1, 5, 16, 20, 17, 21)
    load_l = [
        pltpu.make_async_copy(big_two.at[block(mask)], w_two.at[block(mask)], l_sem.at[i]) for i, mask in enumerate(held)
    ]
    for copy in (load_n, load_w, load_go, *load_l):
        copy.start()
    pl.semaphore_wait(barrier, len(partners))

    def spread_two(mask, over):
        remote(big_two.at[block(mask)], w_two.at[block(mask)], w_send.at[0], w_recv.at[mask | over], over).start()

    def w_wait(mask):
        remote(w_two.at[block(mask)], w_two.at[block(mask)], w_send.at[0], w_recv.at[mask], 1).wait_recv()

    def w_pass(mask):
        w_wait(mask)
        remote(w_two.at[block(mask)], w_two.at[block(mask)], w_send.at[0], w_recv.at[mask | 8], 8).start()

    def n_core(slot):
        return remote(nt.at[slot], nt.at[slot + 1], f_send.at[slot // 2], f_recv.at[slot // 2], 4)

    def n_push(o):
        src = nt.at[2] if o == 3 else nt.at[0]
        return remote(src, nt.at[2 * o], n_send.at[o], n_recv.at[o], (0, 1, 16, 16)[o])

    load_n.wait()
    n_push(1).start()
    n_push(2).start()
    n_core(0).start()
    for mask in held:
        spread_two(mask, 2)
    for mask in held:
        spread_two(mask, 8)
    load_w.wait()
    load_go.wait()

    def first(slot):
        gu = dot(nt[slot], w_one[:, : 2 * one], ((1,), (0,)))
        ga = dot(go[slot], w_one[:, 2 * one :], ((1,), (0,)))
        finish(slot, gu[:, :one], gu[:, one:], ga, 0, 0)

    def finish(slot, gate, up, ga, at_gu, at_act):
        size = gate.shape[1]
        sig = 1.0 / (1.0 + jnp.exp(-gate))
        silu = gate * sig
        act[slot, :, pl.ds(at_act, size)] = (silu * up).astype(low)
        ggu[slot, :, pl.ds(at_gu, size)] = (ga * up * sig * (1.0 + gate * (1.0 - sig))).astype(low)
        ggu[slot, :, pl.ds(at_gu + size, size)] = (ga * silu).astype(low)

    def second(slot):
        gu = dot(nt[slot], w_two[:, : 2 * two], ((1,), (0,)))
        ga = dot(go[slot], w_two[:, 2 * two :], ((1,), (0,)))
        finish(slot, gu[:, :two], gu[:, two:], ga, 2 * one, one)
        grad = dot(ggu[slot, :, : 2 * one], w_one[:, : 2 * one], ((1,), (1,)))
        grad = grad + dot(ggu[slot, :, 2 * one :], w_two[:, : 2 * two], ((1,), (1,)))
        out = dot(act[slot, :, :one], w_one[:, 2 * one :], ((1,), (1,)))
        out = out + dot(act[slot, :, one:], w_two[:, 2 * two :], ((1,), (1,)))
        return (grad.astype(low), out.astype(low))

    def early(o, carry):
        @pl.when(o == 1)
        def _():
            n_push(1).wait_recv()
            n_push(3).start()
            n_core(2).start()
            n_push(2).wait_recv()
            n_core(4).start()

        @pl.when(o == 3)
        def _():
            n_push(3).wait_recv()
            n_core(6).start()

        first(2 * o)

        @pl.when(o == 1)
        def _():
            for mask in (2, 6, 3):
                w_pass(mask)

        @pl.when(o == 2)
        def _():
            for mask in (7, 18, 22):
                w_pass(mask)

        n_core(2 * o).wait_recv()
        first(2 * o + 1)
        return carry

    lax.fori_loop(0, 4, early, 0)
    for mask in (19, 23):
        w_pass(mask)
    def stage_wait(slot, size):
        part_of = stage.at[slot, :, pl.ds(0, size)]
        pltpu.make_async_copy(part_of, part_of, st_sem.at[slot]).wait()

    def weights(size, start_gu, start_act, to, q, carry):
        slot = q % 2

        @pl.when(q > 1)
        def _():
            stage_wait(slot, 3 * size)

        chunk = 8 * shard
        cols = pl.ds(pl.multiple_of(q * chunk, chunk), chunk)

        def product(left, right, start, count, at_col):
            left = left[:, :, cols].reshape(8 * rows, chunk)
            right = right[:, :, pl.ds(start, count)].reshape(8 * rows, count)
            stage[slot, :, pl.ds(at_col, count)] = dot(left, right, ((0,), (0,))).astype(low)

        for start in range(0, 2 * size, one):
            count = min(one, 2 * size - start)
            product(nt, ggu, start_gu + start, count, start)
        product(go, act, start_act, size, 2 * size)
        yr, xr = either(q // 2, y), either(q % 2, x)
        for j in range(8):
            cr, hrel, pr = either(j // 4, c), either((j // 2) % 2, h), either(j % 2, p)
            pltpu.make_async_copy(
                stage.at[slot, pl.ds(j * shard, shard), pl.ds(0, 3 * size)],
                to.at[xr, hrel, yr * 4 + cr * 2 + pr], st_sem.at[slot],
            ).start()
        return carry

    def all_weights(size, start_gu, start_act, to):
        lax.fori_loop(0, 4, functools.partial(weights, size, start_gu, start_act, to), 0)
        stage_wait(0, 3 * size)
        stage_wait(1, 3 * size)

    def far_push(j):
        return remote(grads.at[1, 1, j], far.at[j], x_send.at[j], x_recv.at[j], 8)

    def z_push(j):
        return remote(far.at[j], zin.at[j], z_send.at[j], z_recv.at[j], 2)

    def load_own(k):
        return pltpu.make_async_copy(grads.at[0, 1, pl.ds(4 * k, 4)], own, d_sem.at[0])

    keep_near = pltpu.make_async_copy(far, near, d_sem.at[0])

    def far_pass(*blocks):
        for j in blocks:
            far_push(j).wait_recv()
            far[j] = (far[j].astype(full) + own[j % 4].astype(full)).astype(low)
            if j < 4:
                z_push(j).start()

    all_weights(one, 0, 0, grads)
    for j in range(8):
        far_push(j).start()
    load_own(0).start()

    for mask in (8, 12, 9, 13, 24, 28, 25, 29, 10, 14, 11, 15, 26, 30, 27, 31):
        w_wait(mask)
    for copy in load_l:
        copy.wait()

    def cross(o):
        return remote(stage.at[:, pl.ds(0, rows), pl.ds(0, model)], crecv.at[o % 2], c_send, c_recv.at[o % 2], 4)

    def final(o):
        dst = h_mid if o == 3 else h_in.at[o - 1]
        return remote(part.at[o, 0], dst, o_send.at[o], o_recv.at[o], (0, 1, 16, 16)[o])

    def keep(o):
        return pltpu.make_async_copy(part.at[o, 1], r_part.at[o], io_sem.at[o])

    def combine(o):
        cross(o).wait_recv()
        part[o] = (part[o].astype(full) + crecv[o % 2].astype(full)).astype(low)
        keep(o).start()

    def late(n, carry):
        o = 3 - n
        grad, out = second(2 * o)
        part[o, 0] = grad
        part[o, 1] = out

        @pl.when(n > 0)
        def _():
            combine(o + 1)

        @pl.when(n == 1)
        def _():
            final(3).start()
            load_own(0).wait()
            far_pass(0, 1)

        @pl.when(n == 2)
        def _():
            final(2).start()
            far_pass(2, 3)
            load_own(1).start()

        @pl.when(n == 3)
        def _():
            final(3).wait_recv()
            part[1, 0] = (part[1, 0].astype(full) + h_mid[...].astype(full)).astype(low)
            final(1).start()
            load_own(1).wait()
            far_pass(4, 5)

        grad, out = second(2 * o + 1)

        @pl.when(n > 0)
        def _():
            cross(o).wait_send()

        stage[0, pl.ds(0, rows), pl.ds(0, model)] = grad
        stage[1, pl.ds(0, rows), pl.ds(0, model)] = out
        cross(o).start()
        return carry

    lax.fori_loop(0, 4, late, 0)

    far_pass(6, 7)
    keep_near.start()
    cross(0).wait_send()
    all_weights(two, 2 * one, one, grads_two)
    combine(0)
    grad_two[...] = part[0, 0].astype(full)
    for o in (1, 2):
        final(o).wait_recv()
        grad_two[...] += h_in[o - 1].astype(full)
    keep_near.wait()
    for j in range(8):
        far_push(j).wait_send()
        if j < 4:
            z_push(j).wait()
    for o in range(4):
        keep(o).wait()
        n_core(2 * o).wait_send()
    for o in (1, 2, 3):
        n_push(o).wait_send()
        final(o).wait_send()
    sent = w_two.at[pl.ds(0, 24 * shard)]
    pltpu.make_async_copy(sent, sent, w_send.at[0]).wait()


def ffn_call(ctx_size, shard, n_own, go_all, big, big_two):
    rows, model = n_own.shape
    one, two = big.shape[1] // 3, big_two.shape[1] // 3
    low = jnp.bfloat16
    anywhere = pl.BlockSpec(memory_space=pl.ANY)
    sem = pltpu.SemaphoreType.DMA
    return pl.pallas_call(
        functools.partial(ffn_kernel, ctx_size),
        out_shape=(
            jax.ShapeDtypeStruct((rows, model), jnp.float32),
            jax.ShapeDtypeStruct((4, rows, model), low),
            jax.ShapeDtypeStruct((2, 2, 8, shard, 3 * one), low),
            jax.ShapeDtypeStruct((2, 2, 8, shard, 3 * two), low),
            jax.ShapeDtypeStruct((8, shard, 3 * one), low),
            jax.ShapeDtypeStruct((4, shard, 3 * one), low),
        ),
        in_specs=[anywhere] * 4,
        out_specs=[pl.BlockSpec(memory_space=pltpu.VMEM)] + [anywhere] * 5,
        scratch_shapes=[
            pltpu.VMEM((model, 3 * one), low),
            pltpu.VMEM((model, 3 * two), low),
            pltpu.VMEM((8, rows, model), low),
            pltpu.VMEM((8, rows, model), low),
            pltpu.VMEM((8, rows, 2 * (one + two)), low),
            pltpu.VMEM((8, rows, one + two), low),
            pltpu.VMEM((2, 2, rows, model), low),
            pltpu.VMEM((4, 2, rows, model), low),
            pltpu.VMEM((2, rows, model), low),
            pltpu.VMEM((rows, model), low),
            pltpu.VMEM((2, 8 * shard, 3 * one), low),
            pltpu.VMEM((4, shard, 3 * one), low),
            pltpu.VMEM((8, shard, 3 * one), low),
            sem((4,)), sem((5,)), sem((5,)), sem((4,)), sem((4,)), sem, sem((2,)), sem((4,)), sem((4,)), sem((2,)),
            sem((1,)), sem((32,)), sem((8,)), sem((8,)), sem((8,)), sem((4,)), sem((4,)), sem((1,)),
        ],
        compiler_params=pltpu.CompilerParams(
            collective_id=1, has_side_effects=True, vmem_limit_bytes=65200 << 10
        ),
        name="ffn",
    )(n_own, go_all, big, big_two)


def turn(values, cosine, sine):
    return values * cosine + pltpu.roll(values, HD // 2, 1) * sine


def front_kernel(
    ctx_size, hidden, cosine, sine, pos_q, pos_k, spread, packed, w_out, w_gate, w_up, w_down, grad_out,
    normed_o, query_o, kv_o, total_o, mixed_o, resid_o, normed_two_o, small_o, proj_o, out_o, big, big_two, go, relay,
    proj, out_w, source, source_two, query, kv, mixed,
    load_sem, ag_send, ag_recv, core_send, core_recv, big_send, big_recv, two_recv, relay_recv, go_send, go_recv, kv_send, kv_recv, back_sem,
):
    dp = lax.axis_index("dp")
    ctx = lax.axis_index("ctx")
    me = dp * ctx_size + ctx
    shard, wide = packed.shape
    rows, model = hidden.shape
    one, two = big.shape[1] // 3, big_two.shape[1] // 3
    kv_width = KV_HEADS * HD
    q_width = HEADS * HD
    proj_width = q_width + 2 * kv_width
    groups = HEADS // KV_HEADS

    def at(index):
        return (index // ctx_size, index % ctx_size)

    def block(mask, count=1):
        base = flip(me, mask) // count * count
        return pl.ds(pl.multiple_of(base * shard, shard), shard * count)

    def remote(src, dst, send, recv, mask):
        return pltpu.make_async_remote_copy(
            src_ref=src, dst_ref=dst, send_sem=send, recv_sem=recv, device_id=at(flip(me, mask)), device_id_type=MESH
        )

    def drain(ref, sem):
        pltpu.make_async_copy(ref, ref, sem).wait()

    barrier = pltpu.get_barrier_semaphore()
    partners = (1, 2, 3, 4, 5, 8, 16, 17, 20, 21)
    for mask in partners:
        pl.semaphore_signal(barrier, inc=1, device_id=at(flip(me, mask)), device_id_type=MESH)

    own = (
        pltpu.make_async_copy(packed, proj.at[block(0)], load_sem.at[0]),
        pltpu.make_async_copy(w_out, out_w.at[block(0)], load_sem.at[1]),
    )
    for copy in own:
        copy.start()
    hidden_units = w_gate.shape[1]
    cuts = []
    for k in range(8):
        for n, ref in enumerate((w_gate, w_up, w_down)):
            for to, start, width in ((source, k * (one + two), one), (source_two, k * (one + two) + one, two)):
                size = min(width, hidden_units - start)
                cuts.append((ref.at[:, pl.ds(start, size)], to.at[k, :, pl.ds(n * width, size)]))
                if size < width:
                    to[k, :, pl.ds(n * width + size, width - size)] = jnp.zeros((shard, width - size), to.dtype)
    cuts = [pltpu.make_async_copy(a, b, load_sem.at[2 + i]) for i, (a, b) in enumerate(cuts)]
    for copy in cuts:
        copy.start()
    pl.semaphore_wait(barrier, len(partners))
    for copy in own:
        copy.wait()

    q_cols, k_cols = pl.ds(0, q_width), pl.ds(q_width, wide - q_width)
    streams = ((proj, k_cols), (proj, q_cols), (out_w, q_cols))

    def ag(n, mask, *overs):
        ref, cols = streams[n]
        part = ref.at[block(mask), cols]
        for over in overs:
            remote(part, part, ag_send.at[n], ag_recv.at[n, mask | over], over).start()

    def ag_pass(n, mask, *overs):
        ref, cols = streams[n]
        part = ref.at[block(mask), cols]
        remote(part, part, ag_send.at[n], ag_recv.at[n, mask], 1).wait_recv()
        ag(n, mask, *overs)

    def group(n, mask):
        ref, cols = streams[n]
        part = ref.at[block(mask, 4), cols]
        return remote(part, part, core_send.at[n, mask // 8], core_recv.at[n, mask // 8], 4)

    def group_wait(n):
        ref, cols = streams[n]
        for mask in (0, 8, 16, 24):
            part = ref.at[block(mask | 4, 4), cols]
            remote(part, part, core_send.at[n, mask // 8], core_recv.at[n, mask // 8], 4).wait_recv()

    ag(0, 0, 2, 1, 8, 16)
    ag(1, 0, 2, 1, 8, 16)

    for copy in cuts:
        copy.wait()
    y, x, c = dp // 4, (dp // 2) % 2, dp % 2
    h, p = ctx // 2, ctx % 2

    def column(mask):
        return either(y, mask // 16) * 4 + either(p, mask % 2) * 2 + either(c, (mask // 4) % 2)

    own_big = pltpu.make_async_copy(source.at[column(0)], big.at[block(0)], load_sem.at[0])
    own_big.start()
    own_two = pltpu.make_async_copy(source_two.at[column(0)], big_two.at[block(0)], load_sem.at[1])
    own_two.start()

    def cut(mask):
        remote(source.at[column(mask)], big.at[block(0)], big_send.at[0], big_recv.at[mask], mask).start()

    def cut_two(mask):
        return remote(source_two.at[column(mask)], big_two.at[block(0)], big_send.at[1], two_recv.at[mask], mask)

    held = (0, 4, 1, 5, 16, 20, 17, 21)
    inner = either(h, p) == 1

    def over_z(mask):
        src = big.at[block(mask)] if mask else source.at[column(0)]

        @pl.when(inner)
        def _():
            remote(src, big.at[block(mask)], big_send.at[0], big_recv.at[mask | 2], 2).start()

        @pl.when(jnp.logical_not(inner))
        def _():
            i = held.index(mask)
            remote(src, relay.at[i], big_send.at[0], relay_recv.at[i], 1).start()

    def relay_pass(*masks):
        @pl.when(inner)
        def _():
            for mask in masks:
                i = held.index(mask)
                remote(relay.at[i], relay.at[i], big_send.at[0], relay_recv.at[i], 1).wait_recv()
                remote(relay.at[i], big.at[block(mask ^ 1)], big_send.at[2], big_recv.at[mask | 2], 3).start()

    def big_forward(mask, over):
        if over == 2:
            over_z(mask)
        else:
            remote(big.at[block(mask)], big.at[block(mask)], big_send.at[0], big_recv.at[mask | over], over).start()

    def big_pass(mask, *overs):
        remote(big.at[block(mask)], big.at[block(mask)], big_send.at[0], big_recv.at[mask], 1).wait_recv()
        for over in overs:
            big_forward(mask, over)

    cut(4)
    over_z(0)

    ag_pass(0, 1, 8, 16)
    ag_pass(0, 8, 16)
    ag_pass(0, 2, 1, 8, 16)
    ag_pass(0, 9, 16)
    ag_pass(1, 1, 8, 16)
    ag_pass(1, 8, 16)
    ag_pass(0, 3, 8, 16)
    ag_pass(0, 10, 16)
    ag_pass(1, 2, 1, 8, 16)
    group(0, 0).start()
    remote(source.at[column(0)], big.at[block(0)], big_send.at[0], big_recv.at[8], 8).start()
    cut(1)
    cut(5)
    big_pass(4, 2, 8)
    ag_pass(0, 11, 16)
    group(0, 8).start()
    relay_pass(0)
    ag_pass(1, 9, 16)
    ag(2, 0, 2, 1, 16, 8)
    for mask in (16, 17, 18, 19):
        ag_pass(0, mask)
    group(0, 16).start()
    ag_pass(1, 3, 8, 16)
    group(1, 0).start()
    for mask in (24, 25, 26, 27):
        ag_pass(0, mask)
    group(0, 24).start()
    relay_pass(4)
    group_wait(0)

    small = jnp.transpose(proj[:, proj_width:].astype(jnp.float32))
    small_o[...] = small[:8]
    kv_bias = dot(small[:8].astype(jnp.bfloat16), spread[...], ((1,), (0,)))[3:4]
    values = hidden[...].astype(jnp.float32)
    factor = lax.rsqrt(jnp.mean(values * values, axis=-1, keepdims=True) + norm_eps)
    normed_o[...] = (values * factor * small[0:1]).astype(jnp.bfloat16)
    cos, sin = cosine[...], sine[...]
    raw = dot(normed_o[...], proj[:, q_width:proj_width], ((1,), (0,))) + kv_bias
    mine = block(0)
    for g in range(KV_HEADS):
        kv[ctx, :, pl.ds(g * HD, HD)] = turn(raw[:, g * HD : (g + 1) * HD], cos, sin).astype(jnp.bfloat16)
    kv[ctx, :, pl.ds(kv_width, kv_width)] = raw[:, kv_width:].astype(jnp.bfloat16)

    def kv_push(mask, over):
        slot = flip(ctx, mask)
        return remote(kv.at[slot], kv.at[slot], kv_send.at[mask | over], kv_recv.at[mask | over], over)

    kv_push(0, 2).start()
    kv_push(0, 1).start()
    ag_pass(1, 10, 16)
    ag_pass(1, 11, 16)
    group(1, 8).start()
    big_pass(1, 2, 8)
    ag_pass(2, 1, 16, 8)
    ag_pass(2, 2, 1, 16, 8)
    for mask in (16, 20, 17, 21):
        cut(mask)
    kv_push(0, 2).wait_recv()
    kv_push(2, 1).start()
    big_pass(5, 2, 8)
    relay_pass(1)
    for mask in (16, 17, 18, 19):
        ag_pass(1, mask)
    group(1, 16).start()
    ag_pass(2, 3, 16, 8)
    group(2, 0).start()
    for mask in (24, 25, 26, 27):
        ag_pass(1, mask)
    group(1, 24).start()
    big_pass(16, 2, 8)
    relay_pass(5)
    group_wait(1)
    for half in range(2):
        part = half * (q_width // 2)
        raw = dot(normed_o[...], proj[:, part : part + q_width // 2], ((1,), (0,)))
        raw = raw + small[1:2, part : part + q_width // 2]
        for i in range(HEADS // 2):
            query[half * (HEADS // 2) + i] = turn(raw[:, i * HD : (i + 1) * HD], cos, sin).astype(jnp.bfloat16)
    big_pass(20, 2, 8)
    relay_pass(16)
    for mask in (16, 17, 18, 19):
        ag_pass(2, mask, 8)
    group(2, 16).start()
    big_pass(17, 2, 8)
    big_pass(21, 2, 8)
    relay_pass(20)

    def go_core(o):
        src = go.at[2 * o] if o else grad_out
        return remote(src, go.at[2 * o + 1], go_send.at[3 + o], go_recv.at[2 * o + 1], 4)

    def go_push(o):
        src = go.at[2] if o == 3 else grad_out
        return remote(src, go.at[2 * o], go_send.at[o - 1], go_recv.at[2 * o], (0, 1, 16, 16)[o])

    go_push(2).start()
    go_push(1).start()
    go_core(0).start()
    for mask in (2, 6):
        big_pass(mask, 8)
    kv_push(0, 1).wait_recv()
    kv_push(2, 1).wait_recv()
    query_back = pltpu.make_async_copy(query, query_o, back_sem.at[0])
    query_back.start()
    kv_back = pltpu.make_async_copy(kv, kv_o, back_sem.at[1])
    kv_back.start()

    def head(n, carry):
        g = n // groups
        keys = kv[:, :, pl.ds(pl.multiple_of(g * HD, HD), HD)].reshape(ctx_size * rows, HD)
        vals = kv[:, :, pl.ds(pl.multiple_of(kv_width + g * HD, HD), HD)].reshape(ctx_size * rows, HD)
        scores = dot(query[n], keys, ((1,), (1,))) * HD ** (-0.5)
        scores = jnp.where(pos_k[...] <= pos_q[...], scores, masked_fill)
        top = jnp.max(scores, axis=-1, keepdims=True)
        expo = jnp.exp(scores - top)
        expo_sum = jnp.sum(expo, axis=-1, keepdims=True)
        attend = (expo / expo_sum).astype(jnp.bfloat16)
        mixed[:, pl.ds(pl.multiple_of(n * HD, HD), HD)] = dot(attend, vals, ((1,), (0,))).astype(jnp.bfloat16)
        lane = lax.broadcasted_iota(jnp.int32, (rows, HD), 1)
        total_o[...] = jnp.where(lane == n, top + jnp.log(expo_sum), total_o[...])
        return carry

    total_o[...] = jnp.zeros_like(total_o)
    lax.fori_loop(0, HEADS, head, 0)
    own_go = pltpu.make_async_copy(grad_out, go.at[0], load_sem.at[2])
    own_go.start()
    mixed_back = pltpu.make_async_copy(mixed, mixed_o, back_sem.at[2])
    mixed_back.start()
    relay_pass(17, 21)
    for mask in (3, 7):
        big_pass(mask, 8)
    for mask in (4, 1, 5, 16, 20, 17, 21):
        cut_two(mask).start()
    for n, mask in enumerate((8, 9, 10, 11, 24, 25, 26, 27)):
        ag_pass(2, mask)
        if n % 4 == 3:
            group(2, mask & 24).start()
    group_wait(2)
    proj_back = pltpu.make_async_copy(proj, proj_o, back_sem.at[4])
    proj_back.start()
    out_back = pltpu.make_async_copy(out_w, out_o, back_sem.at[5])
    out_back.start()
    resid = hidden[...].astype(jnp.float32) + dot(mixed[...], out_w[...], ((1,), (1,)))
    resid_o[...] = resid
    factor = lax.rsqrt(jnp.mean(resid * resid, axis=-1, keepdims=True) + norm_eps)
    normed_two_o[...] = (resid * factor * small_o[2:3]).astype(jnp.bfloat16)
    go_push(1).wait_recv()
    go_push(3).start()
    go_core(1).start()
    go_push(2).wait_recv()
    go_core(2).start()
    for mask in (18, 22, 19, 23):
        big_pass(mask, 8)

    for mask in (8, 12, 9, 24, 13, 28, 25, 29, 10, 14, 11, 26, 15, 30, 27, 31):
        big_pass(mask)
    go_push(3).wait_recv()
    go_core(3).start()
    for mask in (4, 1, 5, 16, 20, 17, 21):
        cut_two(mask).wait_recv()
    own_big.wait()
    own_two.wait()
    own_go.wait()
    drain(big.at[pl.ds(0, 31 * shard)], big_send.at[0])
    drain(big_two.at[pl.ds(0, 7 * shard)], big_send.at[1])

    @pl.when(inner)
    def _():
        drain(relay, big_send.at[2])

    for n in range(3):
        ref, cols = streams[n]
        drain(ref.at[pl.ds(0, 15 * shard), cols], ag_send.at[n])
        for mask in (0, 8, 16, 24):
            group(n, mask).wait_send()
    for o in range(4):
        go_core(o).wait()
    for o in (1, 2, 3):
        go_push(o).wait_send()
    kv_push(0, 2).wait_send()
    kv_push(0, 1).wait_send()
    kv_push(2, 1).wait_send()
    for copy in (query_back, kv_back, mixed_back, proj_back, out_back):
        copy.wait()


def front_call(ctx_size, hidden, cosine, sine, pos_q, pos_k, spread, packed, w_out, w_gate, w_up, w_down, grad_out):
    rows, model = hidden.shape
    shard, wide = packed.shape
    kv_width = KV_HEADS * HD
    q_width = HEADS * HD
    one, two = widths(w_gate.shape[1])
    low, full = jnp.bfloat16, jnp.float32
    vmem = pl.BlockSpec(memory_space=pltpu.VMEM)
    anywhere = pl.BlockSpec(memory_space=pl.ANY)
    shapes = (
        ((rows, model), low, vmem),
        ((HEADS, rows, HD), low, anywhere),
        ((ctx_size, rows, 2 * kv_width), low, anywhere),
        ((rows, HD), full, vmem),
        ((rows, q_width), low, anywhere),
        ((rows, model), full, vmem),
        ((rows, model), low, vmem),
        ((8, model), full, vmem),
        ((model, wide), low, anywhere),
        ((model, q_width), low, anywhere),
        ((model, 3 * one), low, anywhere),
        ((model, 3 * two), low, anywhere),
        ((8, rows, model), low, anywhere),
        ((8, shard, 3 * one), low, anywhere),
    )
    sem = pltpu.SemaphoreType.DMA
    return pl.pallas_call(
        functools.partial(front_kernel, ctx_size),
        out_shape=tuple(jax.ShapeDtypeStruct(shape, kind) for shape, kind, _ in shapes),
        in_specs=[vmem] * 6 + [anywhere] * 6,
        out_specs=tuple(spec for _, _, spec in shapes),
        scratch_shapes=[
            pltpu.VMEM((model, wide), low),
            pltpu.VMEM((model, q_width), low),
            pltpu.VMEM((8, shard, 3 * one), low),
            pltpu.VMEM((8, shard, 3 * two), low),
            pltpu.VMEM((HEADS, rows, HD), low),
            pltpu.VMEM((ctx_size, rows, 2 * kv_width), low),
            pltpu.VMEM((rows, q_width), low),
            sem((50,)), sem((3,)), sem((3, 32)), sem((3, 4)), sem((3, 4)), sem((3,)), sem((32,)), sem((32,)), sem((8,)),
            sem((7,)), sem((8,)), sem((4,)), sem((4,)), sem((6,)),
        ],
        compiler_params=pltpu.CompilerParams(
            collective_id=0, has_side_effects=True, vmem_limit_bytes=56 << 20
        ),
        name="front",
    )(hidden, cosine, sine, pos_q, pos_k, spread, packed, w_out, w_gate, w_up, w_down, grad_out)


def back_kernel(
    ctx_size, grad_two, resid, hidden, grad_out, normed, mixed, query, kv, total, cosine, sine, pos_q, pos_k, small, spread,
    proj, out_w, grads, grads_two, near, zin_first, r_part,
    result_o, hidden_o, query_o, key_o, outw_o, gate_o, up_o, down_o, r_in,
    weight, turned, left_n, left_a, right_b, right_p, side, side_in, g_b, g_q, g_k,
    y_b, y_q, y_k, x_b, x_q, x_k, p_b, p_q, p_k, h_b, h_q, h_k,
    own, far, zin, fin, own_two, far_two, zin_two, fin_two, r_mid, r_one, stage, heads_g, lse, dkv, kv_out, kv_p, kv_h, grad_resid,
    load_sem, xs, xr, zs, zr, fs, fr, xs2, xr2, zs2, zr2, fs2, fr2, cs, cr, rs, rr, ks, kr, st_sem, os, orr,
):
    dp = lax.axis_index("dp")
    ctx = lax.axis_index("ctx")
    me = dp * ctx_size + ctx
    y, x, c = dp // 4, (dp // 2) % 2, dp % 2
    h, p = ctx // 2, ctx % 2
    rows, model = resid.shape
    shard = grads.shape[3]
    hidden_units = gate_o.shape[1]
    one, two = widths(hidden_units)
    kv_width = KV_HEADS * HD
    q_width = HEADS * HD
    groups = HEADS // KV_HEADS
    low, full = jnp.bfloat16, jnp.float32
    span = ctx_size * shard

    def at(index):
        return (index // ctx_size, index % ctx_size)

    def remote(src, dst, send, recv, mask):
        return pltpu.make_async_remote_copy(
            src_ref=src, dst_ref=dst, send_sem=send, recv_sem=recv, device_id=at(flip(me, mask)), device_id_type=MESH
        )

    def group_rows(mask):
        return pl.ds(pl.multiple_of(flip(dp, mask // 4) * span, span), span)

    def mask_of(j):
        return (j // 4) * 16 + ((j // 2) % 2) * 4 + j % 2

    barrier = pltpu.get_barrier_semaphore()
    partners = (1, 2, 4, 5, 8, 16, 17, 20, 21)
    for mask in partners:
        pl.semaphore_signal(barrier, inc=1, device_id=at(flip(me, mask)), device_id_type=MESH)
    load_w = pltpu.make_async_copy(out_w, weight.at[:, pl.ds(0, q_width)], load_sem.at[0])
    load_w.start()
    load_own = [
        pltpu.make_async_copy(grads.at[0, 0], own, load_sem.at[1]),
        pltpu.make_async_copy(grads_two.at[0], own_two, load_sem.at[2]),
        pltpu.make_async_copy(zin_first, zin.at[pl.ds(0, 4)], load_sem.at[3]),
        pltpu.make_async_copy(r_part.at[1], r_one, load_sem.at[4]),
    ]
    for copy in load_own:
        copy.start()
    pl.semaphore_wait(barrier, len(partners))

    def far_push(j):
        return remote(grads.at[1, 0, j], far.at[j], xs.at[j], xr.at[j], 8)

    def far_two_push(half, j):
        return remote(grads_two.at[1, half, j], far_two.at[half, j], xs2.at[half, j], xr2.at[half, j], 8)

    def z_push(j):
        return remote(near.at[j], zin.at[j], zs.at[j], zr.at[j], 2)

    def z_two_push(j):
        return remote(far_two.at[1, j], zin_two.at[j], zs2.at[j], zr2.at[j], 2)

    def fin_push(j):
        return remote(own.at[j], fin.at[j], fs.at[j], fr.at[j], mask_of(j))

    def fin_two_push(j):
        return remote(own_two.at[0, j], fin_two.at[j], fs2.at[j], fr2.at[j], mask_of(j))

    def z_two_step(j):
        far_two_push(1, j).wait_recv()
        far_two[1, j] = (far_two[1, j].astype(full) + own_two[1, j].astype(full)).astype(low)
        z_two_push(j).start()

    def total_step(j):
        far_push(j).wait_recv()
        if j > 3:
            z_push(j).wait_recv()
        own[j] = (own[j].astype(full) + far[j].astype(full) + zin[j].astype(full)).astype(low)
        if j:
            fin_push(j).start()

    def total_two_step(j):
        far_two_push(0, j).wait_recv()
        z_two_push(j).wait_recv()
        own_two[0, j] = (own_two[0, j].astype(full) + far_two[0, j].astype(full) + zin_two[j].astype(full)).astype(low)
        if j:
            fin_two_push(j).start()

    def r_push(o):
        src = r_one if o == 1 else r_part.at[o]
        dst = r_mid if o == 3 else r_in.at[o - 1]
        return remote(src, dst, os.at[o], orr.at[o], (0, 1, 16, 16)[o])

    r_push(3).start()
    for j in range(4, 8):
        z_push(j).start()
    for j in range(8):
        far_two_push(1, j).start()
    for j in range(8):
        far_push(j).start()

    def transposed(value, left, n):
        turned[n] = jnp.transpose(value)
        for i, mask in enumerate((0, 8, 16, 24)):
            left[i, :, pl.ds(0, rows)] = turned[n, group_rows(mask)]
            cross_left(left, n, i, mask).start()

    def cross_left(left, n, i, mask):
        return remote(turned.at[n, group_rows(mask | 4)], left.at[i, :, pl.ds(rows, rows)], cs.at[n, i], cr.at[n, i], 4)

    def cross(src, dst, n, i):
        return remote(src, dst, cs.at[n, i], cr.at[n, i], 4)

    transposed(normed[...], left_n, 0)
    right_b[pl.ds(0, rows)] = mixed[...]
    cross_mixed = cross(mixed, right_b.at[pl.ds(rows, rows)], 2, 0)
    cross_mixed.start()

    value = resid[...]
    factor = lax.rsqrt(jnp.mean(value * value, axis=-1, keepdims=True) + norm_eps)
    unit = value * factor
    scaled = grad_two[...] * small[2:3]
    ffn_row = jnp.sum(grad_two[...] * unit, axis=0, keepdims=True)
    grad_resid[...] = grad_out[...].astype(full) + factor * (
        scaled - unit * jnp.mean(scaled * unit, axis=-1, keepdims=True)
    )
    grad_attn = grad_resid[...].astype(low)
    transposed(grad_attn, left_a, 1)
    lse[...] = jnp.transpose(total[...])
    load_w.wait()
    for half in range(2):
        part = half * (q_width // 2)
        moved = dot(grad_attn, weight[:, part : part + q_width // 2], ((1,), (0,))).astype(low)
        for i in range(HEADS // 2):
            heads_g[half * (HEADS // 2) + i] = moved[:, i * HD : (i + 1) * HD]
    load_p = pltpu.make_async_copy(proj, weight, load_sem.at[0])
    load_p.start()

    streams = ((g_b, y_b, x_b, p_b, h_b), (g_q, y_q, x_q, p_q, h_q), (g_k, y_k, x_k, p_k, h_k))

    def add(ref, other):
        ref[...] = (ref[...].astype(full) + other[...].astype(full)).astype(low)

    def y_push(s, k):
        g, yy = streams[s][:2]
        return remote(g.at[2 + k], yy.at[k], rs.at[s, k], rr.at[s, k], 16)

    def x_push(s):
        g, xx = streams[s][0], streams[s][2]
        return remote(g.at[1], xx, rs.at[s, 2], rr.at[s, 2], 8)

    def block_of(hr, other):
        z = 2 * either(h, hr) + either(p, other)
        return pl.ds(pl.multiple_of(z * shard, shard), shard)

    def p_push(s, hr):
        g, pp = streams[s][0], streams[s][3]
        return remote(g.at[0, block_of(hr, 1)], pp.at[hr], rs.at[s, 3 + hr], rr.at[s, 3 + hr], 1)

    def h_push(s):
        g, hh = streams[s][0], streams[s][4]
        return remote(g.at[0, block_of(1, 0)], hh, rs.at[s, 5], rr.at[s, 5], 2)

    def y_pass(s):
        g, yy = streams[s][:2]
        y_push(s, 1).wait_recv()
        add(g.at[1], yy.at[1])
        x_push(s).start()
        y_push(s, 0).wait_recv()
        add(g.at[0], yy.at[0])

    def x_pass(s):
        x_push(s).wait_recv()
        add(streams[s][0].at[0], streams[s][2])
        p_push(s, 1).start()
        p_push(s, 0).start()

    def p_pass(s):
        g, pp = streams[s][0], streams[s][3]
        p_push(s, 1).wait_recv()
        add(g.at[0, block_of(1, 0)], pp.at[1])
        h_push(s).start()
        p_push(s, 0).wait_recv()
        add(g.at[0, block_of(0, 0)], pp.at[0])

    def h_pass(s, out):
        h_push(s).wait_recv()
        out[...] = streams[s][0][0, block_of(0, 0)].astype(full) + streams[s][4][...].astype(full)

    for i, mask in enumerate((0, 8, 16, 24)):
        cross_left(left_a, 1, i, mask).wait_recv()
    cross_mixed.wait_recv()
    for i in (3, 2, 1, 0):
        g_b[i] = dot(left_a[i], right_b[...], ((1,), (0,))).astype(low)
    y_push(0, 1).start()

    def head(n, carry):
        g = n // groups
        k_cols = pl.ds(pl.multiple_of(g * HD, HD), HD)
        v_cols = pl.ds(pl.multiple_of(kv_width + g * HD, HD), HD)
        keys = kv[:, :, k_cols].reshape(ctx_size * rows, HD)
        vals = kv[:, :, v_cols].reshape(ctx_size * rows, HD)
        scores = dot(keys, query[n], ((1,), (1,))) * HD ** (-0.5)
        scores = jnp.where(pos_k[...] <= pos_q[...], scores, masked_fill)
        attend = jnp.exp(scores - lse[pl.ds(n, 1), :])
        grad_attend = dot(vals, heads_g[n], ((1,), (1,)))
        delta = jnp.sum(grad_attend * attend, axis=0, keepdims=True)
        grad_scores = (attend * (grad_attend - delta)).astype(low)
        dkv[:, k_cols] += dot(grad_scores, query[n], ((1,), (0,)))
        dkv[:, v_cols] += dot(attend.astype(low), heads_g[n], ((1,), (0,)))
        back = dot(grad_scores, keys, ((0,), (0,))) * HD ** (-0.5)
        back = turn(back, cosine[...], -sine[...]).astype(low)
        right_p[pl.ds(0, rows), pl.ds(pl.multiple_of(n * HD, HD), HD)] = back
        return carry

    dkv[...] = jnp.zeros_like(dkv)
    lax.fori_loop(0, HEADS, head, 0)

    for z in range(ctx_size):
        part = dkv[pl.ds(z * rows, rows)]
        kv_out[z, :, pl.ds(0, kv_width)] = (part[:, :kv_width] * HD ** (-0.5)).astype(low)
        kv_out[z, :, pl.ds(kv_width, kv_width)] = part[:, kv_width:].astype(low)

    def kv_push(hr):
        return remote(kv_out.at[2 * either(h, hr) + 1 - p], kv_p.at[hr], ks.at[hr], kr.at[hr], 1)

    def kv_cross():
        return remote(kv_out.at[2 * (1 - h) + p], kv_h, ks.at[2], kr.at[2], 2)

    kv_push(1).start()
    kv_push(0).start()
    cross_q = cross(
        right_p.at[pl.ds(0, rows), pl.ds(0, q_width)], right_p.at[pl.ds(rows, rows), pl.ds(0, q_width)], 2, 1
    )
    cross_q.start()
    for copy in load_own:
        copy.wait()
    r_push(3).wait_recv()
    add(r_one, r_mid)
    r_push(1).start()
    for i, mask in enumerate((0, 8, 16, 24)):
        cross_left(left_n, 0, i, mask).wait_recv()
    cross_q.wait_recv()
    for i in (3, 2, 1, 0):
        g_q[i] = dot(left_n[i], right_p[:, pl.ds(0, q_width)], ((1,), (0,))).astype(low)
        if i > 1:
            y_push(1, i - 2).start()
    y_push(0, 0).start()
    load_p.wait()
    hidden_o[...] = dot(right_p[pl.ds(0, rows), pl.ds(0, q_width)], weight[:, pl.ds(0, q_width)], ((1,), (1,)))
    kv_push(1).wait_recv()
    add(kv_out.at[2 * (1 - h) + p], kv_p.at[1])
    kv_cross().start()
    kv_push(0).wait_recv()
    add(kv_out.at[2 * h + p], kv_p.at[0])
    for j in range(8):
        z_two_step(j)
    for j in range(4):
        total_step(j)
    kv_cross().wait_recv()
    final = kv_out[2 * h + p].astype(full) + kv_h[...].astype(full)
    for g in range(KV_HEADS):
        right_p[pl.ds(0, rows), pl.ds(q_width + g * HD, HD)] = turn(
            final[:, g * HD : (g + 1) * HD], cosine[...], -sine[...]
        ).astype(low)
    right_p[pl.ds(0, rows), pl.ds(q_width + kv_width, kv_width)] = final[:, kv_width:].astype(low)
    cross_kv = cross(
        right_p.at[pl.ds(0, rows), pl.ds(q_width, 2 * kv_width)],
        right_p.at[pl.ds(rows, rows), pl.ds(q_width, 2 * kv_width)], 2, 2,
    )
    cross_kv.start()
    grad_one = hidden_o[...] + dot(
        right_p[pl.ds(0, rows), pl.ds(q_width, 2 * kv_width)], weight[:, pl.ds(q_width, 2 * kv_width)], ((1,), (1,))
    )
    value = hidden[...].astype(full)
    factor = lax.rsqrt(jnp.mean(value * value, axis=-1, keepdims=True) + norm_eps)
    unit = value * factor
    scaled = grad_one * small[0:1]
    attn_row = jnp.sum(grad_one * unit, axis=0, keepdims=True)
    hidden_o[...] = grad_resid[...] + factor * (scaled - unit * jnp.mean(scaled * unit, axis=-1, keepdims=True))
    bias = jnp.sum(right_p[pl.ds(0, rows)].astype(full), axis=0, keepdims=True)
    kv_bias = jnp.broadcast_to(bias[:, q_width:], (8, 2 * kv_width)).astype(low)
    kv_row = dot(kv_bias, spread[...], ((1,), (1,)))[:1]
    table = jnp.concatenate([attn_row, bias[:, :q_width], ffn_row, kv_row, jnp.zeros((124, model), full)], axis=0)
    side[...] = jnp.transpose(table).astype(low)

    def cross_side(i, mask):
        return cross(side.at[group_rows(mask | 4)], side_in.at[i], 3, i)

    for i, mask in enumerate((0, 8, 16, 24)):
        cross_side(i, mask).start()
    cross_kv.wait_recv()
    for i, mask in ((3, 24), (2, 16), (1, 8), (0, 0)):
        g_k[i, :, pl.ds(0, 2 * kv_width)] = dot(
            left_n[i], right_p[:, pl.ds(q_width, 2 * kv_width)], ((1,), (0,))
        ).astype(low)
        cross_side(i, mask).wait_recv()
        g_k[i, :, pl.ds(2 * kv_width, HD)] = (
            side[group_rows(mask)].astype(full) + side_in[i].astype(full)
        ).astype(low)
        if i > 1:
            y_push(2, i - 2).start()
    outs = (gate_o, up_o, down_o)
    width = one + two
    last = hidden_units - 7 * width - one

    def piece(j):
        mask = mask_of(j)
        return either(y, mask // 16) * 4 + either(p, mask % 2) * 2 + either(c, (mask // 4) % 2)

    def write(j, start, size, count):
        for n in range(3):
            pltpu.make_async_copy(
                stage.at[j % 2, :, pl.ds(n * size, count)],
                outs[n].at[:, pl.ds(pl.multiple_of(piece(j) * width + start, HD), count)], st_sem.at[j % 2],
            ).start()

    def settle(slot, count):
        part = stage.at[slot, :, pl.ds(0, 3 * count)]
        pltpu.make_async_copy(part, part, st_sem.at[slot]).wait()

    def store(j):
        if j:
            fin_push(j).wait_recv()
        if j > 1:
            settle(j % 2, one)
        stage[j % 2] = (fin[j] if j else own[0]).astype(full)
        write(j, 0, one, one)

    def settle_two(j):
        pl.when(piece(j) < 7)(lambda: settle(j % 2, two))
        pl.when(piece(j) == 7)(lambda: settle(j % 2, last))

    def store_two(j):
        if j:
            fin_two_push(j).wait_recv()
        if j > 1:
            settle_two(j - 2)
        else:
            settle(j % 2, one)
        stage[j % 2, :, pl.ds(0, 3 * two)] = (fin_two[j] if j else own_two[0, 0]).astype(full)
        pl.when(piece(j) < 7)(lambda: write(j, one, two, two))
        pl.when(piece(j) == 7)(lambda: write(j, one, two, last))

    y_pass(1)
    y_pass(2)
    y_pass(0)
    for j in range(8):
        far_two_push(0, j).start()
    for j in range(4):
        store(j)
    x_pass(1)
    x_pass(2)
    r_push(2).start()
    for j in range(4, 8):
        total_step(j)
    p_pass(1)
    p_pass(2)
    x_pass(0)
    for j in range(4, 8):
        store(j)
    for j in range(8):
        total_two_step(j)
    p_pass(0)
    h_pass(1, query_o)
    h_pass(2, key_o)
    h_pass(0, outw_o)
    for j in range(8):
        store_two(j)
    settle_two(6)
    settle_two(7)
    for o in (1, 2):
        r_push(o).wait()
    r_push(3).wait_send()
    tiles = (r_part.at[0], r_in.at[0], r_in.at[1])
    loads = [
        pltpu.make_async_copy(ref, weight.at[pl.ds(o * rows, rows), pl.ds(0, model)], os.at[o])
        for o, ref in enumerate(tiles)
    ]
    for copy in loads:
        copy.start()
    for copy in loads:
        copy.wait()
    value = resid[...]
    for o in range(3):
        value = value + weight[pl.ds(o * rows, rows), pl.ds(0, model)].astype(full)
    result_o[...] = value.astype(low)

    for j in range(8):
        far_push(j).wait_send()
        far_two_push(0, j).wait_send()
        far_two_push(1, j).wait_send()
        if j > 3:
            z_push(j).wait_send()
        z_two_push(j).wait_send()
        if j:
            fin_push(j).wait_send()
            fin_two_push(j).wait_send()
    for i, mask in enumerate((0, 8, 16, 24)):
        cross_left(left_n, 0, i, mask).wait_send()
        cross_left(left_a, 1, i, mask).wait_send()
        cross_side(i, mask).wait_send()
    for copy in (cross_mixed, cross_q, cross_kv):
        copy.wait_send()
    for s in range(3):
        for k in range(2):
            y_push(s, k).wait_send()
            p_push(s, k).wait_send()
        x_push(s).wait_send()
        h_push(s).wait_send()
    kv_push(0).wait_send()
    kv_push(1).wait_send()
    kv_cross().wait_send()


def back_call(
    ctx_size, hidden_units, grad_two, resid, hidden, grad_out, normed, mixed, query, kv, total, cosine, sine, pos_q, pos_k,
    small, spread, proj, out_w, grads, grads_two, near, zin_first, r_part,
):
    rows, model = resid.shape
    shard = grads.shape[3]
    one, two = widths(hidden_units)
    kv_width = KV_HEADS * HD
    q_width = HEADS * HD
    k_cols = 2 * kv_width + HD
    span = ctx_size * shard
    low, full = jnp.bfloat16, jnp.float32
    vmem = pl.BlockSpec(memory_space=pltpu.VMEM)
    anywhere = pl.BlockSpec(memory_space=pl.ANY)
    shapes = (
        ((rows, model), vmem, low),
        ((rows, model), vmem, full),
        ((shard, q_width), vmem, full),
        ((shard, k_cols), vmem, full),
        ((shard, q_width), vmem, full),
        ((shard, hidden_units), anywhere, full),
        ((shard, hidden_units), anywhere, full),
        ((shard, hidden_units), anywhere, full),
        ((2, rows, model), anywhere, low),
    )
    sem = pltpu.SemaphoreType.DMA
    cols = (q_width, q_width, k_cols)

    def each(*lead):
        return [pltpu.VMEM(lead + (n,), low) for n in cols]

    return pl.pallas_call(
        functools.partial(back_kernel, ctx_size),
        out_shape=tuple(jax.ShapeDtypeStruct(shape, kind) for shape, _, kind in shapes),
        in_specs=[vmem] * 15 + [anywhere] * 7,
        out_specs=tuple(spec for _, spec, _ in shapes),
        scratch_shapes=[
            pltpu.VMEM(proj.shape, low),
            pltpu.VMEM((2, model, rows), low),
            pltpu.VMEM((4, span, 2 * rows), low),
            pltpu.VMEM((4, span, 2 * rows), low),
            pltpu.VMEM((2 * rows, q_width), low),
            pltpu.VMEM((2 * rows, q_width + 2 * kv_width), low),
            pltpu.VMEM((model, HD), low),
            pltpu.VMEM((4, span, HD), low),
            *each(4, span),
            *each(2, span),
            *each(span),
            *each(2, shard),
            *each(shard),
            *([pltpu.VMEM((8, shard, 3 * one), low)] * 4),
            *([pltpu.VMEM((2, 8, shard, 3 * two), low)] * 2),
            *([pltpu.VMEM((8, shard, 3 * two), low)] * 2),
            *([pltpu.VMEM((rows, model), low)] * 2),
            pltpu.VMEM((2, shard, 3 * one), full),
            pltpu.VMEM((HEADS, rows, HD), low),
            pltpu.VMEM((HD, rows), full),
            pltpu.VMEM((ctx_size * rows, 2 * kv_width), full),
            pltpu.VMEM((ctx_size, rows, 2 * kv_width), low),
            pltpu.VMEM((2, rows, 2 * kv_width), low),
            pltpu.VMEM((rows, 2 * kv_width), low),
            pltpu.VMEM((rows, model), full),
            sem((5,)), *([sem((8,))] * 6), *([sem((2, 8))] * 2), *([sem((8,))] * 4),
            sem((4, 4)), sem((4, 4)), sem((3, 6)), sem((3, 6)), sem((3,)), sem((3,)), sem((2,)), sem((4,)), sem((4,)),
        ],
        compiler_params=pltpu.CompilerParams(
            collective_id=2, has_side_effects=True, vmem_limit_bytes=63 << 20
        ),
        name="back",
    )(
        grad_two, resid, hidden, grad_out, normed, mixed, query, kv, total, cosine, sine, pos_q, pos_k, small, spread,
        proj, out_w, grads, grads_two, near, zin_first, r_part,
    )


def fits(mesh):
    return mesh.shape["dp"] == 8 and mesh.shape["ctx"] == 4


def fast_device(
    hidden,
    cotangent,
    span_order,
    attn_gain,
    w_query,
    b_query,
    w_key,
    b_key,
    w_value,
    b_value,
    w_out,
    ffn_gain,
    w_gate,
    w_up,
    w_down,
):
    ctx_size = lax.axis_size("ctx")
    ctx_rank = lax.axis_index("ctx")
    batches = hidden.shape[0]
    length = hidden.shape[1]
    span_len = length // 2
    seq_len = length * ctx_size
    row_count = batches * length
    shard_rows = w_query.shape[0]
    kv_width = KV_HEADS * HD
    q_width = HEADS * HD

    grad_out = cotangent.reshape(row_count, D)
    places = jnp.arange(seq_len, dtype=jnp.int32)
    every_pos = jnp.repeat(span_order, span_len, axis=1) * span_len + places[None, :] % span_len
    local_pos = lax.dynamic_slice_in_dim(every_pos, ctx_rank * length, length, 1)
    cosine, sine = angles_for(local_pos.reshape(row_count), HD)
    cos_full = jnp.concatenate([cosine[:, 0], cosine[:, 0]], axis=1)
    sin_full = jnp.concatenate([-sine[:, 0], sine[:, 0]], axis=1)

    gains = jnp.stack([attn_gain, b_query, ffn_gain], axis=1)
    per = b_key.shape[0]
    pair = jnp.pad(jnp.concatenate([b_key, b_value]), (0, shard_rows - 2 * per))
    packed = jnp.concatenate(
        [w_query, w_key, w_value, gains, pair[:, None], jnp.zeros((shard_rows, 124), jnp.bfloat16)], axis=1
    )
    unit = jnp.arange(2 * kv_width)
    unit = unit % kv_width // per * shard_rows + unit // kv_width * per + unit % per
    spread = (jnp.arange(D)[:, None] == unit[None, :]).astype(jnp.bfloat16)
    source = hidden.reshape(row_count, D)
    normed, query_heads, key_value, log_total, mixed, resid, normed_two, small, proj_full, out_full, big, big_two, go_all, _ = front_call(
        ctx_size, source, cos_full, sin_full, local_pos.reshape(length, 1), every_pos.reshape(1, seq_len), spread,
        packed, w_out, w_gate, w_up, w_down, grad_out,
    )
    grad_two, r_part, grads, grads_two, near, zin = ffn_call(ctx_size, shard_rows, normed_two, go_all, big, big_two)
    result, hidden_grad, w_query_grad, kv_sum, w_out_grad, w_gate_grad, w_up_grad, w_down_grad, _ = back_call(
        ctx_size, w_gate.shape[1], grad_two, resid, source, grad_out, normed, mixed, query_heads, key_value, log_total,
        cos_full, sin_full, local_pos.reshape(1, length), every_pos.reshape(seq_len, 1), small, spread,
        proj_full, out_full, grads, grads_two, near, zin, r_part,
    )
    sides = kv_sum[:, 2 * kv_width : 2 * kv_width + 4]
    return (
        result.reshape(batches, length, D),
        hidden_grad.reshape(batches, length, D),
        sides[:, 0],
        w_query_grad,
        sides[:, 1],
        kv_sum[:, :kv_width],
        sides[:per, 3],
        kv_sum[:, kv_width : 2 * kv_width],
        sides[per : 2 * per, 3],
        w_out_grad,
        sides[:, 2],
        w_gate_grad,
        w_up_grad,
        w_down_grad,
    )


def general_device(
    hidden,
    cotangent,
    span_order,
    attn_gain,
    w_query,
    b_query,
    w_key,
    b_key,
    w_value,
    b_value,
    w_out,
    ffn_gain,
    w_gate,
    w_up,
    w_down,
):
    ctx_size = lax.axis_size("ctx")
    ctx_rank = lax.axis_index("ctx")
    batches = hidden.shape[0]
    length = hidden.shape[1]
    span_len = length // 2
    seq_len = length * ctx_size
    row_count = batches * length
    groups = HEADS // KV_HEADS
    shard_rows = w_query.shape[0]
    head_scale = HD ** (-0.5)
    kv_width = KV_HEADS * HD
    q_width = HEADS * HD
    places = jnp.arange(seq_len, dtype=jnp.int32)
    every_pos = jnp.repeat(span_order, span_len, axis=1) * span_len + places[None, :] % span_len
    local_pos = lax.dynamic_slice_in_dim(every_pos, ctx_rank * length, length, 1)
    cosine, sine = angles_for(local_pos.reshape(row_count), HD)
    allowed = (every_pos[:, None, :] <= local_pos[:, :, None])[:, None, None]
    attn_full = (
        lax.all_gather(attn_gain, ("dp", "ctx"), axis=0, tiled=True),
        lax.all_gather(w_query, ("dp", "ctx"), axis=0, tiled=True),
        lax.all_gather(w_key, ("dp", "ctx"), axis=0, tiled=True),
        lax.all_gather(w_value, ("dp", "ctx"), axis=0, tiled=True),
        lax.all_gather(w_out, ("dp", "ctx"), axis=0, tiled=True),
        lax.all_gather(b_query, ("dp", "ctx"), axis=0, tiled=True),
        lax.all_gather(b_key, ("dp", "ctx"), axis=0, tiled=True),
        lax.all_gather(b_value, ("dp", "ctx"), axis=0, tiled=True),
    )
    gain_one = attn_full[0].astype(jnp.float32)
    source = hidden.reshape(row_count, D).astype(jnp.float32)
    attn_factor, normed = norm_forward(source, gain_one)
    query_raw = plain_dot(normed, attn_full[1]) + attn_full[5].astype(jnp.float32)
    key_raw = plain_dot(normed, attn_full[2]) + attn_full[6].astype(jnp.float32)
    value_low = (plain_dot(normed, attn_full[3]) + attn_full[7].astype(jnp.float32)).astype(
        jnp.bfloat16
    )
    query_rot = rotate(query_raw.reshape(row_count, HEADS, HD), cosine, sine).astype(jnp.bfloat16)
    query_rot = query_rot.reshape(batches, length, KV_HEADS, groups, HD)
    key_rot = rotate(key_raw.reshape(row_count, KV_HEADS, HD), cosine, sine).astype(jnp.bfloat16)
    key_rot = key_rot.reshape(batches, length, kv_width)
    key_all, value_all = (
        lax.all_gather(key_rot, "ctx", axis=1, tiled=True),
        lax.all_gather(value_low.reshape(batches, length, kv_width), "ctx", axis=1, tiled=True),
    )
    key_all = key_all.reshape(batches, seq_len, KV_HEADS, HD)
    value_all = value_all.reshape(batches, seq_len, KV_HEADS, HD)
    scores = (
        jnp.einsum("bqkgd,bskd->bkgqs", query_rot, key_all, preferred_element_type=jnp.float32)
        * head_scale
    )
    masked = jnp.where(allowed, scores, masked_fill)
    row_max = jnp.max(masked, axis=-1, keepdims=True)
    expo = jnp.exp(masked - row_max)
    expo_sum = jnp.sum(expo, axis=-1, keepdims=True)
    log_total = row_max + jnp.log(expo_sum)
    attend = (expo / expo_sum).astype(jnp.bfloat16)
    mixed = jnp.einsum("bkgqs,bskd->bqkgd", attend, value_all, preferred_element_type=jnp.float32)
    mixed = mixed.reshape(row_count, q_width).astype(jnp.bfloat16)
    resid = source + right_dot(mixed, attn_full[4])
    ffn_full = (
        lax.all_gather(ffn_gain, ("dp", "ctx"), axis=0, tiled=True),
        lax.all_gather(w_gate, ("dp", "ctx"), axis=0, tiled=True),
        lax.all_gather(w_up, ("dp", "ctx"), axis=0, tiled=True),
        lax.all_gather(w_down, ("dp", "ctx"), axis=0, tiled=True),
    )
    gain_two = ffn_full[0].astype(jnp.float32)
    ffn_factor, normed_two = norm_forward(resid, gain_two)
    gate_pre = plain_dot(normed_two, ffn_full[1])
    up_pre = plain_dot(normed_two, ffn_full[2])
    sigmoid_gate = jax.nn.sigmoid(gate_pre)
    silu_gate = gate_pre * sigmoid_gate
    act = (silu_gate * up_pre).astype(jnp.bfloat16)
    output = resid + right_dot(act, ffn_full[3])
    result = output.astype(jnp.bfloat16).reshape(batches, length, D)
    ffn_back = (
        lax.all_gather(ffn_gain, ("dp", "ctx"), axis=0, tiled=True),
        lax.all_gather(w_gate, ("dp", "ctx"), axis=0, tiled=True),
        lax.all_gather(w_up, ("dp", "ctx"), axis=0, tiled=True),
        lax.all_gather(w_down, ("dp", "ctx"), axis=0, tiled=True),
    )
    grad_out = cotangent.reshape(row_count, D)
    grad_plain = grad_out.astype(jnp.float32)
    grad_act = plain_dot(grad_out, ffn_back[3])
    grad_gate = (grad_act * up_pre * sigmoid_gate * (1.0 + gate_pre * (1.0 - sigmoid_gate))).astype(
        jnp.bfloat16
    )
    grad_up = (grad_act * silu_gate).astype(jnp.bfloat16)
    pieces = (
        lax.all_gather(normed_two, "ctx", axis=0, tiled=True),
        lax.all_gather(grad_gate, "ctx", axis=0, tiled=True),
        lax.all_gather(grad_up, "ctx", axis=0, tiled=True),
        lax.all_gather(act, "ctx", axis=0, tiled=True),
        lax.all_gather(grad_out, "ctx", axis=0, tiled=True),
    )
    picked_in = owned_columns(pieces[0], ctx_size, ctx_rank, shard_rows)
    picked_out = owned_columns(pieces[4], ctx_size, ctx_rank, shard_rows)
    w_gate_grad, w_up_grad, w_down_grad = (
        lax.psum_scatter(
            outer_add(picked_in, pieces[1]).astype(jnp.bfloat16),
            "dp",
            scatter_dimension=0,
            tiled=True,
        ).astype(jnp.float32),
        lax.psum_scatter(
            outer_add(picked_in, pieces[2]).astype(jnp.bfloat16),
            "dp",
            scatter_dimension=0,
            tiled=True,
        ).astype(jnp.float32),
        lax.psum_scatter(
            outer_add(picked_out, pieces[3]).astype(jnp.bfloat16),
            "dp",
            scatter_dimension=0,
            tiled=True,
        ).astype(jnp.float32),
    )
    grad_norm_two = right_dot(grad_gate, ffn_back[1]) + right_dot(grad_up, ffn_back[2])
    resid_back, ffn_gain_part = norm_backward(resid, ffn_factor, gain_two, grad_norm_two)
    grad_resid = grad_plain + resid_back
    attn_back = (
        lax.all_gather(attn_gain, ("dp", "ctx"), axis=0, tiled=True),
        lax.all_gather(w_query, ("dp", "ctx"), axis=0, tiled=True),
        lax.all_gather(w_key, ("dp", "ctx"), axis=0, tiled=True),
        lax.all_gather(w_value, ("dp", "ctx"), axis=0, tiled=True),
        lax.all_gather(w_out, ("dp", "ctx"), axis=0, tiled=True),
        lax.all_gather(b_query, ("dp", "ctx"), axis=0, tiled=True),
        lax.all_gather(b_key, ("dp", "ctx"), axis=0, tiled=True),
        lax.all_gather(b_value, ("dp", "ctx"), axis=0, tiled=True),
    )
    grad_attn = grad_resid.astype(jnp.bfloat16)
    grad_mixed = plain_dot(grad_attn, attn_back[4]).astype(jnp.bfloat16)
    grad_mixed = grad_mixed.reshape(batches, length, KV_HEADS, groups, HD)
    scores = (
        jnp.einsum("bqkgd,bskd->bkgqs", query_rot, key_all, preferred_element_type=jnp.float32)
        * head_scale
    )
    masked = jnp.where(allowed, scores, masked_fill)
    attend_full = jnp.exp(masked - log_total)
    attend = attend_full.astype(jnp.bfloat16)
    grad_attend = jnp.einsum(
        "bqkgd,bskd->bkgqs", grad_mixed, value_all, preferred_element_type=jnp.float32
    )
    value_grad_all = jnp.einsum(
        "bkgqs,bqkgd->bskd", attend, grad_mixed, preferred_element_type=jnp.float32
    )
    delta = jnp.sum(grad_attend * attend_full, axis=-1, keepdims=True)
    grad_scores = (attend_full * (grad_attend - delta)).astype(jnp.bfloat16)
    query_grad_rot = (
        jnp.einsum("bkgqs,bskd->bqkgd", grad_scores, key_all, preferred_element_type=jnp.float32)
        * head_scale
    )
    key_grad_all = (
        jnp.einsum("bkgqs,bqkgd->bskd", grad_scores, query_rot, preferred_element_type=jnp.float32)
        * head_scale
    )
    key_grad_rot, value_grad = (
        lax.psum_scatter(
            key_grad_all.reshape(batches, seq_len, kv_width), "ctx", scatter_dimension=1, tiled=True
        ),
        lax.psum_scatter(
            value_grad_all.reshape(batches, seq_len, kv_width),
            "ctx",
            scatter_dimension=1,
            tiled=True,
        ),
    )
    query_grad = (
        rotate_back(query_grad_rot.reshape(row_count, HEADS, HD), cosine, sine)
        .reshape(row_count, q_width)
        .astype(jnp.bfloat16)
    )
    key_grad = (
        rotate_back(key_grad_rot.reshape(row_count, KV_HEADS, HD), cosine, sine)
        .reshape(row_count, kv_width)
        .astype(jnp.bfloat16)
    )
    value_grad = value_grad.reshape(row_count, kv_width).astype(jnp.bfloat16)
    proj_grad = jnp.concatenate([query_grad, key_grad, value_grad], axis=1)
    pieces = (
        lax.all_gather(normed, "ctx", axis=0, tiled=True),
        lax.all_gather(proj_grad, "ctx", axis=0, tiled=True),
        lax.all_gather(grad_attn, "ctx", axis=0, tiled=True),
        lax.all_gather(mixed, "ctx", axis=0, tiled=True),
    )
    picked_in = owned_columns(pieces[0], ctx_size, ctx_rank, shard_rows)
    picked_out = owned_columns(pieces[2], ctx_size, ctx_rank, shard_rows)
    proj_sum, w_out_grad = (
        lax.psum_scatter(
            outer_add(picked_in, pieces[1]).astype(jnp.bfloat16),
            "dp",
            scatter_dimension=0,
            tiled=True,
        ).astype(jnp.float32),
        lax.psum_scatter(
            outer_add(picked_out, pieces[3]).astype(jnp.bfloat16),
            "dp",
            scatter_dimension=0,
            tiled=True,
        ).astype(jnp.float32),
    )
    grad_norm_one = (
        right_dot(query_grad, attn_back[1])
        + right_dot(key_grad, attn_back[2])
        + right_dot(value_grad, attn_back[3])
    )
    source_back, attn_gain_part = norm_backward(source, attn_factor, gain_one, grad_norm_one)
    hidden_grad = (grad_resid + source_back).reshape(batches, length, D)
    query_bias_part = jnp.sum(query_grad.astype(jnp.float32), axis=0)
    key_bias_part = jnp.sum(key_grad.astype(jnp.float32), axis=0)
    value_bias_part = jnp.sum(value_grad.astype(jnp.float32), axis=0)
    small_sums = (
        lax.psum_scatter(attn_gain_part, ("dp", "ctx"), scatter_dimension=0, tiled=True),
        lax.psum_scatter(query_bias_part, ("dp", "ctx"), scatter_dimension=0, tiled=True),
        lax.psum_scatter(key_bias_part, ("dp", "ctx"), scatter_dimension=0, tiled=True),
        lax.psum_scatter(value_bias_part, ("dp", "ctx"), scatter_dimension=0, tiled=True),
        lax.psum_scatter(ffn_gain_part, ("dp", "ctx"), scatter_dimension=0, tiled=True),
    )
    w_query_grad = proj_sum[:, :q_width]
    w_key_grad = proj_sum[:, q_width : q_width + kv_width]
    w_value_grad = proj_sum[:, q_width + kv_width :]
    return (
        result,
        hidden_grad,
        small_sums[0],
        w_query_grad,
        small_sums[1],
        w_key_grad,
        small_sums[2],
        w_value_grad,
        small_sums[3],
        w_out_grad,
        small_sums[4],
        w_gate_grad,
        w_up_grad,
        w_down_grad,
    )


def solution(mesh):
    placed = (
        P("dp", "ctx", None),
        P("dp", "ctx", None),
        P("dp", None),
        P(("dp", "ctx")),
        P(("dp", "ctx"), None),
        P(("dp", "ctx")),
        P(("dp", "ctx"), None),
        P(("dp", "ctx")),
        P(("dp", "ctx"), None),
        P(("dp", "ctx")),
        P(("dp", "ctx"), None),
        P(("dp", "ctx")),
        P(("dp", "ctx"), None),
        P(("dp", "ctx"), None),
        P(("dp", "ctx"), None),
    )
    return jax.shard_map(
        fast_device if fits(mesh) else general_device,
        mesh=mesh,
        in_specs=placed,
        out_specs=(
            P("dp", "ctx", None),
            P("dp", "ctx", None),
            P(("dp", "ctx")),
            P(("dp", "ctx"), None),
            P(("dp", "ctx")),
            P(("dp", "ctx"), None),
            P(("dp", "ctx")),
            P(("dp", "ctx"), None),
            P(("dp", "ctx")),
            P(("dp", "ctx"), None),
            P(("dp", "ctx")),
            P(("dp", "ctx"), None),
            P(("dp", "ctx"), None),
            P(("dp", "ctx"), None),
        ),
        check_vma=False,
    )
```

```python
import functools

import jax
import jax.numpy as jnp
from jax import lax
from jax.experimental import pallas as pl
from jax.experimental.pallas import tpu as pltpu
from jax.sharding import PartitionSpec as P

D = 1536
HEADS = 12
KV_HEADS = 2
HD = 128


norm_eps = 1e-06
rope_base = 10000.0
masked_fill = -1e30


def angles_for(places, width):
    half = width // 2
    freqs = rope_base ** (-(jnp.arange(half, dtype=jnp.float32) * 2.0 / width))
    angles = places.astype(jnp.float32)[:, None] * freqs[None, :]
    return (jnp.cos(angles)[:, None, :], jnp.sin(angles)[:, None, :])


def rotate(values, cosine, sine):
    half = values.shape[-1] // 2
    first = values[..., :half]
    second = values[..., half:]
    return jnp.concatenate(
        [first * cosine - second * sine, second * cosine + first * sine], axis=-1
    )


def rotate_back(values, cosine, sine):
    half = values.shape[-1] // 2
    first = values[..., :half]
    second = values[..., half:]
    return jnp.concatenate(
        [first * cosine + second * sine, second * cosine - first * sine], axis=-1
    )


def norm_forward(source, gain):
    factor = lax.rsqrt(jnp.mean(source * source, axis=-1, keepdims=True) + norm_eps)
    return (factor, (source * factor * gain).astype(jnp.bfloat16))


def norm_backward(source, factor, gain, grad_normed):
    unit = source * factor
    gain_grad = jnp.sum(grad_normed * unit, axis=0)
    scaled = grad_normed * gain
    source_grad = factor * (scaled - unit * jnp.mean(scaled * unit, axis=-1, keepdims=True))
    return (source_grad, gain_grad)


def right_dot(left, weight):
    return jnp.einsum("rf,df->rd", left, weight, preferred_element_type=jnp.float32)


def plain_dot(left, weight):
    return jnp.dot(left, weight, preferred_element_type=jnp.float32)


def owned_columns(values, ctx_size, ctx_rank, shard_rows):
    rows = values.shape[0]
    blocks = values.shape[1] // (shard_rows * ctx_size)
    shaped = values.reshape(rows, blocks, ctx_size, shard_rows)
    picked = lax.dynamic_index_in_dim(shaped, ctx_rank, axis=2, keepdims=False)
    return picked.reshape(rows, blocks * shard_rows)


def outer_add(left, right):
    return jnp.einsum("rc,rf->cf", left, right, preferred_element_type=jnp.float32)


MESH = pl.DeviceIdType.MESH


def flip(index, mask):
    for bit in (1, 2, 4, 8, 16):
        if mask & bit:
            index = index + bit - 2 * bit * ((index // bit) % 2)
    return index


def either(a, b):
    return a + b - 2 * a * b


def dot(a, b, dims):
    return lax.dot_general(a, b, (dims, ((), ())), preferred_element_type=jnp.float32)


def widths(hidden_units):
    width = -(-hidden_units // (8 * 128)) * 128
    first = width // 384 * 256
    return (first, width - first)


def ffn_kernel(
    ctx_size, n_own, go_all, big, big_two,
    grad_two, r_part, grads, grads_two, near, zin,
    w_one, w_two, nt, go, ggu, act, crecv, part, h_in, h_mid, stage, own, far,
    io_sem, n_send, n_recv, f_send, f_recv, c_send, c_recv, o_send, o_recv, st_sem, w_send, w_recv, l_sem, x_send, x_recv, z_send, z_recv, d_sem,
):
    dp = lax.axis_index("dp")
    ctx = lax.axis_index("ctx")
    me = dp * ctx_size + ctx
    y, x, c = dp // 4, (dp // 2) % 2, dp % 2
    h, p = ctx // 2, ctx % 2
    one, two = w_one.shape[1] // 3, w_two.shape[1] // 3
    shard = grads.shape[3]
    rows, model = n_own.shape
    low, full = jnp.bfloat16, jnp.float32

    def at(index):
        return (index // ctx_size, index % ctx_size)

    def remote(src, dst, send, recv, mask):
        return pltpu.make_async_remote_copy(
            src_ref=src, dst_ref=dst, send_sem=send, recv_sem=recv, device_id=at(flip(me, mask)), device_id_type=MESH
        )

    def block(mask):
        return pl.ds(pl.multiple_of(flip(me, mask) * shard, shard), shard)

    barrier = pltpu.get_barrier_semaphore()
    partners = (1, 2, 4, 8, 16)
    for mask in partners:
        pl.semaphore_signal(barrier, inc=1, device_id=at(flip(me, mask)), device_id_type=MESH)
    load_n = pltpu.make_async_copy(n_own, nt.at[0], io_sem.at[0])
    load_w = pltpu.make_async_copy(big, w_one, io_sem.at[1])
    load_go = pltpu.make_async_copy(go_all, go, io_sem.at[2])
    held = (0, 4, 1, 5, 16, 20, 17, 21, 2, 6, 3, 7)
    load_l = [
        pltpu.make_async_copy(big_two.at[block(mask)], w_two.at[block(mask)], l_sem.at[i]) for i, mask in enumerate(held)
    ]
    for copy in (load_n, load_w, load_go, *load_l):
        copy.start()
    pl.semaphore_wait(barrier, len(partners))

    def spread_two(mask, over):
        remote(big_two.at[block(mask)], w_two.at[block(mask)], w_send.at[0], w_recv.at[mask | over], over).start()

    def w_wait(mask):
        remote(w_two.at[block(mask)], w_two.at[block(mask)], w_send.at[0], w_recv.at[mask], 1).wait_recv()

    def w_pass(mask):
        w_wait(mask)
        remote(w_two.at[block(mask)], w_two.at[block(mask)], w_send.at[0], w_recv.at[mask | 8], 8).start()

    def n_core(slot):
        return remote(nt.at[slot], nt.at[slot + 1], f_send.at[slot // 2], f_recv.at[slot // 2], 4)

    def n_push(o):
        src = nt.at[2] if o == 3 else nt.at[0]
        return remote(src, nt.at[2 * o], n_send.at[o], n_recv.at[o], (0, 1, 16, 16)[o])

    load_n.wait()
    n_push(1).start()
    n_push(2).start()
    n_core(0).start()
    for mask in (16, 20, 17, 21):
        spread_two(mask, 2)
    for mask in held:
        spread_two(mask, 8)
    load_w.wait()
    load_go.wait()

    def first(slot):
        gu = dot(nt[slot], w_one[:, : 2 * one], ((1,), (0,)))
        ga = dot(go[slot], w_one[:, 2 * one :], ((1,), (0,)))
        finish(slot, gu[:, :one], gu[:, one:], ga, 0, 0)

    def finish(slot, gate, up, ga, at_gu, at_act):
        size = gate.shape[1]
        sig = 1.0 / (1.0 + jnp.exp(-gate))
        silu = gate * sig
        act[slot, :, pl.ds(at_act, size)] = (silu * up).astype(low)
        ggu[slot, :, pl.ds(at_gu, size)] = (ga * up * sig * (1.0 + gate * (1.0 - sig))).astype(low)
        ggu[slot, :, pl.ds(at_gu + size, size)] = (ga * silu).astype(low)

    def second(slot):
        gu = dot(nt[slot], w_two[:, : 2 * two], ((1,), (0,)))
        ga = dot(go[slot], w_two[:, 2 * two :], ((1,), (0,)))
        finish(slot, gu[:, :two], gu[:, two:], ga, 2 * one, one)
        grad = dot(ggu[slot, :, : 2 * one], w_one[:, : 2 * one], ((1,), (1,)))
        grad = grad + dot(ggu[slot, :, 2 * one :], w_two[:, : 2 * two], ((1,), (1,)))
        out = dot(act[slot, :, :one], w_one[:, 2 * one :], ((1,), (1,)))
        out = out + dot(act[slot, :, one:], w_two[:, 2 * two :], ((1,), (1,)))
        return (grad.astype(low), out.astype(low))

    def early(o, carry):
        @pl.when(o == 1)
        def _():
            n_push(1).wait_recv()
            n_push(3).start()
            n_core(2).start()
            n_push(2).wait_recv()
            n_core(4).start()

        @pl.when(o == 3)
        def _():
            n_push(3).wait_recv()
            n_core(6).start()

        first(2 * o)


        n_core(2 * o).wait_recv()
        first(2 * o + 1)
        return carry

    lax.fori_loop(0, 4, early, 0)
    def stage_wait(slot, size):
        part_of = stage.at[slot, :, pl.ds(0, size)]
        pltpu.make_async_copy(part_of, part_of, st_sem.at[slot]).wait()

    def weights(size, start_gu, start_act, to, passes, q, carry):
        slot = q % 2

        @pl.when(q > 1)
        def _():
            stage_wait(slot, 3 * size)

        chunk = 8 * shard
        cols = pl.ds(pl.multiple_of(q * chunk, chunk), chunk)

        def product(left, right, start, count, at_col):
            left = left[:, :, cols].reshape(8 * rows, chunk)
            right = right[:, :, pl.ds(start, count)].reshape(8 * rows, count)
            stage[slot, :, pl.ds(at_col, count)] = dot(left, right, ((0,), (0,))).astype(low)

        for start in range(0, 2 * size, one):
            count = min(one, 2 * size - start)
            product(nt, ggu, start_gu + start, count, start)
        product(go, act, start_act, size, 2 * size)
        for n, masks in enumerate(passes):
            @pl.when(q == n)
            def _():
                for mask in masks:
                    w_pass(mask)

        yr, xr = either(q // 2, y), either(q % 2, x)
        for j in range(8):
            cr, hrel, pr = either(j // 4, c), either((j // 2) % 2, h), either(j % 2, p)
            pltpu.make_async_copy(
                stage.at[slot, pl.ds(j * shard, shard), pl.ds(0, 3 * size)],
                to.at[xr, hrel, yr * 4 + cr * 2 + pr], st_sem.at[slot],
            ).start()
        return carry

    def all_weights(size, start_gu, start_act, to, passes=()):
        lax.fori_loop(0, 4, functools.partial(weights, size, start_gu, start_act, to, passes), 0)
        stage_wait(0, 3 * size)
        stage_wait(1, 3 * size)

    def far_push(j):
        return remote(grads.at[1, 1, j], far.at[j], x_send.at[j], x_recv.at[j], 8)

    def z_push(j):
        return remote(far.at[j], zin.at[j], z_send.at[j], z_recv.at[j], 2)

    def load_own(k):
        return pltpu.make_async_copy(grads.at[0, 1, pl.ds(4 * k, 4)], own, d_sem.at[0])

    keep_near = pltpu.make_async_copy(far, near, d_sem.at[0])

    def far_pass(*blocks):
        for j in blocks:
            far_push(j).wait_recv()
            far[j] = (far[j].astype(full) + own[j % 4].astype(full)).astype(low)
            if j < 4:
                z_push(j).start()

    all_weights(one, 0, 0, grads, ((18, 22, 19, 23),))
    for j in range(8):
        far_push(j).start()
    load_own(0).start()

    for mask in (8, 12, 9, 13, 24, 28, 25, 29, 10, 14, 11, 15, 26, 30, 27, 31):
        w_wait(mask)
    for copy in load_l:
        copy.wait()

    def cross(o):
        return remote(stage.at[:, pl.ds(0, rows), pl.ds(0, model)], crecv.at[o % 2], c_send, c_recv.at[o % 2], 4)

    def final(o):
        dst = h_mid if o == 3 else h_in.at[o - 1]
        return remote(part.at[o, 0], dst, o_send.at[o], o_recv.at[o], (0, 1, 16, 16)[o])

    def keep(o):
        return pltpu.make_async_copy(part.at[o, 1], r_part.at[o], io_sem.at[o])

    def combine(o):
        cross(o).wait_recv()
        part[o] = (part[o].astype(full) + crecv[o % 2].astype(full)).astype(low)
        keep(o).start()

    def late(n, carry):
        o = 3 - n
        grad, out = second(2 * o)
        part[o, 0] = grad
        part[o, 1] = out

        @pl.when(n > 0)
        def _():
            combine(o + 1)

        @pl.when(n == 1)
        def _():
            final(3).start()
            load_own(0).wait()
            far_pass(0, 1)

        @pl.when(n == 2)
        def _():
            final(2).start()
            far_pass(2, 3)
            load_own(1).start()

        @pl.when(n == 3)
        def _():
            final(3).wait_recv()
            part[1, 0] = (part[1, 0].astype(full) + h_mid[...].astype(full)).astype(low)
            final(1).start()
            load_own(1).wait()
            far_pass(4, 5)

        grad, out = second(2 * o + 1)

        @pl.when(n > 0)
        def _():
            cross(o).wait_send()

        stage[0, pl.ds(0, rows), pl.ds(0, model)] = grad
        stage[1, pl.ds(0, rows), pl.ds(0, model)] = out
        cross(o).start()
        return carry

    lax.fori_loop(0, 4, late, 0)

    far_pass(6, 7)
    keep_near.start()
    cross(0).wait_send()
    all_weights(two, 2 * one, one, grads_two)
    combine(0)
    grad_two[...] = part[0, 0].astype(full)
    for o in (1, 2):
        final(o).wait_recv()
        grad_two[...] += h_in[o - 1].astype(full)
    keep_near.wait()
    for j in range(8):
        far_push(j).wait_send()
        if j < 4:
            z_push(j).wait()
    for o in range(4):
        keep(o).wait()
        n_core(2 * o).wait_send()
    for o in (1, 2, 3):
        n_push(o).wait_send()
        final(o).wait_send()
    sent = w_two.at[pl.ds(0, 20 * shard)]
    pltpu.make_async_copy(sent, sent, w_send.at[0]).wait()


def ffn_call(ctx_size, shard, n_own, go_all, big, big_two):
    rows, model = n_own.shape
    one, two = big.shape[1] // 3, big_two.shape[1] // 3
    low = jnp.bfloat16
    anywhere = pl.BlockSpec(memory_space=pl.ANY)
    sem = pltpu.SemaphoreType.DMA
    return pl.pallas_call(
        functools.partial(ffn_kernel, ctx_size),
        out_shape=(
            jax.ShapeDtypeStruct((rows, model), jnp.float32),
            jax.ShapeDtypeStruct((4, rows, model), low),
            jax.ShapeDtypeStruct((2, 2, 8, shard, 3 * one), low),
            jax.ShapeDtypeStruct((2, 2, 8, shard, 3 * two), low),
            jax.ShapeDtypeStruct((8, shard, 3 * one), low),
            jax.ShapeDtypeStruct((4, shard, 3 * one), low),
        ),
        in_specs=[anywhere] * 4,
        out_specs=[pl.BlockSpec(memory_space=pltpu.VMEM)] + [anywhere] * 5,
        scratch_shapes=[
            pltpu.VMEM((model, 3 * one), low),
            pltpu.VMEM((model, 3 * two), low),
            pltpu.VMEM((8, rows, model), low),
            pltpu.VMEM((8, rows, model), low),
            pltpu.VMEM((8, rows, 2 * (one + two)), low),
            pltpu.VMEM((8, rows, one + two), low),
            pltpu.VMEM((2, 2, rows, model), low),
            pltpu.VMEM((4, 2, rows, model), low),
            pltpu.VMEM((2, rows, model), low),
            pltpu.VMEM((rows, model), low),
            pltpu.VMEM((2, 8 * shard, 3 * one), low),
            pltpu.VMEM((4, shard, 3 * one), low),
            pltpu.VMEM((8, shard, 3 * one), low),
            sem((4,)), sem((5,)), sem((5,)), sem((4,)), sem((4,)), sem, sem((2,)), sem((4,)), sem((4,)), sem((2,)),
            sem((1,)), sem((32,)), sem((12,)), sem((8,)), sem((8,)), sem((4,)), sem((4,)), sem((1,)),
        ],
        compiler_params=pltpu.CompilerParams(
            collective_id=1, has_side_effects=True, vmem_limit_bytes=65200 << 10
        ),
        name="ffn",
    )(n_own, go_all, big, big_two)


def turn(values, cosine, sine):
    return values * cosine + pltpu.roll(values, HD // 2, 1) * sine


def front_kernel(
    ctx_size, hidden, cosine, sine, pos_q, pos_k, spread, packed, w_out, w_gate, w_up, w_down, grad_out,
    normed_o, query_o, kv_o, total_o, mixed_o, resid_o, normed_two_o, small_o, proj_o, out_o, big, big_two, go, relay,
    proj, out_w, source, source_two, query, kv, mixed,
    load_sem, ag_send, ag_recv, core_send, core_recv, big_send, big_recv, two_recv, relay_recv, go_send, go_recv, kv_send, kv_recv, back_sem,
):
    dp = lax.axis_index("dp")
    ctx = lax.axis_index("ctx")
    me = dp * ctx_size + ctx
    shard, wide = packed.shape
    rows, model = hidden.shape
    one, two = big.shape[1] // 3, big_two.shape[1] // 3
    kv_width = KV_HEADS * HD
    q_width = HEADS * HD
    proj_width = q_width + 2 * kv_width
    groups = HEADS // KV_HEADS

    def at(index):
        return (index // ctx_size, index % ctx_size)

    def block(mask, count=1):
        base = flip(me, mask) // count * count
        return pl.ds(pl.multiple_of(base * shard, shard), shard * count)

    def remote(src, dst, send, recv, mask):
        return pltpu.make_async_remote_copy(
            src_ref=src, dst_ref=dst, send_sem=send, recv_sem=recv, device_id=at(flip(me, mask)), device_id_type=MESH
        )

    def drain(ref, sem):
        pltpu.make_async_copy(ref, ref, sem).wait()

    barrier = pltpu.get_barrier_semaphore()
    partners = (1, 2, 3, 4, 5, 8, 16, 17, 20, 21)
    for mask in partners:
        pl.semaphore_signal(barrier, inc=1, device_id=at(flip(me, mask)), device_id_type=MESH)

    own = (
        pltpu.make_async_copy(packed, proj.at[block(0)], load_sem.at[0]),
        pltpu.make_async_copy(w_out, out_w.at[block(0)], load_sem.at[1]),
    )
    for copy in own:
        copy.start()
    hidden_units = w_gate.shape[1]
    cuts = []
    for k in range(8):
        for n, ref in enumerate((w_gate, w_up, w_down)):
            for to, start, width in ((source, k * (one + two), one), (source_two, k * (one + two) + one, two)):
                size = min(width, hidden_units - start)
                cuts.append((ref.at[:, pl.ds(start, size)], to.at[k, :, pl.ds(n * width, size)]))
                if size < width:
                    to[k, :, pl.ds(n * width + size, width - size)] = jnp.zeros((shard, width - size), to.dtype)
    cuts = [pltpu.make_async_copy(a, b, load_sem.at[2 + i]) for i, (a, b) in enumerate(cuts)]
    for copy in cuts:
        copy.start()
    pl.semaphore_wait(barrier, len(partners))
    for copy in own:
        copy.wait()

    q_cols, k_cols = pl.ds(0, q_width), pl.ds(q_width, wide - q_width)
    streams = ((proj, k_cols), (proj, q_cols), (out_w, q_cols))

    def ag(n, mask, *overs):
        ref, cols = streams[n]
        part = ref.at[block(mask), cols]
        for over in overs:
            remote(part, part, ag_send.at[n], ag_recv.at[n, mask | over], over).start()

    def ag_pass(n, mask, *overs):
        ref, cols = streams[n]
        part = ref.at[block(mask), cols]
        remote(part, part, ag_send.at[n], ag_recv.at[n, mask], 1).wait_recv()
        ag(n, mask, *overs)

    def group(n, mask):
        ref, cols = streams[n]
        part = ref.at[block(mask, 4), cols]
        return remote(part, part, core_send.at[n, mask // 8], core_recv.at[n, mask // 8], 4)

    def group_wait(n):
        ref, cols = streams[n]
        for mask in (0, 8, 16, 24):
            part = ref.at[block(mask | 4, 4), cols]
            remote(part, part, core_send.at[n, mask // 8], core_recv.at[n, mask // 8], 4).wait_recv()

    ag(0, 0, 2, 1, 8, 16)
    ag(1, 0, 2, 1, 8, 16)

    for copy in cuts:
        copy.wait()
    y, x, c = dp // 4, (dp // 2) % 2, dp % 2
    h, p = ctx // 2, ctx % 2

    def column(mask):
        return either(y, mask // 16) * 4 + either(p, mask % 2) * 2 + either(c, (mask // 4) % 2)

    own_big = pltpu.make_async_copy(source.at[column(0)], big.at[block(0)], load_sem.at[0])
    own_big.start()
    own_two = pltpu.make_async_copy(source_two.at[column(0)], big_two.at[block(0)], load_sem.at[1])
    own_two.start()

    def cut(mask):
        remote(source.at[column(mask)], big.at[block(0)], big_send.at[0], big_recv.at[mask], mask).start()

    def cut_two(mask):
        return remote(source_two.at[column(mask)], big_two.at[block(0)], big_send.at[1], two_recv.at[mask], mask)

    held = (0, 4, 1, 5, 16, 20, 17, 21)
    inner = either(h, p) == 1

    def over_z(mask):
        src = big.at[block(mask)] if mask else source.at[column(0)]

        @pl.when(inner)
        def _():
            remote(src, big.at[block(mask)], big_send.at[0], big_recv.at[mask | 2], 2).start()

        @pl.when(jnp.logical_not(inner))
        def _():
            i = held.index(mask)
            remote(src, relay.at[i], big_send.at[0], relay_recv.at[i], 1).start()

    def relay_pass(*masks):
        @pl.when(inner)
        def _():
            for mask in masks:
                i = held.index(mask)
                remote(relay.at[i], relay.at[i], big_send.at[0], relay_recv.at[i], 1).wait_recv()
                remote(relay.at[i], big.at[block(mask ^ 1)], big_send.at[2], big_recv.at[mask | 2], 3).start()

    def big_forward(mask, over):
        if over == 2:
            over_z(mask)
        else:
            remote(big.at[block(mask)], big.at[block(mask)], big_send.at[0], big_recv.at[mask | over], over).start()

    def big_pass(mask, *overs):
        remote(big.at[block(mask)], big.at[block(mask)], big_send.at[0], big_recv.at[mask], 1).wait_recv()
        for over in overs:
            big_forward(mask, over)

    cut(4)
    over_z(0)

    ag_pass(0, 1, 8, 16)
    ag_pass(0, 8, 16)
    ag_pass(0, 2, 1, 8, 16)
    ag_pass(0, 9, 16)
    ag_pass(1, 1, 8, 16)
    ag_pass(1, 8, 16)
    ag_pass(0, 3, 8, 16)
    ag_pass(0, 10, 16)
    ag_pass(1, 2, 1, 8, 16)
    group(0, 0).start()
    remote(source.at[column(0)], big.at[block(0)], big_send.at[0], big_recv.at[8], 8).start()
    cut(1)
    cut(5)
    big_pass(4, 2, 8)
    ag_pass(0, 11, 16)
    group(0, 8).start()
    relay_pass(0)
    ag_pass(1, 9, 16)
    ag(2, 0, 2, 1, 16, 8)
    for mask in (16, 17, 18, 19):
        ag_pass(0, mask)
    group(0, 16).start()
    ag_pass(1, 3, 8, 16)
    group(1, 0).start()
    for mask in (24, 25, 26, 27):
        ag_pass(0, mask)
    group(0, 24).start()
    relay_pass(4)
    group_wait(0)

    small = jnp.transpose(proj[:, proj_width:].astype(jnp.float32))
    small_o[...] = small[:8]
    kv_bias = dot(small[:8].astype(jnp.bfloat16), spread[...], ((1,), (0,)))[3:4]
    values = hidden[...].astype(jnp.float32)
    factor = lax.rsqrt(jnp.mean(values * values, axis=-1, keepdims=True) + norm_eps)
    normed_o[...] = (values * factor * small[0:1]).astype(jnp.bfloat16)
    cos, sin = cosine[...], sine[...]
    raw = dot(normed_o[...], proj[:, q_width:proj_width], ((1,), (0,))) + kv_bias
    mine = block(0)
    for g in range(KV_HEADS):
        kv[ctx, :, pl.ds(g * HD, HD)] = turn(raw[:, g * HD : (g + 1) * HD], cos, sin).astype(jnp.bfloat16)
    kv[ctx, :, pl.ds(kv_width, kv_width)] = raw[:, kv_width:].astype(jnp.bfloat16)

    def kv_push(mask, over):
        slot = flip(ctx, mask)
        return remote(kv.at[slot], kv.at[slot], kv_send.at[mask | over], kv_recv.at[mask | over], over)

    kv_push(0, 2).start()
    kv_push(0, 1).start()
    ag_pass(1, 10, 16)
    ag_pass(1, 11, 16)
    group(1, 8).start()
    big_pass(1, 2, 8)
    ag_pass(2, 1, 16, 8)
    ag_pass(2, 2, 1, 16, 8)
    for mask in (16, 20, 17, 21):
        cut(mask)
    kv_push(0, 2).wait_recv()
    kv_push(2, 1).start()
    big_pass(5, 2, 8)
    relay_pass(1)
    for mask in (16, 17, 18, 19):
        ag_pass(1, mask)
    group(1, 16).start()
    ag_pass(2, 3, 16, 8)
    group(2, 0).start()
    for mask in (24, 25, 26, 27):
        ag_pass(1, mask)
    group(1, 24).start()
    big_pass(16, 2, 8)
    relay_pass(5)
    group_wait(1)
    for half in range(2):
        part = half * (q_width // 2)
        raw = dot(normed_o[...], proj[:, part : part + q_width // 2], ((1,), (0,)))
        raw = raw + small[1:2, part : part + q_width // 2]
        for i in range(HEADS // 2):
            query[half * (HEADS // 2) + i] = turn(raw[:, i * HD : (i + 1) * HD], cos, sin).astype(jnp.bfloat16)
    big_pass(20, 2, 8)
    relay_pass(16)
    for mask in (16, 17, 18, 19):
        ag_pass(2, mask, 8)
    group(2, 16).start()
    big_pass(17, 2, 8)
    big_pass(21, 2, 8)
    relay_pass(20)

    def go_core(o):
        src = go.at[2 * o] if o else grad_out
        return remote(src, go.at[2 * o + 1], go_send.at[3 + o], go_recv.at[2 * o + 1], 4)

    def go_push(o):
        src = go.at[2] if o == 3 else grad_out
        return remote(src, go.at[2 * o], go_send.at[o - 1], go_recv.at[2 * o], (0, 1, 16, 16)[o])

    go_push(2).start()
    go_push(1).start()
    go_core(0).start()
    for mask in (2, 6):
        big_pass(mask, 8)
    kv_push(0, 1).wait_recv()
    kv_push(2, 1).wait_recv()
    query_back = pltpu.make_async_copy(query, query_o, back_sem.at[0])
    query_back.start()
    kv_back = pltpu.make_async_copy(kv, kv_o, back_sem.at[1])
    kv_back.start()

    def head(n, carry):
        g = n // groups
        keys = kv[:, :, pl.ds(pl.multiple_of(g * HD, HD), HD)].reshape(ctx_size * rows, HD)
        vals = kv[:, :, pl.ds(pl.multiple_of(kv_width + g * HD, HD), HD)].reshape(ctx_size * rows, HD)
        scores = dot(query[n], keys, ((1,), (1,))) * HD ** (-0.5)
        scores = jnp.where(pos_k[...] <= pos_q[...], scores, masked_fill)
        top = jnp.max(scores, axis=-1, keepdims=True)
        expo = jnp.exp(scores - top)
        expo_sum = jnp.sum(expo, axis=-1, keepdims=True)
        attend = (expo / expo_sum).astype(jnp.bfloat16)
        mixed[:, pl.ds(pl.multiple_of(n * HD, HD), HD)] = dot(attend, vals, ((1,), (0,))).astype(jnp.bfloat16)
        lane = lax.broadcasted_iota(jnp.int32, (rows, HD), 1)
        total_o[...] = jnp.where(lane == n, top + jnp.log(expo_sum), total_o[...])
        return carry

    total_o[...] = jnp.zeros_like(total_o)
    lax.fori_loop(0, HEADS, head, 0)
    own_go = pltpu.make_async_copy(grad_out, go.at[0], load_sem.at[2])
    own_go.start()
    mixed_back = pltpu.make_async_copy(mixed, mixed_o, back_sem.at[2])
    mixed_back.start()
    relay_pass(17, 21)

    def two_over_z(mask):
        src = big_two.at[block(mask)] if mask else source_two.at[column(0)]
        return remote(src, big_two.at[block(mask)], big_send.at[1], two_recv.at[mask | 2], 2)

    for mask in (3, 7):
        big_pass(mask, 8)
    for mask in (4, 1, 5, 16, 20, 17, 21):
        cut_two(mask).start()
    for n, mask in enumerate((8, 9, 10, 11, 24, 25, 26, 27)):
        ag_pass(2, mask)
        if n % 4 == 3:
            group(2, mask & 24).start()
    group_wait(2)
    proj_back = pltpu.make_async_copy(proj, proj_o, back_sem.at[4])
    proj_back.start()
    out_back = pltpu.make_async_copy(out_w, out_o, back_sem.at[5])
    out_back.start()
    resid = hidden[...].astype(jnp.float32) + dot(mixed[...], out_w[...], ((1,), (1,)))
    resid_o[...] = resid
    factor = lax.rsqrt(jnp.mean(resid * resid, axis=-1, keepdims=True) + norm_eps)
    normed_two_o[...] = (resid * factor * small_o[2:3]).astype(jnp.bfloat16)
    go_push(1).wait_recv()
    go_push(3).start()
    go_core(1).start()
    go_push(2).wait_recv()
    go_core(2).start()
    two_over_z(0).start()
    for mask, passed in ((4, 18), (1, 22), (5, 19), (0, 23)):
        big_pass(passed, 8)
        if mask:
            cut_two(mask).wait_recv()
            two_over_z(mask).start()

    for mask in (8, 12, 9, 24, 13, 28, 25, 29, 10, 14, 11, 26, 15, 30, 27, 31):
        big_pass(mask)
    go_push(3).wait_recv()
    go_core(3).start()
    for mask in (16, 20, 17, 21):
        cut_two(mask).wait_recv()
    for mask in (0, 4, 1, 5):
        two_over_z(mask).wait_recv()
    own_big.wait()
    own_two.wait()
    own_go.wait()
    drain(big.at[pl.ds(0, 31 * shard)], big_send.at[0])
    drain(big_two.at[pl.ds(0, 11 * shard)], big_send.at[1])

    @pl.when(inner)
    def _():
        drain(relay, big_send.at[2])

    for n in range(3):
        ref, cols = streams[n]
        drain(ref.at[pl.ds(0, 15 * shard), cols], ag_send.at[n])
        for mask in (0, 8, 16, 24):
            group(n, mask).wait_send()
    for o in range(4):
        go_core(o).wait()
    for o in (1, 2, 3):
        go_push(o).wait_send()
    kv_push(0, 2).wait_send()
    kv_push(0, 1).wait_send()
    kv_push(2, 1).wait_send()
    for copy in (query_back, kv_back, mixed_back, proj_back, out_back):
        copy.wait()


def front_call(ctx_size, hidden, cosine, sine, pos_q, pos_k, spread, packed, w_out, w_gate, w_up, w_down, grad_out):
    rows, model = hidden.shape
    shard, wide = packed.shape
    kv_width = KV_HEADS * HD
    q_width = HEADS * HD
    one, two = widths(w_gate.shape[1])
    low, full = jnp.bfloat16, jnp.float32
    vmem = pl.BlockSpec(memory_space=pltpu.VMEM)
    anywhere = pl.BlockSpec(memory_space=pl.ANY)
    shapes = (
        ((rows, model), low, vmem),
        ((HEADS, rows, HD), low, anywhere),
        ((ctx_size, rows, 2 * kv_width), low, anywhere),
        ((rows, HD), full, vmem),
        ((rows, q_width), low, anywhere),
        ((rows, model), full, vmem),
        ((rows, model), low, vmem),
        ((8, model), full, vmem),
        ((model, wide), low, anywhere),
        ((model, q_width), low, anywhere),
        ((model, 3 * one), low, anywhere),
        ((model, 3 * two), low, anywhere),
        ((8, rows, model), low, anywhere),
        ((8, shard, 3 * one), low, anywhere),
    )
    sem = pltpu.SemaphoreType.DMA
    return pl.pallas_call(
        functools.partial(front_kernel, ctx_size),
        out_shape=tuple(jax.ShapeDtypeStruct(shape, kind) for shape, kind, _ in shapes),
        in_specs=[vmem] * 6 + [anywhere] * 6,
        out_specs=tuple(spec for _, _, spec in shapes),
        scratch_shapes=[
            pltpu.VMEM((model, wide), low),
            pltpu.VMEM((model, q_width), low),
            pltpu.VMEM((8, shard, 3 * one), low),
            pltpu.VMEM((8, shard, 3 * two), low),
            pltpu.VMEM((HEADS, rows, HD), low),
            pltpu.VMEM((ctx_size, rows, 2 * kv_width), low),
            pltpu.VMEM((rows, q_width), low),
            sem((50,)), sem((3,)), sem((3, 32)), sem((3, 4)), sem((3, 4)), sem((3,)), sem((32,)), sem((32,)), sem((8,)),
            sem((7,)), sem((8,)), sem((4,)), sem((4,)), sem((6,)),
        ],
        compiler_params=pltpu.CompilerParams(
            collective_id=0, has_side_effects=True, vmem_limit_bytes=56 << 20
        ),
        name="front",
    )(hidden, cosine, sine, pos_q, pos_k, spread, packed, w_out, w_gate, w_up, w_down, grad_out)


def back_kernel(
    ctx_size, grad_two, resid, hidden, grad_out, normed, mixed, query, kv, total, cosine, sine, pos_q, pos_k, small, spread,
    proj, out_w, grads, grads_two, near, zin_first, r_part,
    result_o, hidden_o, query_o, key_o, outw_o, gate_o, up_o, down_o, r_in, relay, relay_two,
    weight, turned, left_n, left_a, right_b, right_p, side, side_in, g_b, g_q, g_k,
    y_b, y_q, y_k, x_b, x_q, x_k, p_b, p_q, p_k, h_b, h_q, h_k,
    own, far, zin, fin, own_two, far_two, zin_two, fin_two, r_mid, r_one, stage, heads_g, lse, dkv, kv_out, kv_p, kv_h, grad_resid,
    load_sem, xs, xr, zs, zr, fs, fr, xs2, xr2, zs2, zr2, fs2, fr2, relay_recv, relay_send, cs, cr, rs, rr, ks, kr, st_sem, os, orr,
):
    dp = lax.axis_index("dp")
    ctx = lax.axis_index("ctx")
    me = dp * ctx_size + ctx
    y, x, c = dp // 4, (dp // 2) % 2, dp % 2
    h, p = ctx // 2, ctx % 2
    rows, model = resid.shape
    shard = grads.shape[3]
    hidden_units = gate_o.shape[1]
    one, two = widths(hidden_units)
    kv_width = KV_HEADS * HD
    q_width = HEADS * HD
    groups = HEADS // KV_HEADS
    low, full = jnp.bfloat16, jnp.float32
    span = ctx_size * shard

    def at(index):
        return (index // ctx_size, index % ctx_size)

    def remote(src, dst, send, recv, mask):
        return pltpu.make_async_remote_copy(
            src_ref=src, dst_ref=dst, send_sem=send, recv_sem=recv, device_id=at(flip(me, mask)), device_id_type=MESH
        )

    def group_rows(mask):
        return pl.ds(pl.multiple_of(flip(dp, mask // 4) * span, span), span)

    def mask_of(j):
        return (j // 4) * 16 + ((j // 2) % 2) * 4 + j % 2

    barrier = pltpu.get_barrier_semaphore()
    partners = (1, 2, 3, 4, 5, 8, 16, 17, 20, 21)
    for mask in partners:
        pl.semaphore_signal(barrier, inc=1, device_id=at(flip(me, mask)), device_id_type=MESH)
    load_w = pltpu.make_async_copy(out_w, weight.at[:, pl.ds(0, q_width)], load_sem.at[0])
    load_w.start()
    load_own = [
        pltpu.make_async_copy(grads.at[0, 0], own, load_sem.at[1]),
        pltpu.make_async_copy(grads_two.at[0], own_two, load_sem.at[2]),
        pltpu.make_async_copy(zin_first, zin.at[pl.ds(0, 4)], load_sem.at[3]),
        pltpu.make_async_copy(r_part.at[1], r_one, load_sem.at[4]),
    ]
    for copy in load_own:
        copy.start()
    pl.semaphore_wait(barrier, len(partners))

    def far_push(j):
        return remote(grads.at[1, 0, j], far.at[j], xs.at[j], xr.at[j], 8)

    def far_two_push(half, j):
        return remote(grads_two.at[1, half, j], far_two.at[half, j], xs2.at[half, j], xr2.at[half, j], 8)

    def z_push(j):
        return remote(near.at[j], zin.at[j], zs.at[j], zr.at[j], 2)

    def z_two_push(j):
        return remote(far_two.at[1, j], zin_two.at[j], zs2.at[j], zr2.at[j], 2)

    inner = either(h, p) == 1

    def over_z(push, src, to, send, n):
        @pl.when(inner)
        def _():
            push.start()

        @pl.when(jnp.logical_not(inner))
        def _():
            remote(src, to, send, relay_recv.at[n], 1).start()

    def over_z_one(j):
        over_z(z_push(j), near.at[j], relay.at[j - 4], zs.at[j], j)

    def over_z_two(j):
        over_z(z_two_push(j), far_two.at[1, j], relay_two.at[j], zs2.at[j], 8 + j)

    def relay_one(*blocks):
        @pl.when(inner)
        def _():
            for j in blocks:
                part = relay.at[j - 4]
                remote(part, part, relay_send.at[j], relay_recv.at[j], 1).wait_recv()
                remote(part, zin.at[j], relay_send.at[j], zr.at[j], 3).start()

    def relay_two_pass(*blocks):
        @pl.when(inner)
        def _():
            for j in blocks:
                part = relay_two.at[j]
                remote(part, part, relay_send.at[8 + j], relay_recv.at[8 + j], 1).wait_recv()
                remote(part, zin_two.at[j], relay_send.at[8 + j], zr2.at[j], 3).start()

    def fin_push(j):
        return remote(own.at[j], fin.at[j], fs.at[j], fr.at[j], mask_of(j))

    def fin_two_push(j):
        return remote(own_two.at[0, j], fin_two.at[j], fs2.at[j], fr2.at[j], mask_of(j))

    def z_two_step(j):
        far_two_push(1, j).wait_recv()
        far_two[1, j] = (far_two[1, j].astype(full) + own_two[1, j].astype(full)).astype(low)
        over_z_two(j)

    def total_step(j):
        far_push(j).wait_recv()
        if j > 3:
            z_push(j).wait_recv()
        own[j] = (own[j].astype(full) + far[j].astype(full) + zin[j].astype(full)).astype(low)
        if j:
            fin_push(j).start()

    def total_two_step(j):
        far_two_push(0, j).wait_recv()
        z_two_push(j).wait_recv()
        own_two[0, j] = (own_two[0, j].astype(full) + far_two[0, j].astype(full) + zin_two[j].astype(full)).astype(low)
        if j:
            fin_two_push(j).start()

    def r_push(o):
        src = r_one if o == 1 else r_part.at[o]
        dst = r_mid if o == 3 else r_in.at[o - 1]
        return remote(src, dst, os.at[o], orr.at[o], (0, 1, 16, 16)[o])

    r_push(3).start()
    for j in range(4, 8):
        over_z_one(j)
    for j in range(8):
        far_two_push(1, j).start()
    for j in range(8):
        far_push(j).start()

    def transposed(value, left, n):
        turned[n] = jnp.transpose(value)
        for i, mask in enumerate((0, 8, 16, 24)):
            left[i, :, pl.ds(0, rows)] = turned[n, group_rows(mask)]
            cross_left(left, n, i, mask).start()

    def cross_left(left, n, i, mask):
        return remote(turned.at[n, group_rows(mask | 4)], left.at[i, :, pl.ds(rows, rows)], cs.at[n, i], cr.at[n, i], 4)

    def cross(src, dst, n, i):
        return remote(src, dst, cs.at[n, i], cr.at[n, i], 4)

    transposed(normed[...], left_n, 0)
    right_b[pl.ds(0, rows)] = mixed[...]
    cross_mixed = cross(mixed, right_b.at[pl.ds(rows, rows)], 2, 0)
    cross_mixed.start()

    value = resid[...]
    factor = lax.rsqrt(jnp.mean(value * value, axis=-1, keepdims=True) + norm_eps)
    unit = value * factor
    scaled = grad_two[...] * small[2:3]
    ffn_row = jnp.sum(grad_two[...] * unit, axis=0, keepdims=True)
    grad_resid[...] = grad_out[...].astype(full) + factor * (
        scaled - unit * jnp.mean(scaled * unit, axis=-1, keepdims=True)
    )
    grad_attn = grad_resid[...].astype(low)
    transposed(grad_attn, left_a, 1)
    lse[...] = jnp.transpose(total[...])
    load_w.wait()
    for half in range(2):
        part = half * (q_width // 2)
        moved = dot(grad_attn, weight[:, part : part + q_width // 2], ((1,), (0,))).astype(low)
        for i in range(HEADS // 2):
            heads_g[half * (HEADS // 2) + i] = moved[:, i * HD : (i + 1) * HD]
    load_p = pltpu.make_async_copy(proj, weight, load_sem.at[0])
    load_p.start()

    streams = ((g_b, y_b, x_b, p_b, h_b), (g_q, y_q, x_q, p_q, h_q), (g_k, y_k, x_k, p_k, h_k))

    def add(ref, other):
        ref[...] = (ref[...].astype(full) + other[...].astype(full)).astype(low)

    def y_push(s, k):
        g, yy = streams[s][:2]
        return remote(g.at[2 + k], yy.at[k], rs.at[s, k], rr.at[s, k], 16)

    def x_push(s):
        g, xx = streams[s][0], streams[s][2]
        return remote(g.at[1], xx, rs.at[s, 2], rr.at[s, 2], 8)

    def block_of(hr, other):
        z = 2 * either(h, hr) + either(p, other)
        return pl.ds(pl.multiple_of(z * shard, shard), shard)

    def p_push(s, hr):
        g, pp = streams[s][0], streams[s][3]
        return remote(g.at[0, block_of(hr, 1)], pp.at[hr], rs.at[s, 3 + hr], rr.at[s, 3 + hr], 1)

    def h_push(s):
        g, hh = streams[s][0], streams[s][4]
        return remote(g.at[0, block_of(1, 0)], hh, rs.at[s, 5], rr.at[s, 5], 2)

    def y_pass(s):
        g, yy = streams[s][:2]
        y_push(s, 1).wait_recv()
        add(g.at[1], yy.at[1])
        x_push(s).start()
        y_push(s, 0).wait_recv()
        add(g.at[0], yy.at[0])

    def x_pass(s):
        x_push(s).wait_recv()
        add(streams[s][0].at[0], streams[s][2])
        p_push(s, 1).start()
        p_push(s, 0).start()

    def p_pass(s):
        g, pp = streams[s][0], streams[s][3]
        p_push(s, 1).wait_recv()
        add(g.at[0, block_of(1, 0)], pp.at[1])
        h_push(s).start()
        p_push(s, 0).wait_recv()
        add(g.at[0, block_of(0, 0)], pp.at[0])

    def h_pass(s, out):
        h_push(s).wait_recv()
        out[...] = streams[s][0][0, block_of(0, 0)].astype(full) + streams[s][4][...].astype(full)

    for i, mask in enumerate((0, 8, 16, 24)):
        cross_left(left_a, 1, i, mask).wait_recv()
    cross_mixed.wait_recv()
    for i in (3, 2, 1, 0):
        g_b[i] = dot(left_a[i], right_b[...], ((1,), (0,))).astype(low)
    y_push(0, 1).start()

    def head(n, carry):
        g = n // groups
        k_cols = pl.ds(pl.multiple_of(g * HD, HD), HD)
        v_cols = pl.ds(pl.multiple_of(kv_width + g * HD, HD), HD)
        keys = kv[:, :, k_cols].reshape(ctx_size * rows, HD)
        vals = kv[:, :, v_cols].reshape(ctx_size * rows, HD)
        scores = dot(keys, query[n], ((1,), (1,))) * HD ** (-0.5)
        scores = jnp.where(pos_k[...] <= pos_q[...], scores, masked_fill)
        attend = jnp.exp(scores - lse[pl.ds(n, 1), :])
        grad_attend = dot(vals, heads_g[n], ((1,), (1,)))
        delta = jnp.sum(grad_attend * attend, axis=0, keepdims=True)
        grad_scores = (attend * (grad_attend - delta)).astype(low)
        dkv[:, k_cols] += dot(grad_scores, query[n], ((1,), (0,)))
        dkv[:, v_cols] += dot(attend.astype(low), heads_g[n], ((1,), (0,)))
        back = dot(grad_scores, keys, ((0,), (0,))) * HD ** (-0.5)
        back = turn(back, cosine[...], -sine[...]).astype(low)
        right_p[pl.ds(0, rows), pl.ds(pl.multiple_of(n * HD, HD), HD)] = back
        return carry

    dkv[...] = jnp.zeros_like(dkv)
    lax.fori_loop(0, HEADS // 2, head, 0)
    relay_one(4, 5)
    lax.fori_loop(HEADS // 2, HEADS, head, 0)

    for z in range(ctx_size):
        part = dkv[pl.ds(z * rows, rows)]
        kv_out[z, :, pl.ds(0, kv_width)] = (part[:, :kv_width] * HD ** (-0.5)).astype(low)
        kv_out[z, :, pl.ds(kv_width, kv_width)] = part[:, kv_width:].astype(low)

    def kv_push(hr):
        return remote(kv_out.at[2 * either(h, hr) + 1 - p], kv_p.at[hr], ks.at[hr], kr.at[hr], 1)

    def kv_cross():
        return remote(kv_out.at[2 * (1 - h) + p], kv_h, ks.at[2], kr.at[2], 2)

    kv_push(1).start()
    kv_push(0).start()
    cross_q = cross(
        right_p.at[pl.ds(0, rows), pl.ds(0, q_width)], right_p.at[pl.ds(rows, rows), pl.ds(0, q_width)], 2, 1
    )
    cross_q.start()
    for copy in load_own:
        copy.wait()
    for i, mask in enumerate((0, 8, 16, 24)):
        cross_left(left_n, 0, i, mask).wait_recv()
    cross_q.wait_recv()
    for i in (3, 2, 1, 0):
        g_q[i] = dot(left_n[i], right_p[:, pl.ds(0, q_width)], ((1,), (0,))).astype(low)
        if i > 1:
            y_push(1, i - 2).start()
    load_p.wait()
    hidden_o[...] = dot(right_p[pl.ds(0, rows), pl.ds(0, q_width)], weight[:, pl.ds(0, q_width)], ((1,), (1,)))
    kv_push(1).wait_recv()
    add(kv_out.at[2 * (1 - h) + p], kv_p.at[1])
    kv_cross().start()
    kv_push(0).wait_recv()
    add(kv_out.at[2 * h + p], kv_p.at[0])
    relay_one(6, 7)
    for j in range(8):
        z_two_step(j)
    for j in range(4):
        total_step(j)
    relay_two_pass(0, 1, 2)
    kv_cross().wait_recv()
    final = kv_out[2 * h + p].astype(full) + kv_h[...].astype(full)
    for g in range(KV_HEADS):
        right_p[pl.ds(0, rows), pl.ds(q_width + g * HD, HD)] = turn(
            final[:, g * HD : (g + 1) * HD], cosine[...], -sine[...]
        ).astype(low)
    right_p[pl.ds(0, rows), pl.ds(q_width + kv_width, kv_width)] = final[:, kv_width:].astype(low)
    cross_kv = cross(
        right_p.at[pl.ds(0, rows), pl.ds(q_width, 2 * kv_width)],
        right_p.at[pl.ds(rows, rows), pl.ds(q_width, 2 * kv_width)], 2, 2,
    )
    cross_kv.start()
    grad_one = hidden_o[...] + dot(
        right_p[pl.ds(0, rows), pl.ds(q_width, 2 * kv_width)], weight[:, pl.ds(q_width, 2 * kv_width)], ((1,), (1,))
    )
    value = hidden[...].astype(full)
    factor = lax.rsqrt(jnp.mean(value * value, axis=-1, keepdims=True) + norm_eps)
    unit = value * factor
    scaled = grad_one * small[0:1]
    attn_row = jnp.sum(grad_one * unit, axis=0, keepdims=True)
    hidden_o[...] = grad_resid[...] + factor * (scaled - unit * jnp.mean(scaled * unit, axis=-1, keepdims=True))
    bias = jnp.sum(right_p[pl.ds(0, rows)].astype(full), axis=0, keepdims=True)
    kv_bias = jnp.broadcast_to(bias[:, q_width:], (8, 2 * kv_width)).astype(low)
    kv_row = dot(kv_bias, spread[...], ((1,), (1,)))[:1]
    table = jnp.concatenate([attn_row, bias[:, :q_width], ffn_row, kv_row, jnp.zeros((124, model), full)], axis=0)
    side[...] = jnp.transpose(table).astype(low)

    def cross_side(i, mask):
        return cross(side.at[group_rows(mask | 4)], side_in.at[i], 3, i)

    for i, mask in enumerate((0, 8, 16, 24)):
        cross_side(i, mask).start()
    cross_kv.wait_recv()
    for i, mask in ((3, 24), (2, 16), (1, 8), (0, 0)):
        g_k[i, :, pl.ds(0, 2 * kv_width)] = dot(
            left_n[i], right_p[:, pl.ds(q_width, 2 * kv_width)], ((1,), (0,))
        ).astype(low)
        cross_side(i, mask).wait_recv()
        g_k[i, :, pl.ds(2 * kv_width, HD)] = (
            side[group_rows(mask)].astype(full) + side_in[i].astype(full)
        ).astype(low)
        if i > 1:
            y_push(2, i - 2).start()
    outs = (gate_o, up_o, down_o)
    width = one + two
    last = hidden_units - 7 * width - one

    def piece(j):
        mask = mask_of(j)
        return either(y, mask // 16) * 4 + either(p, mask % 2) * 2 + either(c, (mask // 4) % 2)

    def write(j, start, size, count):
        for n in range(3):
            pltpu.make_async_copy(
                stage.at[j % 2, :, pl.ds(n * size, count)],
                outs[n].at[:, pl.ds(pl.multiple_of(piece(j) * width + start, HD), count)], st_sem.at[j % 2],
            ).start()

    def settle(slot, count):
        part = stage.at[slot, :, pl.ds(0, 3 * count)]
        pltpu.make_async_copy(part, part, st_sem.at[slot]).wait()

    def store(j):
        if j:
            fin_push(j).wait_recv()
        if j > 1:
            settle(j % 2, one)
        stage[j % 2] = (fin[j] if j else own[0]).astype(full)
        write(j, 0, one, one)

    def settle_two(j):
        pl.when(piece(j) < 7)(lambda: settle(j % 2, two))
        pl.when(piece(j) == 7)(lambda: settle(j % 2, last))

    def store_two(j):
        if j:
            fin_two_push(j).wait_recv()
        if j > 1:
            settle_two(j - 2)
        else:
            settle(j % 2, one)
        stage[j % 2, :, pl.ds(0, 3 * two)] = (fin_two[j] if j else own_two[0, 0]).astype(full)
        pl.when(piece(j) < 7)(lambda: write(j, one, two, two))
        pl.when(piece(j) == 7)(lambda: write(j, one, two, last))

    y_push(0, 0).start()
    r_push(3).wait_recv()
    add(r_one, r_mid)
    r_push(1).start()
    relay_two_pass(3, 4, 5, 6, 7)
    for j in range(4, 8):
        total_step(j)
    y_pass(1)
    y_pass(2)
    for j in range(8):
        far_two_push(0, j).start()
    y_pass(0)
    x_pass(1)
    x_pass(2)
    r_push(2).start()
    for j in range(4):
        store(j)
    p_pass(1)
    p_pass(2)
    for j in range(8):
        total_two_step(j)
    for j in range(4, 8):
        store(j)
    x_pass(0)
    p_pass(0)
    h_pass(1, query_o)
    h_pass(2, key_o)
    h_pass(0, outw_o)
    for j in range(8):
        store_two(j)
    settle_two(6)
    settle_two(7)
    for o in (1, 2):
        r_push(o).wait()
    r_push(3).wait_send()
    tiles = (r_part.at[0], r_in.at[0], r_in.at[1])
    loads = [
        pltpu.make_async_copy(ref, weight.at[pl.ds(o * rows, rows), pl.ds(0, model)], os.at[o])
        for o, ref in enumerate(tiles)
    ]
    for copy in loads:
        copy.start()
    for copy in loads:
        copy.wait()
    value = resid[...]
    for o in range(3):
        value = value + weight[pl.ds(o * rows, rows), pl.ds(0, model)].astype(full)
    result_o[...] = value.astype(low)

    for j in range(8):
        far_push(j).wait_send()
        far_two_push(0, j).wait_send()
        far_two_push(1, j).wait_send()
        if j > 3:
            z_push(j).wait_send()
        z_two_push(j).wait_send()
        if j:
            fin_push(j).wait_send()
            fin_two_push(j).wait_send()
    @pl.when(inner)
    def _():
        for j in range(4, 8):
            remote(relay.at[j - 4], relay.at[j - 4], relay_send.at[j], relay_recv.at[j], 1).wait_send()
        for j in range(8):
            remote(relay_two.at[j], relay_two.at[j], relay_send.at[8 + j], relay_recv.at[8 + j], 1).wait_send()

    for i, mask in enumerate((0, 8, 16, 24)):
        cross_left(left_n, 0, i, mask).wait_send()
        cross_left(left_a, 1, i, mask).wait_send()
        cross_side(i, mask).wait_send()
    for copy in (cross_mixed, cross_q, cross_kv):
        copy.wait_send()
    for s in range(3):
        for k in range(2):
            y_push(s, k).wait_send()
            p_push(s, k).wait_send()
        x_push(s).wait_send()
        h_push(s).wait_send()
    kv_push(0).wait_send()
    kv_push(1).wait_send()
    kv_cross().wait_send()


def back_call(
    ctx_size, hidden_units, grad_two, resid, hidden, grad_out, normed, mixed, query, kv, total, cosine, sine, pos_q, pos_k,
    small, spread, proj, out_w, grads, grads_two, near, zin_first, r_part,
):
    rows, model = resid.shape
    shard = grads.shape[3]
    one, two = widths(hidden_units)
    kv_width = KV_HEADS * HD
    q_width = HEADS * HD
    k_cols = 2 * kv_width + HD
    span = ctx_size * shard
    low, full = jnp.bfloat16, jnp.float32
    vmem = pl.BlockSpec(memory_space=pltpu.VMEM)
    anywhere = pl.BlockSpec(memory_space=pl.ANY)
    shapes = (
        ((rows, model), vmem, low),
        ((rows, model), vmem, full),
        ((shard, q_width), vmem, full),
        ((shard, k_cols), vmem, full),
        ((shard, q_width), vmem, full),
        ((shard, hidden_units), anywhere, full),
        ((shard, hidden_units), anywhere, full),
        ((shard, hidden_units), anywhere, full),
        ((2, rows, model), anywhere, low),
        ((4, shard, 3 * one), anywhere, low),
        ((8, shard, 3 * two), anywhere, low),
    )
    sem = pltpu.SemaphoreType.DMA
    cols = (q_width, q_width, k_cols)

    def each(*lead):
        return [pltpu.VMEM(lead + (n,), low) for n in cols]

    return pl.pallas_call(
        functools.partial(back_kernel, ctx_size),
        out_shape=tuple(jax.ShapeDtypeStruct(shape, kind) for shape, _, kind in shapes),
        in_specs=[vmem] * 15 + [anywhere] * 7,
        out_specs=tuple(spec for _, spec, _ in shapes),
        scratch_shapes=[
            pltpu.VMEM(proj.shape, low),
            pltpu.VMEM((2, model, rows), low),
            pltpu.VMEM((4, span, 2 * rows), low),
            pltpu.VMEM((4, span, 2 * rows), low),
            pltpu.VMEM((2 * rows, q_width), low),
            pltpu.VMEM((2 * rows, q_width + 2 * kv_width), low),
            pltpu.VMEM((model, HD), low),
            pltpu.VMEM((4, span, HD), low),
            *each(4, span),
            *each(2, span),
            *each(span),
            *each(2, shard),
            *each(shard),
            *([pltpu.VMEM((8, shard, 3 * one), low)] * 4),
            *([pltpu.VMEM((2, 8, shard, 3 * two), low)] * 2),
            *([pltpu.VMEM((8, shard, 3 * two), low)] * 2),
            *([pltpu.VMEM((rows, model), low)] * 2),
            pltpu.VMEM((2, shard, 3 * one), full),
            pltpu.VMEM((HEADS, rows, HD), low),
            pltpu.VMEM((HD, rows), full),
            pltpu.VMEM((ctx_size * rows, 2 * kv_width), full),
            pltpu.VMEM((ctx_size, rows, 2 * kv_width), low),
            pltpu.VMEM((2, rows, 2 * kv_width), low),
            pltpu.VMEM((rows, 2 * kv_width), low),
            pltpu.VMEM((rows, model), full),
            sem((5,)), *([sem((8,))] * 6), *([sem((2, 8))] * 2), *([sem((8,))] * 4), sem((16,)), sem((16,)),
            sem((4, 4)), sem((4, 4)), sem((3, 6)), sem((3, 6)), sem((3,)), sem((3,)), sem((2,)), sem((4,)), sem((4,)),
        ],
        compiler_params=pltpu.CompilerParams(
            collective_id=2, has_side_effects=True, vmem_limit_bytes=63 << 20
        ),
        name="back",
    )(
        grad_two, resid, hidden, grad_out, normed, mixed, query, kv, total, cosine, sine, pos_q, pos_k, small, spread,
        proj, out_w, grads, grads_two, near, zin_first, r_part,
    )


def fits(mesh):
    return mesh.shape["dp"] == 8 and mesh.shape["ctx"] == 4


def fast_device(
    hidden,
    cotangent,
    span_order,
    attn_gain,
    w_query,
    b_query,
    w_key,
    b_key,
    w_value,
    b_value,
    w_out,
    ffn_gain,
    w_gate,
    w_up,
    w_down,
):
    ctx_size = lax.axis_size("ctx")
    ctx_rank = lax.axis_index("ctx")
    batches = hidden.shape[0]
    length = hidden.shape[1]
    span_len = length // 2
    seq_len = length * ctx_size
    row_count = batches * length
    shard_rows = w_query.shape[0]
    kv_width = KV_HEADS * HD
    q_width = HEADS * HD

    grad_out = cotangent.reshape(row_count, D)
    places = jnp.arange(seq_len, dtype=jnp.int32)
    every_pos = jnp.repeat(span_order, span_len, axis=1) * span_len + places[None, :] % span_len
    local_pos = lax.dynamic_slice_in_dim(every_pos, ctx_rank * length, length, 1)
    cosine, sine = angles_for(local_pos.reshape(row_count), HD)
    cos_full = jnp.concatenate([cosine[:, 0], cosine[:, 0]], axis=1)
    sin_full = jnp.concatenate([-sine[:, 0], sine[:, 0]], axis=1)

    gains = jnp.stack([attn_gain, b_query, ffn_gain], axis=1)
    per = b_key.shape[0]
    pair = jnp.pad(jnp.concatenate([b_key, b_value]), (0, shard_rows - 2 * per))
    packed = jnp.concatenate(
        [w_query, w_key, w_value, gains, pair[:, None], jnp.zeros((shard_rows, 124), jnp.bfloat16)], axis=1
    )
    unit = jnp.arange(2 * kv_width)
    unit = unit % kv_width // per * shard_rows + unit // kv_width * per + unit % per
    spread = (jnp.arange(D)[:, None] == unit[None, :]).astype(jnp.bfloat16)
    source = hidden.reshape(row_count, D)
    normed, query_heads, key_value, log_total, mixed, resid, normed_two, small, proj_full, out_full, big, big_two, go_all, _ = front_call(
        ctx_size, source, cos_full, sin_full, local_pos.reshape(length, 1), every_pos.reshape(1, seq_len), spread,
        packed, w_out, w_gate, w_up, w_down, grad_out,
    )
    grad_two, r_part, grads, grads_two, near, zin, *_ = ffn_call(ctx_size, shard_rows, normed_two, go_all, big, big_two)
    result, hidden_grad, w_query_grad, kv_sum, w_out_grad, w_gate_grad, w_up_grad, w_down_grad, *_ = back_call(
        ctx_size, w_gate.shape[1], grad_two, resid, source, grad_out, normed, mixed, query_heads, key_value, log_total,
        cos_full, sin_full, local_pos.reshape(1, length), every_pos.reshape(seq_len, 1), small, spread,
        proj_full, out_full, grads, grads_two, near, zin, r_part,
    )
    sides = kv_sum[:, 2 * kv_width : 2 * kv_width + 4]
    return (
        result.reshape(batches, length, D),
        hidden_grad.reshape(batches, length, D),
        sides[:, 0],
        w_query_grad,
        sides[:, 1],
        kv_sum[:, :kv_width],
        sides[:per, 3],
        kv_sum[:, kv_width : 2 * kv_width],
        sides[per : 2 * per, 3],
        w_out_grad,
        sides[:, 2],
        w_gate_grad,
        w_up_grad,
        w_down_grad,
    )


def general_device(
    hidden,
    cotangent,
    span_order,
    attn_gain,
    w_query,
    b_query,
    w_key,
    b_key,
    w_value,
    b_value,
    w_out,
    ffn_gain,
    w_gate,
    w_up,
    w_down,
):
    ctx_size = lax.axis_size("ctx")
    ctx_rank = lax.axis_index("ctx")
    batches = hidden.shape[0]
    length = hidden.shape[1]
    span_len = length // 2
    seq_len = length * ctx_size
    row_count = batches * length
    groups = HEADS // KV_HEADS
    shard_rows = w_query.shape[0]
    head_scale = HD ** (-0.5)
    kv_width = KV_HEADS * HD
    q_width = HEADS * HD
    places = jnp.arange(seq_len, dtype=jnp.int32)
    every_pos = jnp.repeat(span_order, span_len, axis=1) * span_len + places[None, :] % span_len
    local_pos = lax.dynamic_slice_in_dim(every_pos, ctx_rank * length, length, 1)
    cosine, sine = angles_for(local_pos.reshape(row_count), HD)
    allowed = (every_pos[:, None, :] <= local_pos[:, :, None])[:, None, None]
    attn_full = (
        lax.all_gather(attn_gain, ("dp", "ctx"), axis=0, tiled=True),
        lax.all_gather(w_query, ("dp", "ctx"), axis=0, tiled=True),
        lax.all_gather(w_key, ("dp", "ctx"), axis=0, tiled=True),
        lax.all_gather(w_value, ("dp", "ctx"), axis=0, tiled=True),
        lax.all_gather(w_out, ("dp", "ctx"), axis=0, tiled=True),
        lax.all_gather(b_query, ("dp", "ctx"), axis=0, tiled=True),
        lax.all_gather(b_key, ("dp", "ctx"), axis=0, tiled=True),
        lax.all_gather(b_value, ("dp", "ctx"), axis=0, tiled=True),
    )
    gain_one = attn_full[0].astype(jnp.float32)
    source = hidden.reshape(row_count, D).astype(jnp.float32)
    attn_factor, normed = norm_forward(source, gain_one)
    query_raw = plain_dot(normed, attn_full[1]) + attn_full[5].astype(jnp.float32)
    key_raw = plain_dot(normed, attn_full[2]) + attn_full[6].astype(jnp.float32)
    value_low = (plain_dot(normed, attn_full[3]) + attn_full[7].astype(jnp.float32)).astype(
        jnp.bfloat16
    )
    query_rot = rotate(query_raw.reshape(row_count, HEADS, HD), cosine, sine).astype(jnp.bfloat16)
    query_rot = query_rot.reshape(batches, length, KV_HEADS, groups, HD)
    key_rot = rotate(key_raw.reshape(row_count, KV_HEADS, HD), cosine, sine).astype(jnp.bfloat16)
    key_rot = key_rot.reshape(batches, length, kv_width)
    key_all, value_all = (
        lax.all_gather(key_rot, "ctx", axis=1, tiled=True),
        lax.all_gather(value_low.reshape(batches, length, kv_width), "ctx", axis=1, tiled=True),
    )
    key_all = key_all.reshape(batches, seq_len, KV_HEADS, HD)
    value_all = value_all.reshape(batches, seq_len, KV_HEADS, HD)
    scores = (
        jnp.einsum("bqkgd,bskd->bkgqs", query_rot, key_all, preferred_element_type=jnp.float32)
        * head_scale
    )
    masked = jnp.where(allowed, scores, masked_fill)
    row_max = jnp.max(masked, axis=-1, keepdims=True)
    expo = jnp.exp(masked - row_max)
    expo_sum = jnp.sum(expo, axis=-1, keepdims=True)
    log_total = row_max + jnp.log(expo_sum)
    attend = (expo / expo_sum).astype(jnp.bfloat16)
    mixed = jnp.einsum("bkgqs,bskd->bqkgd", attend, value_all, preferred_element_type=jnp.float32)
    mixed = mixed.reshape(row_count, q_width).astype(jnp.bfloat16)
    resid = source + right_dot(mixed, attn_full[4])
    ffn_full = (
        lax.all_gather(ffn_gain, ("dp", "ctx"), axis=0, tiled=True),
        lax.all_gather(w_gate, ("dp", "ctx"), axis=0, tiled=True),
        lax.all_gather(w_up, ("dp", "ctx"), axis=0, tiled=True),
        lax.all_gather(w_down, ("dp", "ctx"), axis=0, tiled=True),
    )
    gain_two = ffn_full[0].astype(jnp.float32)
    ffn_factor, normed_two = norm_forward(resid, gain_two)
    gate_pre = plain_dot(normed_two, ffn_full[1])
    up_pre = plain_dot(normed_two, ffn_full[2])
    sigmoid_gate = jax.nn.sigmoid(gate_pre)
    silu_gate = gate_pre * sigmoid_gate
    act = (silu_gate * up_pre).astype(jnp.bfloat16)
    output = resid + right_dot(act, ffn_full[3])
    result = output.astype(jnp.bfloat16).reshape(batches, length, D)
    ffn_back = (
        lax.all_gather(ffn_gain, ("dp", "ctx"), axis=0, tiled=True),
        lax.all_gather(w_gate, ("dp", "ctx"), axis=0, tiled=True),
        lax.all_gather(w_up, ("dp", "ctx"), axis=0, tiled=True),
        lax.all_gather(w_down, ("dp", "ctx"), axis=0, tiled=True),
    )
    grad_out = cotangent.reshape(row_count, D)
    grad_plain = grad_out.astype(jnp.float32)
    grad_act = plain_dot(grad_out, ffn_back[3])
    grad_gate = (grad_act * up_pre * sigmoid_gate * (1.0 + gate_pre * (1.0 - sigmoid_gate))).astype(
        jnp.bfloat16
    )
    grad_up = (grad_act * silu_gate).astype(jnp.bfloat16)
    pieces = (
        lax.all_gather(normed_two, "ctx", axis=0, tiled=True),
        lax.all_gather(grad_gate, "ctx", axis=0, tiled=True),
        lax.all_gather(grad_up, "ctx", axis=0, tiled=True),
        lax.all_gather(act, "ctx", axis=0, tiled=True),
        lax.all_gather(grad_out, "ctx", axis=0, tiled=True),
    )
    picked_in = owned_columns(pieces[0], ctx_size, ctx_rank, shard_rows)
    picked_out = owned_columns(pieces[4], ctx_size, ctx_rank, shard_rows)
    w_gate_grad, w_up_grad, w_down_grad = (
        lax.psum_scatter(
            outer_add(picked_in, pieces[1]).astype(jnp.bfloat16),
            "dp",
            scatter_dimension=0,
            tiled=True,
        ).astype(jnp.float32),
        lax.psum_scatter(
            outer_add(picked_in, pieces[2]).astype(jnp.bfloat16),
            "dp",
            scatter_dimension=0,
            tiled=True,
        ).astype(jnp.float32),
        lax.psum_scatter(
            outer_add(picked_out, pieces[3]).astype(jnp.bfloat16),
            "dp",
            scatter_dimension=0,
            tiled=True,
        ).astype(jnp.float32),
    )
    grad_norm_two = right_dot(grad_gate, ffn_back[1]) + right_dot(grad_up, ffn_back[2])
    resid_back, ffn_gain_part = norm_backward(resid, ffn_factor, gain_two, grad_norm_two)
    grad_resid = grad_plain + resid_back
    attn_back = (
        lax.all_gather(attn_gain, ("dp", "ctx"), axis=0, tiled=True),
        lax.all_gather(w_query, ("dp", "ctx"), axis=0, tiled=True),
        lax.all_gather(w_key, ("dp", "ctx"), axis=0, tiled=True),
        lax.all_gather(w_value, ("dp", "ctx"), axis=0, tiled=True),
        lax.all_gather(w_out, ("dp", "ctx"), axis=0, tiled=True),
        lax.all_gather(b_query, ("dp", "ctx"), axis=0, tiled=True),
        lax.all_gather(b_key, ("dp", "ctx"), axis=0, tiled=True),
        lax.all_gather(b_value, ("dp", "ctx"), axis=0, tiled=True),
    )
    grad_attn = grad_resid.astype(jnp.bfloat16)
    grad_mixed = plain_dot(grad_attn, attn_back[4]).astype(jnp.bfloat16)
    grad_mixed = grad_mixed.reshape(batches, length, KV_HEADS, groups, HD)
    scores = (
        jnp.einsum("bqkgd,bskd->bkgqs", query_rot, key_all, preferred_element_type=jnp.float32)
        * head_scale
    )
    masked = jnp.where(allowed, scores, masked_fill)
    attend_full = jnp.exp(masked - log_total)
    attend = attend_full.astype(jnp.bfloat16)
    grad_attend = jnp.einsum(
        "bqkgd,bskd->bkgqs", grad_mixed, value_all, preferred_element_type=jnp.float32
    )
    value_grad_all = jnp.einsum(
        "bkgqs,bqkgd->bskd", attend, grad_mixed, preferred_element_type=jnp.float32
    )
    delta = jnp.sum(grad_attend * attend_full, axis=-1, keepdims=True)
    grad_scores = (attend_full * (grad_attend - delta)).astype(jnp.bfloat16)
    query_grad_rot = (
        jnp.einsum("bkgqs,bskd->bqkgd", grad_scores, key_all, preferred_element_type=jnp.float32)
        * head_scale
    )
    key_grad_all = (
        jnp.einsum("bkgqs,bqkgd->bskd", grad_scores, query_rot, preferred_element_type=jnp.float32)
        * head_scale
    )
    key_grad_rot, value_grad = (
        lax.psum_scatter(
            key_grad_all.reshape(batches, seq_len, kv_width), "ctx", scatter_dimension=1, tiled=True
        ),
        lax.psum_scatter(
            value_grad_all.reshape(batches, seq_len, kv_width),
            "ctx",
            scatter_dimension=1,
            tiled=True,
        ),
    )
    query_grad = (
        rotate_back(query_grad_rot.reshape(row_count, HEADS, HD), cosine, sine)
        .reshape(row_count, q_width)
        .astype(jnp.bfloat16)
    )
    key_grad = (
        rotate_back(key_grad_rot.reshape(row_count, KV_HEADS, HD), cosine, sine)
        .reshape(row_count, kv_width)
        .astype(jnp.bfloat16)
    )
    value_grad = value_grad.reshape(row_count, kv_width).astype(jnp.bfloat16)
    proj_grad = jnp.concatenate([query_grad, key_grad, value_grad], axis=1)
    pieces = (
        lax.all_gather(normed, "ctx", axis=0, tiled=True),
        lax.all_gather(proj_grad, "ctx", axis=0, tiled=True),
        lax.all_gather(grad_attn, "ctx", axis=0, tiled=True),
        lax.all_gather(mixed, "ctx", axis=0, tiled=True),
    )
    picked_in = owned_columns(pieces[0], ctx_size, ctx_rank, shard_rows)
    picked_out = owned_columns(pieces[2], ctx_size, ctx_rank, shard_rows)
    proj_sum, w_out_grad = (
        lax.psum_scatter(
            outer_add(picked_in, pieces[1]).astype(jnp.bfloat16),
            "dp",
            scatter_dimension=0,
            tiled=True,
        ).astype(jnp.float32),
        lax.psum_scatter(
            outer_add(picked_out, pieces[3]).astype(jnp.bfloat16),
            "dp",
            scatter_dimension=0,
            tiled=True,
        ).astype(jnp.float32),
    )
    grad_norm_one = (
        right_dot(query_grad, attn_back[1])
        + right_dot(key_grad, attn_back[2])
        + right_dot(value_grad, attn_back[3])
    )
    source_back, attn_gain_part = norm_backward(source, attn_factor, gain_one, grad_norm_one)
    hidden_grad = (grad_resid + source_back).reshape(batches, length, D)
    query_bias_part = jnp.sum(query_grad.astype(jnp.float32), axis=0)
    key_bias_part = jnp.sum(key_grad.astype(jnp.float32), axis=0)
    value_bias_part = jnp.sum(value_grad.astype(jnp.float32), axis=0)
    small_sums = (
        lax.psum_scatter(attn_gain_part, ("dp", "ctx"), scatter_dimension=0, tiled=True),
        lax.psum_scatter(query_bias_part, ("dp", "ctx"), scatter_dimension=0, tiled=True),
        lax.psum_scatter(key_bias_part, ("dp", "ctx"), scatter_dimension=0, tiled=True),
        lax.psum_scatter(value_bias_part, ("dp", "ctx"), scatter_dimension=0, tiled=True),
        lax.psum_scatter(ffn_gain_part, ("dp", "ctx"), scatter_dimension=0, tiled=True),
    )
    w_query_grad = proj_sum[:, :q_width]
    w_key_grad = proj_sum[:, q_width : q_width + kv_width]
    w_value_grad = proj_sum[:, q_width + kv_width :]
    return (
        result,
        hidden_grad,
        small_sums[0],
        w_query_grad,
        small_sums[1],
        w_key_grad,
        small_sums[2],
        w_value_grad,
        small_sums[3],
        w_out_grad,
        small_sums[4],
        w_gate_grad,
        w_up_grad,
        w_down_grad,
    )


def solution(mesh):
    placed = (
        P("dp", "ctx", None),
        P("dp", "ctx", None),
        P("dp", None),
        P(("dp", "ctx")),
        P(("dp", "ctx"), None),
        P(("dp", "ctx")),
        P(("dp", "ctx"), None),
        P(("dp", "ctx")),
        P(("dp", "ctx"), None),
        P(("dp", "ctx")),
        P(("dp", "ctx"), None),
        P(("dp", "ctx")),
        P(("dp", "ctx"), None),
        P(("dp", "ctx"), None),
        P(("dp", "ctx"), None),
    )
    return jax.shard_map(
        fast_device if fits(mesh) else general_device,
        mesh=mesh,
        in_specs=placed,
        out_specs=(
            P("dp", "ctx", None),
            P("dp", "ctx", None),
            P(("dp", "ctx")),
            P(("dp", "ctx"), None),
            P(("dp", "ctx")),
            P(("dp", "ctx"), None),
            P(("dp", "ctx")),
            P(("dp", "ctx"), None),
            P(("dp", "ctx")),
            P(("dp", "ctx"), None),
            P(("dp", "ctx")),
            P(("dp", "ctx"), None),
            P(("dp", "ctx"), None),
            P(("dp", "ctx"), None),
        ),
        check_vma=False,
    )
```

```python
import functools

import jax
import jax.numpy as jnp
from jax import lax
from jax.experimental import pallas as pl
from jax.experimental.pallas import tpu as pltpu
from jax.sharding import PartitionSpec as P

D = 1536
HEADS = 12
KV_HEADS = 2
HD = 128


norm_eps = 1e-06
rope_base = 10000.0
masked_fill = -1e30


def angles_for(places, width):
    half = width // 2
    freqs = rope_base ** (-(jnp.arange(half, dtype=jnp.float32) * 2.0 / width))
    angles = places.astype(jnp.float32)[:, None] * freqs[None, :]
    return (jnp.cos(angles)[:, None, :], jnp.sin(angles)[:, None, :])


def rotate(values, cosine, sine):
    half = values.shape[-1] // 2
    first = values[..., :half]
    second = values[..., half:]
    return jnp.concatenate(
        [first * cosine - second * sine, second * cosine + first * sine], axis=-1
    )


def rotate_back(values, cosine, sine):
    half = values.shape[-1] // 2
    first = values[..., :half]
    second = values[..., half:]
    return jnp.concatenate(
        [first * cosine + second * sine, second * cosine - first * sine], axis=-1
    )


def norm_forward(source, gain):
    factor = lax.rsqrt(jnp.mean(source * source, axis=-1, keepdims=True) + norm_eps)
    return (factor, (source * factor * gain).astype(jnp.bfloat16))


def norm_backward(source, factor, gain, grad_normed):
    unit = source * factor
    gain_grad = jnp.sum(grad_normed * unit, axis=0)
    scaled = grad_normed * gain
    source_grad = factor * (scaled - unit * jnp.mean(scaled * unit, axis=-1, keepdims=True))
    return (source_grad, gain_grad)


def right_dot(left, weight):
    return jnp.einsum("rf,df->rd", left, weight, preferred_element_type=jnp.float32)


def plain_dot(left, weight):
    return jnp.dot(left, weight, preferred_element_type=jnp.float32)


def owned_columns(values, ctx_size, ctx_rank, shard_rows):
    rows = values.shape[0]
    blocks = values.shape[1] // (shard_rows * ctx_size)
    shaped = values.reshape(rows, blocks, ctx_size, shard_rows)
    picked = lax.dynamic_index_in_dim(shaped, ctx_rank, axis=2, keepdims=False)
    return picked.reshape(rows, blocks * shard_rows)


def outer_add(left, right):
    return jnp.einsum("rc,rf->cf", left, right, preferred_element_type=jnp.float32)


MESH = pl.DeviceIdType.MESH


def flip(index, mask):
    for bit in (1, 2, 4, 8, 16):
        if mask & bit:
            index = index + bit - 2 * bit * ((index // bit) % 2)
    return index


def either(a, b):
    return a + b - 2 * a * b


def dot(a, b, dims):
    return lax.dot_general(a, b, (dims, ((), ())), preferred_element_type=jnp.float32)


def widths(hidden_units):
    width = -(-hidden_units // (8 * 128)) * 128
    first = width // 384 * 256
    return (first, width - first)


def ffn_kernel(
    ctx_size, n_own, norm_y, go_all, big, big_two,
    grad_two, r_part, grads, grads_two, near, zin,
    w_one, w_two, nt, go, ggu, act, crecv, part, h_in, h_mid, stage, own, far,
    io_sem, n_send, n_recv, f_send, f_recv, c_send, c_recv, o_send, o_recv, st_sem, w_send, w_recv, l_sem, x_send, x_recv, z_send, z_recv, d_sem,
):
    dp = lax.axis_index("dp")
    ctx = lax.axis_index("ctx")
    me = dp * ctx_size + ctx
    y, x, c = dp // 4, (dp // 2) % 2, dp % 2
    h, p = ctx // 2, ctx % 2
    one, two = w_one.shape[1] // 3, w_two.shape[1] // 3
    shard = grads.shape[3]
    rows, model = n_own.shape
    low, full = jnp.bfloat16, jnp.float32

    def at(index):
        return (index // ctx_size, index % ctx_size)

    def remote(src, dst, send, recv, mask):
        return pltpu.make_async_remote_copy(
            src_ref=src, dst_ref=dst, send_sem=send, recv_sem=recv, device_id=at(flip(me, mask)), device_id_type=MESH
        )

    def block(mask):
        return pl.ds(pl.multiple_of(flip(me, mask) * shard, shard), shard)

    barrier = pltpu.get_barrier_semaphore()
    partners = (1, 2, 4, 8, 16)
    for mask in partners:
        pl.semaphore_signal(barrier, inc=1, device_id=at(flip(me, mask)), device_id_type=MESH)
    load_n = pltpu.make_async_copy(n_own, nt.at[0], io_sem.at[0])
    load_y = pltpu.make_async_copy(norm_y, nt.at[4], io_sem.at[3])
    load_w = pltpu.make_async_copy(big, w_one, io_sem.at[1])
    load_go = pltpu.make_async_copy(go_all, go, io_sem.at[2])
    held = (0, 4, 1, 5, 16, 20, 17, 21, 2, 6, 3, 7)
    load_l = [
        pltpu.make_async_copy(big_two.at[block(mask)], w_two.at[block(mask)], l_sem.at[i]) for i, mask in enumerate(held)
    ]
    for copy in (load_n, load_y, load_w, load_go, *load_l):
        copy.start()
    pl.semaphore_wait(barrier, len(partners))

    def spread_two(mask, over):
        remote(big_two.at[block(mask)], w_two.at[block(mask)], w_send.at[0], w_recv.at[mask | over], over).start()

    def w_wait(mask):
        remote(w_two.at[block(mask)], w_two.at[block(mask)], w_send.at[0], w_recv.at[mask], 1).wait_recv()

    def w_pass(mask):
        w_wait(mask)
        remote(w_two.at[block(mask)], w_two.at[block(mask)], w_send.at[0], w_recv.at[mask | 8], 8).start()

    def n_core(slot):
        return remote(nt.at[slot], nt.at[slot + 1], f_send.at[slot // 2], f_recv.at[slot // 2], 4)

    def n_push(o):
        half = pl.ds((o - 1) % 2 * (rows // 2), rows // 2)
        if o == 1:
            return remote(nt.at[0], nt.at[2], n_send.at[1], n_recv.at[1], 1)
        return remote(nt.at[(0, 0, 4, 2)[o], half], nt.at[6, half], n_send.at[o], n_recv.at[o], (0, 0, 1, 16)[o])

    load_n.wait()
    n_push(1).start()
    n_core(0).start()
    load_y.wait()
    n_push(2).start()
    n_core(4).start()
    for mask in (16, 20, 17, 21):
        spread_two(mask, 2)
    for mask in held:
        spread_two(mask, 8)
    load_w.wait()
    load_go.wait()

    def first(slot):
        gu = dot(nt[slot], w_one[:, : 2 * one], ((1,), (0,)))
        ga = dot(go[slot], w_one[:, 2 * one :], ((1,), (0,)))
        finish(slot, gu[:, :one], gu[:, one:], ga, 0, 0)

    def finish(slot, gate, up, ga, at_gu, at_act):
        size = gate.shape[1]
        sig = 1.0 / (1.0 + jnp.exp(-gate))
        silu = gate * sig
        act[slot, :, pl.ds(at_act, size)] = (silu * up).astype(low)
        ggu[slot, :, pl.ds(at_gu, size)] = (ga * up * sig * (1.0 + gate * (1.0 - sig))).astype(low)
        ggu[slot, :, pl.ds(at_gu + size, size)] = (ga * silu).astype(low)

    def second(slot):
        gu = dot(nt[slot], w_two[:, : 2 * two], ((1,), (0,)))
        ga = dot(go[slot], w_two[:, 2 * two :], ((1,), (0,)))
        finish(slot, gu[:, :two], gu[:, two:], ga, 2 * one, one)
        grad = dot(ggu[slot, :, : 2 * one], w_one[:, : 2 * one], ((1,), (1,)))
        grad = grad + dot(ggu[slot, :, 2 * one :], w_two[:, : 2 * two], ((1,), (1,)))
        out = dot(act[slot, :, :one], w_one[:, 2 * one :], ((1,), (1,)))
        out = out + dot(act[slot, :, one:], w_two[:, 2 * two :], ((1,), (1,)))
        return (grad.astype(low), out.astype(low))

    def early(n, carry):
        o = n % 2 * 2 + n // 2

        @pl.when(o == 1)
        def _():
            n_push(1).wait_recv()
            n_push(3).start()
            n_core(2).start()

        @pl.when(o == 3)
        def _():
            n_push(2).wait_recv()
            n_push(3).wait_recv()
            n_core(6).start()

        first(2 * o)


        n_core(2 * o).wait_recv()
        first(2 * o + 1)
        return carry

    lax.fori_loop(0, 4, early, 0)
    def stage_wait(slot, size):
        part_of = stage.at[slot, :, pl.ds(0, size)]
        pltpu.make_async_copy(part_of, part_of, st_sem.at[slot]).wait()

    def weights(size, start_gu, start_act, to, passes, q, carry):
        slot = q % 2

        @pl.when(q > 1)
        def _():
            stage_wait(slot, 3 * size)

        chunk = 8 * shard
        cols = pl.ds(pl.multiple_of(q * chunk, chunk), chunk)

        def product(left, right, start, count, at_col):
            left = left[:, :, cols].reshape(8 * rows, chunk)
            right = right[:, :, pl.ds(start, count)].reshape(8 * rows, count)
            stage[slot, :, pl.ds(at_col, count)] = dot(left, right, ((0,), (0,))).astype(low)

        for start in range(0, 2 * size, one):
            count = min(one, 2 * size - start)
            product(nt, ggu, start_gu + start, count, start)
        product(go, act, start_act, size, 2 * size)
        for n, masks in enumerate(passes):
            @pl.when(q == n)
            def _():
                for mask in masks:
                    w_pass(mask)

        yr, xr = either(q // 2, y), either(q % 2, x)
        for j in range(8):
            cr, hrel, pr = either(j // 4, c), either((j // 2) % 2, h), either(j % 2, p)
            pltpu.make_async_copy(
                stage.at[slot, pl.ds(j * shard, shard), pl.ds(0, 3 * size)],
                to.at[xr, hrel, yr * 4 + cr * 2 + pr], st_sem.at[slot],
            ).start()
        return carry

    def all_weights(size, start_gu, start_act, to, passes=()):
        lax.fori_loop(0, 4, functools.partial(weights, size, start_gu, start_act, to, passes), 0)
        stage_wait(0, 3 * size)
        stage_wait(1, 3 * size)

    def far_push(j):
        return remote(grads.at[1, 1, j], far.at[j], x_send.at[j], x_recv.at[j], 8)

    def z_push(j):
        return remote(far.at[j], zin.at[j], z_send.at[j], z_recv.at[j], 2)

    def load_own(k):
        return pltpu.make_async_copy(grads.at[0, 1, pl.ds(4 * k, 4)], own, d_sem.at[0])

    keep_near = pltpu.make_async_copy(far, near, d_sem.at[0])

    def far_pass(*blocks):
        for j in blocks:
            far_push(j).wait_recv()
            far[j] = (far[j].astype(full) + own[j % 4].astype(full)).astype(low)
            if j < 4:
                z_push(j).start()

    all_weights(one, 0, 0, grads, ((18, 22, 19, 23),))
    for j in range(8):
        far_push(j).start()
    load_own(0).start()

    for mask in (8, 12, 9, 13, 24, 28, 25, 29, 10, 14, 11, 15, 26, 30, 27, 31):
        w_wait(mask)
    for copy in load_l:
        copy.wait()

    def cross(o):
        return remote(stage.at[:, pl.ds(0, rows), pl.ds(0, model)], crecv.at[o % 2], c_send, c_recv.at[o % 2], 4)

    def final(o):
        dst = h_mid if o == 3 else h_in.at[o - 1]
        return remote(part.at[o, 0], dst, o_send.at[o], o_recv.at[o], (0, 1, 16, 16)[o])

    def keep(o):
        return pltpu.make_async_copy(part.at[o, 1], r_part.at[o], io_sem.at[o])

    def combine(o):
        cross(o).wait_recv()
        part[o] = (part[o].astype(full) + crecv[o % 2].astype(full)).astype(low)
        keep(o).start()

    def late(n, carry):
        o = 3 - n
        grad, out = second(2 * o)
        part[o, 0] = grad
        part[o, 1] = out

        @pl.when(n > 0)
        def _():
            combine(o + 1)

        @pl.when(n == 1)
        def _():
            final(3).start()
            load_own(0).wait()
            far_pass(0, 1)

        @pl.when(n == 2)
        def _():
            final(2).start()
            far_pass(2, 3)
            load_own(1).start()

        @pl.when(n == 3)
        def _():
            final(3).wait_recv()
            part[1, 0] = (part[1, 0].astype(full) + h_mid[...].astype(full)).astype(low)
            final(1).start()
            load_own(1).wait()
            far_pass(4, 5)

        grad, out = second(2 * o + 1)

        @pl.when(n > 0)
        def _():
            cross(o).wait_send()

        stage[0, pl.ds(0, rows), pl.ds(0, model)] = grad
        stage[1, pl.ds(0, rows), pl.ds(0, model)] = out
        cross(o).start()
        return carry

    lax.fori_loop(0, 4, late, 0)

    far_pass(6, 7)
    keep_near.start()
    cross(0).wait_send()
    all_weights(two, 2 * one, one, grads_two)
    combine(0)
    grad_two[...] = part[0, 0].astype(full)
    for o in (1, 2):
        final(o).wait_recv()
        grad_two[...] += h_in[o - 1].astype(full)
    keep_near.wait()
    for j in range(8):
        far_push(j).wait_send()
        if j < 4:
            z_push(j).wait()
    for o in range(4):
        keep(o).wait()
        n_core(2 * o).wait_send()
    for o in (1, 2, 3):
        n_push(o).wait_send()
        final(o).wait_send()
    sent = w_two.at[pl.ds(0, 20 * shard)]
    pltpu.make_async_copy(sent, sent, w_send.at[0]).wait()


def ffn_call(ctx_size, shard, n_own, norm_y, go_all, big, big_two):
    rows, model = n_own.shape
    one, two = big.shape[1] // 3, big_two.shape[1] // 3
    low = jnp.bfloat16
    anywhere = pl.BlockSpec(memory_space=pl.ANY)
    sem = pltpu.SemaphoreType.DMA
    return pl.pallas_call(
        functools.partial(ffn_kernel, ctx_size),
        out_shape=(
            jax.ShapeDtypeStruct((rows, model), jnp.float32),
            jax.ShapeDtypeStruct((4, rows, model), low),
            jax.ShapeDtypeStruct((2, 2, 8, shard, 3 * one), low),
            jax.ShapeDtypeStruct((2, 2, 8, shard, 3 * two), low),
            jax.ShapeDtypeStruct((8, shard, 3 * one), low),
            jax.ShapeDtypeStruct((4, shard, 3 * one), low),
        ),
        in_specs=[anywhere] * 5,
        out_specs=[pl.BlockSpec(memory_space=pltpu.VMEM)] + [anywhere] * 5,
        scratch_shapes=[
            pltpu.VMEM((model, 3 * one), low),
            pltpu.VMEM((model, 3 * two), low),
            pltpu.VMEM((8, rows, model), low),
            pltpu.VMEM((8, rows, model), low),
            pltpu.VMEM((8, rows, 2 * (one + two)), low),
            pltpu.VMEM((8, rows, one + two), low),
            pltpu.VMEM((2, 2, rows, model), low),
            pltpu.VMEM((4, 2, rows, model), low),
            pltpu.VMEM((2, rows, model), low),
            pltpu.VMEM((rows, model), low),
            pltpu.VMEM((2, 8 * shard, 3 * one), low),
            pltpu.VMEM((4, shard, 3 * one), low),
            pltpu.VMEM((8, shard, 3 * one), low),
            sem((4,)), sem((5,)), sem((5,)), sem((4,)), sem((4,)), sem, sem((2,)), sem((4,)), sem((4,)), sem((2,)),
            sem((1,)), sem((32,)), sem((12,)), sem((8,)), sem((8,)), sem((4,)), sem((4,)), sem((1,)),
        ],
        compiler_params=pltpu.CompilerParams(
            collective_id=1, has_side_effects=True, vmem_limit_bytes=65200 << 10
        ),
        name="ffn",
    )(n_own, norm_y, go_all, big, big_two)


def turn(values, cosine, sine):
    return values * cosine + pltpu.roll(values, HD // 2, 1) * sine


def front_kernel(
    ctx_size, hidden, cosine, sine, pos_q, pos_k, w_query, w_key, w_value, sides, w_out, w_gate, w_up, w_down, grad_out,
    normed_o, query_o, kv_o, total_o, mixed_o, resid_o, normed_two_o, small_o, proj_o, out_o, big, big_two, go, relay, spread, norm_y,
    proj, out_w, source, source_two, query, kv, mixed,
    load_sem, ag_send, ag_recv, core_send, core_recv, big_send, big_recv, two_recv, relay_recv, go_send, go_recv, kv_send, kv_recv, back_sem, norm_sem,
):
    dp = lax.axis_index("dp")
    ctx = lax.axis_index("ctx")
    me = dp * ctx_size + ctx
    shard, wide = w_out.shape[0], proj.shape[1]
    rows, model = hidden.shape
    one, two = big.shape[1] // 3, big_two.shape[1] // 3
    kv_width = KV_HEADS * HD
    q_width = HEADS * HD
    proj_width = q_width + 2 * kv_width
    groups = HEADS // KV_HEADS

    def at(index):
        return (index // ctx_size, index % ctx_size)

    def block(mask, count=1):
        base = flip(me, mask) // count * count
        return pl.ds(pl.multiple_of(base * shard, shard), shard * count)

    def remote(src, dst, send, recv, mask):
        return pltpu.make_async_remote_copy(
            src_ref=src, dst_ref=dst, send_sem=send, recv_sem=recv, device_id=at(flip(me, mask)), device_id_type=MESH
        )

    def drain(ref, sem):
        pltpu.make_async_copy(ref, ref, sem).wait()

    barrier = pltpu.get_barrier_semaphore()
    partners = (1, 2, 3, 4, 5, 8, 16, 17, 20, 21)
    for mask in partners:
        pl.semaphore_signal(barrier, inc=1, device_id=at(flip(me, mask)), device_id_type=MESH)

    own = (
        pltpu.make_async_copy(w_query, proj.at[block(0), pl.ds(0, q_width)], load_sem.at[0]),
        pltpu.make_async_copy(w_out, out_w.at[block(0)], load_sem.at[1]),
        pltpu.make_async_copy(w_key, proj.at[block(0), pl.ds(q_width, kv_width)], load_sem.at[50]),
        pltpu.make_async_copy(w_value, proj.at[block(0), pl.ds(q_width + kv_width, kv_width)], load_sem.at[51]),
        pltpu.make_async_copy(sides, proj.at[block(0), pl.ds(proj_width, HD)], load_sem.at[52]),
    )
    for copy in own:
        copy.start()
    hidden_units = w_gate.shape[1]
    cuts = []
    for k in range(8):
        for n, ref in enumerate((w_gate, w_up, w_down)):
            for to, start, width in ((source, k * (one + two), one), (source_two, k * (one + two) + one, two)):
                size = min(width, hidden_units - start)
                cuts.append((ref.at[:, pl.ds(start, size)], to.at[k, :, pl.ds(n * width, size)]))
                if size < width:
                    to[k, :, pl.ds(n * width + size, width - size)] = jnp.zeros((shard, width - size), to.dtype)
    cuts = [pltpu.make_async_copy(a, b, load_sem.at[2 + i]) for i, (a, b) in enumerate(cuts)]
    for copy in cuts:
        copy.start()
    pl.semaphore_wait(barrier, len(partners))
    for copy in own:
        copy.wait()

    q_cols, k_cols = pl.ds(0, q_width), pl.ds(q_width, wide - q_width)
    streams = ((proj, k_cols), (proj, q_cols), (out_w, q_cols))

    def ag(n, mask, *overs):
        ref, cols = streams[n]
        part = ref.at[block(mask), cols]
        for over in overs:
            remote(part, part, ag_send.at[n], ag_recv.at[n, mask | over], over).start()

    def ag_pass(n, mask, *overs):
        ref, cols = streams[n]
        part = ref.at[block(mask), cols]
        remote(part, part, ag_send.at[n], ag_recv.at[n, mask], 1).wait_recv()
        ag(n, mask, *overs)

    def group(n, mask):
        ref, cols = streams[n]
        part = ref.at[block(mask, 4), cols]
        return remote(part, part, core_send.at[n, mask // 8], core_recv.at[n, mask // 8], 4)

    def group_wait(n):
        ref, cols = streams[n]
        for mask in (0, 8, 16, 24):
            part = ref.at[block(mask | 4, 4), cols]
            remote(part, part, core_send.at[n, mask // 8], core_recv.at[n, mask // 8], 4).wait_recv()

    ag(0, 0, 2, 1, 8, 16)
    ag(1, 0, 2, 1, 8, 16)

    for copy in cuts:
        copy.wait()
    y, x, c = dp // 4, (dp // 2) % 2, dp % 2
    h, p = ctx // 2, ctx % 2

    def column(mask):
        return either(y, mask // 16) * 4 + either(p, mask % 2) * 2 + either(c, (mask // 4) % 2)

    own_big = pltpu.make_async_copy(source.at[column(0)], big.at[block(0)], load_sem.at[0])
    own_big.start()
    own_two = pltpu.make_async_copy(source_two.at[column(0)], big_two.at[block(0)], load_sem.at[1])
    own_two.start()

    def cut(mask):
        remote(source.at[column(mask)], big.at[block(0)], big_send.at[0], big_recv.at[mask], mask).start()

    def cut_two(mask):
        return remote(source_two.at[column(mask)], big_two.at[block(0)], big_send.at[1], two_recv.at[mask], mask)

    held = (0, 4, 1, 5, 16, 20, 17, 21)
    inner = either(h, p) == 1

    def over_z(mask):
        src = big.at[block(mask)] if mask else source.at[column(0)]

        @pl.when(inner)
        def _():
            remote(src, big.at[block(mask)], big_send.at[0], big_recv.at[mask | 2], 2).start()

        @pl.when(jnp.logical_not(inner))
        def _():
            i = held.index(mask)
            remote(src, relay.at[i], big_send.at[0], relay_recv.at[i], 1).start()

    def relay_pass(*masks):
        @pl.when(inner)
        def _():
            for mask in masks:
                i = held.index(mask)
                remote(relay.at[i], relay.at[i], big_send.at[0], relay_recv.at[i], 1).wait_recv()
                remote(relay.at[i], big.at[block(mask ^ 1)], big_send.at[2], big_recv.at[mask | 2], 3).start()

    def big_forward(mask, over):
        if over == 2:
            over_z(mask)
        else:
            remote(big.at[block(mask)], big.at[block(mask)], big_send.at[0], big_recv.at[mask | over], over).start()

    def big_pass(mask, *overs):
        remote(big.at[block(mask)], big.at[block(mask)], big_send.at[0], big_recv.at[mask], 1).wait_recv()
        for over in overs:
            big_forward(mask, over)

    cut(4)
    over_z(0)

    row = lax.broadcasted_iota(jnp.int32, (model, 2 * kv_width), 0)
    col = lax.broadcasted_iota(jnp.int32, (model, 2 * kv_width), 1)
    per = kv_width * shard // model
    unit = (col % kv_width) // per * shard + col // kv_width * per + col % per
    spread[...] = jnp.where(row == unit, 1.0, 0.0).astype(jnp.bfloat16)
    own_pos = jnp.transpose(jnp.broadcast_to(pos_q[...].astype(jnp.float32), (HD, rows)))[:, :1]
    signs = jnp.where(lax.broadcasted_iota(jnp.int32, (rows, HD), 1) < HD // 2, -1.0, 1.0)

    ag_pass(0, 1, 8, 16)
    ag_pass(0, 8, 16)
    ag_pass(0, 2, 1, 8, 16)
    ag_pass(0, 9, 16)
    ag_pass(1, 1, 8, 16)
    ag_pass(1, 8, 16)
    ag_pass(0, 3, 8, 16)
    ag_pass(0, 10, 16)
    ag_pass(1, 2, 1, 8, 16)
    group(0, 0).start()
    remote(source.at[column(0)], big.at[block(0)], big_send.at[0], big_recv.at[8], 8).start()
    cut(1)
    cut(5)
    big_pass(4, 2, 8)
    ag_pass(0, 11, 16)
    group(0, 8).start()
    relay_pass(0)
    ag_pass(1, 9, 16)
    ag(2, 0, 2, 1, 16, 8)
    for mask in (16, 17, 18, 19):
        ag_pass(0, mask)
    group(0, 16).start()
    ag_pass(1, 3, 8, 16)
    group(1, 0).start()
    for mask in (24, 25, 26, 27):
        ag_pass(0, mask)
    group(0, 24).start()
    relay_pass(4)
    group_wait(0)

    small = jnp.transpose(proj[:, proj_width:].astype(jnp.float32))
    small_o[...] = small[:8]
    kv_bias = dot(small[:8].astype(jnp.bfloat16), spread[...], ((1,), (0,)))[3:4]
    values = hidden[...].astype(jnp.float32)
    factor = lax.rsqrt(jnp.mean(values * values, axis=-1, keepdims=True) + norm_eps)
    normed_o[...] = (values * factor * small[0:1]).astype(jnp.bfloat16)
    cos, sin = cosine[...], sine[...] * signs
    raw = dot(normed_o[...], proj[:, q_width:proj_width], ((1,), (0,))) + kv_bias
    mine = block(0)
    for g in range(KV_HEADS):
        kv[ctx, :, pl.ds(g * HD, HD)] = turn(raw[:, g * HD : (g + 1) * HD], cos, sin).astype(jnp.bfloat16)
    kv[ctx, :, pl.ds(kv_width, kv_width)] = raw[:, kv_width:].astype(jnp.bfloat16)

    def kv_push(mask, over):
        slot = flip(ctx, mask)
        return remote(kv.at[slot], kv.at[slot], kv_send.at[mask | over], kv_recv.at[mask | over], over)

    kv_push(0, 2).start()
    kv_push(0, 1).start()
    ag_pass(1, 10, 16)
    ag_pass(1, 11, 16)
    group(1, 8).start()
    big_pass(1, 2, 8)
    ag_pass(2, 1, 16, 8)
    ag_pass(2, 2, 1, 16, 8)
    for mask in (16, 20, 17, 21):
        cut(mask)
    kv_push(0, 2).wait_recv()
    kv_push(2, 1).start()
    big_pass(5, 2, 8)
    relay_pass(1)
    for mask in (16, 17, 18, 19):
        ag_pass(1, mask)
    group(1, 16).start()
    ag_pass(2, 3, 16, 8)
    group(2, 0).start()
    for mask in (24, 25, 26, 27):
        ag_pass(1, mask)
    group(1, 24).start()
    big_pass(16, 2, 8)
    relay_pass(5)
    group_wait(1)
    for half in range(2):
        part = half * (q_width // 2)
        raw = dot(normed_o[...], proj[:, part : part + q_width // 2], ((1,), (0,)))
        raw = raw + small[1:2, part : part + q_width // 2]
        for i in range(HEADS // 2):
            query[half * (HEADS // 2) + i] = turn(raw[:, i * HD : (i + 1) * HD], cos, sin).astype(jnp.bfloat16)
    big_pass(20, 2, 8)
    relay_pass(16)
    for mask in (16, 17, 18, 19):
        ag_pass(2, mask, 8)
    group(2, 16).start()
    big_pass(17, 2, 8)
    big_pass(21, 2, 8)
    relay_pass(20)

    def go_core(o):
        src = go.at[2 * o] if o else grad_out
        return remote(src, go.at[2 * o + 1], go_send.at[3 + o], go_recv.at[2 * o + 1], 4)

    def go_push(o):
        src = go.at[2] if o == 3 else grad_out
        return remote(src, go.at[2 * o], go_send.at[o - 1], go_recv.at[2 * o], (0, 1, 16, 16)[o])

    go_push(2).start()
    go_push(1).start()
    go_core(0).start()
    for mask in (2, 6):
        big_pass(mask, 8)
    kv_push(0, 1).wait_recv()
    kv_push(2, 1).wait_recv()
    query_back = pltpu.make_async_copy(query, query_o, back_sem.at[0])
    query_back.start()
    kv_back = pltpu.make_async_copy(kv, kv_o, back_sem.at[1])
    kv_back.start()

    def head(n, carry):
        g = n // groups
        keys = kv[:, :, pl.ds(pl.multiple_of(g * HD, HD), HD)].reshape(ctx_size * rows, HD)
        vals = kv[:, :, pl.ds(pl.multiple_of(kv_width + g * HD, HD), HD)].reshape(ctx_size * rows, HD)
        scores = dot(query[n], keys, ((1,), (1,))) * HD ** (-0.5)
        scores = jnp.where(pos_k[...] <= own_pos, scores, masked_fill)
        top = jnp.max(scores, axis=-1, keepdims=True)
        expo = jnp.exp(scores - top)
        expo_sum = jnp.sum(expo, axis=-1, keepdims=True)
        attend = (expo / expo_sum).astype(jnp.bfloat16)
        mixed[:, pl.ds(pl.multiple_of(n * HD, HD), HD)] = dot(attend, vals, ((1,), (0,))).astype(jnp.bfloat16)
        lane = lax.broadcasted_iota(jnp.int32, (rows, HD), 1)
        total_o[...] = jnp.where(lane == n, top + jnp.log(expo_sum), total_o[...])
        return carry

    total_o[...] = jnp.zeros_like(total_o)
    lax.fori_loop(0, HEADS, head, 0)
    own_go = pltpu.make_async_copy(grad_out, go.at[0], load_sem.at[2])
    own_go.start()
    mixed_back = pltpu.make_async_copy(mixed, mixed_o, back_sem.at[2])
    mixed_back.start()
    relay_pass(17, 21)

    def two_over_z(mask):
        src = big_two.at[block(mask)] if mask else source_two.at[column(0)]
        return remote(src, big_two.at[block(mask)], big_send.at[1], two_recv.at[mask | 2], 2)

    for mask in (3, 7):
        big_pass(mask, 8)
    for mask in (4, 1, 5, 16, 20, 17, 21):
        cut_two(mask).start()
    for n, mask in enumerate((8, 9, 10, 11, 24, 25, 26, 27)):
        ag_pass(2, mask)
        if n % 4 == 3:
            group(2, mask & 24).start()
    group_wait(2)
    proj_back = pltpu.make_async_copy(proj, proj_o, back_sem.at[4])
    proj_back.start()
    out_back = pltpu.make_async_copy(out_w, out_o, back_sem.at[5])
    out_back.start()
    resid = hidden[...].astype(jnp.float32) + dot(mixed[...], out_w[...], ((1,), (1,)))
    resid_o[...] = resid
    factor = lax.rsqrt(jnp.mean(resid * resid, axis=-1, keepdims=True) + norm_eps)
    normed_two_o[...] = (resid * factor * small_o[2:3]).astype(jnp.bfloat16)
    norm_push = remote(normed_two_o, norm_y, norm_sem.at[0], norm_sem.at[1], 16)
    norm_push.start()
    go_push(1).wait_recv()
    go_push(3).start()
    go_core(1).start()
    go_push(2).wait_recv()
    go_core(2).start()
    two_over_z(0).start()
    for mask, passed in ((4, 18), (1, 22), (5, 19), (0, 23)):
        big_pass(passed, 8)
        if mask:
            cut_two(mask).wait_recv()
            two_over_z(mask).start()

    norm_push.wait()
    for mask in (8, 12, 9, 24, 13, 28, 25, 29, 10, 14, 11, 26, 15, 30, 27, 31):
        big_pass(mask)
    go_push(3).wait_recv()
    go_core(3).start()
    for mask in (16, 20, 17, 21):
        cut_two(mask).wait_recv()
    for mask in (0, 4, 1, 5):
        two_over_z(mask).wait_recv()
    own_big.wait()
    own_two.wait()
    own_go.wait()
    drain(big.at[pl.ds(0, 31 * shard)], big_send.at[0])
    drain(big_two.at[pl.ds(0, 11 * shard)], big_send.at[1])

    @pl.when(inner)
    def _():
        drain(relay, big_send.at[2])

    for n in range(3):
        ref, cols = streams[n]
        drain(ref.at[pl.ds(0, 15 * shard), cols], ag_send.at[n])
        for mask in (0, 8, 16, 24):
            group(n, mask).wait_send()
    for o in range(4):
        go_core(o).wait()
    for o in (1, 2, 3):
        go_push(o).wait_send()
    kv_push(0, 2).wait_send()
    kv_push(0, 1).wait_send()
    kv_push(2, 1).wait_send()
    for copy in (query_back, kv_back, mixed_back, proj_back, out_back):
        copy.wait()


def front_call(
    ctx_size, hidden, cosine, sine, pos_q, pos_k, w_query, w_key, w_value, sides, w_out, w_gate, w_up, w_down, grad_out
):
    rows, model = hidden.shape
    shard = w_out.shape[0]
    kv_width = KV_HEADS * HD
    q_width = HEADS * HD
    wide = q_width + 2 * kv_width + HD
    one, two = widths(w_gate.shape[1])
    low, full = jnp.bfloat16, jnp.float32
    vmem = pl.BlockSpec(memory_space=pltpu.VMEM)
    anywhere = pl.BlockSpec(memory_space=pl.ANY)
    shapes = (
        ((rows, model), low, vmem),
        ((HEADS, rows, HD), low, anywhere),
        ((ctx_size, rows, 2 * kv_width), low, anywhere),
        ((rows, HD), full, vmem),
        ((rows, q_width), low, anywhere),
        ((rows, model), full, vmem),
        ((rows, model), low, vmem),
        ((8, model), full, vmem),
        ((model, wide), low, anywhere),
        ((model, q_width), low, anywhere),
        ((model, 3 * one), low, anywhere),
        ((model, 3 * two), low, anywhere),
        ((8, rows, model), low, anywhere),
        ((8, shard, 3 * one), low, anywhere),
        ((model, 2 * kv_width), low, vmem),
        ((rows, model), low, anywhere),
    )
    sem = pltpu.SemaphoreType.DMA
    return pl.pallas_call(
        functools.partial(front_kernel, ctx_size),
        out_shape=tuple(jax.ShapeDtypeStruct(shape, kind) for shape, kind, _ in shapes),
        in_specs=[vmem] * 5 + [anywhere] * 9,
        out_specs=tuple(spec for _, _, spec in shapes),
        scratch_shapes=[
            pltpu.VMEM((model, wide), low),
            pltpu.VMEM((model, q_width), low),
            pltpu.VMEM((8, shard, 3 * one), low),
            pltpu.VMEM((8, shard, 3 * two), low),
            pltpu.VMEM((HEADS, rows, HD), low),
            pltpu.VMEM((ctx_size, rows, 2 * kv_width), low),
            pltpu.VMEM((rows, q_width), low),
            sem((53,)), sem((3,)), sem((3, 32)), sem((3, 4)), sem((3, 4)), sem((3,)), sem((32,)), sem((32,)), sem((8,)),
            sem((7,)), sem((8,)), sem((4,)), sem((4,)), sem((6,)), sem((2,)),
        ],
        compiler_params=pltpu.CompilerParams(
            collective_id=0, has_side_effects=True, vmem_limit_bytes=56 << 20
        ),
        name="front",
    )(hidden, cosine, sine, pos_q, pos_k, w_query, w_key, w_value, sides, w_out, w_gate, w_up, w_down, grad_out)


def back_kernel(
    ctx_size, grad_two, resid, hidden, grad_out, normed, mixed, query, kv, total, cosine, sine, pos_q, pos_k, small, spread,
    proj, out_w, grads, grads_two, near, zin_first, r_part,
    hidden_o, query_o, key_o, outw_o, fin, fin_two, r_in, relay, relay_two,
    weight, turned, left_n, left_a, right_b, right_p, side, side_in, g_b, g_q, g_k,
    y_b, y_q, y_k, x_b, x_q, x_k, p_b, p_q, p_k, h_b, h_q, h_k,
    own, far, zin, own_two, far_two, zin_two, r_mid, r_one, heads_g, lse, dkv, kv_out, kv_p, kv_h, grad_resid,
    load_sem, xs, xr, zs, zr, fs, fr, xs2, xr2, zs2, zr2, fs2, fr2, relay_recv, relay_send, cs, cr, rs, rr, ks, kr, os, orr, keep_sem,
):
    dp = lax.axis_index("dp")
    ctx = lax.axis_index("ctx")
    me = dp * ctx_size + ctx
    y, x, c = dp // 4, (dp // 2) % 2, dp % 2
    h, p = ctx // 2, ctx % 2
    rows, model = resid.shape
    shard = grads.shape[3]
    kv_width = KV_HEADS * HD
    q_width = HEADS * HD
    groups = HEADS // KV_HEADS
    low, full = jnp.bfloat16, jnp.float32
    span = ctx_size * shard

    def at(index):
        return (index // ctx_size, index % ctx_size)

    def remote(src, dst, send, recv, mask):
        return pltpu.make_async_remote_copy(
            src_ref=src, dst_ref=dst, send_sem=send, recv_sem=recv, device_id=at(flip(me, mask)), device_id_type=MESH
        )

    def group_rows(mask):
        return pl.ds(pl.multiple_of(flip(dp, mask // 4) * span, span), span)

    def mask_of(j):
        return (j // 4) * 16 + ((j // 2) % 2) * 4 + j % 2

    barrier = pltpu.get_barrier_semaphore()
    partners = (1, 2, 3, 4, 5, 8, 16, 17, 20, 21)
    for mask in partners:
        pl.semaphore_signal(barrier, inc=1, device_id=at(flip(me, mask)), device_id_type=MESH)
    load_w = pltpu.make_async_copy(out_w, weight.at[:, pl.ds(0, q_width)], load_sem.at[0])
    load_w.start()
    load_own = [
        pltpu.make_async_copy(grads.at[0, 0], own, load_sem.at[1]),
        pltpu.make_async_copy(grads_two.at[0], own_two, load_sem.at[2]),
        pltpu.make_async_copy(zin_first, zin.at[pl.ds(0, 4)], load_sem.at[3]),
        pltpu.make_async_copy(r_part.at[1], r_one, load_sem.at[4]),
    ]
    for copy in load_own:
        copy.start()
    pl.semaphore_wait(barrier, len(partners))

    def far_push(j):
        return remote(grads.at[1, 0, j], far.at[j], xs.at[j], xr.at[j], 8)

    def far_two_push(half, j):
        return remote(grads_two.at[1, half, j], far_two.at[half, j], xs2.at[half, j], xr2.at[half, j], 8)

    def z_push(j):
        return remote(near.at[j], zin.at[j], zs.at[j], zr.at[j], 2)

    def z_two_push(j):
        return remote(far_two.at[1, j], zin_two.at[j], zs2.at[j], zr2.at[j], 2)

    inner = either(h, p) == 1

    def over_z(push, src, to, send, n):
        @pl.when(inner)
        def _():
            push.start()

        @pl.when(jnp.logical_not(inner))
        def _():
            remote(src, to, send, relay_recv.at[n], 1).start()

    def over_z_one(j):
        over_z(z_push(j), near.at[j], relay.at[j - 4], zs.at[j], j)

    def over_z_two(j):
        over_z(z_two_push(j), far_two.at[1, j], relay_two.at[j], zs2.at[j], 8 + j)

    def relay_one(*blocks):
        @pl.when(inner)
        def _():
            for j in blocks:
                part = relay.at[j - 4]
                remote(part, part, relay_send.at[j], relay_recv.at[j], 1).wait_recv()
                remote(part, zin.at[j], relay_send.at[j], zr.at[j], 3).start()

    def relay_two_pass(*blocks):
        @pl.when(inner)
        def _():
            for j in blocks:
                part = relay_two.at[j]
                remote(part, part, relay_send.at[8 + j], relay_recv.at[8 + j], 1).wait_recv()
                remote(part, zin_two.at[j], relay_send.at[8 + j], zr2.at[j], 3).start()

    def fin_push(j):
        return remote(own.at[j], fin.at[j], fs.at[j], fr.at[j], mask_of(j))

    def fin_two_push(j):
        return remote(own_two.at[0, j], fin_two.at[j], fs2.at[j], fr2.at[j], mask_of(j))

    keep_one = pltpu.make_async_copy(own.at[0], fin.at[0], keep_sem.at[0])
    keep_two = pltpu.make_async_copy(own_two.at[0, 0], fin_two.at[0], keep_sem.at[1])

    def z_two_step(j):
        far_two_push(1, j).wait_recv()
        far_two[1, j] = (far_two[1, j].astype(full) + own_two[1, j].astype(full)).astype(low)
        over_z_two(j)

    def total_step(j):
        far_push(j).wait_recv()
        if j > 3:
            z_push(j).wait_recv()
        own[j] = (own[j].astype(full) + far[j].astype(full) + zin[j].astype(full)).astype(low)
        if j:
            fin_push(j).start()
        else:
            keep_one.start()

    def total_two_step(j):
        far_two_push(0, j).wait_recv()
        z_two_push(j).wait_recv()
        own_two[0, j] = (own_two[0, j].astype(full) + far_two[0, j].astype(full) + zin_two[j].astype(full)).astype(low)
        if j:
            fin_two_push(j).start()
        else:
            keep_two.start()

    def r_push(o):
        src = r_one if o == 1 else r_part.at[o]
        dst = r_mid if o == 3 else r_in.at[o - 1]
        return remote(src, dst, os.at[o], orr.at[o], (0, 1, 16, 16)[o])

    r_push(3).start()
    for j in range(4, 8):
        over_z_one(j)
    for j in range(8):
        far_two_push(1, j).start()
    for j in range(8):
        far_push(j).start()

    def transposed(value, left, n):
        turned[n] = jnp.transpose(value)
        for i, mask in enumerate((0, 8, 16, 24)):
            left[i, :, pl.ds(0, rows)] = turned[n, group_rows(mask)]
            cross_left(left, n, i, mask).start()

    def cross_left(left, n, i, mask):
        return remote(turned.at[n, group_rows(mask | 4)], left.at[i, :, pl.ds(rows, rows)], cs.at[n, i], cr.at[n, i], 4)

    def cross(src, dst, n, i):
        return remote(src, dst, cs.at[n, i], cr.at[n, i], 4)

    transposed(normed[...], left_n, 0)
    right_b[pl.ds(0, rows)] = mixed[...]
    cross_mixed = cross(mixed, right_b.at[pl.ds(rows, rows)], 2, 0)
    cross_mixed.start()

    value = resid[...]
    factor = lax.rsqrt(jnp.mean(value * value, axis=-1, keepdims=True) + norm_eps)
    unit = value * factor
    scaled = grad_two[...] * small[2:3]
    ffn_row = jnp.sum(grad_two[...] * unit, axis=0, keepdims=True)
    grad_resid[...] = grad_out[...].astype(full) + factor * (
        scaled - unit * jnp.mean(scaled * unit, axis=-1, keepdims=True)
    )
    grad_attn = grad_resid[...].astype(low)
    transposed(grad_attn, left_a, 1)
    lse[...] = jnp.transpose(total[...])
    signs = jnp.where(lax.broadcasted_iota(jnp.int32, (rows, HD), 1) < HD // 2, 1.0, -1.0)
    sin_back = sine[...] * signs
    key_pos = jnp.transpose(jnp.broadcast_to(pos_k[...], (HD, pos_k.shape[1])).astype(full))[:, :1]
    load_w.wait()
    for half in range(2):
        part = half * (q_width // 2)
        moved = dot(grad_attn, weight[:, part : part + q_width // 2], ((1,), (0,))).astype(low)
        for i in range(HEADS // 2):
            heads_g[half * (HEADS // 2) + i] = moved[:, i * HD : (i + 1) * HD]
    load_p = pltpu.make_async_copy(proj, weight, load_sem.at[0])
    load_p.start()

    streams = ((g_b, y_b, x_b, p_b, h_b), (g_q, y_q, x_q, p_q, h_q), (g_k, y_k, x_k, p_k, h_k))

    def add(ref, other):
        ref[...] = (ref[...].astype(full) + other[...].astype(full)).astype(low)

    def y_push(s, k):
        g, yy = streams[s][:2]
        return remote(g.at[2 + k], yy.at[k], rs.at[s, k], rr.at[s, k], 16)

    def x_push(s):
        g, xx = streams[s][0], streams[s][2]
        return remote(g.at[1], xx, rs.at[s, 2], rr.at[s, 2], 8)

    def block_of(hr, other):
        z = 2 * either(h, hr) + either(p, other)
        return pl.ds(pl.multiple_of(z * shard, shard), shard)

    def p_push(s, hr):
        g, pp = streams[s][0], streams[s][3]
        return remote(g.at[0, block_of(hr, 1)], pp.at[hr], rs.at[s, 3 + hr], rr.at[s, 3 + hr], 1)

    def h_push(s):
        g, hh = streams[s][0], streams[s][4]
        return remote(g.at[0, block_of(1, 0)], hh, rs.at[s, 5], rr.at[s, 5], 2)

    def y_pass(s):
        g, yy = streams[s][:2]
        y_push(s, 1).wait_recv()
        add(g.at[1], yy.at[1])
        x_push(s).start()
        y_push(s, 0).wait_recv()
        add(g.at[0], yy.at[0])

    def x_pass(s):
        x_push(s).wait_recv()
        add(streams[s][0].at[0], streams[s][2])
        p_push(s, 1).start()
        p_push(s, 0).start()

    def p_pass(s):
        g, pp = streams[s][0], streams[s][3]
        p_push(s, 1).wait_recv()
        add(g.at[0, block_of(1, 0)], pp.at[1])
        h_push(s).start()
        p_push(s, 0).wait_recv()
        add(g.at[0, block_of(0, 0)], pp.at[0])

    def h_pass(s, out):
        h_push(s).wait_recv()
        out[...] = streams[s][0][0, block_of(0, 0)].astype(full) + streams[s][4][...].astype(full)

    for i, mask in enumerate((0, 8, 16, 24)):
        cross_left(left_a, 1, i, mask).wait_recv()
    cross_mixed.wait_recv()
    for i in (3, 2, 1, 0):
        g_b[i] = dot(left_a[i], right_b[...], ((1,), (0,))).astype(low)
    y_push(0, 1).start()

    def head(n, carry):
        g = n // groups
        k_cols = pl.ds(pl.multiple_of(g * HD, HD), HD)
        v_cols = pl.ds(pl.multiple_of(kv_width + g * HD, HD), HD)
        keys = kv[:, :, k_cols].reshape(ctx_size * rows, HD)
        vals = kv[:, :, v_cols].reshape(ctx_size * rows, HD)
        scores = dot(keys, query[n], ((1,), (1,))) * HD ** (-0.5)
        scores = jnp.where(key_pos <= pos_q[...].astype(full), scores, masked_fill)
        attend = jnp.exp(scores - lse[pl.ds(n, 1), :])
        grad_attend = dot(vals, heads_g[n], ((1,), (1,)))
        delta = jnp.sum(grad_attend * attend, axis=0, keepdims=True)
        grad_scores = (attend * (grad_attend - delta)).astype(low)
        dkv[:, k_cols] += dot(grad_scores, query[n], ((1,), (0,)))
        dkv[:, v_cols] += dot(attend.astype(low), heads_g[n], ((1,), (0,)))
        back = dot(grad_scores, keys, ((0,), (0,))) * HD ** (-0.5)
        back = turn(back, cosine[...], sin_back).astype(low)
        right_p[pl.ds(0, rows), pl.ds(pl.multiple_of(n * HD, HD), HD)] = back
        return carry

    dkv[...] = jnp.zeros_like(dkv)
    lax.fori_loop(0, HEADS // 2, head, 0)
    relay_one(4, 5)
    lax.fori_loop(HEADS // 2, HEADS, head, 0)

    for z in range(ctx_size):
        part = dkv[pl.ds(z * rows, rows)]
        kv_out[z, :, pl.ds(0, kv_width)] = (part[:, :kv_width] * HD ** (-0.5)).astype(low)
        kv_out[z, :, pl.ds(kv_width, kv_width)] = part[:, kv_width:].astype(low)

    def kv_push(hr):
        return remote(kv_out.at[2 * either(h, hr) + 1 - p], kv_p.at[hr], ks.at[hr], kr.at[hr], 1)

    def kv_cross():
        return remote(kv_out.at[2 * (1 - h) + p], kv_h, ks.at[2], kr.at[2], 2)

    kv_push(1).start()
    kv_push(0).start()
    cross_q = cross(
        right_p.at[pl.ds(0, rows), pl.ds(0, q_width)], right_p.at[pl.ds(rows, rows), pl.ds(0, q_width)], 2, 1
    )
    cross_q.start()
    for copy in load_own:
        copy.wait()
    for i, mask in enumerate((0, 8, 16, 24)):
        cross_left(left_n, 0, i, mask).wait_recv()
    cross_q.wait_recv()
    for i in (3, 2, 1, 0):
        g_q[i] = dot(left_n[i], right_p[:, pl.ds(0, q_width)], ((1,), (0,))).astype(low)
        if i > 1:
            y_push(1, i - 2).start()
    load_p.wait()
    hidden_o[...] = dot(right_p[pl.ds(0, rows), pl.ds(0, q_width)], weight[:, pl.ds(0, q_width)], ((1,), (1,)))
    kv_push(1).wait_recv()
    add(kv_out.at[2 * (1 - h) + p], kv_p.at[1])
    kv_cross().start()
    kv_push(0).wait_recv()
    add(kv_out.at[2 * h + p], kv_p.at[0])
    relay_one(6, 7)
    for j in range(8):
        z_two_step(j)
    for j in range(4):
        total_step(j)
    relay_two_pass(0, 1, 2)
    kv_cross().wait_recv()
    final = kv_out[2 * h + p].astype(full) + kv_h[...].astype(full)
    for g in range(KV_HEADS):
        right_p[pl.ds(0, rows), pl.ds(q_width + g * HD, HD)] = turn(
            final[:, g * HD : (g + 1) * HD], cosine[...], sin_back
        ).astype(low)
    right_p[pl.ds(0, rows), pl.ds(q_width + kv_width, kv_width)] = final[:, kv_width:].astype(low)
    cross_kv = cross(
        right_p.at[pl.ds(0, rows), pl.ds(q_width, 2 * kv_width)],
        right_p.at[pl.ds(rows, rows), pl.ds(q_width, 2 * kv_width)], 2, 2,
    )
    cross_kv.start()
    grad_one = hidden_o[...] + dot(
        right_p[pl.ds(0, rows), pl.ds(q_width, 2 * kv_width)], weight[:, pl.ds(q_width, 2 * kv_width)], ((1,), (1,))
    )
    value = hidden[...].astype(full)
    factor = lax.rsqrt(jnp.mean(value * value, axis=-1, keepdims=True) + norm_eps)
    unit = value * factor
    scaled = grad_one * small[0:1]
    attn_row = jnp.sum(grad_one * unit, axis=0, keepdims=True)
    hidden_o[...] = grad_resid[...] + factor * (scaled - unit * jnp.mean(scaled * unit, axis=-1, keepdims=True))
    bias = jnp.sum(right_p[pl.ds(0, rows)].astype(full), axis=0, keepdims=True)
    kv_bias = jnp.broadcast_to(bias[:, q_width:], (8, 2 * kv_width)).astype(low)
    kv_row = dot(kv_bias, spread[...], ((1,), (1,)))[:1]
    table = jnp.concatenate([attn_row, bias[:, :q_width], ffn_row, kv_row, jnp.zeros((124, model), full)], axis=0)
    side[...] = jnp.transpose(table).astype(low)

    def cross_side(i, mask):
        return cross(side.at[group_rows(mask | 4)], side_in.at[i], 3, i)

    for i, mask in enumerate((0, 8, 16, 24)):
        cross_side(i, mask).start()
    cross_kv.wait_recv()
    for i, mask in ((3, 24), (2, 16), (1, 8), (0, 0)):
        g_k[i, :, pl.ds(0, 2 * kv_width)] = dot(
            left_n[i], right_p[:, pl.ds(q_width, 2 * kv_width)], ((1,), (0,))
        ).astype(low)
        cross_side(i, mask).wait_recv()
        g_k[i, :, pl.ds(2 * kv_width, HD)] = (
            side[group_rows(mask)].astype(full) + side_in[i].astype(full)
        ).astype(low)
        if i > 1:
            y_push(2, i - 2).start()
    y_push(0, 0).start()
    r_push(3).wait_recv()
    add(r_one, r_mid)
    r_push(1).start()
    relay_two_pass(3, 4, 5, 6, 7)
    for j in range(4, 8):
        total_step(j)
    y_pass(1)
    y_pass(2)
    for j in range(8):
        far_two_push(0, j).start()
    y_pass(0)
    x_pass(1)
    x_pass(2)
    r_push(2).start()
    p_pass(1)
    p_pass(2)
    for j in range(8):
        total_two_step(j)
    x_pass(0)
    p_pass(0)
    h_pass(1, query_o)
    h_pass(2, key_o)
    h_pass(0, outw_o)
    for j in range(1, 8):
        fin_push(j).wait_recv()
        fin_two_push(j).wait_recv()
    for o in (1, 2):
        r_push(o).wait()
    r_push(3).wait_send()
    keep_one.wait()
    keep_two.wait()

    for j in range(8):
        far_push(j).wait_send()
        far_two_push(0, j).wait_send()
        far_two_push(1, j).wait_send()
        if j > 3:
            z_push(j).wait_send()
        z_two_push(j).wait_send()
        if j:
            fin_push(j).wait_send()
            fin_two_push(j).wait_send()
    @pl.when(inner)
    def _():
        for j in range(4, 8):
            remote(relay.at[j - 4], relay.at[j - 4], relay_send.at[j], relay_recv.at[j], 1).wait_send()
        for j in range(8):
            remote(relay_two.at[j], relay_two.at[j], relay_send.at[8 + j], relay_recv.at[8 + j], 1).wait_send()

    for i, mask in enumerate((0, 8, 16, 24)):
        cross_left(left_n, 0, i, mask).wait_send()
        cross_left(left_a, 1, i, mask).wait_send()
        cross_side(i, mask).wait_send()
    for copy in (cross_mixed, cross_q, cross_kv):
        copy.wait_send()
    for s in range(3):
        for k in range(2):
            y_push(s, k).wait_send()
            p_push(s, k).wait_send()
        x_push(s).wait_send()
        h_push(s).wait_send()
    kv_push(0).wait_send()
    kv_push(1).wait_send()
    kv_cross().wait_send()


def back_call(
    ctx_size, grad_two, resid, hidden, grad_out, normed, mixed, query, kv, total, cosine, sine, pos_q, pos_k,
    small, spread, proj, out_w, grads, grads_two, near, zin_first, r_part,
):
    rows, model = resid.shape
    shard = grads.shape[3]
    one, two = grads.shape[4] // 3, grads_two.shape[4] // 3
    kv_width = KV_HEADS * HD
    q_width = HEADS * HD
    k_cols = 2 * kv_width + HD
    span = ctx_size * shard
    low, full = jnp.bfloat16, jnp.float32
    vmem = pl.BlockSpec(memory_space=pltpu.VMEM)
    anywhere = pl.BlockSpec(memory_space=pl.ANY)
    shapes = (
        ((rows, model), vmem, full),
        ((shard, q_width), vmem, full),
        ((shard, k_cols), vmem, full),
        ((shard, q_width), vmem, full),
        ((8, shard, 3 * one), anywhere, low),
        ((8, shard, 3 * two), anywhere, low),
        ((2, rows, model), anywhere, low),
        ((4, shard, 3 * one), anywhere, low),
        ((8, shard, 3 * two), anywhere, low),
    )
    sem = pltpu.SemaphoreType.DMA
    cols = (q_width, q_width, k_cols)

    def each(*lead):
        return [pltpu.VMEM(lead + (n,), low) for n in cols]

    return pl.pallas_call(
        functools.partial(back_kernel, ctx_size),
        out_shape=tuple(jax.ShapeDtypeStruct(shape, kind) for shape, _, kind in shapes),
        in_specs=[vmem] * 15 + [anywhere] * 7,
        out_specs=tuple(spec for _, spec, _ in shapes),
        scratch_shapes=[
            pltpu.VMEM(proj.shape, low),
            pltpu.VMEM((2, model, rows), low),
            pltpu.VMEM((4, span, 2 * rows), low),
            pltpu.VMEM((4, span, 2 * rows), low),
            pltpu.VMEM((2 * rows, q_width), low),
            pltpu.VMEM((2 * rows, q_width + 2 * kv_width), low),
            pltpu.VMEM((model, HD), low),
            pltpu.VMEM((4, span, HD), low),
            *each(4, span),
            *each(2, span),
            *each(span),
            *each(2, shard),
            *each(shard),
            *([pltpu.VMEM((8, shard, 3 * one), low)] * 3),
            *([pltpu.VMEM((2, 8, shard, 3 * two), low)] * 2),
            pltpu.VMEM((8, shard, 3 * two), low),
            *([pltpu.VMEM((rows, model), low)] * 2),
            pltpu.VMEM((HEADS, rows, HD), low),
            pltpu.VMEM((HD, rows), full),
            pltpu.VMEM((ctx_size * rows, 2 * kv_width), full),
            pltpu.VMEM((ctx_size, rows, 2 * kv_width), low),
            pltpu.VMEM((2, rows, 2 * kv_width), low),
            pltpu.VMEM((rows, 2 * kv_width), low),
            pltpu.VMEM((rows, model), full),
            sem((5,)), *([sem((8,))] * 6), *([sem((2, 8))] * 2), *([sem((8,))] * 4), sem((16,)), sem((16,)),
            sem((4, 4)), sem((4, 4)), sem((3, 6)), sem((3, 6)), sem((3,)), sem((3,)), sem((4,)), sem((4,)), sem((2,)),
        ],
        compiler_params=pltpu.CompilerParams(
            collective_id=2, has_side_effects=True, vmem_limit_bytes=63 << 20
        ),
        name="back",
    )(
        grad_two, resid, hidden, grad_out, normed, mixed, query, kv, total, cosine, sine, pos_q, pos_k, small, spread,
        proj, out_w, grads, grads_two, near, zin_first, r_part,
    )


def finish_kernel(
    ctx_size, fin, fin_two, key, resid, r_part, r_in, hidden, query, outw,
    result_o, hidden_o, attn_o, query_o, bias_q, key_o, bias_k, value_o, bias_v, outw_o, ffn_o, gate_o, up_o, down_o,
    one_v, two_v, tiles, sems,
):
    dp = lax.axis_index("dp")
    ctx = lax.axis_index("ctx")
    y, c, p = dp // 4, dp % 2, ctx % 2
    full = jnp.float32
    rows, model = resid.shape
    shard = key.shape[0]
    one, two = fin.shape[2] // 3, fin_two.shape[2] // 3
    width = one + two
    kv_width = key_o.shape[1]
    per = bias_k.shape[1]
    moves = [
        pltpu.make_async_copy(fin, one_v, sems.at[0]),
        pltpu.make_async_copy(fin_two, two_v, sems.at[1]),
        pltpu.make_async_copy(r_part.at[0], tiles.at[0], sems.at[2]),
        pltpu.make_async_copy(r_in, tiles.at[pl.ds(1, 2)], sems.at[3]),
    ]
    for copy in moves:
        copy.start()
    hidden_o[...] = hidden[...]
    query_o[...] = query[...]
    outw_o[...] = outw[...]
    key_o[...] = key[:, :kv_width]
    value_o[...] = key[:, kv_width : 2 * kv_width]
    side = jnp.transpose(key[:, 2 * kv_width :])
    attn_o[...] = side[0:1]
    bias_q[...] = side[1:2]
    ffn_o[...] = side[2:3]
    bias_k[...] = side[3:4, :per]
    bias_v[...] = side[3:4, per : 2 * per]
    moves[0].wait()
    moves[1].wait()
    last = gate_o.shape[1] - 7 * width - one
    for j in range(8):
        k = either(y, j // 4) * 4 + either(p, j % 2) * 2 + either(c, (j // 2) % 2)
        for n, out in enumerate((gate_o, up_o, down_o)):
            at = pl.multiple_of(k * width, HD)
            out[:, pl.ds(at, one)] = one_v[j, :, n * one : (n + 1) * one].astype(full)

            @pl.when(k < 7)
            def _():
                out[:, pl.ds(at + one, two)] = two_v[j, :, n * two : (n + 1) * two].astype(full)

            @pl.when(k == 7)
            def _():
                out[:, pl.ds(7 * width + one, last)] = two_v[j, :, n * two : n * two + last].astype(full)

    moves[2].wait()
    moves[3].wait()
    value = resid[...]
    for o in range(3):
        value = value + tiles[o].astype(full)
    result_o[...] = value.astype(result_o.dtype)


def finish_call(ctx_size, hidden_units, per, fin, fin_two, key, resid, r_part, r_in, hidden, query, outw):
    rows, model = resid.shape
    shard = key.shape[0]
    kv_width = KV_HEADS * HD
    low, full = jnp.bfloat16, jnp.float32
    vmem = pl.BlockSpec(memory_space=pltpu.VMEM)
    anywhere = pl.BlockSpec(memory_space=pl.ANY)
    shapes = (
        ((rows, model), low, vmem),
        ((rows, model), full, vmem),
        ((1, shard), full, vmem),
        (query.shape, full, vmem),
        ((1, shard), full, vmem),
        ((shard, kv_width), full, vmem),
        ((1, per), full, vmem),
        ((shard, kv_width), full, vmem),
        ((1, per), full, vmem),
        (outw.shape, full, vmem),
        ((1, shard), full, vmem),
        ((shard, hidden_units), full, vmem),
        ((shard, hidden_units), full, vmem),
        ((shard, hidden_units), full, vmem),
    )
    return pl.pallas_call(
        functools.partial(finish_kernel, ctx_size),
        out_shape=tuple(jax.ShapeDtypeStruct(shape, kind) for shape, kind, _ in shapes),
        in_specs=[anywhere, anywhere, vmem, vmem, anywhere, anywhere] + [vmem] * 3,
        out_specs=tuple(spec for _, _, spec in shapes),
        scratch_shapes=[
            pltpu.VMEM(fin.shape, low),
            pltpu.VMEM(fin_two.shape, low),
            pltpu.VMEM((3, rows, model), low),
            pltpu.SemaphoreType.DMA((4,)),
        ],
        compiler_params=pltpu.CompilerParams(vmem_limit_bytes=63 << 20),
        name="finish",
    )(fin, fin_two, key, resid, r_part, r_in, hidden, query, outw)


def fits(mesh):
    return mesh.shape["dp"] == 8 and mesh.shape["ctx"] == 4


def fast_device(
    hidden,
    cotangent,
    span_order,
    attn_gain,
    w_query,
    b_query,
    w_key,
    b_key,
    w_value,
    b_value,
    w_out,
    ffn_gain,
    w_gate,
    w_up,
    w_down,
):
    ctx_size = lax.axis_size("ctx")
    ctx_rank = lax.axis_index("ctx")
    batches = hidden.shape[0]
    length = hidden.shape[1]
    span_len = length // 2
    seq_len = length * ctx_size
    row_count = batches * length
    shard_rows = w_query.shape[0]
    kv_width = KV_HEADS * HD
    q_width = HEADS * HD

    grad_out = cotangent.reshape(row_count, D)
    places = jnp.arange(seq_len, dtype=jnp.int32)
    every_pos = jnp.repeat(span_order, span_len, axis=1) * span_len + places[None, :] % span_len
    local_pos = lax.dynamic_slice_in_dim(every_pos, ctx_rank * length, length, 1)
    freqs = rope_base ** (-((jnp.arange(HD) % (HD // 2)).astype(jnp.float32) * 2.0 / HD))
    angles = local_pos.reshape(row_count, 1).astype(jnp.float32) * freqs[None, :]
    cosine, sine = jnp.cos(angles), jnp.sin(angles)

    per = b_key.shape[0]
    pair = jnp.pad(jnp.concatenate([b_key, b_value]), (0, shard_rows - 2 * per))
    sides = jnp.pad(jnp.stack([attn_gain, b_query, ffn_gain, pair]), ((0, HD - 4), (0, 0))).T
    source = hidden.reshape(row_count, D)
    normed, query_heads, key_value, log_total, mixed, resid, normed_two, small, proj_full, out_full, big, big_two, go_all, _, spread, norm_y = front_call(
        ctx_size, source, cosine, sine, local_pos, every_pos, w_query, w_key, w_value, sides, w_out, w_gate, w_up,
        w_down, grad_out,
    )
    grad_two, r_part, grads, grads_two, near, zin, *_ = ffn_call(ctx_size, shard_rows, normed_two, norm_y, go_all, big, big_two)
    hidden_back, query_sum, kv_sum, out_sum, fin, fin_two, r_in, *_ = back_call(
        ctx_size, grad_two, resid, source, grad_out, normed, mixed, query_heads, key_value, log_total,
        cosine, sine, local_pos, every_pos, small, spread,
        proj_full, out_full, grads, grads_two, near, zin, r_part,
    )
    (
        result, hidden_grad, attn_gain_grad, w_query_grad, b_query_grad, w_key_grad, b_key_grad, w_value_grad,
        b_value_grad, w_out_grad, ffn_gain_grad, w_gate_grad, w_up_grad, w_down_grad,
    ) = finish_call(
        ctx_size, w_gate.shape[1], per, fin, fin_two, kv_sum, resid, r_part, r_in, hidden_back, query_sum, out_sum
    )
    return (
        result.reshape(batches, length, D),
        hidden_grad.reshape(batches, length, D),
        attn_gain_grad.reshape(shard_rows),
        w_query_grad,
        b_query_grad.reshape(shard_rows),
        w_key_grad,
        b_key_grad.reshape(per),
        w_value_grad,
        b_value_grad.reshape(per),
        w_out_grad,
        ffn_gain_grad.reshape(shard_rows),
        w_gate_grad,
        w_up_grad,
        w_down_grad,
    )


def general_device(
    hidden,
    cotangent,
    span_order,
    attn_gain,
    w_query,
    b_query,
    w_key,
    b_key,
    w_value,
    b_value,
    w_out,
    ffn_gain,
    w_gate,
    w_up,
    w_down,
):
    ctx_size = lax.axis_size("ctx")
    ctx_rank = lax.axis_index("ctx")
    batches = hidden.shape[0]
    length = hidden.shape[1]
    span_len = length // 2
    seq_len = length * ctx_size
    row_count = batches * length
    groups = HEADS // KV_HEADS
    shard_rows = w_query.shape[0]
    head_scale = HD ** (-0.5)
    kv_width = KV_HEADS * HD
    q_width = HEADS * HD
    places = jnp.arange(seq_len, dtype=jnp.int32)
    every_pos = jnp.repeat(span_order, span_len, axis=1) * span_len + places[None, :] % span_len
    local_pos = lax.dynamic_slice_in_dim(every_pos, ctx_rank * length, length, 1)
    cosine, sine = angles_for(local_pos.reshape(row_count), HD)
    allowed = (every_pos[:, None, :] <= local_pos[:, :, None])[:, None, None]
    attn_full = (
        lax.all_gather(attn_gain, ("dp", "ctx"), axis=0, tiled=True),
        lax.all_gather(w_query, ("dp", "ctx"), axis=0, tiled=True),
        lax.all_gather(w_key, ("dp", "ctx"), axis=0, tiled=True),
        lax.all_gather(w_value, ("dp", "ctx"), axis=0, tiled=True),
        lax.all_gather(w_out, ("dp", "ctx"), axis=0, tiled=True),
        lax.all_gather(b_query, ("dp", "ctx"), axis=0, tiled=True),
        lax.all_gather(b_key, ("dp", "ctx"), axis=0, tiled=True),
        lax.all_gather(b_value, ("dp", "ctx"), axis=0, tiled=True),
    )
    gain_one = attn_full[0].astype(jnp.float32)
    source = hidden.reshape(row_count, D).astype(jnp.float32)
    attn_factor, normed = norm_forward(source, gain_one)
    query_raw = plain_dot(normed, attn_full[1]) + attn_full[5].astype(jnp.float32)
    key_raw = plain_dot(normed, attn_full[2]) + attn_full[6].astype(jnp.float32)
    value_low = (plain_dot(normed, attn_full[3]) + attn_full[7].astype(jnp.float32)).astype(
        jnp.bfloat16
    )
    query_rot = rotate(query_raw.reshape(row_count, HEADS, HD), cosine, sine).astype(jnp.bfloat16)
    query_rot = query_rot.reshape(batches, length, KV_HEADS, groups, HD)
    key_rot = rotate(key_raw.reshape(row_count, KV_HEADS, HD), cosine, sine).astype(jnp.bfloat16)
    key_rot = key_rot.reshape(batches, length, kv_width)
    key_all, value_all = (
        lax.all_gather(key_rot, "ctx", axis=1, tiled=True),
        lax.all_gather(value_low.reshape(batches, length, kv_width), "ctx", axis=1, tiled=True),
    )
    key_all = key_all.reshape(batches, seq_len, KV_HEADS, HD)
    value_all = value_all.reshape(batches, seq_len, KV_HEADS, HD)
    scores = (
        jnp.einsum("bqkgd,bskd->bkgqs", query_rot, key_all, preferred_element_type=jnp.float32)
        * head_scale
    )
    masked = jnp.where(allowed, scores, masked_fill)
    row_max = jnp.max(masked, axis=-1, keepdims=True)
    expo = jnp.exp(masked - row_max)
    expo_sum = jnp.sum(expo, axis=-1, keepdims=True)
    log_total = row_max + jnp.log(expo_sum)
    attend = (expo / expo_sum).astype(jnp.bfloat16)
    mixed = jnp.einsum("bkgqs,bskd->bqkgd", attend, value_all, preferred_element_type=jnp.float32)
    mixed = mixed.reshape(row_count, q_width).astype(jnp.bfloat16)
    resid = source + right_dot(mixed, attn_full[4])
    ffn_full = (
        lax.all_gather(ffn_gain, ("dp", "ctx"), axis=0, tiled=True),
        lax.all_gather(w_gate, ("dp", "ctx"), axis=0, tiled=True),
        lax.all_gather(w_up, ("dp", "ctx"), axis=0, tiled=True),
        lax.all_gather(w_down, ("dp", "ctx"), axis=0, tiled=True),
    )
    gain_two = ffn_full[0].astype(jnp.float32)
    ffn_factor, normed_two = norm_forward(resid, gain_two)
    gate_pre = plain_dot(normed_two, ffn_full[1])
    up_pre = plain_dot(normed_two, ffn_full[2])
    sigmoid_gate = jax.nn.sigmoid(gate_pre)
    silu_gate = gate_pre * sigmoid_gate
    act = (silu_gate * up_pre).astype(jnp.bfloat16)
    output = resid + right_dot(act, ffn_full[3])
    result = output.astype(jnp.bfloat16).reshape(batches, length, D)
    ffn_back = (
        lax.all_gather(ffn_gain, ("dp", "ctx"), axis=0, tiled=True),
        lax.all_gather(w_gate, ("dp", "ctx"), axis=0, tiled=True),
        lax.all_gather(w_up, ("dp", "ctx"), axis=0, tiled=True),
        lax.all_gather(w_down, ("dp", "ctx"), axis=0, tiled=True),
    )
    grad_out = cotangent.reshape(row_count, D)
    grad_plain = grad_out.astype(jnp.float32)
    grad_act = plain_dot(grad_out, ffn_back[3])
    grad_gate = (grad_act * up_pre * sigmoid_gate * (1.0 + gate_pre * (1.0 - sigmoid_gate))).astype(
        jnp.bfloat16
    )
    grad_up = (grad_act * silu_gate).astype(jnp.bfloat16)
    pieces = (
        lax.all_gather(normed_two, "ctx", axis=0, tiled=True),
        lax.all_gather(grad_gate, "ctx", axis=0, tiled=True),
        lax.all_gather(grad_up, "ctx", axis=0, tiled=True),
        lax.all_gather(act, "ctx", axis=0, tiled=True),
        lax.all_gather(grad_out, "ctx", axis=0, tiled=True),
    )
    picked_in = owned_columns(pieces[0], ctx_size, ctx_rank, shard_rows)
    picked_out = owned_columns(pieces[4], ctx_size, ctx_rank, shard_rows)
    w_gate_grad, w_up_grad, w_down_grad = (
        lax.psum_scatter(
            outer_add(picked_in, pieces[1]).astype(jnp.bfloat16),
            "dp",
            scatter_dimension=0,
            tiled=True,
        ).astype(jnp.float32),
        lax.psum_scatter(
            outer_add(picked_in, pieces[2]).astype(jnp.bfloat16),
            "dp",
            scatter_dimension=0,
            tiled=True,
        ).astype(jnp.float32),
        lax.psum_scatter(
            outer_add(picked_out, pieces[3]).astype(jnp.bfloat16),
            "dp",
            scatter_dimension=0,
            tiled=True,
        ).astype(jnp.float32),
    )
    grad_norm_two = right_dot(grad_gate, ffn_back[1]) + right_dot(grad_up, ffn_back[2])
    resid_back, ffn_gain_part = norm_backward(resid, ffn_factor, gain_two, grad_norm_two)
    grad_resid = grad_plain + resid_back
    attn_back = (
        lax.all_gather(attn_gain, ("dp", "ctx"), axis=0, tiled=True),
        lax.all_gather(w_query, ("dp", "ctx"), axis=0, tiled=True),
        lax.all_gather(w_key, ("dp", "ctx"), axis=0, tiled=True),
        lax.all_gather(w_value, ("dp", "ctx"), axis=0, tiled=True),
        lax.all_gather(w_out, ("dp", "ctx"), axis=0, tiled=True),
        lax.all_gather(b_query, ("dp", "ctx"), axis=0, tiled=True),
        lax.all_gather(b_key, ("dp", "ctx"), axis=0, tiled=True),
        lax.all_gather(b_value, ("dp", "ctx"), axis=0, tiled=True),
    )
    grad_attn = grad_resid.astype(jnp.bfloat16)
    grad_mixed = plain_dot(grad_attn, attn_back[4]).astype(jnp.bfloat16)
    grad_mixed = grad_mixed.reshape(batches, length, KV_HEADS, groups, HD)
    scores = (
        jnp.einsum("bqkgd,bskd->bkgqs", query_rot, key_all, preferred_element_type=jnp.float32)
        * head_scale
    )
    masked = jnp.where(allowed, scores, masked_fill)
    attend_full = jnp.exp(masked - log_total)
    attend = attend_full.astype(jnp.bfloat16)
    grad_attend = jnp.einsum(
        "bqkgd,bskd->bkgqs", grad_mixed, value_all, preferred_element_type=jnp.float32
    )
    value_grad_all = jnp.einsum(
        "bkgqs,bqkgd->bskd", attend, grad_mixed, preferred_element_type=jnp.float32
    )
    delta = jnp.sum(grad_attend * attend_full, axis=-1, keepdims=True)
    grad_scores = (attend_full * (grad_attend - delta)).astype(jnp.bfloat16)
    query_grad_rot = (
        jnp.einsum("bkgqs,bskd->bqkgd", grad_scores, key_all, preferred_element_type=jnp.float32)
        * head_scale
    )
    key_grad_all = (
        jnp.einsum("bkgqs,bqkgd->bskd", grad_scores, query_rot, preferred_element_type=jnp.float32)
        * head_scale
    )
    key_grad_rot, value_grad = (
        lax.psum_scatter(
            key_grad_all.reshape(batches, seq_len, kv_width), "ctx", scatter_dimension=1, tiled=True
        ),
        lax.psum_scatter(
            value_grad_all.reshape(batches, seq_len, kv_width),
            "ctx",
            scatter_dimension=1,
            tiled=True,
        ),
    )
    query_grad = (
        rotate_back(query_grad_rot.reshape(row_count, HEADS, HD), cosine, sine)
        .reshape(row_count, q_width)
        .astype(jnp.bfloat16)
    )
    key_grad = (
        rotate_back(key_grad_rot.reshape(row_count, KV_HEADS, HD), cosine, sine)
        .reshape(row_count, kv_width)
        .astype(jnp.bfloat16)
    )
    value_grad = value_grad.reshape(row_count, kv_width).astype(jnp.bfloat16)
    proj_grad = jnp.concatenate([query_grad, key_grad, value_grad], axis=1)
    pieces = (
        lax.all_gather(normed, "ctx", axis=0, tiled=True),
        lax.all_gather(proj_grad, "ctx", axis=0, tiled=True),
        lax.all_gather(grad_attn, "ctx", axis=0, tiled=True),
        lax.all_gather(mixed, "ctx", axis=0, tiled=True),
    )
    picked_in = owned_columns(pieces[0], ctx_size, ctx_rank, shard_rows)
    picked_out = owned_columns(pieces[2], ctx_size, ctx_rank, shard_rows)
    proj_sum, w_out_grad = (
        lax.psum_scatter(
            outer_add(picked_in, pieces[1]).astype(jnp.bfloat16),
            "dp",
            scatter_dimension=0,
            tiled=True,
        ).astype(jnp.float32),
        lax.psum_scatter(
            outer_add(picked_out, pieces[3]).astype(jnp.bfloat16),
            "dp",
            scatter_dimension=0,
            tiled=True,
        ).astype(jnp.float32),
    )
    grad_norm_one = (
        right_dot(query_grad, attn_back[1])
        + right_dot(key_grad, attn_back[2])
        + right_dot(value_grad, attn_back[3])
    )
    source_back, attn_gain_part = norm_backward(source, attn_factor, gain_one, grad_norm_one)
    hidden_grad = (grad_resid + source_back).reshape(batches, length, D)
    query_bias_part = jnp.sum(query_grad.astype(jnp.float32), axis=0)
    key_bias_part = jnp.sum(key_grad.astype(jnp.float32), axis=0)
    value_bias_part = jnp.sum(value_grad.astype(jnp.float32), axis=0)
    small_sums = (
        lax.psum_scatter(attn_gain_part, ("dp", "ctx"), scatter_dimension=0, tiled=True),
        lax.psum_scatter(query_bias_part, ("dp", "ctx"), scatter_dimension=0, tiled=True),
        lax.psum_scatter(key_bias_part, ("dp", "ctx"), scatter_dimension=0, tiled=True),
        lax.psum_scatter(value_bias_part, ("dp", "ctx"), scatter_dimension=0, tiled=True),
        lax.psum_scatter(ffn_gain_part, ("dp", "ctx"), scatter_dimension=0, tiled=True),
    )
    w_query_grad = proj_sum[:, :q_width]
    w_key_grad = proj_sum[:, q_width : q_width + kv_width]
    w_value_grad = proj_sum[:, q_width + kv_width :]
    return (
        result,
        hidden_grad,
        small_sums[0],
        w_query_grad,
        small_sums[1],
        w_key_grad,
        small_sums[2],
        w_value_grad,
        small_sums[3],
        w_out_grad,
        small_sums[4],
        w_gate_grad,
        w_up_grad,
        w_down_grad,
    )


def solution(mesh):
    placed = (
        P("dp", "ctx", None),
        P("dp", "ctx", None),
        P("dp", None),
        P(("dp", "ctx")),
        P(("dp", "ctx"), None),
        P(("dp", "ctx")),
        P(("dp", "ctx"), None),
        P(("dp", "ctx")),
        P(("dp", "ctx"), None),
        P(("dp", "ctx")),
        P(("dp", "ctx"), None),
        P(("dp", "ctx")),
        P(("dp", "ctx"), None),
        P(("dp", "ctx"), None),
        P(("dp", "ctx"), None),
    )
    return jax.shard_map(
        fast_device if fits(mesh) else general_device,
        mesh=mesh,
        in_specs=placed,
        out_specs=(
            P("dp", "ctx", None),
            P("dp", "ctx", None),
            P(("dp", "ctx")),
            P(("dp", "ctx"), None),
            P(("dp", "ctx")),
            P(("dp", "ctx"), None),
            P(("dp", "ctx")),
            P(("dp", "ctx"), None),
            P(("dp", "ctx")),
            P(("dp", "ctx"), None),
            P(("dp", "ctx")),
            P(("dp", "ctx"), None),
            P(("dp", "ctx"), None),
            P(("dp", "ctx"), None),
        ),
        check_vma=False,
    )
```

```python
import functools
import math

import jax
import jax.numpy as jnp
from jax import lax
from jax.experimental import pallas as pl
from jax.experimental.pallas import tpu as pltpu
from jax.sharding import PartitionSpec as P

D = 1536
HEADS = 12
KV_HEADS = 2
HD = 128


norm_eps = 1e-06
rope_base = 10000.0
masked_fill = -1e30


def angles_for(places, width):
    half = width // 2
    freqs = rope_base ** (-(jnp.arange(half, dtype=jnp.float32) * 2.0 / width))
    angles = places.astype(jnp.float32)[:, None] * freqs[None, :]
    return (jnp.cos(angles)[:, None, :], jnp.sin(angles)[:, None, :])


def rotate(values, cosine, sine):
    half = values.shape[-1] // 2
    first = values[..., :half]
    second = values[..., half:]
    return jnp.concatenate(
        [first * cosine - second * sine, second * cosine + first * sine], axis=-1
    )


def rotate_back(values, cosine, sine):
    half = values.shape[-1] // 2
    first = values[..., :half]
    second = values[..., half:]
    return jnp.concatenate(
        [first * cosine + second * sine, second * cosine - first * sine], axis=-1
    )


def norm_forward(source, gain):
    factor = lax.rsqrt(jnp.mean(source * source, axis=-1, keepdims=True) + norm_eps)
    return (factor, (source * factor * gain).astype(jnp.bfloat16))


def norm_backward(source, factor, gain, grad_normed):
    unit = source * factor
    gain_grad = jnp.sum(grad_normed * unit, axis=0)
    scaled = grad_normed * gain
    source_grad = factor * (scaled - unit * jnp.mean(scaled * unit, axis=-1, keepdims=True))
    return (source_grad, gain_grad)


def right_dot(left, weight):
    return jnp.einsum("rf,df->rd", left, weight, preferred_element_type=jnp.float32)


def plain_dot(left, weight):
    return jnp.dot(left, weight, preferred_element_type=jnp.float32)


def owned_columns(values, ctx_size, ctx_rank, shard_rows):
    rows = values.shape[0]
    blocks = values.shape[1] // (shard_rows * ctx_size)
    shaped = values.reshape(rows, blocks, ctx_size, shard_rows)
    picked = lax.dynamic_index_in_dim(shaped, ctx_rank, axis=2, keepdims=False)
    return picked.reshape(rows, blocks * shard_rows)


def outer_add(left, right):
    return jnp.einsum("rc,rf->cf", left, right, preferred_element_type=jnp.float32)


MESH = pl.DeviceIdType.MESH


def flip(index, mask):
    for bit in (1, 2, 4, 8, 16):
        if mask & bit:
            index = index + bit - 2 * bit * ((index // bit) % 2)
    return index


def either(a, b):
    return a + b - 2 * a * b


def dot(a, b, dims):
    return lax.dot_general(a, b, (dims, ((), ())), preferred_element_type=jnp.float32)


def widths(hidden_units):
    width = -(-hidden_units // (8 * 128)) * 128
    first = width // 384 * 256
    return (first, width - first)


def ffn_kernel(
    ctx_size, n_own, norm_y, go_all, big, big_two,
    grad_two, r_part, grads, grads_two, near, zin,
    w_one, w_two, nt, go, ggu, act, crecv, part, h_in, h_mid, stage, own, far,
    io_sem, n_send, n_recv, f_send, f_recv, c_send, c_recv, o_send, o_recv, st_sem, w_send, w_recv, l_sem, x_send, x_recv, z_send, z_recv, d_sem,
):
    dp = lax.axis_index("dp")
    ctx = lax.axis_index("ctx")
    me = dp * ctx_size + ctx
    y, x, c = dp // 4, (dp // 2) % 2, dp % 2
    h, p = ctx // 2, ctx % 2
    one, two = w_one.shape[1] // 3, w_two.shape[1] // 3
    shard = grads.shape[3]
    rows, model = n_own.shape
    low, full = jnp.bfloat16, jnp.float32

    def at(index):
        return (index // ctx_size, index % ctx_size)

    def remote(src, dst, send, recv, mask):
        return pltpu.make_async_remote_copy(
            src_ref=src, dst_ref=dst, send_sem=send, recv_sem=recv, device_id=at(flip(me, mask)), device_id_type=MESH
        )

    def block(mask):
        return pl.ds(pl.multiple_of(flip(me, mask) * shard, shard), shard)

    barrier = pltpu.get_barrier_semaphore()
    partners = (1, 2, 4, 8, 16)
    for mask in partners:
        pl.semaphore_signal(barrier, inc=1, device_id=at(flip(me, mask)), device_id_type=MESH)
    load_n = pltpu.make_async_copy(n_own, nt.at[0], io_sem.at[0])
    load_y = pltpu.make_async_copy(norm_y, nt.at[4], io_sem.at[3])
    load_w = pltpu.make_async_copy(big, w_one, io_sem.at[1])
    load_go = pltpu.make_async_copy(go_all, go, io_sem.at[2])
    held = (0, 4, 1, 5, 16, 20, 17, 21, 2, 6, 3, 7)
    load_l = [
        pltpu.make_async_copy(big_two.at[block(mask)], w_two.at[block(mask)], l_sem.at[i]) for i, mask in enumerate(held)
    ]
    for copy in (load_n, load_y, load_w, load_go, *load_l):
        copy.start()
    pl.semaphore_wait(barrier, len(partners))

    def spread_two(mask, over):
        remote(big_two.at[block(mask)], w_two.at[block(mask)], w_send.at[0], w_recv.at[mask | over], over).start()

    def w_wait(mask):
        remote(w_two.at[block(mask)], w_two.at[block(mask)], w_send.at[0], w_recv.at[mask], 1).wait_recv()

    def w_pass(mask):
        w_wait(mask)
        remote(w_two.at[block(mask)], w_two.at[block(mask)], w_send.at[0], w_recv.at[mask | 8], 8).start()

    def n_core(slot):
        return remote(nt.at[slot], nt.at[slot + 1], f_send.at[slot // 2], f_recv.at[slot // 2], 4)

    def n_push(o):
        half = pl.ds((o - 1) % 2 * (rows // 2), rows // 2)
        if o == 1:
            return remote(nt.at[0], nt.at[2], n_send.at[1], n_recv.at[1], 1)
        return remote(nt.at[(0, 0, 4, 2)[o], half], nt.at[6, half], n_send.at[o], n_recv.at[o], (0, 0, 1, 16)[o])

    load_n.wait()
    n_push(1).start()
    n_core(0).start()
    load_y.wait()
    n_push(2).start()
    n_core(4).start()
    for mask in (16, 20, 17, 21):
        spread_two(mask, 2)
    for mask in held:
        spread_two(mask, 8)
    load_w.wait()
    load_go.wait()

    def first(slot):
        gu = dot(nt[slot], w_one[:, : 2 * one], ((1,), (0,)))
        ga = dot(go[slot], w_one[:, 2 * one :], ((1,), (0,)))
        finish(slot, gu[:, :one], gu[:, one:], ga, 0, 0)

    def finish(slot, gate, up, ga, at_gu, at_act):
        size = gate.shape[1]
        sig = 1.0 / (1.0 + jnp.exp(-gate))
        silu = gate * sig
        act[slot, :, pl.ds(at_act, size)] = (silu * up).astype(low)
        ggu[slot, :, pl.ds(at_gu, size)] = (ga * up * sig * (1.0 + gate * (1.0 - sig))).astype(low)
        ggu[slot, :, pl.ds(at_gu + size, size)] = (ga * silu).astype(low)

    def second(slot):
        gu = dot(nt[slot], w_two[:, : 2 * two], ((1,), (0,)))
        ga = dot(go[slot], w_two[:, 2 * two :], ((1,), (0,)))
        finish(slot, gu[:, :two], gu[:, two:], ga, 2 * one, one)
        grad = dot(ggu[slot, :, : 2 * one], w_one[:, : 2 * one], ((1,), (1,)))
        grad = grad + dot(ggu[slot, :, 2 * one :], w_two[:, : 2 * two], ((1,), (1,)))
        out = dot(act[slot, :, :one], w_one[:, 2 * one :], ((1,), (1,)))
        out = out + dot(act[slot, :, one:], w_two[:, 2 * two :], ((1,), (1,)))
        return (grad.astype(low), out.astype(low))

    def early(n, carry):
        o = n % 2 * 2 + n // 2

        @pl.when(o == 1)
        def _():
            n_push(1).wait_recv()
            n_push(3).start()
            n_core(2).start()

        @pl.when(o == 3)
        def _():
            n_push(2).wait_recv()
            n_push(3).wait_recv()
            n_core(6).start()

        first(2 * o)


        n_core(2 * o).wait_recv()
        first(2 * o + 1)
        return carry

    lax.fori_loop(0, 4, early, 0)
    def stage_wait(slot, size):
        part_of = stage.at[slot, :, pl.ds(0, size)]
        pltpu.make_async_copy(part_of, part_of, st_sem.at[slot]).wait()

    def weights(size, start_gu, start_act, to, passes, q, carry):
        slot = q % 2

        @pl.when(q > 1)
        def _():
            stage_wait(slot, 3 * size)

        chunk = 8 * shard
        cols = pl.ds(pl.multiple_of(q * chunk, chunk), chunk)

        def product(left, right, start, count, at_col):
            left = left[:, :, cols].reshape(8 * rows, chunk)
            right = right[:, :, pl.ds(start, count)].reshape(8 * rows, count)
            stage[slot, :, pl.ds(at_col, count)] = dot(left, right, ((0,), (0,))).astype(low)

        for start in range(0, 2 * size, one):
            count = min(one, 2 * size - start)
            product(nt, ggu, start_gu + start, count, start)
        product(go, act, start_act, size, 2 * size)
        for n, masks in enumerate(passes):
            @pl.when(q == n)
            def _():
                for mask in masks:
                    w_pass(mask)

        yr, xr = either(q // 2, y), either(q % 2, x)
        for j in range(8):
            cr, hrel, pr = either(j // 4, c), either((j // 2) % 2, h), either(j % 2, p)
            pltpu.make_async_copy(
                stage.at[slot, pl.ds(j * shard, shard), pl.ds(0, 3 * size)],
                to.at[xr, hrel, yr * 4 + cr * 2 + pr], st_sem.at[slot],
            ).start()
        return carry

    def all_weights(size, start_gu, start_act, to, passes=()):
        lax.fori_loop(0, 4, functools.partial(weights, size, start_gu, start_act, to, passes), 0)
        stage_wait(0, 3 * size)
        stage_wait(1, 3 * size)

    def far_push(j):
        return remote(grads.at[1, 1, j], far.at[j], x_send.at[j], x_recv.at[j], 8)

    def z_push(j):
        return remote(far.at[j], zin.at[j], z_send.at[j], z_recv.at[j], 2)

    def load_own(k):
        return pltpu.make_async_copy(grads.at[0, 1, pl.ds(4 * k, 4)], own, d_sem.at[0])

    keep_near = pltpu.make_async_copy(far, near, d_sem.at[0])

    def far_pass(*blocks):
        for j in blocks:
            far_push(j).wait_recv()
            far[j] = (far[j].astype(full) + own[j % 4].astype(full)).astype(low)
            if j < 4:
                z_push(j).start()

    all_weights(one, 0, 0, grads, ((18, 22, 19, 23),))
    for j in range(8):
        far_push(j).start()
    load_own(0).start()

    for mask in (8, 12, 9, 13, 24, 28, 25, 29, 10, 14, 11, 15, 26, 30, 27, 31):
        w_wait(mask)
    for copy in load_l:
        copy.wait()

    def cross(o):
        return remote(stage.at[:, pl.ds(0, rows), pl.ds(0, model)], crecv.at[o % 2], c_send, c_recv.at[o % 2], 4)

    def final(o):
        dst = h_mid if o == 3 else h_in.at[o - 1]
        return remote(part.at[o, 0], dst, o_send.at[o], o_recv.at[o], (0, 1, 16, 16)[o])

    def keep(o):
        return pltpu.make_async_copy(part.at[o, 1], r_part.at[o], io_sem.at[o])

    def combine(o):
        cross(o).wait_recv()
        part[o] = (part[o].astype(full) + crecv[o % 2].astype(full)).astype(low)
        keep(o).start()

    def late(n, carry):
        o = 3 - n
        grad, out = second(2 * o)
        part[o, 0] = grad
        part[o, 1] = out

        @pl.when(n > 0)
        def _():
            combine(o + 1)

        @pl.when(n == 1)
        def _():
            final(3).start()
            load_own(0).wait()
            far_pass(0, 1)

        @pl.when(n == 2)
        def _():
            final(2).start()
            far_pass(2, 3)
            load_own(1).start()

        @pl.when(n == 3)
        def _():
            final(3).wait_recv()
            part[1, 0] = (part[1, 0].astype(full) + h_mid[...].astype(full)).astype(low)
            final(1).start()
            load_own(1).wait()
            far_pass(4, 5)

        grad, out = second(2 * o + 1)

        @pl.when(n > 0)
        def _():
            cross(o).wait_send()

        stage[0, pl.ds(0, rows), pl.ds(0, model)] = grad
        stage[1, pl.ds(0, rows), pl.ds(0, model)] = out
        cross(o).start()
        return carry

    lax.fori_loop(0, 4, late, 0)

    far_pass(6, 7)
    keep_near.start()
    cross(0).wait_send()
    all_weights(two, 2 * one, one, grads_two)
    combine(0)
    grad_two[...] = part[0, 0].astype(full)
    for o in (1, 2):
        final(o).wait_recv()
        grad_two[...] += h_in[o - 1].astype(full)
    keep_near.wait()
    for j in range(8):
        far_push(j).wait_send()
        if j < 4:
            z_push(j).wait()
    for o in range(4):
        keep(o).wait()
        n_core(2 * o).wait_send()
    for o in (1, 2, 3):
        n_push(o).wait_send()
        final(o).wait_send()
    sent = w_two.at[pl.ds(0, 20 * shard)]
    pltpu.make_async_copy(sent, sent, w_send.at[0]).wait()


def ffn_call(ctx_size, shard, n_own, norm_y, go_all, big, big_two):
    rows, model = n_own.shape
    one, two = big.shape[1] // 3, big_two.shape[1] // 3
    low = jnp.bfloat16
    anywhere = pl.BlockSpec(memory_space=pl.ANY)
    sem = pltpu.SemaphoreType.DMA
    return pl.pallas_call(
        functools.partial(ffn_kernel, ctx_size),
        out_shape=(
            jax.ShapeDtypeStruct((rows, model), jnp.float32),
            jax.ShapeDtypeStruct((4, rows, model), low),
            jax.ShapeDtypeStruct((2, 2, 8, shard, 3 * one), low),
            jax.ShapeDtypeStruct((2, 2, 8, shard, 3 * two), low),
            jax.ShapeDtypeStruct((8, shard, 3 * one), low),
            jax.ShapeDtypeStruct((4, shard, 3 * one), low),
        ),
        in_specs=[anywhere] * 5,
        out_specs=[pl.BlockSpec(memory_space=pltpu.VMEM)] + [anywhere] * 5,
        scratch_shapes=[
            pltpu.VMEM((model, 3 * one), low),
            pltpu.VMEM((model, 3 * two), low),
            pltpu.VMEM((8, rows, model), low),
            pltpu.VMEM((8, rows, model), low),
            pltpu.VMEM((8, rows, 2 * (one + two)), low),
            pltpu.VMEM((8, rows, one + two), low),
            pltpu.VMEM((2, 2, rows, model), low),
            pltpu.VMEM((4, 2, rows, model), low),
            pltpu.VMEM((2, rows, model), low),
            pltpu.VMEM((rows, model), low),
            pltpu.VMEM((2, 8 * shard, 3 * one), low),
            pltpu.VMEM((4, shard, 3 * one), low),
            pltpu.VMEM((8, shard, 3 * one), low),
            sem((4,)), sem((5,)), sem((5,)), sem((4,)), sem((4,)), sem, sem((2,)), sem((4,)), sem((4,)), sem((2,)),
            sem((1,)), sem((32,)), sem((12,)), sem((8,)), sem((8,)), sem((4,)), sem((4,)), sem((1,)),
        ],
        compiler_params=pltpu.CompilerParams(
            collective_id=1, has_side_effects=True, vmem_limit_bytes=65200 << 10
        ),
        name="ffn",
    )(n_own, norm_y, go_all, big, big_two)


def turn(values, cosine, sine):
    return values * cosine + pltpu.roll(values, HD // 2, 1) * sine


def front_kernel(
    ctx_size, span, hidden, sides, w_query, w_key, w_value, w_out, w_gate, w_up, w_down, grad_out,
    normed_o, query_o, kv_o, total_o, mixed_o, resid_o, normed_two_o, small_o, proj_o, out_o, big, big_two, go, relay, spread, norm_y, cosine, sine, pos_k, pos_q,
    proj, out_w, source, source_two, query, kv, mixed,
    load_sem, ag_send, ag_recv, core_send, core_recv, big_send, big_recv, two_recv, relay_recv, go_send, go_recv, kv_send, kv_recv, back_sem, norm_sem,
):
    dp = lax.axis_index("dp")
    ctx = lax.axis_index("ctx")
    me = dp * ctx_size + ctx
    shard, wide = w_out.shape[0], proj.shape[1]
    rows, model = hidden.shape
    one, two = big.shape[1] // 3, big_two.shape[1] // 3
    kv_width = KV_HEADS * HD
    q_width = HEADS * HD
    proj_width = q_width + 2 * kv_width
    groups = HEADS // KV_HEADS

    def at(index):
        return (index // ctx_size, index % ctx_size)

    def block(mask, count=1):
        base = flip(me, mask) // count * count
        return pl.ds(pl.multiple_of(base * shard, shard), shard * count)

    def remote(src, dst, send, recv, mask):
        return pltpu.make_async_remote_copy(
            src_ref=src, dst_ref=dst, send_sem=send, recv_sem=recv, device_id=at(flip(me, mask)), device_id_type=MESH
        )

    def drain(ref, sem):
        pltpu.make_async_copy(ref, ref, sem).wait()

    barrier = pltpu.get_barrier_semaphore()
    partners = (1, 2, 3, 4, 5, 8, 16, 17, 20, 21)
    for mask in partners:
        pl.semaphore_signal(barrier, inc=1, device_id=at(flip(me, mask)), device_id_type=MESH)

    own = (
        pltpu.make_async_copy(w_query, proj.at[block(0), pl.ds(0, q_width)], load_sem.at[0]),
        pltpu.make_async_copy(w_out, out_w.at[block(0)], load_sem.at[1]),
        pltpu.make_async_copy(w_key, proj.at[block(0), pl.ds(q_width, kv_width)], load_sem.at[50]),
        pltpu.make_async_copy(w_value, proj.at[block(0), pl.ds(q_width + kv_width, kv_width)], load_sem.at[51]),
        pltpu.make_async_copy(sides, proj.at[block(0), pl.ds(proj_width, HD)], load_sem.at[52]),
    )
    for copy in own:
        copy.start()
    hidden_units = w_gate.shape[1]
    cuts = []
    for k in range(8):
        for n, ref in enumerate((w_gate, w_up, w_down)):
            for to, start, width in ((source, k * (one + two), one), (source_two, k * (one + two) + one, two)):
                size = min(width, hidden_units - start)
                cuts.append((ref.at[:, pl.ds(start, size)], to.at[k, :, pl.ds(n * width, size)]))
                if size < width:
                    to[k, :, pl.ds(n * width + size, width - size)] = jnp.zeros((shard, width - size), to.dtype)
    cuts = [pltpu.make_async_copy(a, b, load_sem.at[2 + i]) for i, (a, b) in enumerate(cuts)]
    for copy in cuts:
        copy.start()
    pl.semaphore_wait(barrier, len(partners))
    for copy in own:
        copy.wait()

    q_cols, k_cols = pl.ds(0, q_width), pl.ds(q_width, wide - q_width)
    streams = ((proj, k_cols), (proj, q_cols), (out_w, q_cols))

    def ag(n, mask, *overs):
        ref, cols = streams[n]
        part = ref.at[block(mask), cols]
        for over in overs:
            remote(part, part, ag_send.at[n], ag_recv.at[n, mask | over], over).start()

    def ag_pass(n, mask, *overs):
        ref, cols = streams[n]
        part = ref.at[block(mask), cols]
        remote(part, part, ag_send.at[n], ag_recv.at[n, mask], 1).wait_recv()
        ag(n, mask, *overs)

    def group(n, mask):
        ref, cols = streams[n]
        part = ref.at[block(mask, 4), cols]
        return remote(part, part, core_send.at[n, mask // 8], core_recv.at[n, mask // 8], 4)

    def group_wait(n):
        ref, cols = streams[n]
        for mask in (0, 8, 16, 24):
            part = ref.at[block(mask | 4, 4), cols]
            remote(part, part, core_send.at[n, mask // 8], core_recv.at[n, mask // 8], 4).wait_recv()

    ag(0, 0, 2, 1, 8, 16)
    ag(1, 0, 2, 1, 8, 16)

    for copy in cuts:
        copy.wait()
    y, x, c = dp // 4, (dp // 2) % 2, dp % 2
    h, p = ctx // 2, ctx % 2

    def column(mask):
        return either(y, mask // 16) * 4 + either(p, mask % 2) * 2 + either(c, (mask // 4) % 2)

    own_big = pltpu.make_async_copy(source.at[column(0)], big.at[block(0)], load_sem.at[0])
    own_big.start()
    own_two = pltpu.make_async_copy(source_two.at[column(0)], big_two.at[block(0)], load_sem.at[1])
    own_two.start()

    def cut(mask):
        remote(source.at[column(mask)], big.at[block(0)], big_send.at[0], big_recv.at[mask], mask).start()

    def cut_two(mask):
        return remote(source_two.at[column(mask)], big_two.at[block(0)], big_send.at[1], two_recv.at[mask], mask)

    held = (0, 4, 1, 5, 16, 20, 17, 21)
    inner = either(h, p) == 1

    def over_z(mask):
        src = big.at[block(mask)] if mask else source.at[column(0)]

        @pl.when(inner)
        def _():
            remote(src, big.at[block(mask)], big_send.at[0], big_recv.at[mask | 2], 2).start()

        @pl.when(jnp.logical_not(inner))
        def _():
            i = held.index(mask)
            remote(src, relay.at[i], big_send.at[0], relay_recv.at[i], 1).start()

    def relay_pass(*masks):
        @pl.when(inner)
        def _():
            for mask in masks:
                i = held.index(mask)
                remote(relay.at[i], relay.at[i], big_send.at[0], relay_recv.at[i], 1).wait_recv()
                remote(relay.at[i], big.at[block(mask ^ 1)], big_send.at[2], big_recv.at[mask | 2], 3).start()

    def big_forward(mask, over):
        if over == 2:
            over_z(mask)
        else:
            remote(big.at[block(mask)], big.at[block(mask)], big_send.at[0], big_recv.at[mask | over], over).start()

    def big_pass(mask, *overs):
        remote(big.at[block(mask)], big.at[block(mask)], big_send.at[0], big_recv.at[mask], 1).wait_recv()
        for over in overs:
            big_forward(mask, over)

    cut(4)
    over_z(0)

    row = lax.broadcasted_iota(jnp.int32, (model, 2 * kv_width), 0)
    col = lax.broadcasted_iota(jnp.int32, (model, 2 * kv_width), 1)
    per = kv_width * shard // model
    unit = (col % kv_width) // per * shard + col // kv_width * per + col % per
    spread[...] = jnp.where(row == unit, 1.0, 0.0).astype(jnp.bfloat16)
    length = rows // 2
    for j in range(2 * ctx_size):
        lane = lax.broadcasted_iota(jnp.int32, (1, length), 1)
        pos_k[:, pl.ds(j * length, length)] = (span[0, j] * length + lane).astype(jnp.float32)
    pos_q[...] = pos_k[:, pl.ds(pl.multiple_of(ctx * rows, rows), rows)]
    own_pos = jnp.transpose(jnp.broadcast_to(pos_q[...], (HD, rows)))
    lane = lax.broadcasted_iota(jnp.int32, (rows, HD), 1)
    turns = (lane % (HD // 2)).astype(jnp.float32) * (2.0 / HD)
    angles = own_pos * jnp.exp(turns * -math.log(rope_base))
    cosine[...] = jnp.cos(angles)
    sine[...] = jnp.sin(angles) * jnp.where(lane < HD // 2, -1.0, 1.0)
    own_pos = own_pos[:, :1]

    ag_pass(0, 1, 8, 16)
    ag_pass(0, 8, 16)
    ag_pass(0, 2, 1, 8, 16)
    ag_pass(0, 9, 16)
    ag_pass(1, 1, 8, 16)
    ag_pass(1, 8, 16)
    ag_pass(0, 3, 8, 16)
    ag_pass(0, 10, 16)
    ag_pass(1, 2, 1, 8, 16)
    group(0, 0).start()
    remote(source.at[column(0)], big.at[block(0)], big_send.at[0], big_recv.at[8], 8).start()
    cut(1)
    cut(5)
    big_pass(4, 2, 8)
    ag_pass(0, 11, 16)
    group(0, 8).start()
    relay_pass(0)
    ag_pass(1, 9, 16)
    ag(2, 0, 2, 1, 16, 8)
    for mask in (16, 17, 18, 19):
        ag_pass(0, mask)
    group(0, 16).start()
    ag_pass(1, 3, 8, 16)
    group(1, 0).start()
    for mask in (24, 25, 26, 27):
        ag_pass(0, mask)
    group(0, 24).start()
    relay_pass(4)
    group_wait(0)

    small = jnp.transpose(proj[:, proj_width:].astype(jnp.float32))
    small_o[...] = small[:8]
    kv_bias = dot(small[:8].astype(jnp.bfloat16), spread[...], ((1,), (0,)))[3:4]
    values = hidden[...].astype(jnp.float32)
    factor = lax.rsqrt(jnp.mean(values * values, axis=-1, keepdims=True) + norm_eps)
    normed_o[...] = (values * factor * small[0:1]).astype(jnp.bfloat16)
    cos, sin = cosine[...], sine[...]
    raw = dot(normed_o[...], proj[:, q_width:proj_width], ((1,), (0,))) + kv_bias
    mine = block(0)
    for g in range(KV_HEADS):
        kv[ctx, :, pl.ds(g * HD, HD)] = turn(raw[:, g * HD : (g + 1) * HD], cos, sin).astype(jnp.bfloat16)
    kv[ctx, :, pl.ds(kv_width, kv_width)] = raw[:, kv_width:].astype(jnp.bfloat16)

    def kv_push(mask, over):
        slot = flip(ctx, mask)
        return remote(kv.at[slot], kv.at[slot], kv_send.at[mask | over], kv_recv.at[mask | over], over)

    kv_push(0, 2).start()
    kv_push(0, 1).start()
    ag_pass(1, 10, 16)
    ag_pass(1, 11, 16)
    group(1, 8).start()
    big_pass(1, 2, 8)
    ag_pass(2, 1, 16, 8)
    ag_pass(2, 2, 1, 16, 8)
    for mask in (16, 20, 17, 21):
        cut(mask)
    kv_push(0, 2).wait_recv()
    kv_push(2, 1).start()
    big_pass(5, 2, 8)
    relay_pass(1)
    for mask in (16, 17, 18, 19):
        ag_pass(1, mask)
    group(1, 16).start()
    ag_pass(2, 3, 16, 8)
    group(2, 0).start()
    for mask in (24, 25, 26, 27):
        ag_pass(1, mask)
    group(1, 24).start()
    big_pass(16, 2, 8)
    relay_pass(5)
    group_wait(1)
    for half in range(2):
        part = half * (q_width // 2)
        raw = dot(normed_o[...], proj[:, part : part + q_width // 2], ((1,), (0,)))
        raw = raw + small[1:2, part : part + q_width // 2]
        for i in range(HEADS // 2):
            query[half * (HEADS // 2) + i] = turn(raw[:, i * HD : (i + 1) * HD], cos, sin).astype(jnp.bfloat16)
    big_pass(20, 2, 8)
    relay_pass(16)
    for mask in (16, 17, 18, 19):
        ag_pass(2, mask, 8)
    group(2, 16).start()
    big_pass(17, 2, 8)
    big_pass(21, 2, 8)
    relay_pass(20)

    def go_core(o):
        src = go.at[2 * o] if o else grad_out
        return remote(src, go.at[2 * o + 1], go_send.at[3 + o], go_recv.at[2 * o + 1], 4)

    def go_push(o):
        src = go.at[2] if o == 3 else grad_out
        return remote(src, go.at[2 * o], go_send.at[o - 1], go_recv.at[2 * o], (0, 1, 16, 16)[o])

    go_push(2).start()
    go_push(1).start()
    go_core(0).start()
    for mask in (2, 6):
        big_pass(mask, 8)
    kv_push(0, 1).wait_recv()
    kv_push(2, 1).wait_recv()
    query_back = pltpu.make_async_copy(query, query_o, back_sem.at[0])
    query_back.start()
    kv_back = pltpu.make_async_copy(kv, kv_o, back_sem.at[1])
    kv_back.start()

    def head(n, carry):
        g = n // groups
        keys = kv[:, :, pl.ds(pl.multiple_of(g * HD, HD), HD)].reshape(ctx_size * rows, HD)
        vals = kv[:, :, pl.ds(pl.multiple_of(kv_width + g * HD, HD), HD)].reshape(ctx_size * rows, HD)
        scores = dot(query[n], keys, ((1,), (1,))) * HD ** (-0.5)
        scores = jnp.where(pos_k[...] <= own_pos, scores, masked_fill)
        top = jnp.max(scores, axis=-1, keepdims=True)
        expo = jnp.exp(scores - top)
        expo_sum = jnp.sum(expo, axis=-1, keepdims=True)
        attend = (expo / expo_sum).astype(jnp.bfloat16)
        mixed[:, pl.ds(pl.multiple_of(n * HD, HD), HD)] = dot(attend, vals, ((1,), (0,))).astype(jnp.bfloat16)
        lane = lax.broadcasted_iota(jnp.int32, (rows, HD), 1)
        total_o[...] = jnp.where(lane == n, top + jnp.log(expo_sum), total_o[...])
        return carry

    total_o[...] = jnp.zeros_like(total_o)
    lax.fori_loop(0, HEADS, head, 0)
    own_go = pltpu.make_async_copy(grad_out, go.at[0], load_sem.at[2])
    own_go.start()
    mixed_back = pltpu.make_async_copy(mixed, mixed_o, back_sem.at[2])
    mixed_back.start()
    relay_pass(17, 21)

    def two_over_z(mask):
        src = big_two.at[block(mask)] if mask else source_two.at[column(0)]
        return remote(src, big_two.at[block(mask)], big_send.at[1], two_recv.at[mask | 2], 2)

    for mask in (3, 7):
        big_pass(mask, 8)
    for mask in (4, 1, 5, 16, 20, 17, 21):
        cut_two(mask).start()
    for n, mask in enumerate((8, 9, 10, 11, 24, 25, 26, 27)):
        ag_pass(2, mask)
        if n % 4 == 3:
            group(2, mask & 24).start()
    group_wait(2)
    proj_back = pltpu.make_async_copy(proj, proj_o, back_sem.at[4])
    proj_back.start()
    out_back = pltpu.make_async_copy(out_w, out_o, back_sem.at[5])
    out_back.start()
    resid = hidden[...].astype(jnp.float32) + dot(mixed[...], out_w[...], ((1,), (1,)))
    resid_o[...] = resid
    factor = lax.rsqrt(jnp.mean(resid * resid, axis=-1, keepdims=True) + norm_eps)
    normed_two_o[...] = (resid * factor * small_o[2:3]).astype(jnp.bfloat16)
    norm_push = remote(normed_two_o, norm_y, norm_sem.at[0], norm_sem.at[1], 16)
    norm_push.start()
    go_push(1).wait_recv()
    go_push(3).start()
    go_core(1).start()
    go_push(2).wait_recv()
    go_core(2).start()
    two_over_z(0).start()
    for mask, passed in ((4, 18), (1, 22), (5, 19), (0, 23)):
        big_pass(passed, 8)
        if mask:
            cut_two(mask).wait_recv()
            two_over_z(mask).start()

    norm_push.wait()
    for mask in (8, 12, 9, 24, 13, 28, 25, 29, 10, 14, 11, 26, 15, 30, 27, 31):
        big_pass(mask)
    go_push(3).wait_recv()
    go_core(3).start()
    for mask in (16, 20, 17, 21):
        cut_two(mask).wait_recv()
    for mask in (0, 4, 1, 5):
        two_over_z(mask).wait_recv()
    own_big.wait()
    own_two.wait()
    own_go.wait()
    drain(big.at[pl.ds(0, 31 * shard)], big_send.at[0])
    drain(big_two.at[pl.ds(0, 11 * shard)], big_send.at[1])

    @pl.when(inner)
    def _():
        drain(relay, big_send.at[2])

    for n in range(3):
        ref, cols = streams[n]
        drain(ref.at[pl.ds(0, 15 * shard), cols], ag_send.at[n])
        for mask in (0, 8, 16, 24):
            group(n, mask).wait_send()
    for o in range(4):
        go_core(o).wait()
    for o in (1, 2, 3):
        go_push(o).wait_send()
    kv_push(0, 2).wait_send()
    kv_push(0, 1).wait_send()
    kv_push(2, 1).wait_send()
    for copy in (query_back, kv_back, mixed_back, proj_back, out_back):
        copy.wait()


def front_call(
    ctx_size, span, hidden, sides, w_query, w_key, w_value, w_out, w_gate, w_up, w_down, grad_out
):
    rows, model = hidden.shape
    shard = w_out.shape[0]
    kv_width = KV_HEADS * HD
    q_width = HEADS * HD
    wide = q_width + 2 * kv_width + HD
    one, two = widths(w_gate.shape[1])
    low, full = jnp.bfloat16, jnp.float32
    vmem = pl.BlockSpec(memory_space=pltpu.VMEM)
    anywhere = pl.BlockSpec(memory_space=pl.ANY)
    shapes = (
        ((rows, model), low, vmem),
        ((HEADS, rows, HD), low, anywhere),
        ((ctx_size, rows, 2 * kv_width), low, anywhere),
        ((rows, HD), full, vmem),
        ((rows, q_width), low, anywhere),
        ((rows, model), full, vmem),
        ((rows, model), low, vmem),
        ((8, model), full, vmem),
        ((model, wide), low, anywhere),
        ((model, q_width), low, anywhere),
        ((model, 3 * one), low, anywhere),
        ((model, 3 * two), low, anywhere),
        ((8, rows, model), low, anywhere),
        ((8, shard, 3 * one), low, anywhere),
        ((model, 2 * kv_width), low, vmem),
        ((rows, model), low, anywhere),
        ((rows, HD), full, vmem),
        ((rows, HD), full, vmem),
        ((1, ctx_size * rows), full, vmem),
        ((1, rows), full, vmem),
    )
    sem = pltpu.SemaphoreType.DMA
    return pl.pallas_call(
        functools.partial(front_kernel, ctx_size),
        out_shape=tuple(jax.ShapeDtypeStruct(shape, kind) for shape, kind, _ in shapes),
        in_specs=[pl.BlockSpec(memory_space=pltpu.SMEM), vmem] + [anywhere] * 9,
        out_specs=tuple(spec for _, _, spec in shapes),
        scratch_shapes=[
            pltpu.VMEM((model, wide), low),
            pltpu.VMEM((model, q_width), low),
            pltpu.VMEM((8, shard, 3 * one), low),
            pltpu.VMEM((8, shard, 3 * two), low),
            pltpu.VMEM((HEADS, rows, HD), low),
            pltpu.VMEM((ctx_size, rows, 2 * kv_width), low),
            pltpu.VMEM((rows, q_width), low),
            sem((53,)), sem((3,)), sem((3, 32)), sem((3, 4)), sem((3, 4)), sem((3,)), sem((32,)), sem((32,)), sem((8,)),
            sem((7,)), sem((8,)), sem((4,)), sem((4,)), sem((6,)), sem((2,)),
        ],
        compiler_params=pltpu.CompilerParams(
            collective_id=0, has_side_effects=True, vmem_limit_bytes=56 << 20
        ),
        name="front",
    )(span, hidden, sides, w_query, w_key, w_value, w_out, w_gate, w_up, w_down, grad_out)


def back_kernel(
    ctx_size, grad_two, resid, hidden, grad_out, normed, mixed, query, kv, total, cosine, sine, pos_q, pos_k, small, spread,
    proj, out_w, grads, grads_two, near, zin_first, r_part,
    hidden_o, query_o, key_o, outw_o, fin, fin_two, r_in, relay, relay_two,
    weight, turned, left_n, left_a, right_b, right_p, side, side_in, g_b, g_q, g_k,
    y_b, y_q, y_k, x_b, x_q, x_k, p_b, p_q, p_k, h_b, h_q, h_k,
    own, far, zin, own_two, far_two, zin_two, r_mid, r_one, heads_g, lse, dkv, kv_out, kv_p, kv_h, grad_resid,
    load_sem, xs, xr, zs, zr, fs, fr, xs2, xr2, zs2, zr2, fs2, fr2, relay_recv, relay_send, cs, cr, rs, rr, ks, kr, os, orr, keep_sem,
):
    dp = lax.axis_index("dp")
    ctx = lax.axis_index("ctx")
    me = dp * ctx_size + ctx
    y, x, c = dp // 4, (dp // 2) % 2, dp % 2
    h, p = ctx // 2, ctx % 2
    rows, model = resid.shape
    shard = grads.shape[3]
    kv_width = KV_HEADS * HD
    q_width = HEADS * HD
    groups = HEADS // KV_HEADS
    low, full = jnp.bfloat16, jnp.float32
    span = ctx_size * shard

    def at(index):
        return (index // ctx_size, index % ctx_size)

    def remote(src, dst, send, recv, mask):
        return pltpu.make_async_remote_copy(
            src_ref=src, dst_ref=dst, send_sem=send, recv_sem=recv, device_id=at(flip(me, mask)), device_id_type=MESH
        )

    def group_rows(mask):
        return pl.ds(pl.multiple_of(flip(dp, mask // 4) * span, span), span)

    def mask_of(j):
        return (j // 4) * 16 + ((j // 2) % 2) * 4 + j % 2

    barrier = pltpu.get_barrier_semaphore()
    partners = (1, 2, 3, 4, 5, 8, 16, 17, 20, 21)
    for mask in partners:
        pl.semaphore_signal(barrier, inc=1, device_id=at(flip(me, mask)), device_id_type=MESH)
    load_w = pltpu.make_async_copy(out_w, weight.at[:, pl.ds(0, q_width)], load_sem.at[0])
    load_w.start()
    load_own = [
        pltpu.make_async_copy(grads.at[0, 0], own, load_sem.at[1]),
        pltpu.make_async_copy(grads_two.at[0], own_two, load_sem.at[2]),
        pltpu.make_async_copy(zin_first, zin.at[pl.ds(0, 4)], load_sem.at[3]),
        pltpu.make_async_copy(r_part.at[1], r_one, load_sem.at[4]),
    ]
    for copy in load_own:
        copy.start()
    pl.semaphore_wait(barrier, len(partners))

    def far_push(j):
        return remote(grads.at[1, 0, j], far.at[j], xs.at[j], xr.at[j], 8)

    def far_two_push(half, j):
        return remote(grads_two.at[1, half, j], far_two.at[half, j], xs2.at[half, j], xr2.at[half, j], 8)

    def z_push(j):
        return remote(near.at[j], zin.at[j], zs.at[j], zr.at[j], 2)

    def z_two_push(j):
        return remote(far_two.at[1, j], zin_two.at[j], zs2.at[j], zr2.at[j], 2)

    inner = either(h, p) == 1

    def over_z(push, src, to, send, n):
        @pl.when(inner)
        def _():
            push.start()

        @pl.when(jnp.logical_not(inner))
        def _():
            remote(src, to, send, relay_recv.at[n], 1).start()

    def over_z_one(j):
        over_z(z_push(j), near.at[j], relay.at[j - 4], zs.at[j], j)

    def over_z_two(j):
        over_z(z_two_push(j), far_two.at[1, j], relay_two.at[j], zs2.at[j], 8 + j)

    def relay_one(*blocks):
        @pl.when(inner)
        def _():
            for j in blocks:
                part = relay.at[j - 4]
                remote(part, part, relay_send.at[j], relay_recv.at[j], 1).wait_recv()
                remote(part, zin.at[j], relay_send.at[j], zr.at[j], 3).start()

    def relay_two_pass(*blocks):
        @pl.when(inner)
        def _():
            for j in blocks:
                part = relay_two.at[j]
                remote(part, part, relay_send.at[8 + j], relay_recv.at[8 + j], 1).wait_recv()
                remote(part, zin_two.at[j], relay_send.at[8 + j], zr2.at[j], 3).start()

    def fin_push(j):
        return remote(own.at[j], fin.at[j], fs.at[j], fr.at[j], mask_of(j))

    def fin_two_push(j):
        return remote(own_two.at[0, j], fin_two.at[j], fs2.at[j], fr2.at[j], mask_of(j))

    keep_one = pltpu.make_async_copy(own.at[0], fin.at[0], keep_sem.at[0])
    keep_two = pltpu.make_async_copy(own_two.at[0, 0], fin_two.at[0], keep_sem.at[1])

    def z_two_step(j):
        far_two_push(1, j).wait_recv()
        far_two[1, j] = (far_two[1, j].astype(full) + own_two[1, j].astype(full)).astype(low)
        over_z_two(j)

    def total_step(j):
        far_push(j).wait_recv()
        if j > 3:
            z_push(j).wait_recv()
        own[j] = (own[j].astype(full) + far[j].astype(full) + zin[j].astype(full)).astype(low)
        if j:
            fin_push(j).start()
        else:
            keep_one.start()

    def total_two_step(j):
        far_two_push(0, j).wait_recv()
        z_two_push(j).wait_recv()
        own_two[0, j] = (own_two[0, j].astype(full) + far_two[0, j].astype(full) + zin_two[j].astype(full)).astype(low)
        if j:
            fin_two_push(j).start()
        else:
            keep_two.start()

    def r_push(o):
        src = r_one if o == 1 else r_part.at[o]
        dst = r_mid if o == 3 else r_in.at[o - 1]
        return remote(src, dst, os.at[o], orr.at[o], (0, 1, 16, 16)[o])

    r_push(3).start()
    for j in range(4, 8):
        over_z_one(j)
    for j in range(8):
        far_two_push(1, j).start()
    for j in range(8):
        far_push(j).start()

    def transposed(value, left, n):
        turned[n] = jnp.transpose(value)
        for i, mask in enumerate((0, 8, 16, 24)):
            left[i, :, pl.ds(0, rows)] = turned[n, group_rows(mask)]
            cross_left(left, n, i, mask).start()

    def cross_left(left, n, i, mask):
        return remote(turned.at[n, group_rows(mask | 4)], left.at[i, :, pl.ds(rows, rows)], cs.at[n, i], cr.at[n, i], 4)

    def cross(src, dst, n, i):
        return remote(src, dst, cs.at[n, i], cr.at[n, i], 4)

    transposed(normed[...], left_n, 0)
    right_b[pl.ds(0, rows)] = mixed[...]
    cross_mixed = cross(mixed, right_b.at[pl.ds(rows, rows)], 2, 0)
    cross_mixed.start()

    value = resid[...]
    factor = lax.rsqrt(jnp.mean(value * value, axis=-1, keepdims=True) + norm_eps)
    unit = value * factor
    scaled = grad_two[...] * small[2:3]
    ffn_row = jnp.sum(grad_two[...] * unit, axis=0, keepdims=True)
    grad_resid[...] = grad_out[...].astype(full) + factor * (
        scaled - unit * jnp.mean(scaled * unit, axis=-1, keepdims=True)
    )
    grad_attn = grad_resid[...].astype(low)
    transposed(grad_attn, left_a, 1)
    lse[...] = jnp.transpose(total[...])
    sin_back = -sine[...]
    key_pos = jnp.transpose(jnp.broadcast_to(pos_k[...], (HD, pos_k.shape[1])))[:, :1]
    load_w.wait()
    for half in range(2):
        part = half * (q_width // 2)
        moved = dot(grad_attn, weight[:, part : part + q_width // 2], ((1,), (0,))).astype(low)
        for i in range(HEADS // 2):
            heads_g[half * (HEADS // 2) + i] = moved[:, i * HD : (i + 1) * HD]
    load_p = pltpu.make_async_copy(proj, weight, load_sem.at[0])
    load_p.start()

    streams = ((g_b, y_b, x_b, p_b, h_b), (g_q, y_q, x_q, p_q, h_q), (g_k, y_k, x_k, p_k, h_k))

    def add(ref, other):
        ref[...] = (ref[...].astype(full) + other[...].astype(full)).astype(low)

    def y_push(s, k):
        g, yy = streams[s][:2]
        return remote(g.at[2 + k], yy.at[k], rs.at[s, k], rr.at[s, k], 16)

    def x_push(s):
        g, xx = streams[s][0], streams[s][2]
        return remote(g.at[1], xx, rs.at[s, 2], rr.at[s, 2], 8)

    def block_of(hr, other):
        z = 2 * either(h, hr) + either(p, other)
        return pl.ds(pl.multiple_of(z * shard, shard), shard)

    def p_push(s, hr):
        g, pp = streams[s][0], streams[s][3]
        return remote(g.at[0, block_of(hr, 1)], pp.at[hr], rs.at[s, 3 + hr], rr.at[s, 3 + hr], 1)

    def h_push(s):
        g, hh = streams[s][0], streams[s][4]
        return remote(g.at[0, block_of(1, 0)], hh, rs.at[s, 5], rr.at[s, 5], 2)

    def y_pass(s):
        g, yy = streams[s][:2]
        y_push(s, 1).wait_recv()
        add(g.at[1], yy.at[1])
        x_push(s).start()
        y_push(s, 0).wait_recv()
        add(g.at[0], yy.at[0])

    def x_pass(s):
        x_push(s).wait_recv()
        add(streams[s][0].at[0], streams[s][2])
        p_push(s, 1).start()
        p_push(s, 0).start()

    def p_pass(s):
        g, pp = streams[s][0], streams[s][3]
        p_push(s, 1).wait_recv()
        add(g.at[0, block_of(1, 0)], pp.at[1])
        h_push(s).start()
        p_push(s, 0).wait_recv()
        add(g.at[0, block_of(0, 0)], pp.at[0])

    def h_pass(s, out):
        h_push(s).wait_recv()
        out[...] = streams[s][0][0, block_of(0, 0)].astype(full) + streams[s][4][...].astype(full)

    for i, mask in enumerate((0, 8, 16, 24)):
        cross_left(left_a, 1, i, mask).wait_recv()
    cross_mixed.wait_recv()
    for i in (3, 2, 1, 0):
        g_b[i] = dot(left_a[i], right_b[...], ((1,), (0,))).astype(low)
    y_push(0, 1).start()

    def head(n, carry):
        g = n // groups
        k_cols = pl.ds(pl.multiple_of(g * HD, HD), HD)
        v_cols = pl.ds(pl.multiple_of(kv_width + g * HD, HD), HD)
        keys = kv[:, :, k_cols].reshape(ctx_size * rows, HD)
        vals = kv[:, :, v_cols].reshape(ctx_size * rows, HD)
        scores = dot(keys, query[n], ((1,), (1,))) * HD ** (-0.5)
        scores = jnp.where(key_pos <= pos_q[...], scores, masked_fill)
        attend = jnp.exp(scores - lse[pl.ds(n, 1), :])
        grad_attend = dot(vals, heads_g[n], ((1,), (1,)))
        delta = jnp.sum(grad_attend * attend, axis=0, keepdims=True)
        grad_scores = (attend * (grad_attend - delta)).astype(low)
        dkv[:, k_cols] += dot(grad_scores, query[n], ((1,), (0,)))
        dkv[:, v_cols] += dot(attend.astype(low), heads_g[n], ((1,), (0,)))
        back = dot(grad_scores, keys, ((0,), (0,))) * HD ** (-0.5)
        back = turn(back, cosine[...], sin_back).astype(low)
        right_p[pl.ds(0, rows), pl.ds(pl.multiple_of(n * HD, HD), HD)] = back
        return carry

    dkv[...] = jnp.zeros_like(dkv)
    lax.fori_loop(0, HEADS // 2, head, 0)
    relay_one(4, 5)
    lax.fori_loop(HEADS // 2, HEADS, head, 0)

    for z in range(ctx_size):
        part = dkv[pl.ds(z * rows, rows)]
        kv_out[z, :, pl.ds(0, kv_width)] = (part[:, :kv_width] * HD ** (-0.5)).astype(low)
        kv_out[z, :, pl.ds(kv_width, kv_width)] = part[:, kv_width:].astype(low)

    def kv_push(hr):
        return remote(kv_out.at[2 * either(h, hr) + 1 - p], kv_p.at[hr], ks.at[hr], kr.at[hr], 1)

    def kv_cross():
        return remote(kv_out.at[2 * (1 - h) + p], kv_h, ks.at[2], kr.at[2], 2)

    kv_push(1).start()
    kv_push(0).start()
    cross_q = cross(
        right_p.at[pl.ds(0, rows), pl.ds(0, q_width)], right_p.at[pl.ds(rows, rows), pl.ds(0, q_width)], 2, 1
    )
    cross_q.start()
    for copy in load_own:
        copy.wait()
    for i, mask in enumerate((0, 8, 16, 24)):
        cross_left(left_n, 0, i, mask).wait_recv()
    cross_q.wait_recv()
    for i in (3, 2, 1, 0):
        g_q[i] = dot(left_n[i], right_p[:, pl.ds(0, q_width)], ((1,), (0,))).astype(low)
        if i > 1:
            y_push(1, i - 2).start()
    load_p.wait()
    hidden_o[...] = dot(right_p[pl.ds(0, rows), pl.ds(0, q_width)], weight[:, pl.ds(0, q_width)], ((1,), (1,)))
    kv_push(1).wait_recv()
    add(kv_out.at[2 * (1 - h) + p], kv_p.at[1])
    kv_cross().start()
    kv_push(0).wait_recv()
    add(kv_out.at[2 * h + p], kv_p.at[0])
    relay_one(6, 7)
    for j in range(8):
        z_two_step(j)
    for j in range(4):
        total_step(j)
    relay_two_pass(0, 1, 2)
    kv_cross().wait_recv()
    final = kv_out[2 * h + p].astype(full) + kv_h[...].astype(full)
    for g in range(KV_HEADS):
        right_p[pl.ds(0, rows), pl.ds(q_width + g * HD, HD)] = turn(
            final[:, g * HD : (g + 1) * HD], cosine[...], sin_back
        ).astype(low)
    right_p[pl.ds(0, rows), pl.ds(q_width + kv_width, kv_width)] = final[:, kv_width:].astype(low)
    cross_kv = cross(
        right_p.at[pl.ds(0, rows), pl.ds(q_width, 2 * kv_width)],
        right_p.at[pl.ds(rows, rows), pl.ds(q_width, 2 * kv_width)], 2, 2,
    )
    cross_kv.start()
    grad_one = hidden_o[...] + dot(
        right_p[pl.ds(0, rows), pl.ds(q_width, 2 * kv_width)], weight[:, pl.ds(q_width, 2 * kv_width)], ((1,), (1,))
    )
    value = hidden[...].astype(full)
    factor = lax.rsqrt(jnp.mean(value * value, axis=-1, keepdims=True) + norm_eps)
    unit = value * factor
    scaled = grad_one * small[0:1]
    attn_row = jnp.sum(grad_one * unit, axis=0, keepdims=True)
    hidden_o[...] = grad_resid[...] + factor * (scaled - unit * jnp.mean(scaled * unit, axis=-1, keepdims=True))
    bias = jnp.sum(right_p[pl.ds(0, rows)].astype(full), axis=0, keepdims=True)
    kv_bias = jnp.broadcast_to(bias[:, q_width:], (8, 2 * kv_width)).astype(low)
    kv_row = dot(kv_bias, spread[...], ((1,), (1,)))[:1]
    table = jnp.concatenate([attn_row, bias[:, :q_width], ffn_row, kv_row, jnp.zeros((124, model), full)], axis=0)
    side[...] = jnp.transpose(table).astype(low)

    def cross_side(i, mask):
        return cross(side.at[group_rows(mask | 4)], side_in.at[i], 3, i)

    for i, mask in enumerate((0, 8, 16, 24)):
        cross_side(i, mask).start()
    cross_kv.wait_recv()
    for i, mask in ((3, 24), (2, 16), (1, 8), (0, 0)):
        g_k[i, :, pl.ds(0, 2 * kv_width)] = dot(
            left_n[i], right_p[:, pl.ds(q_width, 2 * kv_width)], ((1,), (0,))
        ).astype(low)
        cross_side(i, mask).wait_recv()
        g_k[i, :, pl.ds(2 * kv_width, HD)] = (
            side[group_rows(mask)].astype(full) + side_in[i].astype(full)
        ).astype(low)
        if i > 1:
            y_push(2, i - 2).start()
    y_push(0, 0).start()
    r_push(3).wait_recv()
    add(r_one, r_mid)
    r_push(1).start()
    relay_two_pass(3, 4, 5, 6, 7)
    for j in range(4, 8):
        total_step(j)
    y_pass(1)
    y_pass(2)
    for j in range(8):
        far_two_push(0, j).start()
    y_pass(0)
    x_pass(1)
    x_pass(2)
    r_push(2).start()
    p_pass(1)
    p_pass(2)
    for j in range(8):
        total_two_step(j)
    x_pass(0)
    p_pass(0)
    h_pass(1, query_o)
    h_pass(2, key_o)
    h_pass(0, outw_o)
    for j in range(1, 8):
        fin_push(j).wait_recv()
        fin_two_push(j).wait_recv()
    for o in (1, 2):
        r_push(o).wait()
    r_push(3).wait_send()
    keep_one.wait()
    keep_two.wait()

    for j in range(8):
        far_push(j).wait_send()
        far_two_push(0, j).wait_send()
        far_two_push(1, j).wait_send()
        if j > 3:
            z_push(j).wait_send()
        z_two_push(j).wait_send()
        if j:
            fin_push(j).wait_send()
            fin_two_push(j).wait_send()
    @pl.when(inner)
    def _():
        for j in range(4, 8):
            remote(relay.at[j - 4], relay.at[j - 4], relay_send.at[j], relay_recv.at[j], 1).wait_send()
        for j in range(8):
            remote(relay_two.at[j], relay_two.at[j], relay_send.at[8 + j], relay_recv.at[8 + j], 1).wait_send()

    for i, mask in enumerate((0, 8, 16, 24)):
        cross_left(left_n, 0, i, mask).wait_send()
        cross_left(left_a, 1, i, mask).wait_send()
        cross_side(i, mask).wait_send()
    for copy in (cross_mixed, cross_q, cross_kv):
        copy.wait_send()
    for s in range(3):
        for k in range(2):
            y_push(s, k).wait_send()
            p_push(s, k).wait_send()
        x_push(s).wait_send()
        h_push(s).wait_send()
    kv_push(0).wait_send()
    kv_push(1).wait_send()
    kv_cross().wait_send()


def back_call(
    ctx_size, grad_two, resid, hidden, grad_out, normed, mixed, query, kv, total, cosine, sine, pos_q, pos_k,
    small, spread, proj, out_w, grads, grads_two, near, zin_first, r_part,
):
    rows, model = resid.shape
    shard = grads.shape[3]
    one, two = grads.shape[4] // 3, grads_two.shape[4] // 3
    kv_width = KV_HEADS * HD
    q_width = HEADS * HD
    k_cols = 2 * kv_width + HD
    span = ctx_size * shard
    low, full = jnp.bfloat16, jnp.float32
    vmem = pl.BlockSpec(memory_space=pltpu.VMEM)
    anywhere = pl.BlockSpec(memory_space=pl.ANY)
    shapes = (
        ((rows, model), vmem, full),
        ((shard, q_width), vmem, full),
        ((shard, k_cols), vmem, full),
        ((shard, q_width), vmem, full),
        ((8, shard, 3 * one), anywhere, low),
        ((8, shard, 3 * two), anywhere, low),
        ((2, rows, model), anywhere, low),
        ((4, shard, 3 * one), anywhere, low),
        ((8, shard, 3 * two), anywhere, low),
    )
    sem = pltpu.SemaphoreType.DMA
    cols = (q_width, q_width, k_cols)

    def each(*lead):
        return [pltpu.VMEM(lead + (n,), low) for n in cols]

    return pl.pallas_call(
        functools.partial(back_kernel, ctx_size),
        out_shape=tuple(jax.ShapeDtypeStruct(shape, kind) for shape, _, kind in shapes),
        in_specs=[vmem] * 15 + [anywhere] * 7,
        out_specs=tuple(spec for _, spec, _ in shapes),
        scratch_shapes=[
            pltpu.VMEM(proj.shape, low),
            pltpu.VMEM((2, model, rows), low),
            pltpu.VMEM((4, span, 2 * rows), low),
            pltpu.VMEM((4, span, 2 * rows), low),
            pltpu.VMEM((2 * rows, q_width), low),
            pltpu.VMEM((2 * rows, q_width + 2 * kv_width), low),
            pltpu.VMEM((model, HD), low),
            pltpu.VMEM((4, span, HD), low),
            *each(4, span),
            *each(2, span),
            *each(span),
            *each(2, shard),
            *each(shard),
            *([pltpu.VMEM((8, shard, 3 * one), low)] * 3),
            *([pltpu.VMEM((2, 8, shard, 3 * two), low)] * 2),
            pltpu.VMEM((8, shard, 3 * two), low),
            *([pltpu.VMEM((rows, model), low)] * 2),
            pltpu.VMEM((HEADS, rows, HD), low),
            pltpu.VMEM((HD, rows), full),
            pltpu.VMEM((ctx_size * rows, 2 * kv_width), full),
            pltpu.VMEM((ctx_size, rows, 2 * kv_width), low),
            pltpu.VMEM((2, rows, 2 * kv_width), low),
            pltpu.VMEM((rows, 2 * kv_width), low),
            pltpu.VMEM((rows, model), full),
            sem((5,)), *([sem((8,))] * 6), *([sem((2, 8))] * 2), *([sem((8,))] * 4), sem((16,)), sem((16,)),
            sem((4, 4)), sem((4, 4)), sem((3, 6)), sem((3, 6)), sem((3,)), sem((3,)), sem((4,)), sem((4,)), sem((2,)),
        ],
        compiler_params=pltpu.CompilerParams(
            collective_id=2, has_side_effects=True, vmem_limit_bytes=63 << 20
        ),
        name="back",
    )(
        grad_two, resid, hidden, grad_out, normed, mixed, query, kv, total, cosine, sine, pos_q, pos_k, small, spread,
        proj, out_w, grads, grads_two, near, zin_first, r_part,
    )


def finish_kernel(
    ctx_size, fin, fin_two, key, resid, r_part, r_in, hidden, query, outw,
    result_o, hidden_o, attn_o, query_o, bias_q, key_o, bias_k, value_o, bias_v, outw_o, ffn_o, gate_o, up_o, down_o,
    one_v, two_v, tiles, full_v, sems,
):
    dp = lax.axis_index("dp")
    ctx = lax.axis_index("ctx")
    y, c, p = dp // 4, dp % 2, ctx % 2
    full = jnp.float32
    rows, model = resid.shape
    shard = key.shape[0]
    one, two = fin.shape[2] // 3, fin_two.shape[2] // 3
    width = one + two
    kv_width = key_o.shape[1]
    per = bias_k.shape[1]
    moves = [
        pltpu.make_async_copy(fin, one_v, sems.at[0]),
        pltpu.make_async_copy(fin_two, two_v, sems.at[1]),
        pltpu.make_async_copy(r_part.at[0], tiles.at[0], sems.at[2]),
        pltpu.make_async_copy(r_in, tiles.at[pl.ds(1, 2)], sems.at[3]),
    ]
    for copy in moves:
        copy.start()
    hidden_o[...] = hidden[...]
    query_o[...] = query[...]
    outw_o[...] = outw[...]
    key_o[...] = key[:, :kv_width]
    value_o[...] = key[:, kv_width : 2 * kv_width]
    side = jnp.transpose(key[:, 2 * kv_width :])
    attn_o[...] = side[0:1]
    bias_q[...] = side[1:2]
    ffn_o[...] = side[2:3]
    bias_k[...] = side[3:4, :per]
    bias_v[...] = side[3:4, per : 2 * per]
    moves[0].wait()
    moves[1].wait()
    last = gate_o.shape[1] - 7 * width - one
    for j in range(8):
        k = either(y, j // 4) * 4 + either(p, j % 2) * 2 + either(c, (j // 2) % 2)
        for n, out in enumerate((gate_o, up_o, down_o)):
            at = pl.multiple_of(k * width, HD)
            full_v[n, :, pl.ds(at, one)] = one_v[j, :, n * one : (n + 1) * one].astype(full)

            @pl.when(k < 7)
            def _():
                whole = pl.ds(at, width)
                full_v[n, :, pl.ds(at + one, two)] = two_v[j, :, n * two : (n + 1) * two].astype(full)
                pltpu.make_async_copy(full_v.at[n, :, whole], out.at[:, whole], sems.at[4]).start()

            @pl.when(k == 7)
            def _():
                whole = pl.ds(7 * width, one + last)
                full_v[n, :, pl.ds(7 * width + one, last)] = two_v[j, :, n * two : n * two + last].astype(full)
                pltpu.make_async_copy(full_v.at[n, :, whole], out.at[:, whole], sems.at[4]).start()

    moves[2].wait()
    moves[3].wait()
    value = resid[...]
    for o in range(3):
        value = value + tiles[o].astype(full)
    result_o[...] = value.astype(result_o.dtype)
    pltpu.make_async_copy(full_v, full_v, sems.at[4]).wait()


def finish_call(ctx_size, hidden_units, per, fin, fin_two, key, resid, r_part, r_in, hidden, query, outw):
    rows, model = resid.shape
    shard = key.shape[0]
    kv_width = KV_HEADS * HD
    low, full = jnp.bfloat16, jnp.float32
    vmem = pl.BlockSpec(memory_space=pltpu.VMEM)
    anywhere = pl.BlockSpec(memory_space=pl.ANY)
    shapes = (
        ((rows, model), low, vmem),
        ((rows, model), full, vmem),
        ((1, shard), full, vmem),
        (query.shape, full, vmem),
        ((1, shard), full, vmem),
        ((shard, kv_width), full, vmem),
        ((1, per), full, vmem),
        ((shard, kv_width), full, vmem),
        ((1, per), full, vmem),
        (outw.shape, full, vmem),
        ((1, shard), full, vmem),
        ((shard, hidden_units), full, anywhere),
        ((shard, hidden_units), full, anywhere),
        ((shard, hidden_units), full, anywhere),
    )
    return pl.pallas_call(
        functools.partial(finish_kernel, ctx_size),
        out_shape=tuple(jax.ShapeDtypeStruct(shape, kind) for shape, kind, _ in shapes),
        in_specs=[anywhere, anywhere, vmem, vmem, anywhere, anywhere] + [vmem] * 3,
        out_specs=tuple(spec for _, _, spec in shapes),
        scratch_shapes=[
            pltpu.VMEM(fin.shape, low),
            pltpu.VMEM(fin_two.shape, low),
            pltpu.VMEM((3, rows, model), low),
            pltpu.VMEM((3, shard, hidden_units), full),
            pltpu.SemaphoreType.DMA((5,)),
        ],
        compiler_params=pltpu.CompilerParams(vmem_limit_bytes=63 << 20),
        name="finish",
    )(fin, fin_two, key, resid, r_part, r_in, hidden, query, outw)


def fits(mesh):
    return mesh.shape["dp"] == 8 and mesh.shape["ctx"] == 4


def fast_device(
    hidden,
    cotangent,
    span_order,
    attn_gain,
    w_query,
    b_query,
    w_key,
    b_key,
    w_value,
    b_value,
    w_out,
    ffn_gain,
    w_gate,
    w_up,
    w_down,
):
    ctx_size = lax.axis_size("ctx")
    batches = hidden.shape[0]
    length = hidden.shape[1]
    row_count = batches * length
    shard_rows = w_query.shape[0]
    kv_width = KV_HEADS * HD
    q_width = HEADS * HD

    grad_out = cotangent.reshape(row_count, D)
    per = b_key.shape[0]
    pair = jnp.pad(jnp.concatenate([b_key, b_value]), (0, shard_rows - 2 * per))
    sides = jnp.pad(jnp.stack([attn_gain, b_query, ffn_gain, pair]), ((0, HD - 4), (0, 0))).T
    source = hidden.reshape(row_count, D)
    normed, query_heads, key_value, log_total, mixed, resid, normed_two, small, proj_full, out_full, big, big_two, go_all, _, spread, norm_y, *turns = front_call(
        ctx_size, span_order, source, sides, w_query, w_key, w_value, w_out, w_gate, w_up, w_down, grad_out
    )
    grad_two, r_part, grads, grads_two, near, zin, *_ = ffn_call(ctx_size, shard_rows, normed_two, norm_y, go_all, big, big_two)
    hidden_back, query_sum, kv_sum, out_sum, fin, fin_two, r_in, *_ = back_call(
        ctx_size, grad_two, resid, source, grad_out, normed, mixed, query_heads, key_value, log_total,
        turns[0], turns[1], turns[3], turns[2], small, spread,
        proj_full, out_full, grads, grads_two, near, zin, r_part,
    )
    (
        result, hidden_grad, attn_gain_grad, w_query_grad, b_query_grad, w_key_grad, b_key_grad, w_value_grad,
        b_value_grad, w_out_grad, ffn_gain_grad, w_gate_grad, w_up_grad, w_down_grad,
    ) = finish_call(
        ctx_size, w_gate.shape[1], per, fin, fin_two, kv_sum, resid, r_part, r_in, hidden_back, query_sum, out_sum
    )
    return (
        result.reshape(batches, length, D),
        hidden_grad.reshape(batches, length, D),
        attn_gain_grad.reshape(shard_rows),
        w_query_grad,
        b_query_grad.reshape(shard_rows),
        w_key_grad,
        b_key_grad.reshape(per),
        w_value_grad,
        b_value_grad.reshape(per),
        w_out_grad,
        ffn_gain_grad.reshape(shard_rows),
        w_gate_grad,
        w_up_grad,
        w_down_grad,
    )


def general_device(
    hidden,
    cotangent,
    span_order,
    attn_gain,
    w_query,
    b_query,
    w_key,
    b_key,
    w_value,
    b_value,
    w_out,
    ffn_gain,
    w_gate,
    w_up,
    w_down,
):
    ctx_size = lax.axis_size("ctx")
    ctx_rank = lax.axis_index("ctx")
    batches = hidden.shape[0]
    length = hidden.shape[1]
    span_len = length // 2
    seq_len = length * ctx_size
    row_count = batches * length
    groups = HEADS // KV_HEADS
    shard_rows = w_query.shape[0]
    head_scale = HD ** (-0.5)
    kv_width = KV_HEADS * HD
    q_width = HEADS * HD
    places = jnp.arange(seq_len, dtype=jnp.int32)
    every_pos = jnp.repeat(span_order, span_len, axis=1) * span_len + places[None, :] % span_len
    local_pos = lax.dynamic_slice_in_dim(every_pos, ctx_rank * length, length, 1)
    cosine, sine = angles_for(local_pos.reshape(row_count), HD)
    allowed = (every_pos[:, None, :] <= local_pos[:, :, None])[:, None, None]
    attn_full = (
        lax.all_gather(attn_gain, ("dp", "ctx"), axis=0, tiled=True),
        lax.all_gather(w_query, ("dp", "ctx"), axis=0, tiled=True),
        lax.all_gather(w_key, ("dp", "ctx"), axis=0, tiled=True),
        lax.all_gather(w_value, ("dp", "ctx"), axis=0, tiled=True),
        lax.all_gather(w_out, ("dp", "ctx"), axis=0, tiled=True),
        lax.all_gather(b_query, ("dp", "ctx"), axis=0, tiled=True),
        lax.all_gather(b_key, ("dp", "ctx"), axis=0, tiled=True),
        lax.all_gather(b_value, ("dp", "ctx"), axis=0, tiled=True),
    )
    gain_one = attn_full[0].astype(jnp.float32)
    source = hidden.reshape(row_count, D).astype(jnp.float32)
    attn_factor, normed = norm_forward(source, gain_one)
    query_raw = plain_dot(normed, attn_full[1]) + attn_full[5].astype(jnp.float32)
    key_raw = plain_dot(normed, attn_full[2]) + attn_full[6].astype(jnp.float32)
    value_low = (plain_dot(normed, attn_full[3]) + attn_full[7].astype(jnp.float32)).astype(
        jnp.bfloat16
    )
    query_rot = rotate(query_raw.reshape(row_count, HEADS, HD), cosine, sine).astype(jnp.bfloat16)
    query_rot = query_rot.reshape(batches, length, KV_HEADS, groups, HD)
    key_rot = rotate(key_raw.reshape(row_count, KV_HEADS, HD), cosine, sine).astype(jnp.bfloat16)
    key_rot = key_rot.reshape(batches, length, kv_width)
    key_all, value_all = (
        lax.all_gather(key_rot, "ctx", axis=1, tiled=True),
        lax.all_gather(value_low.reshape(batches, length, kv_width), "ctx", axis=1, tiled=True),
    )
    key_all = key_all.reshape(batches, seq_len, KV_HEADS, HD)
    value_all = value_all.reshape(batches, seq_len, KV_HEADS, HD)
    scores = (
        jnp.einsum("bqkgd,bskd->bkgqs", query_rot, key_all, preferred_element_type=jnp.float32)
        * head_scale
    )
    masked = jnp.where(allowed, scores, masked_fill)
    row_max = jnp.max(masked, axis=-1, keepdims=True)
    expo = jnp.exp(masked - row_max)
    expo_sum = jnp.sum(expo, axis=-1, keepdims=True)
    log_total = row_max + jnp.log(expo_sum)
    attend = (expo / expo_sum).astype(jnp.bfloat16)
    mixed = jnp.einsum("bkgqs,bskd->bqkgd", attend, value_all, preferred_element_type=jnp.float32)
    mixed = mixed.reshape(row_count, q_width).astype(jnp.bfloat16)
    resid = source + right_dot(mixed, attn_full[4])
    ffn_full = (
        lax.all_gather(ffn_gain, ("dp", "ctx"), axis=0, tiled=True),
        lax.all_gather(w_gate, ("dp", "ctx"), axis=0, tiled=True),
        lax.all_gather(w_up, ("dp", "ctx"), axis=0, tiled=True),
        lax.all_gather(w_down, ("dp", "ctx"), axis=0, tiled=True),
    )
    gain_two = ffn_full[0].astype(jnp.float32)
    ffn_factor, normed_two = norm_forward(resid, gain_two)
    gate_pre = plain_dot(normed_two, ffn_full[1])
    up_pre = plain_dot(normed_two, ffn_full[2])
    sigmoid_gate = jax.nn.sigmoid(gate_pre)
    silu_gate = gate_pre * sigmoid_gate
    act = (silu_gate * up_pre).astype(jnp.bfloat16)
    output = resid + right_dot(act, ffn_full[3])
    result = output.astype(jnp.bfloat16).reshape(batches, length, D)
    ffn_back = (
        lax.all_gather(ffn_gain, ("dp", "ctx"), axis=0, tiled=True),
        lax.all_gather(w_gate, ("dp", "ctx"), axis=0, tiled=True),
        lax.all_gather(w_up, ("dp", "ctx"), axis=0, tiled=True),
        lax.all_gather(w_down, ("dp", "ctx"), axis=0, tiled=True),
    )
    grad_out = cotangent.reshape(row_count, D)
    grad_plain = grad_out.astype(jnp.float32)
    grad_act = plain_dot(grad_out, ffn_back[3])
    grad_gate = (grad_act * up_pre * sigmoid_gate * (1.0 + gate_pre * (1.0 - sigmoid_gate))).astype(
        jnp.bfloat16
    )
    grad_up = (grad_act * silu_gate).astype(jnp.bfloat16)
    pieces = (
        lax.all_gather(normed_two, "ctx", axis=0, tiled=True),
        lax.all_gather(grad_gate, "ctx", axis=0, tiled=True),
        lax.all_gather(grad_up, "ctx", axis=0, tiled=True),
        lax.all_gather(act, "ctx", axis=0, tiled=True),
        lax.all_gather(grad_out, "ctx", axis=0, tiled=True),
    )
    picked_in = owned_columns(pieces[0], ctx_size, ctx_rank, shard_rows)
    picked_out = owned_columns(pieces[4], ctx_size, ctx_rank, shard_rows)
    w_gate_grad, w_up_grad, w_down_grad = (
        lax.psum_scatter(
            outer_add(picked_in, pieces[1]).astype(jnp.bfloat16),
            "dp",
            scatter_dimension=0,
            tiled=True,
        ).astype(jnp.float32),
        lax.psum_scatter(
            outer_add(picked_in, pieces[2]).astype(jnp.bfloat16),
            "dp",
            scatter_dimension=0,
            tiled=True,
        ).astype(jnp.float32),
        lax.psum_scatter(
            outer_add(picked_out, pieces[3]).astype(jnp.bfloat16),
            "dp",
            scatter_dimension=0,
            tiled=True,
        ).astype(jnp.float32),
    )
    grad_norm_two = right_dot(grad_gate, ffn_back[1]) + right_dot(grad_up, ffn_back[2])
    resid_back, ffn_gain_part = norm_backward(resid, ffn_factor, gain_two, grad_norm_two)
    grad_resid = grad_plain + resid_back
    attn_back = (
        lax.all_gather(attn_gain, ("dp", "ctx"), axis=0, tiled=True),
        lax.all_gather(w_query, ("dp", "ctx"), axis=0, tiled=True),
        lax.all_gather(w_key, ("dp", "ctx"), axis=0, tiled=True),
        lax.all_gather(w_value, ("dp", "ctx"), axis=0, tiled=True),
        lax.all_gather(w_out, ("dp", "ctx"), axis=0, tiled=True),
        lax.all_gather(b_query, ("dp", "ctx"), axis=0, tiled=True),
        lax.all_gather(b_key, ("dp", "ctx"), axis=0, tiled=True),
        lax.all_gather(b_value, ("dp", "ctx"), axis=0, tiled=True),
    )
    grad_attn = grad_resid.astype(jnp.bfloat16)
    grad_mixed = plain_dot(grad_attn, attn_back[4]).astype(jnp.bfloat16)
    grad_mixed = grad_mixed.reshape(batches, length, KV_HEADS, groups, HD)
    scores = (
        jnp.einsum("bqkgd,bskd->bkgqs", query_rot, key_all, preferred_element_type=jnp.float32)
        * head_scale
    )
    masked = jnp.where(allowed, scores, masked_fill)
    attend_full = jnp.exp(masked - log_total)
    attend = attend_full.astype(jnp.bfloat16)
    grad_attend = jnp.einsum(
        "bqkgd,bskd->bkgqs", grad_mixed, value_all, preferred_element_type=jnp.float32
    )
    value_grad_all = jnp.einsum(
        "bkgqs,bqkgd->bskd", attend, grad_mixed, preferred_element_type=jnp.float32
    )
    delta = jnp.sum(grad_attend * attend_full, axis=-1, keepdims=True)
    grad_scores = (attend_full * (grad_attend - delta)).astype(jnp.bfloat16)
    query_grad_rot = (
        jnp.einsum("bkgqs,bskd->bqkgd", grad_scores, key_all, preferred_element_type=jnp.float32)
        * head_scale
    )
    key_grad_all = (
        jnp.einsum("bkgqs,bqkgd->bskd", grad_scores, query_rot, preferred_element_type=jnp.float32)
        * head_scale
    )
    key_grad_rot, value_grad = (
        lax.psum_scatter(
            key_grad_all.reshape(batches, seq_len, kv_width), "ctx", scatter_dimension=1, tiled=True
        ),
        lax.psum_scatter(
            value_grad_all.reshape(batches, seq_len, kv_width),
            "ctx",
            scatter_dimension=1,
            tiled=True,
        ),
    )
    query_grad = (
        rotate_back(query_grad_rot.reshape(row_count, HEADS, HD), cosine, sine)
        .reshape(row_count, q_width)
        .astype(jnp.bfloat16)
    )
    key_grad = (
        rotate_back(key_grad_rot.reshape(row_count, KV_HEADS, HD), cosine, sine)
        .reshape(row_count, kv_width)
        .astype(jnp.bfloat16)
    )
    value_grad = value_grad.reshape(row_count, kv_width).astype(jnp.bfloat16)
    proj_grad = jnp.concatenate([query_grad, key_grad, value_grad], axis=1)
    pieces = (
        lax.all_gather(normed, "ctx", axis=0, tiled=True),
        lax.all_gather(proj_grad, "ctx", axis=0, tiled=True),
        lax.all_gather(grad_attn, "ctx", axis=0, tiled=True),
        lax.all_gather(mixed, "ctx", axis=0, tiled=True),
    )
    picked_in = owned_columns(pieces[0], ctx_size, ctx_rank, shard_rows)
    picked_out = owned_columns(pieces[2], ctx_size, ctx_rank, shard_rows)
    proj_sum, w_out_grad = (
        lax.psum_scatter(
            outer_add(picked_in, pieces[1]).astype(jnp.bfloat16),
            "dp",
            scatter_dimension=0,
            tiled=True,
        ).astype(jnp.float32),
        lax.psum_scatter(
            outer_add(picked_out, pieces[3]).astype(jnp.bfloat16),
            "dp",
            scatter_dimension=0,
            tiled=True,
        ).astype(jnp.float32),
    )
    grad_norm_one = (
        right_dot(query_grad, attn_back[1])
        + right_dot(key_grad, attn_back[2])
        + right_dot(value_grad, attn_back[3])
    )
    source_back, attn_gain_part = norm_backward(source, attn_factor, gain_one, grad_norm_one)
    hidden_grad = (grad_resid + source_back).reshape(batches, length, D)
    query_bias_part = jnp.sum(query_grad.astype(jnp.float32), axis=0)
    key_bias_part = jnp.sum(key_grad.astype(jnp.float32), axis=0)
    value_bias_part = jnp.sum(value_grad.astype(jnp.float32), axis=0)
    small_sums = (
        lax.psum_scatter(attn_gain_part, ("dp", "ctx"), scatter_dimension=0, tiled=True),
        lax.psum_scatter(query_bias_part, ("dp", "ctx"), scatter_dimension=0, tiled=True),
        lax.psum_scatter(key_bias_part, ("dp", "ctx"), scatter_dimension=0, tiled=True),
        lax.psum_scatter(value_bias_part, ("dp", "ctx"), scatter_dimension=0, tiled=True),
        lax.psum_scatter(ffn_gain_part, ("dp", "ctx"), scatter_dimension=0, tiled=True),
    )
    w_query_grad = proj_sum[:, :q_width]
    w_key_grad = proj_sum[:, q_width : q_width + kv_width]
    w_value_grad = proj_sum[:, q_width + kv_width :]
    return (
        result,
        hidden_grad,
        small_sums[0],
        w_query_grad,
        small_sums[1],
        w_key_grad,
        small_sums[2],
        w_value_grad,
        small_sums[3],
        w_out_grad,
        small_sums[4],
        w_gate_grad,
        w_up_grad,
        w_down_grad,
    )


def solution(mesh):
    placed = (
        P("dp", "ctx", None),
        P("dp", "ctx", None),
        P("dp", None),
        P(("dp", "ctx")),
        P(("dp", "ctx"), None),
        P(("dp", "ctx")),
        P(("dp", "ctx"), None),
        P(("dp", "ctx")),
        P(("dp", "ctx"), None),
        P(("dp", "ctx")),
        P(("dp", "ctx"), None),
        P(("dp", "ctx")),
        P(("dp", "ctx"), None),
        P(("dp", "ctx"), None),
        P(("dp", "ctx"), None),
    )
    return jax.shard_map(
        fast_device if fits(mesh) else general_device,
        mesh=mesh,
        in_specs=placed,
        out_specs=(
            P("dp", "ctx", None),
            P("dp", "ctx", None),
            P(("dp", "ctx")),
            P(("dp", "ctx"), None),
            P(("dp", "ctx")),
            P(("dp", "ctx"), None),
            P(("dp", "ctx")),
            P(("dp", "ctx"), None),
            P(("dp", "ctx")),
            P(("dp", "ctx"), None),
            P(("dp", "ctx")),
            P(("dp", "ctx"), None),
            P(("dp", "ctx"), None),
            P(("dp", "ctx"), None),
        ),
        check_vma=False,
    )
```

```python
import functools
import math

import jax
import jax.numpy as jnp
from jax import lax
from jax.experimental import pallas as pl
from jax.experimental.pallas import tpu as pltpu
from jax.sharding import PartitionSpec as P

D = 1536
HEADS = 12
KV_HEADS = 2
HD = 128


norm_eps = 1e-06
rope_base = 10000.0
masked_fill = -1e30


def angles_for(places, width):
    half = width // 2
    freqs = rope_base ** (-(jnp.arange(half, dtype=jnp.float32) * 2.0 / width))
    angles = places.astype(jnp.float32)[:, None] * freqs[None, :]
    return (jnp.cos(angles)[:, None, :], jnp.sin(angles)[:, None, :])


def rotate(values, cosine, sine):
    half = values.shape[-1] // 2
    first = values[..., :half]
    second = values[..., half:]
    return jnp.concatenate(
        [first * cosine - second * sine, second * cosine + first * sine], axis=-1
    )


def rotate_back(values, cosine, sine):
    half = values.shape[-1] // 2
    first = values[..., :half]
    second = values[..., half:]
    return jnp.concatenate(
        [first * cosine + second * sine, second * cosine - first * sine], axis=-1
    )


def norm_forward(source, gain):
    factor = lax.rsqrt(jnp.mean(source * source, axis=-1, keepdims=True) + norm_eps)
    return (factor, (source * factor * gain).astype(jnp.bfloat16))


def norm_backward(source, factor, gain, grad_normed):
    unit = source * factor
    gain_grad = jnp.sum(grad_normed * unit, axis=0)
    scaled = grad_normed * gain
    source_grad = factor * (scaled - unit * jnp.mean(scaled * unit, axis=-1, keepdims=True))
    return (source_grad, gain_grad)


def right_dot(left, weight):
    return jnp.einsum("rf,df->rd", left, weight, preferred_element_type=jnp.float32)


def plain_dot(left, weight):
    return jnp.dot(left, weight, preferred_element_type=jnp.float32)


def owned_columns(values, ctx_size, ctx_rank, shard_rows):
    rows = values.shape[0]
    blocks = values.shape[1] // (shard_rows * ctx_size)
    shaped = values.reshape(rows, blocks, ctx_size, shard_rows)
    picked = lax.dynamic_index_in_dim(shaped, ctx_rank, axis=2, keepdims=False)
    return picked.reshape(rows, blocks * shard_rows)


def outer_add(left, right):
    return jnp.einsum("rc,rf->cf", left, right, preferred_element_type=jnp.float32)


MESH = pl.DeviceIdType.MESH


def flip(index, mask):
    for bit in (1, 2, 4, 8, 16):
        if mask & bit:
            index = index + bit - 2 * bit * ((index // bit) % 2)
    return index


def either(a, b):
    return a + b - 2 * a * b


def dot(a, b, dims):
    return lax.dot_general(a, b, (dims, ((), ())), preferred_element_type=jnp.float32)


def widths(hidden_units):
    width = -(-hidden_units // (8 * 128)) * 128
    first = width // 384 * 256
    return (first, width - first)


def ffn_kernel(
    ctx_size, n_own, norm_y, go_all, big, big_two,
    grad_two, r_part, grads, grads_two, near, zin,
    w_one, w_two, nt, go, ggu, act, crecv, part, h_in, h_mid, stage, own, far,
    io_sem, n_send, n_recv, f_send, f_recv, c_send, c_recv, o_send, o_recv, st_sem, w_send, w_recv, l_sem, x_send, x_recv, z_send, z_recv, d_sem,
):
    dp = lax.axis_index("dp")
    ctx = lax.axis_index("ctx")
    me = dp * ctx_size + ctx
    y, x, c = dp // 4, (dp // 2) % 2, dp % 2
    h, p = ctx // 2, ctx % 2
    one, two = w_one.shape[1] // 3, w_two.shape[1] // 3
    shard = grads.shape[3]
    rows, model = n_own.shape
    low, full = jnp.bfloat16, jnp.float32

    def at(index):
        return (index // ctx_size, index % ctx_size)

    def remote(src, dst, send, recv, mask):
        return pltpu.make_async_remote_copy(
            src_ref=src, dst_ref=dst, send_sem=send, recv_sem=recv, device_id=at(flip(me, mask)), device_id_type=MESH
        )

    def block(mask):
        return pl.ds(pl.multiple_of(flip(me, mask) * shard, shard), shard)

    barrier = pltpu.get_barrier_semaphore()
    partners = (1, 2, 4, 8, 16)
    for mask in partners:
        pl.semaphore_signal(barrier, inc=1, device_id=at(flip(me, mask)), device_id_type=MESH)
    load_n = pltpu.make_async_copy(n_own, nt.at[0], io_sem.at[0])
    load_y = pltpu.make_async_copy(norm_y, nt.at[4], io_sem.at[3])
    load_w = pltpu.make_async_copy(big, w_one, io_sem.at[1])
    load_go = pltpu.make_async_copy(go_all, go, io_sem.at[2])
    held = (0, 4, 1, 5, 16, 20, 17, 21, 2, 6, 3, 7)
    load_l = [
        pltpu.make_async_copy(big_two.at[block(mask)], w_two.at[block(mask)], l_sem.at[i]) for i, mask in enumerate(held)
    ]
    for copy in (load_n, load_y, load_w, load_go, *load_l):
        copy.start()
    pl.semaphore_wait(barrier, len(partners))

    def spread_two(mask, over):
        remote(big_two.at[block(mask)], w_two.at[block(mask)], w_send.at[0], w_recv.at[mask | over], over).start()

    def w_wait(mask):
        remote(w_two.at[block(mask)], w_two.at[block(mask)], w_send.at[0], w_recv.at[mask], 1).wait_recv()

    def w_pass(mask):
        w_wait(mask)
        remote(w_two.at[block(mask)], w_two.at[block(mask)], w_send.at[0], w_recv.at[mask | 8], 8).start()

    def n_core(slot):
        return remote(nt.at[slot], nt.at[slot + 1], f_send.at[slot // 2], f_recv.at[slot // 2], 4)

    def n_push(o):
        half = pl.ds((o - 1) % 2 * (rows // 2), rows // 2)
        if o == 1:
            return remote(nt.at[0], nt.at[2], n_send.at[1], n_recv.at[1], 1)
        return remote(nt.at[(0, 0, 4, 2)[o], half], nt.at[6, half], n_send.at[o], n_recv.at[o], (0, 0, 1, 16)[o])

    load_n.wait()
    n_push(1).start()
    n_core(0).start()
    load_y.wait()
    n_push(2).start()
    n_core(4).start()
    for mask in (16, 20, 17, 21):
        spread_two(mask, 2)
    for mask in held:
        spread_two(mask, 8)
    load_w.wait()
    load_go.wait()

    def first(slot):
        gu = dot(nt[slot], w_one[:, : 2 * one], ((1,), (0,)))
        ga = dot(go[slot], w_one[:, 2 * one :], ((1,), (0,)))
        finish(slot, gu[:, :one], gu[:, one:], ga, 0, 0)

    def finish(slot, gate, up, ga, at_gu, at_act):
        size = gate.shape[1]
        sig = 1.0 / (1.0 + jnp.exp(-gate))
        silu = gate * sig
        act[slot, :, pl.ds(at_act, size)] = (silu * up).astype(low)
        ggu[slot, :, pl.ds(at_gu, size)] = (ga * up * sig * (1.0 + gate * (1.0 - sig))).astype(low)
        ggu[slot, :, pl.ds(at_gu + size, size)] = (ga * silu).astype(low)

    def second(slot):
        gu = dot(nt[slot], w_two[:, : 2 * two], ((1,), (0,)))
        ga = dot(go[slot], w_two[:, 2 * two :], ((1,), (0,)))
        finish(slot, gu[:, :two], gu[:, two:], ga, 2 * one, one)
        grad = dot(ggu[slot, :, : 2 * one], w_one[:, : 2 * one], ((1,), (1,)))
        grad = grad + dot(ggu[slot, :, 2 * one :], w_two[:, : 2 * two], ((1,), (1,)))
        out = dot(act[slot, :, :one], w_one[:, 2 * one :], ((1,), (1,)))
        out = out + dot(act[slot, :, one:], w_two[:, 2 * two :], ((1,), (1,)))
        return (grad.astype(low), out.astype(low))

    def early(n, carry):
        o = n % 2 * 2 + n // 2

        @pl.when(o == 1)
        def _():
            n_push(1).wait_recv()
            n_push(3).start()
            n_core(2).start()

        @pl.when(o == 3)
        def _():
            n_push(2).wait_recv()
            n_push(3).wait_recv()
            n_core(6).start()

        first(2 * o)


        n_core(2 * o).wait_recv()
        first(2 * o + 1)
        return carry

    lax.fori_loop(0, 4, early, 0)
    def stage_wait(slot, size):
        part_of = stage.at[slot, :, pl.ds(0, size)]
        pltpu.make_async_copy(part_of, part_of, st_sem.at[slot]).wait()

    def weights(size, start_gu, start_act, to, passes, q, carry):
        slot = q % 2

        @pl.when(q > 1)
        def _():
            stage_wait(slot, 3 * size)

        chunk = 8 * shard
        cols = pl.ds(pl.multiple_of(q * chunk, chunk), chunk)

        def product(left, right, start, count, at_col):
            left = left[:, :, cols].reshape(8 * rows, chunk)
            right = right[:, :, pl.ds(start, count)].reshape(8 * rows, count)
            stage[slot, :, pl.ds(at_col, count)] = dot(left, right, ((0,), (0,))).astype(low)

        for start in range(0, 2 * size, one):
            count = min(one, 2 * size - start)
            product(nt, ggu, start_gu + start, count, start)
        product(go, act, start_act, size, 2 * size)
        for n, masks in enumerate(passes):
            @pl.when(q == n)
            def _():
                for mask in masks:
                    w_pass(mask)

        yr, xr = either(q // 2, y), either(q % 2, x)
        for j in range(8):
            cr, hrel, pr = either(j // 4, c), either((j // 2) % 2, h), either(j % 2, p)
            pltpu.make_async_copy(
                stage.at[slot, pl.ds(j * shard, shard), pl.ds(0, 3 * size)],
                to.at[xr, hrel, yr * 4 + cr * 2 + pr], st_sem.at[slot],
            ).start()
        return carry

    def all_weights(size, start_gu, start_act, to, passes=()):
        lax.fori_loop(0, 4, functools.partial(weights, size, start_gu, start_act, to, passes), 0)
        stage_wait(0, 3 * size)
        stage_wait(1, 3 * size)

    def far_push(j):
        return remote(grads.at[1, 1, j], far.at[j], x_send.at[j], x_recv.at[j], 8)

    def z_push(j):
        return remote(far.at[j], zin.at[j], z_send.at[j], z_recv.at[j], 2)

    def load_own(k):
        return pltpu.make_async_copy(grads.at[0, 1, pl.ds(4 * k, 4)], own, d_sem.at[0])

    keep_near = pltpu.make_async_copy(far, near, d_sem.at[0])

    def far_pass(*blocks):
        for j in blocks:
            far_push(j).wait_recv()
            far[j] = (far[j].astype(full) + own[j % 4].astype(full)).astype(low)
            if j < 4:
                z_push(j).start()

    all_weights(one, 0, 0, grads, ((18, 22, 19, 23),))
    for j in range(8):
        far_push(j).start()
    load_own(0).start()

    for mask in (8, 12, 9, 13, 24, 28, 25, 29, 10, 14, 11, 15, 26, 30, 27, 31):
        w_wait(mask)
    for copy in load_l:
        copy.wait()

    def cross(o):
        return remote(stage.at[:, pl.ds(0, rows), pl.ds(0, model)], crecv.at[o % 2], c_send, c_recv.at[o % 2], 4)

    def final(o):
        dst = h_mid if o == 3 else h_in.at[o - 1]
        return remote(part.at[o, 0], dst, o_send.at[o], o_recv.at[o], (0, 1, 16, 16)[o])

    def keep(o):
        return pltpu.make_async_copy(part.at[o, 1], r_part.at[o], io_sem.at[o])

    def combine(o):
        cross(o).wait_recv()
        part[o] = (part[o].astype(full) + crecv[o % 2].astype(full)).astype(low)
        keep(o).start()

    def late(n, carry):
        o = 3 - n
        grad, out = second(2 * o)
        part[o, 0] = grad
        part[o, 1] = out

        @pl.when(n > 0)
        def _():
            combine(o + 1)

        @pl.when(n == 1)
        def _():
            final(3).start()
            load_own(0).wait()
            far_pass(0, 1)

        @pl.when(n == 2)
        def _():
            final(2).start()
            far_pass(2, 3)
            load_own(1).start()

        @pl.when(n == 3)
        def _():
            final(3).wait_recv()
            part[1, 0] = (part[1, 0].astype(full) + h_mid[...].astype(full)).astype(low)
            final(1).start()
            load_own(1).wait()
            far_pass(4, 5)

        grad, out = second(2 * o + 1)

        @pl.when(n > 0)
        def _():
            cross(o).wait_send()

        stage[0, pl.ds(0, rows), pl.ds(0, model)] = grad
        stage[1, pl.ds(0, rows), pl.ds(0, model)] = out
        cross(o).start()
        return carry

    lax.fori_loop(0, 4, late, 0)

    far_pass(6, 7)
    keep_near.start()
    cross(0).wait_send()
    all_weights(two, 2 * one, one, grads_two)
    combine(0)
    grad_two[...] = part[0, 0].astype(full)
    for o in (1, 2):
        final(o).wait_recv()
        grad_two[...] += h_in[o - 1].astype(full)
    keep_near.wait()
    for j in range(8):
        far_push(j).wait_send()
        if j < 4:
            z_push(j).wait()
    for o in range(4):
        keep(o).wait()
        n_core(2 * o).wait_send()
    for o in (1, 2, 3):
        n_push(o).wait_send()
        final(o).wait_send()
    sent = w_two.at[pl.ds(0, 20 * shard)]
    pltpu.make_async_copy(sent, sent, w_send.at[0]).wait()


def ffn_call(ctx_size, shard, n_own, norm_y, go_all, big, big_two):
    rows, model = n_own.shape
    one, two = big.shape[1] // 3, big_two.shape[1] // 3
    low = jnp.bfloat16
    anywhere = pl.BlockSpec(memory_space=pl.ANY)
    sem = pltpu.SemaphoreType.DMA
    return pl.pallas_call(
        functools.partial(ffn_kernel, ctx_size),
        out_shape=(
            jax.ShapeDtypeStruct((rows, model), jnp.float32),
            jax.ShapeDtypeStruct((4, rows, model), low),
            jax.ShapeDtypeStruct((2, 2, 8, shard, 3 * one), low),
            jax.ShapeDtypeStruct((2, 2, 8, shard, 3 * two), low),
            jax.ShapeDtypeStruct((8, shard, 3 * one), low),
            jax.ShapeDtypeStruct((4, shard, 3 * one), low),
        ),
        in_specs=[anywhere] * 5,
        out_specs=[pl.BlockSpec(memory_space=pltpu.VMEM)] + [anywhere] * 5,
        scratch_shapes=[
            pltpu.VMEM((model, 3 * one), low),
            pltpu.VMEM((model, 3 * two), low),
            pltpu.VMEM((8, rows, model), low),
            pltpu.VMEM((8, rows, model), low),
            pltpu.VMEM((8, rows, 2 * (one + two)), low),
            pltpu.VMEM((8, rows, one + two), low),
            pltpu.VMEM((2, 2, rows, model), low),
            pltpu.VMEM((4, 2, rows, model), low),
            pltpu.VMEM((2, rows, model), low),
            pltpu.VMEM((rows, model), low),
            pltpu.VMEM((2, 8 * shard, 3 * one), low),
            pltpu.VMEM((4, shard, 3 * one), low),
            pltpu.VMEM((8, shard, 3 * one), low),
            sem((4,)), sem((5,)), sem((5,)), sem((4,)), sem((4,)), sem, sem((2,)), sem((4,)), sem((4,)), sem((2,)),
            sem((1,)), sem((32,)), sem((12,)), sem((8,)), sem((8,)), sem((4,)), sem((4,)), sem((1,)),
        ],
        compiler_params=pltpu.CompilerParams(
            collective_id=1, has_side_effects=True, vmem_limit_bytes=65200 << 10
        ),
        name="ffn",
    )(n_own, norm_y, go_all, big, big_two)


def turn(values, cosine, sine):
    return values * cosine + pltpu.roll(values, HD // 2, 1) * sine


def front_kernel(
    ctx_size, span, hidden, sides, w_query, w_key, w_value, w_out, w_gate, w_up, w_down, grad_out,
    normed_o, query_o, kv_o, total_o, mixed_o, resid_o, normed_two_o, small_o, proj_o, out_o, big, big_two, go, relay, spread, norm_y, cosine, sine, pos_k, pos_q,
    proj, out_w, source, source_two, query, kv, mixed,
    load_sem, ag_send, ag_recv, core_send, core_recv, big_send, big_recv, two_recv, relay_recv, go_send, go_recv, kv_send, kv_recv, back_sem, norm_sem,
):
    dp = lax.axis_index("dp")
    ctx = lax.axis_index("ctx")
    me = dp * ctx_size + ctx
    shard, wide = w_out.shape[0], proj.shape[1]
    rows, model = hidden.shape
    one, two = big.shape[1] // 3, big_two.shape[1] // 3
    kv_width = KV_HEADS * HD
    q_width = HEADS * HD
    proj_width = q_width + 2 * kv_width
    groups = HEADS // KV_HEADS

    def at(index):
        return (index // ctx_size, index % ctx_size)

    def block(mask, count=1):
        base = flip(me, mask) // count * count
        return pl.ds(pl.multiple_of(base * shard, shard), shard * count)

    def remote(src, dst, send, recv, mask):
        return pltpu.make_async_remote_copy(
            src_ref=src, dst_ref=dst, send_sem=send, recv_sem=recv, device_id=at(flip(me, mask)), device_id_type=MESH
        )

    def drain(ref, sem):
        pltpu.make_async_copy(ref, ref, sem).wait()

    barrier = pltpu.get_barrier_semaphore()
    partners = (1, 2, 3, 4, 5, 8, 16, 17, 20, 21)
    for mask in partners:
        pl.semaphore_signal(barrier, inc=1, device_id=at(flip(me, mask)), device_id_type=MESH)

    own = (
        pltpu.make_async_copy(w_query, proj.at[block(0), pl.ds(0, q_width)], load_sem.at[0]),
        pltpu.make_async_copy(w_out, out_w.at[block(0)], load_sem.at[1]),
        pltpu.make_async_copy(w_key, proj.at[block(0), pl.ds(q_width, kv_width)], load_sem.at[50]),
        pltpu.make_async_copy(w_value, proj.at[block(0), pl.ds(q_width + kv_width, kv_width)], load_sem.at[51]),
    )
    for copy in own:
        copy.start()
    table = jnp.concatenate([sides[...].astype(jnp.float32), jnp.zeros((HD - 8, shard), jnp.float32)], axis=0)
    proj[block(0), pl.ds(proj_width, HD)] = jnp.transpose(table).astype(jnp.bfloat16)
    hidden_units = w_gate.shape[1]
    cuts = []
    for k in range(8):
        for n, ref in enumerate((w_gate, w_up, w_down)):
            for to, start, width in ((source, k * (one + two), one), (source_two, k * (one + two) + one, two)):
                size = min(width, hidden_units - start)
                cuts.append((ref.at[:, pl.ds(start, size)], to.at[k, :, pl.ds(n * width, size)]))
                if size < width:
                    to[k, :, pl.ds(n * width + size, width - size)] = jnp.zeros((shard, width - size), to.dtype)
    cuts = [pltpu.make_async_copy(a, b, load_sem.at[2 + i]) for i, (a, b) in enumerate(cuts)]
    for copy in cuts:
        copy.start()
    pl.semaphore_wait(barrier, len(partners))
    for copy in own:
        copy.wait()

    q_cols, k_cols = pl.ds(0, q_width), pl.ds(q_width, wide - q_width)
    streams = ((proj, k_cols), (proj, q_cols), (out_w, q_cols))

    def ag(n, mask, *overs):
        ref, cols = streams[n]
        part = ref.at[block(mask), cols]
        for over in overs:
            remote(part, part, ag_send.at[n], ag_recv.at[n, mask | over], over).start()

    def ag_pass(n, mask, *overs):
        ref, cols = streams[n]
        part = ref.at[block(mask), cols]
        remote(part, part, ag_send.at[n], ag_recv.at[n, mask], 1).wait_recv()
        ag(n, mask, *overs)

    def group(n, mask):
        ref, cols = streams[n]
        part = ref.at[block(mask, 4), cols]
        return remote(part, part, core_send.at[n, mask // 8], core_recv.at[n, mask // 8], 4)

    def group_wait(n):
        ref, cols = streams[n]
        for mask in (0, 8, 16, 24):
            part = ref.at[block(mask | 4, 4), cols]
            remote(part, part, core_send.at[n, mask // 8], core_recv.at[n, mask // 8], 4).wait_recv()

    ag(0, 0, 2, 1, 8, 16)
    ag(1, 0, 2, 1, 8, 16)

    for copy in cuts:
        copy.wait()
    y, x, c = dp // 4, (dp // 2) % 2, dp % 2
    h, p = ctx // 2, ctx % 2

    def column(mask):
        return either(y, mask // 16) * 4 + either(p, mask % 2) * 2 + either(c, (mask // 4) % 2)

    own_big = pltpu.make_async_copy(source.at[column(0)], big.at[block(0)], load_sem.at[0])
    own_big.start()
    own_two = pltpu.make_async_copy(source_two.at[column(0)], big_two.at[block(0)], load_sem.at[1])
    own_two.start()

    def cut(mask):
        remote(source.at[column(mask)], big.at[block(0)], big_send.at[0], big_recv.at[mask], mask).start()

    def cut_two(mask):
        return remote(source_two.at[column(mask)], big_two.at[block(0)], big_send.at[1], two_recv.at[mask], mask)

    held = (0, 4, 1, 5, 16, 20, 17, 21)
    inner = either(h, p) == 1

    def over_z(mask):
        src = big.at[block(mask)] if mask else source.at[column(0)]

        @pl.when(inner)
        def _():
            remote(src, big.at[block(mask)], big_send.at[0], big_recv.at[mask | 2], 2).start()

        @pl.when(jnp.logical_not(inner))
        def _():
            i = held.index(mask)
            remote(src, relay.at[i], big_send.at[0], relay_recv.at[i], 1).start()

    def relay_pass(*masks):
        @pl.when(inner)
        def _():
            for mask in masks:
                i = held.index(mask)
                remote(relay.at[i], relay.at[i], big_send.at[0], relay_recv.at[i], 1).wait_recv()
                remote(relay.at[i], big.at[block(mask ^ 1)], big_send.at[2], big_recv.at[mask | 2], 3).start()

    def big_forward(mask, over):
        if over == 2:
            over_z(mask)
        else:
            remote(big.at[block(mask)], big.at[block(mask)], big_send.at[0], big_recv.at[mask | over], over).start()

    def big_pass(mask, *overs):
        remote(big.at[block(mask)], big.at[block(mask)], big_send.at[0], big_recv.at[mask], 1).wait_recv()
        for over in overs:
            big_forward(mask, over)

    cut(4)
    over_z(0)

    row = lax.broadcasted_iota(jnp.int32, (model, 2 * kv_width), 0)
    col = lax.broadcasted_iota(jnp.int32, (model, 2 * kv_width), 1)
    per = kv_width * shard // model
    unit = (col % kv_width) // per * shard + col // kv_width * per + col % per
    spread[...] = jnp.where(row == unit, 1.0, 0.0).astype(jnp.bfloat16)
    length = rows // 2
    for j in range(2 * ctx_size):
        lane = lax.broadcasted_iota(jnp.int32, (1, length), 1)
        pos_k[:, pl.ds(j * length, length)] = (span[0, j] * length + lane).astype(jnp.float32)
    pos_q[...] = pos_k[:, pl.ds(pl.multiple_of(ctx * rows, rows), rows)]
    own_pos = jnp.transpose(jnp.broadcast_to(pos_q[...], (HD, rows)))
    lane = lax.broadcasted_iota(jnp.int32, (rows, HD), 1)
    turns = (lane % (HD // 2)).astype(jnp.float32) * (2.0 / HD)
    angles = own_pos * jnp.exp(turns * -math.log(rope_base))
    cosine[...] = jnp.cos(angles)
    sine[...] = jnp.sin(angles) * jnp.where(lane < HD // 2, -1.0, 1.0)
    own_pos = own_pos[:, :1]

    ag_pass(0, 1, 8, 16)
    ag_pass(0, 8, 16)
    ag_pass(0, 2, 1, 8, 16)
    ag_pass(0, 9, 16)
    ag_pass(1, 1, 8, 16)
    ag_pass(1, 8, 16)
    ag_pass(0, 3, 8, 16)
    ag_pass(0, 10, 16)
    ag_pass(1, 2, 1, 8, 16)
    group(0, 0).start()
    remote(source.at[column(0)], big.at[block(0)], big_send.at[0], big_recv.at[8], 8).start()
    cut(1)
    cut(5)
    big_pass(4, 2, 8)
    ag_pass(0, 11, 16)
    group(0, 8).start()
    relay_pass(0)
    ag_pass(1, 9, 16)
    ag(2, 0, 2, 1, 16, 8)
    for mask in (16, 17, 18, 19):
        ag_pass(0, mask)
    group(0, 16).start()
    ag_pass(1, 3, 8, 16)
    group(1, 0).start()
    for mask in (24, 25, 26, 27):
        ag_pass(0, mask)
    group(0, 24).start()
    relay_pass(4)
    group_wait(0)

    small = jnp.transpose(proj[:, proj_width:].astype(jnp.float32))
    small_o[...] = small[:8]
    kv_bias = dot(small[:8].astype(jnp.bfloat16), spread[...], ((1,), (0,)))[3:4]
    values = hidden[...].astype(jnp.float32)
    factor = lax.rsqrt(jnp.mean(values * values, axis=-1, keepdims=True) + norm_eps)
    normed_o[...] = (values * factor * small[0:1]).astype(jnp.bfloat16)
    cos, sin = cosine[...], sine[...]
    raw = dot(normed_o[...], proj[:, q_width:proj_width], ((1,), (0,))) + kv_bias
    mine = block(0)
    for g in range(KV_HEADS):
        kv[ctx, :, pl.ds(g * HD, HD)] = turn(raw[:, g * HD : (g + 1) * HD], cos, sin).astype(jnp.bfloat16)
    kv[ctx, :, pl.ds(kv_width, kv_width)] = raw[:, kv_width:].astype(jnp.bfloat16)
    def kv_push(mask, over):
        slot = flip(ctx, mask)
        return remote(kv.at[slot], kv.at[slot], kv_send.at[mask | over], kv_recv.at[mask | over], over)
    kv_push(0, 2).start()
    kv_push(0, 1).start()
    ag_pass(1, 10, 16)
    ag_pass(1, 11, 16)
    group(1, 8).start()
    big_pass(1, 2, 8)
    ag_pass(2, 1, 16, 8)
    relay_pass(1)
    ag_pass(2, 2, 1, 16, 8)
    cut(16)
    cut(20)
    cut(17)
    cut(21)
    kv_push(0, 2).wait_recv()
    kv_push(2, 1).start()
    big_pass(5, 2, 8)
    for mask in (16, 17, 18, 19):
        ag_pass(1, mask)
    group(1, 16).start()
    ag_pass(2, 3, 16, 8)
    group(2, 0).start()
    for mask in (24, 25, 26, 27):
        ag_pass(1, mask)
    group(1, 24).start()
    big_pass(16, 2, 8)
    relay_pass(5)
    group_wait(1)
    for half in range(2):
        part = half * (q_width // 2)
        raw = dot(normed_o[...], proj[:, part : part + q_width // 2], ((1,), (0,)))
        raw = raw + small[1:2, part : part + q_width // 2]
        for i in range(HEADS // 2):
            query[half * (HEADS // 2) + i] = turn(raw[:, i * HD : (i + 1) * HD], cos, sin).astype(jnp.bfloat16)
    big_pass(20, 2, 8)
    relay_pass(16)
    for mask in (16, 17, 18, 19):
        ag_pass(2, mask, 8)
    group(2, 16).start()
    big_pass(17, 2, 8)
    big_pass(21, 2, 8)
    relay_pass(20)
    def go_core(o):
        src = go.at[2 * o] if o else grad_out
        return remote(src, go.at[2 * o + 1], go_send.at[3 + o], go_recv.at[2 * o + 1], 4)
    def go_push(o):
        src = go.at[2] if o == 3 else grad_out
        return remote(src, go.at[2 * o], go_send.at[o - 1], go_recv.at[2 * o], (0, 1, 16, 16)[o])
    go_push(2).start()
    go_push(1).start()
    go_core(0).start()
    big_pass(2, 8)
    big_pass(6, 8)
    kv_push(0, 1).wait_recv()
    kv_push(2, 1).wait_recv()
    query_back = pltpu.make_async_copy(query, query_o, back_sem.at[0])
    query_back.start()
    kv_back = pltpu.make_async_copy(kv, kv_o, back_sem.at[1])
    kv_back.start()
    def head(n, carry):
        g = n // groups
        keys = kv[:, :, pl.ds(pl.multiple_of(g * HD, HD), HD)].reshape(ctx_size * rows, HD)
        vals = kv[:, :, pl.ds(pl.multiple_of(kv_width + g * HD, HD), HD)].reshape(ctx_size * rows, HD)
        scores = dot(query[n], keys, ((1,), (1,))) * HD ** (-0.5)
        scores = jnp.where(pos_k[...] <= own_pos, scores, masked_fill)
        top = jnp.max(scores, axis=-1, keepdims=True)
        expo = jnp.exp(scores - top)
        expo_sum = jnp.sum(expo, axis=-1, keepdims=True)
        attend = (expo / expo_sum).astype(jnp.bfloat16)
        mixed[:, pl.ds(pl.multiple_of(n * HD, HD), HD)] = dot(attend, vals, ((1,), (0,))).astype(jnp.bfloat16)
        lane = lax.broadcasted_iota(jnp.int32, (rows, HD), 1)
        total_o[...] = jnp.where(lane == n, top + jnp.log(expo_sum), total_o[...])
        return carry
    total_o[...] = jnp.zeros_like(total_o)
    lax.fori_loop(0, HEADS, head, 0)
    own_go = pltpu.make_async_copy(grad_out, go.at[0], load_sem.at[2])
    own_go.start()
    big_pass(3, 8)
    mixed_back = pltpu.make_async_copy(mixed, mixed_o, back_sem.at[2])
    mixed_back.start()
    relay_pass(17)
    relay_pass(21)
    def two_over_z(mask):
        src = big_two.at[block(mask)] if mask else source_two.at[column(0)]
        return remote(src, big_two.at[block(mask)], big_send.at[1], two_recv.at[mask | 2], 2)
    big_pass(7, 8)
    cut_two(1).start()
    cut_two(5).start()
    cut_two(16).start()
    cut_two(20).start()
    cut_two(17).start()
    cut_two(21).start()
    for n, mask in enumerate((8, 9, 10, 11, 24, 25, 26, 27)):
        ag_pass(2, mask)
        if n % 4 == 3:
            group(2, mask & 24).start()
    group_wait(2)
    cut_two(4).start()
    proj_back = pltpu.make_async_copy(proj, proj_o, back_sem.at[4])
    proj_back.start()
    out_back = pltpu.make_async_copy(out_w, out_o, back_sem.at[5])
    out_back.start()
    resid = hidden[...].astype(jnp.float32) + dot(mixed[...], out_w[...], ((1,), (1,)))
    resid_o[...] = resid
    factor = lax.rsqrt(jnp.mean(resid * resid, axis=-1, keepdims=True) + norm_eps)
    normed_two_o[...] = (resid * factor * small_o[2:3]).astype(jnp.bfloat16)
    norm_push = remote(normed_two_o, norm_y, norm_sem.at[0], norm_sem.at[1], 16)
    norm_push.start()
    go_push(1).wait_recv()
    go_push(3).start()
    go_core(1).start()
    go_push(2).wait_recv()
    go_core(2).start()
    two_over_z(0).start()
    for mask, passed in ((4, 18), (1, 22), (5, 19), (0, 23)):
        big_pass(passed, 8)
        if mask:
            cut_two(mask).wait_recv()
            two_over_z(mask).start()

    norm_push.wait()
    for mask in (8, 12, 9, 24, 13, 28, 25, 29, 10, 14, 11, 26, 15, 30, 27, 31):
        big_pass(mask)
    go_push(3).wait_recv()
    go_core(3).start()
    for mask in (16, 20, 17, 21):
        cut_two(mask).wait_recv()
    for mask in (0, 4, 1, 5):
        two_over_z(mask).wait_recv()
    own_big.wait()
    own_two.wait()
    own_go.wait()
    drain(big.at[pl.ds(0, 31 * shard)], big_send.at[0])
    drain(big_two.at[pl.ds(0, 11 * shard)], big_send.at[1])

    @pl.when(inner)
    def _():
        drain(relay, big_send.at[2])

    for n in range(3):
        ref, cols = streams[n]
        drain(ref.at[pl.ds(0, 15 * shard), cols], ag_send.at[n])
        for mask in (0, 8, 16, 24):
            group(n, mask).wait_send()
    for o in range(4):
        go_core(o).wait()
    for o in (1, 2, 3):
        go_push(o).wait_send()
    kv_push(0, 2).wait_send()
    kv_push(0, 1).wait_send()
    kv_push(2, 1).wait_send()
    for copy in (query_back, kv_back, mixed_back, proj_back, out_back):
        copy.wait()


def front_call(
    ctx_size, span, hidden, sides, w_query, w_key, w_value, w_out, w_gate, w_up, w_down, grad_out
):
    rows, model = hidden.shape
    shard = w_out.shape[0]
    kv_width = KV_HEADS * HD
    q_width = HEADS * HD
    wide = q_width + 2 * kv_width + HD
    one, two = widths(w_gate.shape[1])
    low, full = jnp.bfloat16, jnp.float32
    vmem = pl.BlockSpec(memory_space=pltpu.VMEM)
    anywhere = pl.BlockSpec(memory_space=pl.ANY)
    shapes = (
        ((rows, model), low, vmem),
        ((HEADS, rows, HD), low, anywhere),
        ((ctx_size, rows, 2 * kv_width), low, anywhere),
        ((rows, HD), full, vmem),
        ((rows, q_width), low, anywhere),
        ((rows, model), full, vmem),
        ((rows, model), low, vmem),
        ((8, model), full, vmem),
        ((model, wide), low, anywhere),
        ((model, q_width), low, anywhere),
        ((model, 3 * one), low, anywhere),
        ((model, 3 * two), low, anywhere),
        ((8, rows, model), low, anywhere),
        ((8, shard, 3 * one), low, anywhere),
        ((model, 2 * kv_width), low, vmem),
        ((rows, model), low, anywhere),
        ((rows, HD), full, vmem),
        ((rows, HD), full, vmem),
        ((1, ctx_size * rows), full, vmem),
        ((1, rows), full, vmem),
    )
    sem = pltpu.SemaphoreType.DMA
    return pl.pallas_call(
        functools.partial(front_kernel, ctx_size),
        out_shape=tuple(jax.ShapeDtypeStruct(shape, kind) for shape, kind, _ in shapes),
        in_specs=[pl.BlockSpec(memory_space=pltpu.SMEM), vmem, vmem] + [anywhere] * 8,
        out_specs=tuple(spec for _, _, spec in shapes),
        scratch_shapes=[
            pltpu.VMEM((model, wide), low),
            pltpu.VMEM((model, q_width), low),
            pltpu.VMEM((8, shard, 3 * one), low),
            pltpu.VMEM((8, shard, 3 * two), low),
            pltpu.VMEM((HEADS, rows, HD), low),
            pltpu.VMEM((ctx_size, rows, 2 * kv_width), low),
            pltpu.VMEM((rows, q_width), low),
            sem((52,)), sem((3,)), sem((3, 32)), sem((3, 4)), sem((3, 4)), sem((3,)), sem((32,)), sem((32,)), sem((8,)),
            sem((7,)), sem((8,)), sem((4,)), sem((4,)), sem((6,)), sem((2,)),
        ],
        compiler_params=pltpu.CompilerParams(
            collective_id=0, has_side_effects=True, vmem_limit_bytes=56 << 20
        ),
        name="front",
    )(span, hidden, sides, w_query, w_key, w_value, w_out, w_gate, w_up, w_down, grad_out)


def back_kernel(
    ctx_size, grad_two, resid, hidden, grad_out, normed, mixed, query, kv, total, cosine, sine, pos_q, pos_k, small, spread,
    proj, out_w, grads, grads_two, near, zin_first, r_part,
    hidden_o, query_o, key_o, outw_o, fin, fin_two, r_in, relay, relay_two,
    weight, turned, left_n, left_a, right_b, right_p, side, side_in, g_b, g_q, g_k,
    y_b, y_q, y_k, x_b, x_q, x_k, p_b, p_q, p_k, h_b, h_q, h_k,
    own, far, zin, own_two, far_two, zin_two, r_mid, r_one, heads_g, lse, dkv, kv_out, kv_p, kv_h, grad_resid,
    load_sem, xs, xr, zs, zr, fs, fr, xs2, xr2, zs2, zr2, fs2, fr2, relay_recv, relay_send, cs, cr, rs, rr, ks, kr, os, orr, keep_sem,
):
    dp = lax.axis_index("dp")
    ctx = lax.axis_index("ctx")
    me = dp * ctx_size + ctx
    y, x, c = dp // 4, (dp // 2) % 2, dp % 2
    h, p = ctx // 2, ctx % 2
    rows, model = resid.shape
    shard = grads.shape[3]
    kv_width = KV_HEADS * HD
    q_width = HEADS * HD
    groups = HEADS // KV_HEADS
    low, full = jnp.bfloat16, jnp.float32
    span = ctx_size * shard

    def at(index):
        return (index // ctx_size, index % ctx_size)

    def remote(src, dst, send, recv, mask):
        return pltpu.make_async_remote_copy(
            src_ref=src, dst_ref=dst, send_sem=send, recv_sem=recv, device_id=at(flip(me, mask)), device_id_type=MESH
        )

    def group_rows(mask):
        return pl.ds(pl.multiple_of(flip(dp, mask // 4) * span, span), span)

    def mask_of(j):
        return (j // 4) * 16 + ((j // 2) % 2) * 4 + j % 2

    barrier = pltpu.get_barrier_semaphore()
    partners = (1, 2, 3, 4, 5, 8, 16, 17, 20, 21)
    for mask in partners:
        pl.semaphore_signal(barrier, inc=1, device_id=at(flip(me, mask)), device_id_type=MESH)
    load_w = pltpu.make_async_copy(out_w, weight.at[:, pl.ds(0, q_width)], load_sem.at[0])
    load_w.start()
    load_own = [
        pltpu.make_async_copy(grads.at[0, 0], own, load_sem.at[1]),
        pltpu.make_async_copy(grads_two.at[0], own_two, load_sem.at[2]),
        pltpu.make_async_copy(zin_first, zin.at[pl.ds(0, 4)], load_sem.at[3]),
        pltpu.make_async_copy(r_part.at[1], r_one, load_sem.at[4]),
    ]
    for copy in load_own:
        copy.start()
    pl.semaphore_wait(barrier, len(partners))

    def far_push(j):
        return remote(grads.at[1, 0, j], far.at[j], xs.at[j], xr.at[j], 8)

    def far_two_push(half, j):
        return remote(grads_two.at[1, half, j], far_two.at[half, j], xs2.at[half, j], xr2.at[half, j], 8)

    def z_push(j):
        return remote(near.at[j], zin.at[j], zs.at[j], zr.at[j], 2)

    def z_two_push(j):
        return remote(far_two.at[1, j], zin_two.at[j], zs2.at[j], zr2.at[j], 2)

    inner = either(h, p) == 1

    def over_z(push, src, to, send, n):
        @pl.when(inner)
        def _():
            push.start()

        @pl.when(jnp.logical_not(inner))
        def _():
            remote(src, to, send, relay_recv.at[n], 1).start()

    def over_z_one(j):
        over_z(z_push(j), near.at[j], relay.at[j - 4], zs.at[j], j)

    def over_z_two(j):
        over_z(z_two_push(j), far_two.at[1, j], relay_two.at[j], zs2.at[j], 8 + j)

    def relay_one(*blocks):
        @pl.when(inner)
        def _():
            for j in blocks:
                part = relay.at[j - 4]
                remote(part, part, relay_send.at[j], relay_recv.at[j], 1).wait_recv()
                remote(part, zin.at[j], relay_send.at[j], zr.at[j], 3).start()

    def relay_two_pass(*blocks):
        @pl.when(inner)
        def _():
            for j in blocks:
                part = relay_two.at[j]
                remote(part, part, relay_send.at[8 + j], relay_recv.at[8 + j], 1).wait_recv()
                remote(part, zin_two.at[j], relay_send.at[8 + j], zr2.at[j], 3).start()

    def fin_push(j):
        return remote(own.at[j], fin.at[j], fs.at[j], fr.at[j], mask_of(j))

    def fin_two_push(j):
        return remote(own_two.at[0, j], fin_two.at[j], fs2.at[j], fr2.at[j], mask_of(j))

    keep_one = pltpu.make_async_copy(own.at[0], fin.at[0], keep_sem.at[0])
    keep_two = pltpu.make_async_copy(own_two.at[0, 0], fin_two.at[0], keep_sem.at[1])

    def z_two_step(j):
        far_two_push(1, j).wait_recv()
        far_two[1, j] = (far_two[1, j].astype(full) + own_two[1, j].astype(full)).astype(low)
        over_z_two(j)

    def total_step(j):
        far_push(j).wait_recv()
        if j > 3:
            z_push(j).wait_recv()
        own[j] = (own[j].astype(full) + far[j].astype(full) + zin[j].astype(full)).astype(low)
        if j:
            fin_push(j).start()
        else:
            keep_one.start()

    def total_two_step(j):
        far_two_push(0, j).wait_recv()
        z_two_push(j).wait_recv()
        own_two[0, j] = (own_two[0, j].astype(full) + far_two[0, j].astype(full) + zin_two[j].astype(full)).astype(low)
        if j:
            fin_two_push(j).start()
        else:
            keep_two.start()

    def r_push(o):
        src = r_one if o == 1 else r_part.at[o]
        dst = r_mid if o == 3 else r_in.at[o - 1]
        return remote(src, dst, os.at[o], orr.at[o], (0, 1, 16, 16)[o])

    r_push(3).start()
    for j in range(4, 8):
        over_z_one(j)
    for j in range(8):
        far_two_push(1, j).start()
    for j in range(8):
        far_push(j).start()

    def transposed(value, left, n):
        turned[n] = jnp.transpose(value)
        for i, mask in enumerate((0, 8, 16, 24)):
            left[i, :, pl.ds(0, rows)] = turned[n, group_rows(mask)]
            cross_left(left, n, i, mask).start()

    def cross_left(left, n, i, mask):
        return remote(turned.at[n, group_rows(mask | 4)], left.at[i, :, pl.ds(rows, rows)], cs.at[n, i], cr.at[n, i], 4)

    def cross(src, dst, n, i):
        return remote(src, dst, cs.at[n, i], cr.at[n, i], 4)

    transposed(normed[...], left_n, 0)
    right_b[pl.ds(0, rows)] = mixed[...]
    cross_mixed = cross(mixed, right_b.at[pl.ds(rows, rows)], 2, 0)
    cross_mixed.start()

    value = resid[...]
    factor = lax.rsqrt(jnp.mean(value * value, axis=-1, keepdims=True) + norm_eps)
    unit = value * factor
    scaled = grad_two[...] * small[2:3]
    ffn_row = jnp.sum(grad_two[...] * unit, axis=0, keepdims=True)
    grad_resid[...] = grad_out[...].astype(full) + factor * (
        scaled - unit * jnp.mean(scaled * unit, axis=-1, keepdims=True)
    )
    grad_attn = grad_resid[...].astype(low)
    transposed(grad_attn, left_a, 1)
    lse[...] = jnp.transpose(total[...])
    sin_back = -sine[...]
    key_pos = jnp.transpose(jnp.broadcast_to(pos_k[...], (HD, pos_k.shape[1])))[:, :1]
    load_w.wait()
    for half in range(2):
        part = half * (q_width // 2)
        moved = dot(grad_attn, weight[:, part : part + q_width // 2], ((1,), (0,))).astype(low)
        for i in range(HEADS // 2):
            heads_g[half * (HEADS // 2) + i] = moved[:, i * HD : (i + 1) * HD]
    load_p = pltpu.make_async_copy(proj, weight, load_sem.at[0])
    load_p.start()

    streams = ((g_b, y_b, x_b, p_b, h_b), (g_q, y_q, x_q, p_q, h_q), (g_k, y_k, x_k, p_k, h_k))

    def add(ref, other):
        ref[...] = (ref[...].astype(full) + other[...].astype(full)).astype(low)

    def y_push(s, k):
        g, yy = streams[s][:2]
        return remote(g.at[2 + k], yy.at[k], rs.at[s, k], rr.at[s, k], 16)

    def x_push(s):
        g, xx = streams[s][0], streams[s][2]
        return remote(g.at[1], xx, rs.at[s, 2], rr.at[s, 2], 8)

    def block_of(hr, other):
        z = 2 * either(h, hr) + either(p, other)
        return pl.ds(pl.multiple_of(z * shard, shard), shard)

    def p_push(s, hr):
        g, pp = streams[s][0], streams[s][3]
        return remote(g.at[0, block_of(hr, 1)], pp.at[hr], rs.at[s, 3 + hr], rr.at[s, 3 + hr], 1)

    def h_push(s):
        g, hh = streams[s][0], streams[s][4]
        return remote(g.at[0, block_of(1, 0)], hh, rs.at[s, 5], rr.at[s, 5], 2)

    def y_pass(s):
        g, yy = streams[s][:2]
        y_push(s, 1).wait_recv()
        add(g.at[1], yy.at[1])
        x_push(s).start()
        y_push(s, 0).wait_recv()
        add(g.at[0], yy.at[0])

    def x_pass(s):
        x_push(s).wait_recv()
        add(streams[s][0].at[0], streams[s][2])
        p_push(s, 1).start()
        p_push(s, 0).start()

    def p_pass(s):
        g, pp = streams[s][0], streams[s][3]
        p_push(s, 1).wait_recv()
        add(g.at[0, block_of(1, 0)], pp.at[1])
        h_push(s).start()
        p_push(s, 0).wait_recv()
        add(g.at[0, block_of(0, 0)], pp.at[0])

    def h_pass(s, out):
        h_push(s).wait_recv()
        out[...] = streams[s][0][0, block_of(0, 0)].astype(full) + streams[s][4][...].astype(full)

    for i, mask in enumerate((0, 8, 16, 24)):
        cross_left(left_a, 1, i, mask).wait_recv()
    cross_mixed.wait_recv()
    for i in (3, 2, 1, 0):
        g_b[i] = dot(left_a[i], right_b[...], ((1,), (0,))).astype(low)
    y_push(0, 1).start()

    def head(n, carry):
        g = n // groups
        k_cols = pl.ds(pl.multiple_of(g * HD, HD), HD)
        v_cols = pl.ds(pl.multiple_of(kv_width + g * HD, HD), HD)
        keys = kv[:, :, k_cols].reshape(ctx_size * rows, HD)
        vals = kv[:, :, v_cols].reshape(ctx_size * rows, HD)
        scores = dot(keys, query[n], ((1,), (1,))) * HD ** (-0.5)
        scores = jnp.where(key_pos <= pos_q[...], scores, masked_fill)
        attend = jnp.exp(scores - lse[pl.ds(n, 1), :])
        grad_attend = dot(vals, heads_g[n], ((1,), (1,)))
        delta = jnp.sum(grad_attend * attend, axis=0, keepdims=True)
        grad_scores = (attend * (grad_attend - delta)).astype(low)
        dkv[:, k_cols] += dot(grad_scores, query[n], ((1,), (0,)))
        dkv[:, v_cols] += dot(attend.astype(low), heads_g[n], ((1,), (0,)))
        back = dot(grad_scores, keys, ((0,), (0,))) * HD ** (-0.5)
        back = turn(back, cosine[...], sin_back).astype(low)
        right_p[pl.ds(0, rows), pl.ds(pl.multiple_of(n * HD, HD), HD)] = back
        return carry

    dkv[...] = jnp.zeros_like(dkv)
    lax.fori_loop(0, HEADS // 2, head, 0)
    relay_one(4, 5)
    lax.fori_loop(HEADS // 2, HEADS, head, 0)

    for z in range(ctx_size):
        part = dkv[pl.ds(z * rows, rows)]
        kv_out[z, :, pl.ds(0, kv_width)] = (part[:, :kv_width] * HD ** (-0.5)).astype(low)
        kv_out[z, :, pl.ds(kv_width, kv_width)] = part[:, kv_width:].astype(low)

    def kv_push(hr):
        return remote(kv_out.at[2 * either(h, hr) + 1 - p], kv_p.at[hr], ks.at[hr], kr.at[hr], 1)

    def kv_cross():
        return remote(kv_out.at[2 * (1 - h) + p], kv_h, ks.at[2], kr.at[2], 2)

    kv_push(1).start()
    kv_push(0).start()
    cross_q = cross(
        right_p.at[pl.ds(0, rows), pl.ds(0, q_width)], right_p.at[pl.ds(rows, rows), pl.ds(0, q_width)], 2, 1
    )
    cross_q.start()
    for copy in load_own:
        copy.wait()
    for i, mask in enumerate((0, 8, 16, 24)):
        cross_left(left_n, 0, i, mask).wait_recv()
    cross_q.wait_recv()
    for i in (3, 2, 1, 0):
        g_q[i] = dot(left_n[i], right_p[:, pl.ds(0, q_width)], ((1,), (0,))).astype(low)
        if i > 1:
            y_push(1, i - 2).start()
    load_p.wait()
    hidden_o[...] = dot(right_p[pl.ds(0, rows), pl.ds(0, q_width)], weight[:, pl.ds(0, q_width)], ((1,), (1,)))
    kv_push(1).wait_recv()
    add(kv_out.at[2 * (1 - h) + p], kv_p.at[1])
    kv_cross().start()
    kv_push(0).wait_recv()
    add(kv_out.at[2 * h + p], kv_p.at[0])
    relay_one(6, 7)
    for j in range(8):
        z_two_step(j)
    for j in range(4):
        total_step(j)
    relay_two_pass(0, 1, 2)
    kv_cross().wait_recv()
    final = kv_out[2 * h + p].astype(full) + kv_h[...].astype(full)
    for g in range(KV_HEADS):
        right_p[pl.ds(0, rows), pl.ds(q_width + g * HD, HD)] = turn(
            final[:, g * HD : (g + 1) * HD], cosine[...], sin_back
        ).astype(low)
    right_p[pl.ds(0, rows), pl.ds(q_width + kv_width, kv_width)] = final[:, kv_width:].astype(low)
    cross_kv = cross(
        right_p.at[pl.ds(0, rows), pl.ds(q_width, 2 * kv_width)],
        right_p.at[pl.ds(rows, rows), pl.ds(q_width, 2 * kv_width)], 2, 2,
    )
    cross_kv.start()
    grad_one = hidden_o[...] + dot(
        right_p[pl.ds(0, rows), pl.ds(q_width, 2 * kv_width)], weight[:, pl.ds(q_width, 2 * kv_width)], ((1,), (1,))
    )
    value = hidden[...].astype(full)
    factor = lax.rsqrt(jnp.mean(value * value, axis=-1, keepdims=True) + norm_eps)
    unit = value * factor
    scaled = grad_one * small[0:1]
    attn_row = jnp.sum(grad_one * unit, axis=0, keepdims=True)
    hidden_o[...] = grad_resid[...] + factor * (scaled - unit * jnp.mean(scaled * unit, axis=-1, keepdims=True))
    bias = jnp.sum(right_p[pl.ds(0, rows)].astype(full), axis=0, keepdims=True)
    kv_bias = jnp.broadcast_to(bias[:, q_width:], (8, 2 * kv_width)).astype(low)
    kv_row = dot(kv_bias, spread[...], ((1,), (1,)))[:1]
    table = jnp.concatenate([attn_row, bias[:, :q_width], ffn_row, kv_row, jnp.zeros((124, model), full)], axis=0)
    side[...] = jnp.transpose(table).astype(low)

    def cross_side(i, mask):
        return cross(side.at[group_rows(mask | 4)], side_in.at[i], 3, i)

    for i, mask in enumerate((0, 8, 16, 24)):
        cross_side(i, mask).start()
    cross_kv.wait_recv()
    for i, mask in ((3, 24), (2, 16), (1, 8), (0, 0)):
        g_k[i, :, pl.ds(0, 2 * kv_width)] = dot(
            left_n[i], right_p[:, pl.ds(q_width, 2 * kv_width)], ((1,), (0,))
        ).astype(low)
        cross_side(i, mask).wait_recv()
        g_k[i, :, pl.ds(2 * kv_width, HD)] = (
            side[group_rows(mask)].astype(full) + side_in[i].astype(full)
        ).astype(low)
        if i > 1:
            y_push(2, i - 2).start()
    y_push(0, 0).start()
    r_push(3).wait_recv()
    add(r_one, r_mid)
    r_push(1).start()
    relay_two_pass(3)
    relay_two_pass(4)
    relay_two_pass(5)
    relay_two_pass(6)
    relay_two_pass(7)
    total_step(4)
    total_step(5)
    total_step(6)
    total_step(7)
    y_pass(1)
    y_pass(2)
    far_two_push(0, 2).start()
    far_two_push(0, 0).start()
    far_two_push(0, 3).start()
    far_two_push(0, 1).start()
    far_two_push(0, 4).start()
    far_two_push(0, 5).start()
    far_two_push(0, 6).start()
    total_two_step(1)
    far_two_push(0, 7).start()
    y_pass(0)
    x_pass(1)
    x_pass(2)
    r_push(2).start()
    p_pass(1)
    p_pass(2)
    total_two_step(0)
    total_two_step(2)
    total_two_step(4)
    total_two_step(5)
    total_two_step(6)
    total_two_step(7)
    x_pass(0)
    p_pass(0)
    h_pass(1, query_o)
    h_pass(2, key_o)
    total_two_step(3)
    h_pass(0, outw_o)

    for j in range(1, 8):
        fin_push(j).wait_recv()
        fin_two_push(j).wait_recv()
    for o in (1, 2):
        r_push(o).wait()
    r_push(3).wait_send()
    keep_one.wait()
    keep_two.wait()

    for j in range(8):
        far_push(j).wait_send()
        far_two_push(0, j).wait_send()
        far_two_push(1, j).wait_send()
        if j > 3:
            z_push(j).wait_send()
        z_two_push(j).wait_send()
        if j:
            fin_push(j).wait_send()
            fin_two_push(j).wait_send()
    @pl.when(inner)
    def _():
        for j in range(4, 8):
            remote(relay.at[j - 4], relay.at[j - 4], relay_send.at[j], relay_recv.at[j], 1).wait_send()
        for j in range(8):
            remote(relay_two.at[j], relay_two.at[j], relay_send.at[8 + j], relay_recv.at[8 + j], 1).wait_send()

    for i, mask in enumerate((0, 8, 16, 24)):
        cross_left(left_n, 0, i, mask).wait_send()
        cross_left(left_a, 1, i, mask).wait_send()
        cross_side(i, mask).wait_send()
    for copy in (cross_mixed, cross_q, cross_kv):
        copy.wait_send()
    for s in range(3):
        for k in range(2):
            y_push(s, k).wait_send()
            p_push(s, k).wait_send()
        x_push(s).wait_send()
        h_push(s).wait_send()
    kv_push(0).wait_send()
    kv_push(1).wait_send()
    kv_cross().wait_send()


def back_call(
    ctx_size, grad_two, resid, hidden, grad_out, normed, mixed, query, kv, total, cosine, sine, pos_q, pos_k,
    small, spread, proj, out_w, grads, grads_two, near, zin_first, r_part,
):
    rows, model = resid.shape
    shard = grads.shape[3]
    one, two = grads.shape[4] // 3, grads_two.shape[4] // 3
    kv_width = KV_HEADS * HD
    q_width = HEADS * HD
    k_cols = 2 * kv_width + HD
    span = ctx_size * shard
    low, full = jnp.bfloat16, jnp.float32
    vmem = pl.BlockSpec(memory_space=pltpu.VMEM)
    anywhere = pl.BlockSpec(memory_space=pl.ANY)
    shapes = (
        ((rows, model), vmem, full),
        ((shard, q_width), vmem, full),
        ((shard, k_cols), vmem, full),
        ((shard, q_width), vmem, full),
        ((8, shard, 3 * one), anywhere, low),
        ((8, shard, 3 * two), anywhere, low),
        ((2, rows, model), anywhere, low),
        ((4, shard, 3 * one), anywhere, low),
        ((8, shard, 3 * two), anywhere, low),
    )
    sem = pltpu.SemaphoreType.DMA
    cols = (q_width, q_width, k_cols)

    def each(*lead):
        return [pltpu.VMEM(lead + (n,), low) for n in cols]

    return pl.pallas_call(
        functools.partial(back_kernel, ctx_size),
        out_shape=tuple(jax.ShapeDtypeStruct(shape, kind) for shape, _, kind in shapes),
        in_specs=[vmem] * 15 + [anywhere] * 7,
        out_specs=tuple(spec for _, spec, _ in shapes),
        scratch_shapes=[
            pltpu.VMEM(proj.shape, low),
            pltpu.VMEM((2, model, rows), low),
            pltpu.VMEM((4, span, 2 * rows), low),
            pltpu.VMEM((4, span, 2 * rows), low),
            pltpu.VMEM((2 * rows, q_width), low),
            pltpu.VMEM((2 * rows, q_width + 2 * kv_width), low),
            pltpu.VMEM((model, HD), low),
            pltpu.VMEM((4, span, HD), low),
            *each(4, span),
            *each(2, span),
            *each(span),
            *each(2, shard),
            *each(shard),
            *([pltpu.VMEM((8, shard, 3 * one), low)] * 3),
            *([pltpu.VMEM((2, 8, shard, 3 * two), low)] * 2),
            pltpu.VMEM((8, shard, 3 * two), low),
            *([pltpu.VMEM((rows, model), low)] * 2),
            pltpu.VMEM((HEADS, rows, HD), low),
            pltpu.VMEM((HD, rows), full),
            pltpu.VMEM((ctx_size * rows, 2 * kv_width), full),
            pltpu.VMEM((ctx_size, rows, 2 * kv_width), low),
            pltpu.VMEM((2, rows, 2 * kv_width), low),
            pltpu.VMEM((rows, 2 * kv_width), low),
            pltpu.VMEM((rows, model), full),
            sem((5,)), *([sem((8,))] * 6), *([sem((2, 8))] * 2), *([sem((8,))] * 4), sem((16,)), sem((16,)),
            sem((4, 4)), sem((4, 4)), sem((3, 6)), sem((3, 6)), sem((3,)), sem((3,)), sem((4,)), sem((4,)), sem((2,)),
        ],
        compiler_params=pltpu.CompilerParams(
            collective_id=2, has_side_effects=True, vmem_limit_bytes=63 << 20
        ),
        name="back",
    )(
        grad_two, resid, hidden, grad_out, normed, mixed, query, kv, total, cosine, sine, pos_q, pos_k, small, spread,
        proj, out_w, grads, grads_two, near, zin_first, r_part,
    )


def finish_kernel(
    ctx_size, fin, fin_two, key, resid, r_part, r_in, hidden, query, outw,
    result_o, hidden_o, attn_o, query_o, bias_q, key_o, bias_k, value_o, bias_v, outw_o, ffn_o, gate_o, up_o, down_o,
    one_v, two_v, tiles, full_v, sems,
):
    dp = lax.axis_index("dp")
    ctx = lax.axis_index("ctx")
    y, c, p = dp // 4, dp % 2, ctx % 2
    full = jnp.float32
    rows, model = resid.shape
    shard = key.shape[0]
    one, two = fin.shape[2] // 3, fin_two.shape[2] // 3
    width = one + two
    kv_width = key_o.shape[1]
    per = bias_k.shape[1]
    moves = [
        pltpu.make_async_copy(fin, one_v, sems.at[0]),
        pltpu.make_async_copy(fin_two, two_v, sems.at[1]),
        pltpu.make_async_copy(r_part.at[0], tiles.at[0], sems.at[2]),
        pltpu.make_async_copy(r_in, tiles.at[pl.ds(1, 2)], sems.at[3]),
    ]
    for copy in moves:
        copy.start()
    hidden_o[...] = hidden[...]
    query_o[...] = query[...]
    outw_o[...] = outw[...]
    key_o[...] = key[:, :kv_width]
    value_o[...] = key[:, kv_width : 2 * kv_width]
    side = jnp.transpose(key[:, 2 * kv_width :])
    attn_o[...] = side[0:1]
    bias_q[...] = side[1:2]
    ffn_o[...] = side[2:3]
    bias_k[...] = side[3:4, :per]
    bias_v[...] = side[3:4, per : 2 * per]
    moves[0].wait()
    moves[1].wait()
    last = gate_o.shape[1] - 7 * width - one
    for j in range(8):
        k = either(y, j // 4) * 4 + either(p, j % 2) * 2 + either(c, (j // 2) % 2)
        for n, out in enumerate((gate_o, up_o, down_o)):
            at = pl.multiple_of(k * width, HD)
            full_v[n, :, pl.ds(at, one)] = one_v[j, :, n * one : (n + 1) * one].astype(full)

            @pl.when(k < 7)
            def _():
                whole = pl.ds(at, width)
                full_v[n, :, pl.ds(at + one, two)] = two_v[j, :, n * two : (n + 1) * two].astype(full)
                pltpu.make_async_copy(full_v.at[n, :, whole], out.at[:, whole], sems.at[4]).start()

            @pl.when(k == 7)
            def _():
                whole = pl.ds(7 * width, one + last)
                full_v[n, :, pl.ds(7 * width + one, last)] = two_v[j, :, n * two : n * two + last].astype(full)
                pltpu.make_async_copy(full_v.at[n, :, whole], out.at[:, whole], sems.at[4]).start()

    moves[2].wait()
    moves[3].wait()
    value = resid[...]
    for o in range(3):
        value = value + tiles[o].astype(full)
    result_o[...] = value.astype(result_o.dtype)
    pltpu.make_async_copy(full_v, full_v, sems.at[4]).wait()


def finish_call(ctx_size, hidden_units, per, fin, fin_two, key, resid, r_part, r_in, hidden, query, outw):
    rows, model = resid.shape
    shard = key.shape[0]
    kv_width = KV_HEADS * HD
    low, full = jnp.bfloat16, jnp.float32
    vmem = pl.BlockSpec(memory_space=pltpu.VMEM)
    anywhere = pl.BlockSpec(memory_space=pl.ANY)
    shapes = (
        ((rows, model), low, vmem),
        ((rows, model), full, vmem),
        ((1, shard), full, vmem),
        (query.shape, full, vmem),
        ((1, shard), full, vmem),
        ((shard, kv_width), full, vmem),
        ((1, per), full, vmem),
        ((shard, kv_width), full, vmem),
        ((1, per), full, vmem),
        (outw.shape, full, vmem),
        ((1, shard), full, vmem),
        ((shard, hidden_units), full, anywhere),
        ((shard, hidden_units), full, anywhere),
        ((shard, hidden_units), full, anywhere),
    )
    return pl.pallas_call(
        functools.partial(finish_kernel, ctx_size),
        out_shape=tuple(jax.ShapeDtypeStruct(shape, kind) for shape, kind, _ in shapes),
        in_specs=[anywhere, anywhere, vmem, vmem, anywhere, anywhere] + [vmem] * 3,
        out_specs=tuple(spec for _, _, spec in shapes),
        scratch_shapes=[
            pltpu.VMEM(fin.shape, low),
            pltpu.VMEM(fin_two.shape, low),
            pltpu.VMEM((3, rows, model), low),
            pltpu.VMEM((3, shard, hidden_units), full),
            pltpu.SemaphoreType.DMA((5,)),
        ],
        compiler_params=pltpu.CompilerParams(vmem_limit_bytes=63 << 20),
        name="finish",
    )(fin, fin_two, key, resid, r_part, r_in, hidden, query, outw)


def fits(mesh):
    return mesh.shape["dp"] == 8 and mesh.shape["ctx"] == 4


def fast_device(
    hidden,
    cotangent,
    span_order,
    attn_gain,
    w_query,
    b_query,
    w_key,
    b_key,
    w_value,
    b_value,
    w_out,
    ffn_gain,
    w_gate,
    w_up,
    w_down,
):
    ctx_size = lax.axis_size("ctx")
    batches = hidden.shape[0]
    length = hidden.shape[1]
    row_count = batches * length
    shard_rows = w_query.shape[0]
    kv_width = KV_HEADS * HD
    q_width = HEADS * HD

    grad_out = cotangent.reshape(row_count, D)
    per = b_key.shape[0]
    flat = jnp.concatenate([attn_gain, b_query, ffn_gain, b_key, b_value])
    sides = jnp.pad(flat, (0, 8 * shard_rows - flat.shape[0])).reshape(8, shard_rows)
    source = hidden.reshape(row_count, D)
    normed, query_heads, key_value, log_total, mixed, resid, normed_two, small, proj_full, out_full, big, big_two, go_all, _, spread, norm_y, *turns = front_call(
        ctx_size, span_order, source, sides, w_query, w_key, w_value, w_out, w_gate, w_up, w_down, grad_out
    )
    grad_two, r_part, grads, grads_two, near, zin, *_ = ffn_call(ctx_size, shard_rows, normed_two, norm_y, go_all, big, big_two)
    hidden_back, query_sum, kv_sum, out_sum, fin, fin_two, r_in, *_ = back_call(
        ctx_size, grad_two, resid, source, grad_out, normed, mixed, query_heads, key_value, log_total,
        turns[0], turns[1], turns[3], turns[2], small, spread,
        proj_full, out_full, grads, grads_two, near, zin, r_part,
    )
    (
        result, hidden_grad, attn_gain_grad, w_query_grad, b_query_grad, w_key_grad, b_key_grad, w_value_grad,
        b_value_grad, w_out_grad, ffn_gain_grad, w_gate_grad, w_up_grad, w_down_grad,
    ) = finish_call(
        ctx_size, w_gate.shape[1], per, fin, fin_two, kv_sum, resid, r_part, r_in, hidden_back, query_sum, out_sum
    )
    return (
        result.reshape(batches, length, D),
        hidden_grad.reshape(batches, length, D),
        attn_gain_grad.reshape(shard_rows),
        w_query_grad,
        b_query_grad.reshape(shard_rows),
        w_key_grad,
        b_key_grad.reshape(per),
        w_value_grad,
        b_value_grad.reshape(per),
        w_out_grad,
        ffn_gain_grad.reshape(shard_rows),
        w_gate_grad,
        w_up_grad,
        w_down_grad,
    )


def general_device(
    hidden,
    cotangent,
    span_order,
    attn_gain,
    w_query,
    b_query,
    w_key,
    b_key,
    w_value,
    b_value,
    w_out,
    ffn_gain,
    w_gate,
    w_up,
    w_down,
):
    ctx_size = lax.axis_size("ctx")
    ctx_rank = lax.axis_index("ctx")
    batches = hidden.shape[0]
    length = hidden.shape[1]
    span_len = length // 2
    seq_len = length * ctx_size
    row_count = batches * length
    groups = HEADS // KV_HEADS
    shard_rows = w_query.shape[0]
    head_scale = HD ** (-0.5)
    kv_width = KV_HEADS * HD
    q_width = HEADS * HD
    places = jnp.arange(seq_len, dtype=jnp.int32)
    every_pos = jnp.repeat(span_order, span_len, axis=1) * span_len + places[None, :] % span_len
    local_pos = lax.dynamic_slice_in_dim(every_pos, ctx_rank * length, length, 1)
    cosine, sine = angles_for(local_pos.reshape(row_count), HD)
    allowed = (every_pos[:, None, :] <= local_pos[:, :, None])[:, None, None]
    attn_full = (
        lax.all_gather(attn_gain, ("dp", "ctx"), axis=0, tiled=True),
        lax.all_gather(w_query, ("dp", "ctx"), axis=0, tiled=True),
        lax.all_gather(w_key, ("dp", "ctx"), axis=0, tiled=True),
        lax.all_gather(w_value, ("dp", "ctx"), axis=0, tiled=True),
        lax.all_gather(w_out, ("dp", "ctx"), axis=0, tiled=True),
        lax.all_gather(b_query, ("dp", "ctx"), axis=0, tiled=True),
        lax.all_gather(b_key, ("dp", "ctx"), axis=0, tiled=True),
        lax.all_gather(b_value, ("dp", "ctx"), axis=0, tiled=True),
    )
    gain_one = attn_full[0].astype(jnp.float32)
    source = hidden.reshape(row_count, D).astype(jnp.float32)
    attn_factor, normed = norm_forward(source, gain_one)
    query_raw = plain_dot(normed, attn_full[1]) + attn_full[5].astype(jnp.float32)
    key_raw = plain_dot(normed, attn_full[2]) + attn_full[6].astype(jnp.float32)
    value_low = (plain_dot(normed, attn_full[3]) + attn_full[7].astype(jnp.float32)).astype(
        jnp.bfloat16
    )
    query_rot = rotate(query_raw.reshape(row_count, HEADS, HD), cosine, sine).astype(jnp.bfloat16)
    query_rot = query_rot.reshape(batches, length, KV_HEADS, groups, HD)
    key_rot = rotate(key_raw.reshape(row_count, KV_HEADS, HD), cosine, sine).astype(jnp.bfloat16)
    key_rot = key_rot.reshape(batches, length, kv_width)
    key_all, value_all = (
        lax.all_gather(key_rot, "ctx", axis=1, tiled=True),
        lax.all_gather(value_low.reshape(batches, length, kv_width), "ctx", axis=1, tiled=True),
    )
    key_all = key_all.reshape(batches, seq_len, KV_HEADS, HD)
    value_all = value_all.reshape(batches, seq_len, KV_HEADS, HD)
    scores = (
        jnp.einsum("bqkgd,bskd->bkgqs", query_rot, key_all, preferred_element_type=jnp.float32)
        * head_scale
    )
    masked = jnp.where(allowed, scores, masked_fill)
    row_max = jnp.max(masked, axis=-1, keepdims=True)
    expo = jnp.exp(masked - row_max)
    expo_sum = jnp.sum(expo, axis=-1, keepdims=True)
    log_total = row_max + jnp.log(expo_sum)
    attend = (expo / expo_sum).astype(jnp.bfloat16)
    mixed = jnp.einsum("bkgqs,bskd->bqkgd", attend, value_all, preferred_element_type=jnp.float32)
    mixed = mixed.reshape(row_count, q_width).astype(jnp.bfloat16)
    resid = source + right_dot(mixed, attn_full[4])
    ffn_full = (
        lax.all_gather(ffn_gain, ("dp", "ctx"), axis=0, tiled=True),
        lax.all_gather(w_gate, ("dp", "ctx"), axis=0, tiled=True),
        lax.all_gather(w_up, ("dp", "ctx"), axis=0, tiled=True),
        lax.all_gather(w_down, ("dp", "ctx"), axis=0, tiled=True),
    )
    gain_two = ffn_full[0].astype(jnp.float32)
    ffn_factor, normed_two = norm_forward(resid, gain_two)
    gate_pre = plain_dot(normed_two, ffn_full[1])
    up_pre = plain_dot(normed_two, ffn_full[2])
    sigmoid_gate = jax.nn.sigmoid(gate_pre)
    silu_gate = gate_pre * sigmoid_gate
    act = (silu_gate * up_pre).astype(jnp.bfloat16)
    output = resid + right_dot(act, ffn_full[3])
    result = output.astype(jnp.bfloat16).reshape(batches, length, D)
    ffn_back = (
        lax.all_gather(ffn_gain, ("dp", "ctx"), axis=0, tiled=True),
        lax.all_gather(w_gate, ("dp", "ctx"), axis=0, tiled=True),
        lax.all_gather(w_up, ("dp", "ctx"), axis=0, tiled=True),
        lax.all_gather(w_down, ("dp", "ctx"), axis=0, tiled=True),
    )
    grad_out = cotangent.reshape(row_count, D)
    grad_plain = grad_out.astype(jnp.float32)
    grad_act = plain_dot(grad_out, ffn_back[3])
    grad_gate = (grad_act * up_pre * sigmoid_gate * (1.0 + gate_pre * (1.0 - sigmoid_gate))).astype(
        jnp.bfloat16
    )
    grad_up = (grad_act * silu_gate).astype(jnp.bfloat16)
    pieces = (
        lax.all_gather(normed_two, "ctx", axis=0, tiled=True),
        lax.all_gather(grad_gate, "ctx", axis=0, tiled=True),
        lax.all_gather(grad_up, "ctx", axis=0, tiled=True),
        lax.all_gather(act, "ctx", axis=0, tiled=True),
        lax.all_gather(grad_out, "ctx", axis=0, tiled=True),
    )
    picked_in = owned_columns(pieces[0], ctx_size, ctx_rank, shard_rows)
    picked_out = owned_columns(pieces[4], ctx_size, ctx_rank, shard_rows)
    w_gate_grad, w_up_grad, w_down_grad = (
        lax.psum_scatter(
            outer_add(picked_in, pieces[1]).astype(jnp.bfloat16),
            "dp",
            scatter_dimension=0,
            tiled=True,
        ).astype(jnp.float32),
        lax.psum_scatter(
            outer_add(picked_in, pieces[2]).astype(jnp.bfloat16),
            "dp",
            scatter_dimension=0,
            tiled=True,
        ).astype(jnp.float32),
        lax.psum_scatter(
            outer_add(picked_out, pieces[3]).astype(jnp.bfloat16),
            "dp",
            scatter_dimension=0,
            tiled=True,
        ).astype(jnp.float32),
    )
    grad_norm_two = right_dot(grad_gate, ffn_back[1]) + right_dot(grad_up, ffn_back[2])
    resid_back, ffn_gain_part = norm_backward(resid, ffn_factor, gain_two, grad_norm_two)
    grad_resid = grad_plain + resid_back
    attn_back = (
        lax.all_gather(attn_gain, ("dp", "ctx"), axis=0, tiled=True),
        lax.all_gather(w_query, ("dp", "ctx"), axis=0, tiled=True),
        lax.all_gather(w_key, ("dp", "ctx"), axis=0, tiled=True),
        lax.all_gather(w_value, ("dp", "ctx"), axis=0, tiled=True),
        lax.all_gather(w_out, ("dp", "ctx"), axis=0, tiled=True),
        lax.all_gather(b_query, ("dp", "ctx"), axis=0, tiled=True),
        lax.all_gather(b_key, ("dp", "ctx"), axis=0, tiled=True),
        lax.all_gather(b_value, ("dp", "ctx"), axis=0, tiled=True),
    )
    grad_attn = grad_resid.astype(jnp.bfloat16)
    grad_mixed = plain_dot(grad_attn, attn_back[4]).astype(jnp.bfloat16)
    grad_mixed = grad_mixed.reshape(batches, length, KV_HEADS, groups, HD)
    scores = (
        jnp.einsum("bqkgd,bskd->bkgqs", query_rot, key_all, preferred_element_type=jnp.float32)
        * head_scale
    )
    masked = jnp.where(allowed, scores, masked_fill)
    attend_full = jnp.exp(masked - log_total)
    attend = attend_full.astype(jnp.bfloat16)
    grad_attend = jnp.einsum(
        "bqkgd,bskd->bkgqs", grad_mixed, value_all, preferred_element_type=jnp.float32
    )
    value_grad_all = jnp.einsum(
        "bkgqs,bqkgd->bskd", attend, grad_mixed, preferred_element_type=jnp.float32
    )
    delta = jnp.sum(grad_attend * attend_full, axis=-1, keepdims=True)
    grad_scores = (attend_full * (grad_attend - delta)).astype(jnp.bfloat16)
    query_grad_rot = (
        jnp.einsum("bkgqs,bskd->bqkgd", grad_scores, key_all, preferred_element_type=jnp.float32)
        * head_scale
    )
    key_grad_all = (
        jnp.einsum("bkgqs,bqkgd->bskd", grad_scores, query_rot, preferred_element_type=jnp.float32)
        * head_scale
    )
    key_grad_rot, value_grad = (
        lax.psum_scatter(
            key_grad_all.reshape(batches, seq_len, kv_width), "ctx", scatter_dimension=1, tiled=True
        ),
        lax.psum_scatter(
            value_grad_all.reshape(batches, seq_len, kv_width),
            "ctx",
            scatter_dimension=1,
            tiled=True,
        ),
    )
    query_grad = (
        rotate_back(query_grad_rot.reshape(row_count, HEADS, HD), cosine, sine)
        .reshape(row_count, q_width)
        .astype(jnp.bfloat16)
    )
    key_grad = (
        rotate_back(key_grad_rot.reshape(row_count, KV_HEADS, HD), cosine, sine)
        .reshape(row_count, kv_width)
        .astype(jnp.bfloat16)
    )
    value_grad = value_grad.reshape(row_count, kv_width).astype(jnp.bfloat16)
    proj_grad = jnp.concatenate([query_grad, key_grad, value_grad], axis=1)
    pieces = (
        lax.all_gather(normed, "ctx", axis=0, tiled=True),
        lax.all_gather(proj_grad, "ctx", axis=0, tiled=True),
        lax.all_gather(grad_attn, "ctx", axis=0, tiled=True),
        lax.all_gather(mixed, "ctx", axis=0, tiled=True),
    )
    picked_in = owned_columns(pieces[0], ctx_size, ctx_rank, shard_rows)
    picked_out = owned_columns(pieces[2], ctx_size, ctx_rank, shard_rows)
    proj_sum, w_out_grad = (
        lax.psum_scatter(
            outer_add(picked_in, pieces[1]).astype(jnp.bfloat16),
            "dp",
            scatter_dimension=0,
            tiled=True,
        ).astype(jnp.float32),
        lax.psum_scatter(
            outer_add(picked_out, pieces[3]).astype(jnp.bfloat16),
            "dp",
            scatter_dimension=0,
            tiled=True,
        ).astype(jnp.float32),
    )
    grad_norm_one = (
        right_dot(query_grad, attn_back[1])
        + right_dot(key_grad, attn_back[2])
        + right_dot(value_grad, attn_back[3])
    )
    source_back, attn_gain_part = norm_backward(source, attn_factor, gain_one, grad_norm_one)
    hidden_grad = (grad_resid + source_back).reshape(batches, length, D)
    query_bias_part = jnp.sum(query_grad.astype(jnp.float32), axis=0)
    key_bias_part = jnp.sum(key_grad.astype(jnp.float32), axis=0)
    value_bias_part = jnp.sum(value_grad.astype(jnp.float32), axis=0)
    small_sums = (
        lax.psum_scatter(attn_gain_part, ("dp", "ctx"), scatter_dimension=0, tiled=True),
        lax.psum_scatter(query_bias_part, ("dp", "ctx"), scatter_dimension=0, tiled=True),
        lax.psum_scatter(key_bias_part, ("dp", "ctx"), scatter_dimension=0, tiled=True),
        lax.psum_scatter(value_bias_part, ("dp", "ctx"), scatter_dimension=0, tiled=True),
        lax.psum_scatter(ffn_gain_part, ("dp", "ctx"), scatter_dimension=0, tiled=True),
    )
    w_query_grad = proj_sum[:, :q_width]
    w_key_grad = proj_sum[:, q_width : q_width + kv_width]
    w_value_grad = proj_sum[:, q_width + kv_width :]
    return (
        result,
        hidden_grad,
        small_sums[0],
        w_query_grad,
        small_sums[1],
        w_key_grad,
        small_sums[2],
        w_value_grad,
        small_sums[3],
        w_out_grad,
        small_sums[4],
        w_gate_grad,
        w_up_grad,
        w_down_grad,
    )


def solution(mesh):
    placed = (
        P("dp", "ctx", None),
        P("dp", "ctx", None),
        P("dp", None),
        P(("dp", "ctx")),
        P(("dp", "ctx"), None),
        P(("dp", "ctx")),
        P(("dp", "ctx"), None),
        P(("dp", "ctx")),
        P(("dp", "ctx"), None),
        P(("dp", "ctx")),
        P(("dp", "ctx"), None),
        P(("dp", "ctx")),
        P(("dp", "ctx"), None),
        P(("dp", "ctx"), None),
        P(("dp", "ctx"), None),
    )
    return jax.shard_map(
        fast_device if fits(mesh) else general_device,
        mesh=mesh,
        in_specs=placed,
        out_specs=(
            P("dp", "ctx", None),
            P("dp", "ctx", None),
            P(("dp", "ctx")),
            P(("dp", "ctx"), None),
            P(("dp", "ctx")),
            P(("dp", "ctx"), None),
            P(("dp", "ctx")),
            P(("dp", "ctx"), None),
            P(("dp", "ctx")),
            P(("dp", "ctx"), None),
            P(("dp", "ctx")),
            P(("dp", "ctx"), None),
            P(("dp", "ctx"), None),
            P(("dp", "ctx"), None),
        ),
        check_vma=False,
    )
```

```python
import functools
import math

import jax
import jax.numpy as jnp
from jax import lax
from jax.experimental import pallas as pl
from jax.experimental.pallas import tpu as pltpu
from jax.sharding import PartitionSpec as P

D = 1536
HEADS = 12
KV_HEADS = 2
HD = 128


norm_eps = 1e-06
rope_base = 10000.0
masked_fill = -1e30


def angles_for(places, width):
    half = width // 2
    freqs = rope_base ** (-(jnp.arange(half, dtype=jnp.float32) * 2.0 / width))
    angles = places.astype(jnp.float32)[:, None] * freqs[None, :]
    return (jnp.cos(angles)[:, None, :], jnp.sin(angles)[:, None, :])


def rotate(values, cosine, sine):
    half = values.shape[-1] // 2
    first = values[..., :half]
    second = values[..., half:]
    return jnp.concatenate(
        [first * cosine - second * sine, second * cosine + first * sine], axis=-1
    )


def rotate_back(values, cosine, sine):
    half = values.shape[-1] // 2
    first = values[..., :half]
    second = values[..., half:]
    return jnp.concatenate(
        [first * cosine + second * sine, second * cosine - first * sine], axis=-1
    )


def norm_forward(source, gain):
    factor = lax.rsqrt(jnp.mean(source * source, axis=-1, keepdims=True) + norm_eps)
    return (factor, (source * factor * gain).astype(jnp.bfloat16))


def norm_backward(source, factor, gain, grad_normed):
    unit = source * factor
    gain_grad = jnp.sum(grad_normed * unit, axis=0)
    scaled = grad_normed * gain
    source_grad = factor * (scaled - unit * jnp.mean(scaled * unit, axis=-1, keepdims=True))
    return (source_grad, gain_grad)


def right_dot(left, weight):
    return jnp.einsum("rf,df->rd", left, weight, preferred_element_type=jnp.float32)


def plain_dot(left, weight):
    return jnp.dot(left, weight, preferred_element_type=jnp.float32)


def owned_columns(values, ctx_size, ctx_rank, shard_rows):
    rows = values.shape[0]
    blocks = values.shape[1] // (shard_rows * ctx_size)
    shaped = values.reshape(rows, blocks, ctx_size, shard_rows)
    picked = lax.dynamic_index_in_dim(shaped, ctx_rank, axis=2, keepdims=False)
    return picked.reshape(rows, blocks * shard_rows)


def outer_add(left, right):
    return jnp.einsum("rc,rf->cf", left, right, preferred_element_type=jnp.float32)


MESH = pl.DeviceIdType.MESH


def flip(index, mask):
    for bit in (1, 2, 4, 8, 16):
        if mask & bit:
            index = index + bit - 2 * bit * ((index // bit) % 2)
    return index


def either(a, b):
    return a + b - 2 * a * b


def dot(a, b, dims):
    return lax.dot_general(a, b, (dims, ((), ())), preferred_element_type=jnp.float32)


def widths(hidden_units):
    width = -(-hidden_units // (8 * 128)) * 128
    first = width // 384 * 256
    return (first, width - first)


def ffn_kernel(
    ctx_size, n_own, norm_y, go_all, big, big_two,
    grad_two, r_part, grads, grads_two, near, zin,
    w_one, w_two, nt, go, ggu, act, crecv, part, h_in, h_mid, stage, own, far,
    io_sem, n_send, n_recv, f_send, f_recv, c_send, c_recv, o_send, o_recv, st_sem, w_send, w_recv, l_sem, x_send, x_recv, z_send, z_recv, d_sem,
):
    dp = lax.axis_index("dp")
    ctx = lax.axis_index("ctx")
    me = dp * ctx_size + ctx
    y, x, c = dp // 4, (dp // 2) % 2, dp % 2
    h, p = ctx // 2, ctx % 2
    one, two = w_one.shape[1] // 3, w_two.shape[1] // 3
    shard = grads.shape[3]
    rows, model = n_own.shape
    low, full = jnp.bfloat16, jnp.float32

    def at(index):
        return (index // ctx_size, index % ctx_size)

    def remote(src, dst, send, recv, mask):
        return pltpu.make_async_remote_copy(
            src_ref=src, dst_ref=dst, send_sem=send, recv_sem=recv, device_id=at(flip(me, mask)), device_id_type=MESH
        )

    def block(mask):
        return pl.ds(pl.multiple_of(flip(me, mask) * shard, shard), shard)

    barrier = pltpu.get_barrier_semaphore()
    partners = (1, 2, 4, 8, 16)
    for mask in partners:
        pl.semaphore_signal(barrier, inc=1, device_id=at(flip(me, mask)), device_id_type=MESH)
    load_n = pltpu.make_async_copy(n_own, nt.at[0], io_sem.at[0])
    load_y = pltpu.make_async_copy(norm_y, nt.at[4], io_sem.at[3])
    load_w = pltpu.make_async_copy(big, w_one, io_sem.at[1])
    load_go = pltpu.make_async_copy(go_all, go, io_sem.at[2])
    held = (0, 4, 1, 5, 16, 20, 17, 21, 2, 6, 3, 7)
    load_l = [
        pltpu.make_async_copy(big_two.at[block(mask)], w_two.at[block(mask)], l_sem.at[i]) for i, mask in enumerate(held)
    ]
    for copy in (load_n, load_y, load_w, load_go, *load_l):
        copy.start()
    pl.semaphore_wait(barrier, len(partners))

    def spread_two(mask, over):
        remote(big_two.at[block(mask)], w_two.at[block(mask)], w_send.at[0], w_recv.at[mask | over], over).start()

    def w_wait(mask):
        remote(w_two.at[block(mask)], w_two.at[block(mask)], w_send.at[0], w_recv.at[mask], 1).wait_recv()

    def w_pass(mask):
        w_wait(mask)
        remote(w_two.at[block(mask)], w_two.at[block(mask)], w_send.at[0], w_recv.at[mask | 8], 8).start()

    def n_core(slot):
        return remote(nt.at[slot], nt.at[slot + 1], f_send.at[slot // 2], f_recv.at[slot // 2], 4)

    def n_push(o):
        half = pl.ds((o - 1) % 2 * (rows // 2), rows // 2)
        if o == 1:
            return remote(nt.at[0], nt.at[2], n_send.at[1], n_recv.at[1], 1)
        return remote(nt.at[(0, 0, 4, 2)[o], half], nt.at[6, half], n_send.at[o], n_recv.at[o], (0, 0, 1, 16)[o])

    load_n.wait()
    n_push(1).start()
    n_core(0).start()
    load_y.wait()
    n_push(2).start()
    n_core(4).start()
    for mask in (16, 20, 17, 21):
        spread_two(mask, 2)
    for mask in held:
        spread_two(mask, 8)
    load_w.wait()
    load_go.wait()

    def first(slot):
        gu = dot(nt[slot], w_one[:, : 2 * one], ((1,), (0,)))
        ga = dot(go[slot], w_one[:, 2 * one :], ((1,), (0,)))
        finish(slot, gu[:, :one], gu[:, one:], ga, 0, 0)

    def finish(slot, gate, up, ga, at_gu, at_act):
        size = gate.shape[1]
        sig = 1.0 / (1.0 + jnp.exp(-gate))
        silu = gate * sig
        act[slot, :, pl.ds(at_act, size)] = (silu * up).astype(low)
        ggu[slot, :, pl.ds(at_gu, size)] = (ga * up * sig * (1.0 + gate * (1.0 - sig))).astype(low)
        ggu[slot, :, pl.ds(at_gu + size, size)] = (ga * silu).astype(low)

    def second(slot):
        gu = dot(nt[slot], w_two[:, : 2 * two], ((1,), (0,)))
        ga = dot(go[slot], w_two[:, 2 * two :], ((1,), (0,)))
        finish(slot, gu[:, :two], gu[:, two:], ga, 2 * one, one)
        grad = dot(ggu[slot, :, : 2 * one], w_one[:, : 2 * one], ((1,), (1,)))
        grad = grad + dot(ggu[slot, :, 2 * one :], w_two[:, : 2 * two], ((1,), (1,)))
        out = dot(act[slot, :, :one], w_one[:, 2 * one :], ((1,), (1,)))
        out = out + dot(act[slot, :, one:], w_two[:, 2 * two :], ((1,), (1,)))
        return (grad.astype(low), out.astype(low))

    def early(n, carry):
        o = n % 2 * 2 + n // 2

        @pl.when(o == 1)
        def _():
            n_push(1).wait_recv()
            n_push(3).start()
            n_core(2).start()

        @pl.when(o == 3)
        def _():
            n_push(2).wait_recv()
            n_push(3).wait_recv()
            n_core(6).start()

        first(2 * o)


        n_core(2 * o).wait_recv()
        first(2 * o + 1)
        return carry

    lax.fori_loop(0, 4, early, 0)
    def stage_wait(slot, size):
        part_of = stage.at[slot, :, pl.ds(0, size)]
        pltpu.make_async_copy(part_of, part_of, st_sem.at[slot]).wait()

    def weights(size, start_gu, start_act, to, passes, q, carry):
        slot = q % 2

        @pl.when(q > 1)
        def _():
            stage_wait(slot, 3 * size)

        chunk = 8 * shard
        cols = pl.ds(pl.multiple_of(q * chunk, chunk), chunk)

        def product(left, right, start, count, at_col):
            left = left[:, :, cols].reshape(8 * rows, chunk)
            right = right[:, :, pl.ds(start, count)].reshape(8 * rows, count)
            stage[slot, :, pl.ds(at_col, count)] = dot(left, right, ((0,), (0,))).astype(low)

        for start in range(0, 2 * size, one):
            count = min(one, 2 * size - start)
            product(nt, ggu, start_gu + start, count, start)
        product(go, act, start_act, size, 2 * size)
        for n, masks in enumerate(passes):
            @pl.when(q == n)
            def _():
                for mask in masks:
                    w_pass(mask)

        yr, xr = either(q // 2, y), either(q % 2, x)
        for j in range(8):
            cr, hrel, pr = either(j // 4, c), either((j // 2) % 2, h), either(j % 2, p)
            pltpu.make_async_copy(
                stage.at[slot, pl.ds(j * shard, shard), pl.ds(0, 3 * size)],
                to.at[xr, hrel, yr * 4 + cr * 2 + pr], st_sem.at[slot],
            ).start()
        return carry

    def all_weights(size, start_gu, start_act, to, passes=()):
        lax.fori_loop(0, 4, functools.partial(weights, size, start_gu, start_act, to, passes), 0)
        stage_wait(0, 3 * size)
        stage_wait(1, 3 * size)

    def far_push(j):
        return remote(grads.at[1, 1, j], far.at[j], x_send.at[j], x_recv.at[j], 8)

    def z_push(j):
        return remote(far.at[j], zin.at[j], z_send.at[j], z_recv.at[j], 2)

    def load_own(k):
        return pltpu.make_async_copy(grads.at[0, 1, pl.ds(4 * k, 4)], own, d_sem.at[0])

    keep_near = pltpu.make_async_copy(far, near, d_sem.at[0])

    def far_pass(*blocks):
        for j in blocks:
            far_push(j).wait_recv()
            far[j] = (far[j].astype(full) + own[j % 4].astype(full)).astype(low)
            if j < 4:
                z_push(j).start()

    all_weights(one, 0, 0, grads, ((18, 22, 19, 23),))
    for j in range(8):
        far_push(j).start()
    load_own(0).start()

    for mask in (8, 12, 9, 13, 24, 28, 25, 29, 10, 14, 11, 15, 26, 30, 27, 31):
        w_wait(mask)
    for copy in load_l:
        copy.wait()

    def cross(o):
        return remote(stage.at[:, pl.ds(0, rows), pl.ds(0, model)], crecv.at[o % 2], c_send, c_recv.at[o % 2], 4)

    def final(o):
        dst = h_mid if o == 3 else h_in.at[o - 1]
        return remote(part.at[o, 0], dst, o_send.at[o], o_recv.at[o], (0, 1, 16, 16)[o])

    def keep(o):
        return pltpu.make_async_copy(part.at[o, 1], r_part.at[o], io_sem.at[o])

    def combine(o):
        cross(o).wait_recv()
        part[o] = (part[o].astype(full) + crecv[o % 2].astype(full)).astype(low)
        keep(o).start()

    def late(n, carry):
        o = 3 - n
        grad, out = second(2 * o)
        part[o, 0] = grad
        part[o, 1] = out

        @pl.when(n > 0)
        def _():
            combine(o + 1)

        @pl.when(n == 1)
        def _():
            final(3).start()
            load_own(0).wait()
            far_pass(0, 1)

        @pl.when(n == 2)
        def _():
            final(2).start()
            far_pass(2, 3)
            load_own(1).start()

        @pl.when(n == 3)
        def _():
            final(3).wait_recv()
            part[1, 0] = (part[1, 0].astype(full) + h_mid[...].astype(full)).astype(low)
            final(1).start()
            load_own(1).wait()
            far_pass(4, 5)

        grad, out = second(2 * o + 1)

        @pl.when(n > 0)
        def _():
            cross(o).wait_send()

        stage[0, pl.ds(0, rows), pl.ds(0, model)] = grad
        stage[1, pl.ds(0, rows), pl.ds(0, model)] = out
        cross(o).start()
        return carry

    lax.fori_loop(0, 4, late, 0)

    far_pass(6, 7)
    keep_near.start()
    cross(0).wait_send()
    all_weights(two, 2 * one, one, grads_two)
    combine(0)
    grad_two[...] = part[0, 0].astype(full)
    for o in (1, 2):
        final(o).wait_recv()
        grad_two[...] += h_in[o - 1].astype(full)
    keep_near.wait()
    for j in range(8):
        far_push(j).wait_send()
        if j < 4:
            z_push(j).wait()
    for o in range(4):
        keep(o).wait()
        n_core(2 * o).wait_send()
    for o in (1, 2, 3):
        n_push(o).wait_send()
        final(o).wait_send()
    sent = w_two.at[pl.ds(0, 20 * shard)]
    pltpu.make_async_copy(sent, sent, w_send.at[0]).wait()


def ffn_call(ctx_size, shard, n_own, norm_y, go_all, big, big_two):
    rows, model = n_own.shape
    one, two = big.shape[1] // 3, big_two.shape[1] // 3
    low = jnp.bfloat16
    anywhere = pl.BlockSpec(memory_space=pl.ANY)
    sem = pltpu.SemaphoreType.DMA
    return pl.pallas_call(
        functools.partial(ffn_kernel, ctx_size),
        out_shape=(
            jax.ShapeDtypeStruct((rows, model), jnp.float32),
            jax.ShapeDtypeStruct((4, rows, model), low),
            jax.ShapeDtypeStruct((2, 2, 8, shard, 3 * one), low),
            jax.ShapeDtypeStruct((2, 2, 8, shard, 3 * two), low),
            jax.ShapeDtypeStruct((8, shard, 3 * one), low),
            jax.ShapeDtypeStruct((4, shard, 3 * one), low),
        ),
        in_specs=[anywhere] * 5,
        out_specs=[pl.BlockSpec(memory_space=pltpu.VMEM)] + [anywhere] * 5,
        scratch_shapes=[
            pltpu.VMEM((model, 3 * one), low),
            pltpu.VMEM((model, 3 * two), low),
            pltpu.VMEM((8, rows, model), low),
            pltpu.VMEM((8, rows, model), low),
            pltpu.VMEM((8, rows, 2 * (one + two)), low),
            pltpu.VMEM((8, rows, one + two), low),
            pltpu.VMEM((2, 2, rows, model), low),
            pltpu.VMEM((4, 2, rows, model), low),
            pltpu.VMEM((2, rows, model), low),
            pltpu.VMEM((rows, model), low),
            pltpu.VMEM((2, 8 * shard, 3 * one), low),
            pltpu.VMEM((4, shard, 3 * one), low),
            pltpu.VMEM((8, shard, 3 * one), low),
            sem((4,)), sem((5,)), sem((5,)), sem((4,)), sem((4,)), sem, sem((2,)), sem((4,)), sem((4,)), sem((2,)),
            sem((1,)), sem((32,)), sem((12,)), sem((8,)), sem((8,)), sem((4,)), sem((4,)), sem((1,)),
        ],
        compiler_params=pltpu.CompilerParams(
            collective_id=1, has_side_effects=True, vmem_limit_bytes=65200 << 10
        ),
        name="ffn",
    )(n_own, norm_y, go_all, big, big_two)


def turn(values, cosine, sine):
    return values * cosine + pltpu.roll(values, HD // 2, 1) * sine


def front_kernel(
    ctx_size, span, hidden, sides, w_query, w_key, w_value, w_out, w_gate, w_up, w_down, grad_out,
    normed_o, query_o, kv_o, total_o, mixed_o, resid_o, normed_two_o, small_o, proj_o, out_o, big, big_two, go, relay, spread, norm_y, cosine, sine, pos_k, pos_q,
    proj, out_w, source, source_two, query, kv, mixed,
    load_sem, ag_send, ag_recv, core_send, core_recv, big_send, big_recv, two_recv, relay_recv, go_send, go_recv, kv_send, kv_recv, back_sem, norm_sem,
):
    dp = lax.axis_index("dp")
    ctx = lax.axis_index("ctx")
    me = dp * ctx_size + ctx
    shard, wide = w_out.shape[0], proj.shape[1]
    rows, model = hidden.shape
    one, two = big.shape[1] // 3, big_two.shape[1] // 3
    kv_width = KV_HEADS * HD
    q_width = HEADS * HD
    proj_width = q_width + 2 * kv_width
    groups = HEADS // KV_HEADS

    def at(index):
        return (index // ctx_size, index % ctx_size)

    def block(mask, count=1):
        base = flip(me, mask) // count * count
        return pl.ds(pl.multiple_of(base * shard, shard), shard * count)

    def remote(src, dst, send, recv, mask):
        return pltpu.make_async_remote_copy(
            src_ref=src, dst_ref=dst, send_sem=send, recv_sem=recv, device_id=at(flip(me, mask)), device_id_type=MESH
        )

    def drain(ref, sem):
        pltpu.make_async_copy(ref, ref, sem).wait()

    barrier = pltpu.get_barrier_semaphore()
    partners = (1, 2, 3, 4, 5, 8, 16, 17, 20, 21)
    for mask in partners:
        pl.semaphore_signal(barrier, inc=1, device_id=at(flip(me, mask)), device_id_type=MESH)

    own = (
        pltpu.make_async_copy(w_query, proj.at[block(0), pl.ds(0, q_width)], load_sem.at[0]),
        pltpu.make_async_copy(w_out, out_w.at[block(0)], load_sem.at[1]),
        pltpu.make_async_copy(w_key, proj.at[block(0), pl.ds(q_width, kv_width)], load_sem.at[50]),
        pltpu.make_async_copy(w_value, proj.at[block(0), pl.ds(q_width + kv_width, kv_width)], load_sem.at[51]),
        pltpu.make_async_copy(sides, proj.at[block(0), pl.ds(proj_width, HD)], load_sem.at[52]),
    )
    for copy in own:
        copy.start()
    hidden_units = w_gate.shape[1]
    cuts = []
    for k in range(8):
        for n, ref in enumerate((w_gate, w_up, w_down)):
            for to, start, width in ((source, k * (one + two), one), (source_two, k * (one + two) + one, two)):
                size = min(width, hidden_units - start)
                cuts.append((ref.at[:, pl.ds(start, size)], to.at[k, :, pl.ds(n * width, size)]))
                if size < width:
                    to[k, :, pl.ds(n * width + size, width - size)] = jnp.zeros((shard, width - size), to.dtype)
    cuts = [pltpu.make_async_copy(a, b, load_sem.at[2 + i]) for i, (a, b) in enumerate(cuts)]
    for copy in cuts:
        copy.start()
    pl.semaphore_wait(barrier, len(partners))
    for copy in own:
        copy.wait()

    q_cols, k_cols = pl.ds(0, q_width), pl.ds(q_width, wide - q_width)
    streams = ((proj, k_cols), (proj, q_cols), (out_w, q_cols))

    def ag(n, mask, *overs):
        ref, cols = streams[n]
        part = ref.at[block(mask), cols]
        for over in overs:
            remote(part, part, ag_send.at[n], ag_recv.at[n, mask | over], over).start()

    def ag_pass(n, mask, *overs):
        ref, cols = streams[n]
        part = ref.at[block(mask), cols]
        remote(part, part, ag_send.at[n], ag_recv.at[n, mask], 1).wait_recv()
        ag(n, mask, *overs)

    def group(n, mask):
        ref, cols = streams[n]
        part = ref.at[block(mask, 4), cols]
        return remote(part, part, core_send.at[n, mask // 8], core_recv.at[n, mask // 8], 4)

    def group_wait(n):
        ref, cols = streams[n]
        for mask in (0, 8, 16, 24):
            part = ref.at[block(mask | 4, 4), cols]
            remote(part, part, core_send.at[n, mask // 8], core_recv.at[n, mask // 8], 4).wait_recv()

    ag(0, 0, 2, 1, 8, 16)
    ag(1, 0, 2, 1, 8, 16)

    for copy in cuts:
        copy.wait()
    y, x, c = dp // 4, (dp // 2) % 2, dp % 2
    h, p = ctx // 2, ctx % 2

    def column(mask):
        return either(y, mask // 16) * 4 + either(p, mask % 2) * 2 + either(c, (mask // 4) % 2)

    own_big = pltpu.make_async_copy(source.at[column(0)], big.at[block(0)], load_sem.at[0])
    own_big.start()
    own_two = pltpu.make_async_copy(source_two.at[column(0)], big_two.at[block(0)], load_sem.at[1])
    own_two.start()

    def cut(mask):
        remote(source.at[column(mask)], big.at[block(0)], big_send.at[0], big_recv.at[mask], mask).start()

    def cut_two(mask):
        return remote(source_two.at[column(mask)], big_two.at[block(0)], big_send.at[1], two_recv.at[mask], mask)

    held = (0, 4, 1, 5, 16, 20, 17, 21)
    inner = either(h, p) == 1

    def over_z(mask):
        src = big.at[block(mask)] if mask else source.at[column(0)]

        @pl.when(inner)
        def _():
            remote(src, big.at[block(mask)], big_send.at[0], big_recv.at[mask | 2], 2).start()

        @pl.when(jnp.logical_not(inner))
        def _():
            i = held.index(mask)
            remote(src, relay.at[i], big_send.at[0], relay_recv.at[i], 1).start()

    def relay_pass(*masks):
        @pl.when(inner)
        def _():
            for mask in masks:
                i = held.index(mask)
                remote(relay.at[i], relay.at[i], big_send.at[0], relay_recv.at[i], 1).wait_recv()
                remote(relay.at[i], big.at[block(mask ^ 1)], big_send.at[2], big_recv.at[mask | 2], 3).start()

    def big_forward(mask, over):
        if over == 2:
            over_z(mask)
        else:
            remote(big.at[block(mask)], big.at[block(mask)], big_send.at[0], big_recv.at[mask | over], over).start()

    def big_pass(mask, *overs):
        remote(big.at[block(mask)], big.at[block(mask)], big_send.at[0], big_recv.at[mask], 1).wait_recv()
        for over in overs:
            big_forward(mask, over)

    cut(4)
    over_z(0)

    row = lax.broadcasted_iota(jnp.int32, (model, 2 * kv_width), 0)
    col = lax.broadcasted_iota(jnp.int32, (model, 2 * kv_width), 1)
    per = kv_width * shard // model
    unit = (col % kv_width) // per * shard + col // kv_width * per + col % per
    spread[...] = jnp.where(row == unit, 1.0, 0.0).astype(jnp.bfloat16)
    length = rows // 2
    for j in range(2 * ctx_size):
        lane = lax.broadcasted_iota(jnp.int32, (1, length), 1)
        pos_k[:, pl.ds(j * length, length)] = (span[0, j] * length + lane).astype(jnp.float32)
    pos_q[...] = pos_k[:, pl.ds(pl.multiple_of(ctx * rows, rows), rows)]
    own_pos = jnp.transpose(jnp.broadcast_to(pos_q[...], (HD, rows)))
    lane = lax.broadcasted_iota(jnp.int32, (rows, HD), 1)
    turns = (lane % (HD // 2)).astype(jnp.float32) * (2.0 / HD)
    angles = own_pos * jnp.exp(turns * -math.log(rope_base))
    cosine[...] = jnp.cos(angles)
    sine[...] = jnp.sin(angles) * jnp.where(lane < HD // 2, -1.0, 1.0)
    own_pos = own_pos[:, :1]

    ag_pass(0, 1, 8, 16)
    ag_pass(0, 8, 16)
    ag_pass(0, 2, 1, 8, 16)
    ag_pass(0, 9, 16)
    ag_pass(1, 1, 8, 16)
    ag_pass(1, 8, 16)
    ag_pass(0, 3, 8, 16)
    ag_pass(0, 10, 16)
    ag_pass(1, 2, 1, 8, 16)
    group(0, 0).start()
    remote(source.at[column(0)], big.at[block(0)], big_send.at[0], big_recv.at[8], 8).start()
    cut(1)
    cut(5)
    big_pass(4, 2, 8)
    ag_pass(0, 11, 16)
    group(0, 8).start()
    relay_pass(0)
    ag_pass(1, 9, 16)
    ag(2, 0, 2, 1, 16, 8)
    for mask in (16, 17, 18, 19):
        ag_pass(0, mask)
    group(0, 16).start()
    ag_pass(1, 3, 8, 16)
    group(1, 0).start()
    for mask in (24, 25, 26, 27):
        ag_pass(0, mask)
    group(0, 24).start()
    relay_pass(4)
    group_wait(0)

    small = jnp.transpose(proj[:, proj_width:].astype(jnp.float32))
    small_o[...] = small[:8]
    kv_bias = dot(small[:8].astype(jnp.bfloat16), spread[...], ((1,), (0,)))[3:4]
    values = hidden[...].astype(jnp.float32)
    factor = lax.rsqrt(jnp.mean(values * values, axis=-1, keepdims=True) + norm_eps)
    normed_o[...] = (values * factor * small[0:1]).astype(jnp.bfloat16)
    cos, sin = cosine[...], sine[...]
    raw = dot(normed_o[...], proj[:, q_width:proj_width], ((1,), (0,))) + kv_bias
    mine = block(0)
    for g in range(KV_HEADS):
        kv[ctx, :, pl.ds(g * HD, HD)] = turn(raw[:, g * HD : (g + 1) * HD], cos, sin).astype(jnp.bfloat16)
    kv[ctx, :, pl.ds(kv_width, kv_width)] = raw[:, kv_width:].astype(jnp.bfloat16)
    def kv_push(mask, over):
        slot = flip(ctx, mask)
        return remote(kv.at[slot], kv.at[slot], kv_send.at[mask | over], kv_recv.at[mask | over], over)
    kv_push(0, 2).start()
    kv_push(0, 1).start()
    ag_pass(1, 10, 16)
    ag_pass(1, 11, 16)
    group(1, 8).start()
    big_pass(1, 2, 8)
    ag_pass(2, 1, 16, 8)
    relay_pass(1)
    ag_pass(2, 2, 1, 16, 8)
    cut(16)
    cut(20)
    cut(17)
    cut(21)
    kv_push(0, 2).wait_recv()
    kv_push(2, 1).start()
    big_pass(5, 2, 8)
    for mask in (16, 17, 18, 19):
        ag_pass(1, mask)
    group(1, 16).start()
    ag_pass(2, 3, 16, 8)
    group(2, 0).start()
    for mask in (24, 25, 26, 27):
        ag_pass(1, mask)
    group(1, 24).start()
    big_pass(16, 2, 8)
    relay_pass(5)
    group_wait(1)
    for half in range(2):
        part = half * (q_width // 2)
        raw = dot(normed_o[...], proj[:, part : part + q_width // 2], ((1,), (0,)))
        raw = raw + small[1:2, part : part + q_width // 2]
        for i in range(HEADS // 2):
            query[half * (HEADS // 2) + i] = turn(raw[:, i * HD : (i + 1) * HD], cos, sin).astype(jnp.bfloat16)
    big_pass(20, 2, 8)
    relay_pass(16)
    for mask in (16, 17, 18, 19):
        ag_pass(2, mask, 8)
    group(2, 16).start()
    big_pass(17, 2, 8)
    big_pass(21, 2, 8)
    relay_pass(20)
    def go_core(o):
        src = go.at[2 * o] if o else grad_out
        return remote(src, go.at[2 * o + 1], go_send.at[3 + o], go_recv.at[2 * o + 1], 4)
    def go_push(o):
        src = go.at[2] if o == 3 else grad_out
        return remote(src, go.at[2 * o], go_send.at[o - 1], go_recv.at[2 * o], (0, 1, 16, 16)[o])
    go_push(2).start()
    go_push(1).start()
    go_core(0).start()
    big_pass(2, 8)
    big_pass(6, 8)
    kv_push(0, 1).wait_recv()
    kv_push(2, 1).wait_recv()
    query_back = pltpu.make_async_copy(query, query_o, back_sem.at[0])
    query_back.start()
    kv_back = pltpu.make_async_copy(kv, kv_o, back_sem.at[1])
    kv_back.start()
    def head(n, carry):
        g = n // groups
        keys = kv[:, :, pl.ds(pl.multiple_of(g * HD, HD), HD)].reshape(ctx_size * rows, HD)
        vals = kv[:, :, pl.ds(pl.multiple_of(kv_width + g * HD, HD), HD)].reshape(ctx_size * rows, HD)
        scores = dot(query[n], keys, ((1,), (1,))) * HD ** (-0.5)
        scores = jnp.where(pos_k[...] <= own_pos, scores, masked_fill)
        top = jnp.max(scores, axis=-1, keepdims=True)
        expo = jnp.exp(scores - top)
        expo_sum = jnp.sum(expo, axis=-1, keepdims=True)
        attend = (expo / expo_sum).astype(jnp.bfloat16)
        mixed[:, pl.ds(pl.multiple_of(n * HD, HD), HD)] = dot(attend, vals, ((1,), (0,))).astype(jnp.bfloat16)
        lane = lax.broadcasted_iota(jnp.int32, (rows, HD), 1)
        total_o[...] = jnp.where(lane == n, top + jnp.log(expo_sum), total_o[...])
        return carry
    total_o[...] = jnp.zeros_like(total_o)
    lax.fori_loop(0, HEADS, head, 0)
    own_go = pltpu.make_async_copy(grad_out, go.at[0], load_sem.at[2])
    own_go.start()
    big_pass(3, 8)
    mixed_back = pltpu.make_async_copy(mixed, mixed_o, back_sem.at[2])
    mixed_back.start()
    relay_pass(17)
    relay_pass(21)
    def two_over_z(mask):
        src = big_two.at[block(mask)] if mask else source_two.at[column(0)]
        return remote(src, big_two.at[block(mask)], big_send.at[1], two_recv.at[mask | 2], 2)
    big_pass(7, 8)
    cut_two(1).start()
    cut_two(5).start()
    cut_two(16).start()
    cut_two(20).start()
    cut_two(17).start()
    cut_two(21).start()
    for n, mask in enumerate((8, 9, 10, 11, 24, 25, 26, 27)):
        ag_pass(2, mask)
        if n % 4 == 3:
            group(2, mask & 24).start()
    group_wait(2)
    cut_two(4).start()
    proj_back = pltpu.make_async_copy(proj, proj_o, back_sem.at[4])
    proj_back.start()
    out_back = pltpu.make_async_copy(out_w, out_o, back_sem.at[5])
    out_back.start()
    resid = hidden[...].astype(jnp.float32) + dot(mixed[...], out_w[...], ((1,), (1,)))
    resid_o[...] = resid
    factor = lax.rsqrt(jnp.mean(resid * resid, axis=-1, keepdims=True) + norm_eps)
    normed_two_o[...] = (resid * factor * small_o[2:3]).astype(jnp.bfloat16)
    norm_push = remote(normed_two_o, norm_y, norm_sem.at[0], norm_sem.at[1], 16)
    norm_push.start()
    go_push(1).wait_recv()
    go_push(3).start()
    go_core(1).start()
    go_push(2).wait_recv()
    go_core(2).start()
    two_over_z(0).start()
    for mask, passed in ((4, 18), (1, 22), (5, 19), (0, 23)):
        big_pass(passed, 8)
        if mask:
            cut_two(mask).wait_recv()
            two_over_z(mask).start()

    norm_push.wait()
    for mask in (8, 12, 9, 24, 13, 28, 25, 29, 10, 14, 11, 26, 15, 30, 27, 31):
        big_pass(mask)
    go_push(3).wait_recv()
    go_core(3).start()
    for mask in (16, 20, 17, 21):
        cut_two(mask).wait_recv()
    for mask in (0, 4, 1, 5):
        two_over_z(mask).wait_recv()
    own_big.wait()
    own_two.wait()
    own_go.wait()
    drain(big.at[pl.ds(0, 31 * shard)], big_send.at[0])
    drain(big_two.at[pl.ds(0, 11 * shard)], big_send.at[1])

    @pl.when(inner)
    def _():
        drain(relay, big_send.at[2])

    for n in range(3):
        ref, cols = streams[n]
        drain(ref.at[pl.ds(0, 15 * shard), cols], ag_send.at[n])
        for mask in (0, 8, 16, 24):
            group(n, mask).wait_send()
    for o in range(4):
        go_core(o).wait()
    for o in (1, 2, 3):
        go_push(o).wait_send()
    kv_push(0, 2).wait_send()
    kv_push(0, 1).wait_send()
    kv_push(2, 1).wait_send()
    for copy in (query_back, kv_back, mixed_back, proj_back, out_back):
        copy.wait()


def front_call(
    ctx_size, span, hidden, sides, w_query, w_key, w_value, w_out, w_gate, w_up, w_down, grad_out
):
    rows, model = hidden.shape
    shard = w_out.shape[0]
    kv_width = KV_HEADS * HD
    q_width = HEADS * HD
    wide = q_width + 2 * kv_width + HD
    one, two = widths(w_gate.shape[1])
    low, full = jnp.bfloat16, jnp.float32
    vmem = pl.BlockSpec(memory_space=pltpu.VMEM)
    anywhere = pl.BlockSpec(memory_space=pl.ANY)
    shapes = (
        ((rows, model), low, vmem),
        ((HEADS, rows, HD), low, anywhere),
        ((ctx_size, rows, 2 * kv_width), low, anywhere),
        ((rows, HD), full, vmem),
        ((rows, q_width), low, anywhere),
        ((rows, model), full, vmem),
        ((rows, model), low, vmem),
        ((8, model), full, vmem),
        ((model, wide), low, anywhere),
        ((model, q_width), low, anywhere),
        ((model, 3 * one), low, anywhere),
        ((model, 3 * two), low, anywhere),
        ((8, rows, model), low, anywhere),
        ((8, shard, 3 * one), low, anywhere),
        ((model, 2 * kv_width), low, vmem),
        ((rows, model), low, anywhere),
        ((rows, HD), full, vmem),
        ((rows, HD), full, vmem),
        ((1, ctx_size * rows), full, vmem),
        ((1, rows), full, vmem),
    )
    sem = pltpu.SemaphoreType.DMA
    return pl.pallas_call(
        functools.partial(front_kernel, ctx_size),
        out_shape=tuple(jax.ShapeDtypeStruct(shape, kind) for shape, kind, _ in shapes),
        in_specs=[pl.BlockSpec(memory_space=pltpu.SMEM), vmem] + [anywhere] * 9,
        out_specs=tuple(spec for _, _, spec in shapes),
        scratch_shapes=[
            pltpu.VMEM((model, wide), low),
            pltpu.VMEM((model, q_width), low),
            pltpu.VMEM((8, shard, 3 * one), low),
            pltpu.VMEM((8, shard, 3 * two), low),
            pltpu.VMEM((HEADS, rows, HD), low),
            pltpu.VMEM((ctx_size, rows, 2 * kv_width), low),
            pltpu.VMEM((rows, q_width), low),
            sem((53,)), sem((3,)), sem((3, 32)), sem((3, 4)), sem((3, 4)), sem((3,)), sem((32,)), sem((32,)), sem((8,)),
            sem((7,)), sem((8,)), sem((4,)), sem((4,)), sem((6,)), sem((2,)),
        ],
        compiler_params=pltpu.CompilerParams(
            collective_id=0, has_side_effects=True, vmem_limit_bytes=56 << 20
        ),
        name="front",
    )(span, hidden, sides, w_query, w_key, w_value, w_out, w_gate, w_up, w_down, grad_out)


def back_kernel(
    ctx_size, grad_two, resid, hidden, grad_out, normed, mixed, query, kv, total, cosine, sine, pos_q, pos_k, small, spread,
    proj, out_w, grads, grads_two, near, zin_first, r_part,
    hidden_o, query_o, key_o, outw_o, fin, fin_two, r_in, relay, relay_two,
    weight, turned, left_n, left_a, right_b, right_p, side, side_in, g_b, g_q, g_k,
    y_b, y_q, y_k, x_b, x_q, x_k, p_b, p_q, p_k, h_b, h_q, h_k,
    own, far, zin, own_two, far_two, zin_two, r_mid, r_one, heads_g, lse, dkv, kv_out, kv_p, kv_h, grad_resid,
    load_sem, xs, xr, zs, zr, fs, fr, xs2, xr2, zs2, zr2, fs2, fr2, relay_recv, relay_send, cs, cr, rs, rr, ks, kr, os, orr, keep_sem,
):
    dp = lax.axis_index("dp")
    ctx = lax.axis_index("ctx")
    me = dp * ctx_size + ctx
    y, x, c = dp // 4, (dp // 2) % 2, dp % 2
    h, p = ctx // 2, ctx % 2
    rows, model = resid.shape
    shard = grads.shape[3]
    kv_width = KV_HEADS * HD
    q_width = HEADS * HD
    groups = HEADS // KV_HEADS
    low, full = jnp.bfloat16, jnp.float32
    span = ctx_size * shard

    def at(index):
        return (index // ctx_size, index % ctx_size)

    def remote(src, dst, send, recv, mask):
        return pltpu.make_async_remote_copy(
            src_ref=src, dst_ref=dst, send_sem=send, recv_sem=recv, device_id=at(flip(me, mask)), device_id_type=MESH
        )

    def group_rows(mask):
        return pl.ds(pl.multiple_of(flip(dp, mask // 4) * span, span), span)

    def mask_of(j):
        return (j // 4) * 16 + ((j // 2) % 2) * 4 + j % 2

    barrier = pltpu.get_barrier_semaphore()
    partners = (1, 2, 3, 4, 5, 8, 16, 17, 20, 21)
    for mask in partners:
        pl.semaphore_signal(barrier, inc=1, device_id=at(flip(me, mask)), device_id_type=MESH)
    load_w = pltpu.make_async_copy(out_w, weight.at[:, pl.ds(0, q_width)], load_sem.at[0])
    load_w.start()
    load_own = [
        pltpu.make_async_copy(grads.at[0, 0], own, load_sem.at[1]),
        pltpu.make_async_copy(grads_two.at[0], own_two, load_sem.at[2]),
        pltpu.make_async_copy(zin_first, zin.at[pl.ds(0, 4)], load_sem.at[3]),
        pltpu.make_async_copy(r_part.at[1], r_one, load_sem.at[4]),
    ]
    for copy in load_own:
        copy.start()
    pl.semaphore_wait(barrier, len(partners))

    def far_push(j):
        return remote(grads.at[1, 0, j], far.at[j], xs.at[j], xr.at[j], 8)

    def far_two_push(half, j):
        return remote(grads_two.at[1, half, j], far_two.at[half, j], xs2.at[half, j], xr2.at[half, j], 8)

    def z_push(j):
        return remote(near.at[j], zin.at[j], zs.at[j], zr.at[j], 2)

    def z_two_push(j):
        return remote(far_two.at[1, j], zin_two.at[j], zs2.at[j], zr2.at[j], 2)

    inner = either(h, p) == 1

    def over_z(push, src, to, send, n):
        @pl.when(inner)
        def _():
            push.start()

        @pl.when(jnp.logical_not(inner))
        def _():
            remote(src, to, send, relay_recv.at[n], 1).start()

    def over_z_one(j):
        over_z(z_push(j), near.at[j], relay.at[j - 4], zs.at[j], j)

    def over_z_two(j):
        over_z(z_two_push(j), far_two.at[1, j], relay_two.at[j], zs2.at[j], 8 + j)

    def relay_one(*blocks):
        @pl.when(inner)
        def _():
            for j in blocks:
                part = relay.at[j - 4]
                remote(part, part, relay_send.at[j], relay_recv.at[j], 1).wait_recv()
                remote(part, zin.at[j], relay_send.at[j], zr.at[j], 3).start()

    def relay_two_pass(*blocks):
        @pl.when(inner)
        def _():
            for j in blocks:
                part = relay_two.at[j]
                remote(part, part, relay_send.at[8 + j], relay_recv.at[8 + j], 1).wait_recv()
                remote(part, zin_two.at[j], relay_send.at[8 + j], zr2.at[j], 3).start()

    def fin_push(j):
        return remote(own.at[j], fin.at[j], fs.at[j], fr.at[j], mask_of(j))

    def fin_two_push(j):
        return remote(own_two.at[0, j], fin_two.at[j], fs2.at[j], fr2.at[j], mask_of(j))

    keep_one = pltpu.make_async_copy(own.at[0], fin.at[0], keep_sem.at[0])
    keep_two = pltpu.make_async_copy(own_two.at[0, 0], fin_two.at[0], keep_sem.at[1])

    def z_two_step(j):
        far_two_push(1, j).wait_recv()
        far_two[1, j] = (far_two[1, j].astype(full) + own_two[1, j].astype(full)).astype(low)
        over_z_two(j)

    def total_step(j):
        far_push(j).wait_recv()
        if j > 3:
            z_push(j).wait_recv()
        own[j] = (own[j].astype(full) + far[j].astype(full) + zin[j].astype(full)).astype(low)
        if j:
            fin_push(j).start()
        else:
            keep_one.start()

    def total_two_step(j):
        far_two_push(0, j).wait_recv()
        z_two_push(j).wait_recv()
        own_two[0, j] = (own_two[0, j].astype(full) + far_two[0, j].astype(full) + zin_two[j].astype(full)).astype(low)
        if j:
            fin_two_push(j).start()
        else:
            keep_two.start()

    def r_push(o):
        src = r_one if o == 1 else r_part.at[o]
        dst = r_mid if o == 3 else r_in.at[o - 1]
        return remote(src, dst, os.at[o], orr.at[o], (0, 1, 16, 16)[o])

    r_push(3).start()
    for j in range(4, 8):
        over_z_one(j)
    for j in range(8):
        far_two_push(1, j).start()
    for j in range(8):
        far_push(j).start()

    def transposed(value, left, n):
        turned[n] = jnp.transpose(value)
        for i, mask in enumerate((0, 8, 16, 24)):
            left[i, :, pl.ds(0, rows)] = turned[n, group_rows(mask)]
            cross_left(left, n, i, mask).start()

    def cross_left(left, n, i, mask):
        return remote(turned.at[n, group_rows(mask | 4)], left.at[i, :, pl.ds(rows, rows)], cs.at[n, i], cr.at[n, i], 4)

    def cross(src, dst, n, i):
        return remote(src, dst, cs.at[n, i], cr.at[n, i], 4)

    transposed(normed[...], left_n, 0)
    right_b[pl.ds(0, rows)] = mixed[...]
    cross_mixed = cross(mixed, right_b.at[pl.ds(rows, rows)], 2, 0)
    cross_mixed.start()

    value = resid[...]
    factor = lax.rsqrt(jnp.mean(value * value, axis=-1, keepdims=True) + norm_eps)
    unit = value * factor
    scaled = grad_two[...] * small[2:3]
    ffn_row = jnp.sum(grad_two[...] * unit, axis=0, keepdims=True)
    grad_resid[...] = grad_out[...].astype(full) + factor * (
        scaled - unit * jnp.mean(scaled * unit, axis=-1, keepdims=True)
    )
    grad_attn = grad_resid[...].astype(low)
    transposed(grad_attn, left_a, 1)
    lse[...] = jnp.transpose(total[...])
    sin_back = -sine[...]
    key_pos = jnp.transpose(jnp.broadcast_to(pos_k[...], (HD, pos_k.shape[1])))[:, :1]
    load_w.wait()
    for half in range(2):
        part = half * (q_width // 2)
        moved = dot(grad_attn, weight[:, part : part + q_width // 2], ((1,), (0,))).astype(low)
        for i in range(HEADS // 2):
            heads_g[half * (HEADS // 2) + i] = moved[:, i * HD : (i + 1) * HD]
    load_p = pltpu.make_async_copy(proj, weight, load_sem.at[0])
    load_p.start()

    streams = ((g_b, y_b, x_b, p_b, h_b), (g_q, y_q, x_q, p_q, h_q), (g_k, y_k, x_k, p_k, h_k))

    def add(ref, other):
        ref[...] = (ref[...].astype(full) + other[...].astype(full)).astype(low)

    def y_push(s, k):
        g, yy = streams[s][:2]
        return remote(g.at[2 + k], yy.at[k], rs.at[s, k], rr.at[s, k], 16)

    def x_push(s):
        g, xx = streams[s][0], streams[s][2]
        return remote(g.at[1], xx, rs.at[s, 2], rr.at[s, 2], 8)

    def block_of(hr, other):
        z = 2 * either(h, hr) + either(p, other)
        return pl.ds(pl.multiple_of(z * shard, shard), shard)

    def p_push(s, hr):
        g, pp = streams[s][0], streams[s][3]
        return remote(g.at[0, block_of(hr, 1)], pp.at[hr], rs.at[s, 3 + hr], rr.at[s, 3 + hr], 1)

    def h_push(s):
        g, hh = streams[s][0], streams[s][4]
        return remote(g.at[0, block_of(1, 0)], hh, rs.at[s, 5], rr.at[s, 5], 2)

    def y_pass(s):
        g, yy = streams[s][:2]
        y_push(s, 1).wait_recv()
        add(g.at[1], yy.at[1])
        x_push(s).start()
        y_push(s, 0).wait_recv()
        add(g.at[0], yy.at[0])

    def x_pass(s):
        x_push(s).wait_recv()
        add(streams[s][0].at[0], streams[s][2])
        p_push(s, 1).start()
        p_push(s, 0).start()

    def p_pass(s):
        g, pp = streams[s][0], streams[s][3]
        p_push(s, 1).wait_recv()
        add(g.at[0, block_of(1, 0)], pp.at[1])
        h_push(s).start()
        p_push(s, 0).wait_recv()
        add(g.at[0, block_of(0, 0)], pp.at[0])

    def h_pass(s, out):
        h_push(s).wait_recv()
        out[...] = streams[s][0][0, block_of(0, 0)].astype(full) + streams[s][4][...].astype(full)

    for i, mask in enumerate((0, 8, 16, 24)):
        cross_left(left_a, 1, i, mask).wait_recv()
    cross_mixed.wait_recv()
    for i in (3, 2, 1, 0):
        g_b[i] = dot(left_a[i], right_b[...], ((1,), (0,))).astype(low)
    y_push(0, 1).start()

    def head(n, carry):
        g = n // groups
        k_cols = pl.ds(pl.multiple_of(g * HD, HD), HD)
        v_cols = pl.ds(pl.multiple_of(kv_width + g * HD, HD), HD)
        keys = kv[:, :, k_cols].reshape(ctx_size * rows, HD)
        vals = kv[:, :, v_cols].reshape(ctx_size * rows, HD)
        scores = dot(keys, query[n], ((1,), (1,))) * HD ** (-0.5)
        scores = jnp.where(key_pos <= pos_q[...], scores, masked_fill)
        attend = jnp.exp(scores - lse[pl.ds(n, 1), :])
        grad_attend = dot(vals, heads_g[n], ((1,), (1,)))
        delta = jnp.sum(grad_attend * attend, axis=0, keepdims=True)
        grad_scores = (attend * (grad_attend - delta)).astype(low)
        dkv[:, k_cols] += dot(grad_scores, query[n], ((1,), (0,)))
        dkv[:, v_cols] += dot(attend.astype(low), heads_g[n], ((1,), (0,)))
        back = dot(grad_scores, keys, ((0,), (0,))) * HD ** (-0.5)
        back = turn(back, cosine[...], sin_back).astype(low)
        right_p[pl.ds(0, rows), pl.ds(pl.multiple_of(n * HD, HD), HD)] = back
        return carry

    dkv[...] = jnp.zeros_like(dkv)
    lax.fori_loop(0, HEADS // 2, head, 0)
    relay_one(4, 5)
    lax.fori_loop(HEADS // 2, HEADS, head, 0)

    for z in range(ctx_size):
        part = dkv[pl.ds(z * rows, rows)]
        kv_out[z, :, pl.ds(0, kv_width)] = (part[:, :kv_width] * HD ** (-0.5)).astype(low)
        kv_out[z, :, pl.ds(kv_width, kv_width)] = part[:, kv_width:].astype(low)

    def kv_push(hr):
        return remote(kv_out.at[2 * either(h, hr) + 1 - p], kv_p.at[hr], ks.at[hr], kr.at[hr], 1)

    def kv_cross():
        return remote(kv_out.at[2 * (1 - h) + p], kv_h, ks.at[2], kr.at[2], 2)

    kv_push(1).start()
    kv_push(0).start()
    cross_q = cross(
        right_p.at[pl.ds(0, rows), pl.ds(0, q_width)], right_p.at[pl.ds(rows, rows), pl.ds(0, q_width)], 2, 1
    )
    cross_q.start()
    for copy in load_own:
        copy.wait()
    for i, mask in enumerate((0, 8, 16, 24)):
        cross_left(left_n, 0, i, mask).wait_recv()
    cross_q.wait_recv()
    for i in (3, 2, 1, 0):
        g_q[i] = dot(left_n[i], right_p[:, pl.ds(0, q_width)], ((1,), (0,))).astype(low)
        if i > 1:
            y_push(1, i - 2).start()
    load_p.wait()
    hidden_o[...] = dot(right_p[pl.ds(0, rows), pl.ds(0, q_width)], weight[:, pl.ds(0, q_width)], ((1,), (1,)))
    kv_push(1).wait_recv()
    add(kv_out.at[2 * (1 - h) + p], kv_p.at[1])
    kv_cross().start()
    kv_push(0).wait_recv()
    add(kv_out.at[2 * h + p], kv_p.at[0])
    relay_one(6, 7)
    for j in range(8):
        z_two_step(j)
    for j in range(4):
        total_step(j)
    relay_two_pass(0, 1, 2)
    kv_cross().wait_recv()
    final = kv_out[2 * h + p].astype(full) + kv_h[...].astype(full)
    for g in range(KV_HEADS):
        right_p[pl.ds(0, rows), pl.ds(q_width + g * HD, HD)] = turn(
            final[:, g * HD : (g + 1) * HD], cosine[...], sin_back
        ).astype(low)
    right_p[pl.ds(0, rows), pl.ds(q_width + kv_width, kv_width)] = final[:, kv_width:].astype(low)
    cross_kv = cross(
        right_p.at[pl.ds(0, rows), pl.ds(q_width, 2 * kv_width)],
        right_p.at[pl.ds(rows, rows), pl.ds(q_width, 2 * kv_width)], 2, 2,
    )
    cross_kv.start()
    grad_one = hidden_o[...] + dot(
        right_p[pl.ds(0, rows), pl.ds(q_width, 2 * kv_width)], weight[:, pl.ds(q_width, 2 * kv_width)], ((1,), (1,))
    )
    value = hidden[...].astype(full)
    factor = lax.rsqrt(jnp.mean(value * value, axis=-1, keepdims=True) + norm_eps)
    unit = value * factor
    scaled = grad_one * small[0:1]
    attn_row = jnp.sum(grad_one * unit, axis=0, keepdims=True)
    hidden_o[...] = grad_resid[...] + factor * (scaled - unit * jnp.mean(scaled * unit, axis=-1, keepdims=True))
    bias = jnp.sum(right_p[pl.ds(0, rows)].astype(full), axis=0, keepdims=True)
    kv_bias = jnp.broadcast_to(bias[:, q_width:], (8, 2 * kv_width)).astype(low)
    kv_row = dot(kv_bias, spread[...], ((1,), (1,)))[:1]
    table = jnp.concatenate([attn_row, bias[:, :q_width], ffn_row, kv_row, jnp.zeros((124, model), full)], axis=0)
    side[...] = jnp.transpose(table).astype(low)

    def cross_side(i, mask):
        return cross(side.at[group_rows(mask | 4)], side_in.at[i], 3, i)

    for i, mask in enumerate((0, 8, 16, 24)):
        cross_side(i, mask).start()
    cross_kv.wait_recv()
    for i, mask in ((3, 24), (2, 16), (1, 8), (0, 0)):
        g_k[i, :, pl.ds(0, 2 * kv_width)] = dot(
            left_n[i], right_p[:, pl.ds(q_width, 2 * kv_width)], ((1,), (0,))
        ).astype(low)
        cross_side(i, mask).wait_recv()
        g_k[i, :, pl.ds(2 * kv_width, HD)] = (
            side[group_rows(mask)].astype(full) + side_in[i].astype(full)
        ).astype(low)
        if i > 1:
            y_push(2, i - 2).start()
    y_push(0, 0).start()
    r_push(3).wait_recv()
    add(r_one, r_mid)
    r_push(1).start()
    relay_two_pass(3)
    relay_two_pass(4)
    relay_two_pass(5)
    relay_two_pass(6)
    relay_two_pass(7)
    total_step(4)
    total_step(5)
    total_step(6)
    total_step(7)
    y_pass(1)
    y_pass(2)
    far_two_push(0, 2).start()
    far_two_push(0, 0).start()
    far_two_push(0, 3).start()
    far_two_push(0, 1).start()
    far_two_push(0, 4).start()
    far_two_push(0, 5).start()
    far_two_push(0, 6).start()
    total_two_step(1)
    far_two_push(0, 7).start()
    y_pass(0)
    x_pass(1)
    x_pass(2)
    r_push(2).start()
    p_pass(1)
    p_pass(2)
    total_two_step(0)
    total_two_step(2)
    total_two_step(4)
    total_two_step(5)
    total_two_step(6)
    total_two_step(7)
    x_pass(0)
    p_pass(0)
    h_pass(1, query_o)
    h_pass(2, key_o)
    total_two_step(3)
    h_pass(0, outw_o)

    for j in range(1, 8):
        fin_push(j).wait_recv()
        fin_two_push(j).wait_recv()
    for o in (1, 2):
        r_push(o).wait()
    r_push(3).wait_send()
    keep_one.wait()
    keep_two.wait()

    for j in range(8):
        far_push(j).wait_send()
        far_two_push(0, j).wait_send()
        far_two_push(1, j).wait_send()
        if j > 3:
            z_push(j).wait_send()
        z_two_push(j).wait_send()
        if j:
            fin_push(j).wait_send()
            fin_two_push(j).wait_send()
    @pl.when(inner)
    def _():
        for j in range(4, 8):
            remote(relay.at[j - 4], relay.at[j - 4], relay_send.at[j], relay_recv.at[j], 1).wait_send()
        for j in range(8):
            remote(relay_two.at[j], relay_two.at[j], relay_send.at[8 + j], relay_recv.at[8 + j], 1).wait_send()

    for i, mask in enumerate((0, 8, 16, 24)):
        cross_left(left_n, 0, i, mask).wait_send()
        cross_left(left_a, 1, i, mask).wait_send()
        cross_side(i, mask).wait_send()
    for copy in (cross_mixed, cross_q, cross_kv):
        copy.wait_send()
    for s in range(3):
        for k in range(2):
            y_push(s, k).wait_send()
            p_push(s, k).wait_send()
        x_push(s).wait_send()
        h_push(s).wait_send()
    kv_push(0).wait_send()
    kv_push(1).wait_send()
    kv_cross().wait_send()


def back_call(
    ctx_size, grad_two, resid, hidden, grad_out, normed, mixed, query, kv, total, cosine, sine, pos_q, pos_k,
    small, spread, proj, out_w, grads, grads_two, near, zin_first, r_part,
):
    rows, model = resid.shape
    shard = grads.shape[3]
    one, two = grads.shape[4] // 3, grads_two.shape[4] // 3
    kv_width = KV_HEADS * HD
    q_width = HEADS * HD
    k_cols = 2 * kv_width + HD
    span = ctx_size * shard
    low, full = jnp.bfloat16, jnp.float32
    vmem = pl.BlockSpec(memory_space=pltpu.VMEM)
    anywhere = pl.BlockSpec(memory_space=pl.ANY)
    shapes = (
        ((rows, model), vmem, full),
        ((shard, q_width), vmem, full),
        ((shard, k_cols), vmem, full),
        ((shard, q_width), vmem, full),
        ((8, shard, 3 * one), anywhere, low),
        ((8, shard, 3 * two), anywhere, low),
        ((2, rows, model), anywhere, low),
        ((4, shard, 3 * one), anywhere, low),
        ((8, shard, 3 * two), anywhere, low),
    )
    sem = pltpu.SemaphoreType.DMA
    cols = (q_width, q_width, k_cols)

    def each(*lead):
        return [pltpu.VMEM(lead + (n,), low) for n in cols]

    return pl.pallas_call(
        functools.partial(back_kernel, ctx_size),
        out_shape=tuple(jax.ShapeDtypeStruct(shape, kind) for shape, _, kind in shapes),
        in_specs=[vmem] * 15 + [anywhere] * 7,
        out_specs=tuple(spec for _, spec, _ in shapes),
        scratch_shapes=[
            pltpu.VMEM(proj.shape, low),
            pltpu.VMEM((2, model, rows), low),
            pltpu.VMEM((4, span, 2 * rows), low),
            pltpu.VMEM((4, span, 2 * rows), low),
            pltpu.VMEM((2 * rows, q_width), low),
            pltpu.VMEM((2 * rows, q_width + 2 * kv_width), low),
            pltpu.VMEM((model, HD), low),
            pltpu.VMEM((4, span, HD), low),
            *each(4, span),
            *each(2, span),
            *each(span),
            *each(2, shard),
            *each(shard),
            *([pltpu.VMEM((8, shard, 3 * one), low)] * 3),
            *([pltpu.VMEM((2, 8, shard, 3 * two), low)] * 2),
            pltpu.VMEM((8, shard, 3 * two), low),
            *([pltpu.VMEM((rows, model), low)] * 2),
            pltpu.VMEM((HEADS, rows, HD), low),
            pltpu.VMEM((HD, rows), full),
            pltpu.VMEM((ctx_size * rows, 2 * kv_width), full),
            pltpu.VMEM((ctx_size, rows, 2 * kv_width), low),
            pltpu.VMEM((2, rows, 2 * kv_width), low),
            pltpu.VMEM((rows, 2 * kv_width), low),
            pltpu.VMEM((rows, model), full),
            sem((5,)), *([sem((8,))] * 6), *([sem((2, 8))] * 2), *([sem((8,))] * 4), sem((16,)), sem((16,)),
            sem((4, 4)), sem((4, 4)), sem((3, 6)), sem((3, 6)), sem((3,)), sem((3,)), sem((4,)), sem((4,)), sem((2,)),
        ],
        compiler_params=pltpu.CompilerParams(
            collective_id=2, has_side_effects=True, vmem_limit_bytes=63 << 20
        ),
        name="back",
    )(
        grad_two, resid, hidden, grad_out, normed, mixed, query, kv, total, cosine, sine, pos_q, pos_k, small, spread,
        proj, out_w, grads, grads_two, near, zin_first, r_part,
    )


def finish_kernel(
    ctx_size, fin, fin_two, key, resid, r_part, r_in, hidden, query, outw,
    result_o, hidden_o, attn_o, query_o, bias_q, key_o, bias_k, value_o, bias_v, outw_o, ffn_o, gate_o, up_o, down_o,
    one_v, two_v, tiles, full_v, sems,
):
    dp = lax.axis_index("dp")
    ctx = lax.axis_index("ctx")
    y, c, p = dp // 4, dp % 2, ctx % 2
    full = jnp.float32
    rows, model = resid.shape
    shard = key.shape[0]
    one, two = fin.shape[2] // 3, fin_two.shape[2] // 3
    width = one + two
    kv_width = key_o.shape[1]
    per = bias_k.shape[1]
    moves = [
        pltpu.make_async_copy(fin, one_v, sems.at[0]),
        pltpu.make_async_copy(fin_two, two_v, sems.at[1]),
        pltpu.make_async_copy(r_part.at[0], tiles.at[0], sems.at[2]),
        pltpu.make_async_copy(r_in, tiles.at[pl.ds(1, 2)], sems.at[3]),
    ]
    for copy in moves:
        copy.start()
    hidden_o[...] = hidden[...]
    query_o[...] = query[...]
    outw_o[...] = outw[...]
    key_o[...] = key[:, :kv_width]
    value_o[...] = key[:, kv_width : 2 * kv_width]
    side = jnp.transpose(key[:, 2 * kv_width :])
    attn_o[...] = side[0:1]
    bias_q[...] = side[1:2]
    ffn_o[...] = side[2:3]
    bias_k[...] = side[3:4, :per]
    bias_v[...] = side[3:4, per : 2 * per]
    moves[0].wait()
    moves[1].wait()
    last = gate_o.shape[1] - 7 * width - one
    for j in range(8):
        k = either(y, j // 4) * 4 + either(p, j % 2) * 2 + either(c, (j // 2) % 2)
        for n, out in enumerate((gate_o, up_o, down_o)):
            at = pl.multiple_of(k * width, HD)
            full_v[n, :, pl.ds(at, one)] = one_v[j, :, n * one : (n + 1) * one].astype(full)

            @pl.when(k < 7)
            def _():
                whole = pl.ds(at, width)
                full_v[n, :, pl.ds(at + one, two)] = two_v[j, :, n * two : (n + 1) * two].astype(full)
                pltpu.make_async_copy(full_v.at[n, :, whole], out.at[:, whole], sems.at[4]).start()

            @pl.when(k == 7)
            def _():
                whole = pl.ds(7 * width, one + last)
                full_v[n, :, pl.ds(7 * width + one, last)] = two_v[j, :, n * two : n * two + last].astype(full)
                pltpu.make_async_copy(full_v.at[n, :, whole], out.at[:, whole], sems.at[4]).start()

    moves[2].wait()
    moves[3].wait()
    value = resid[...]
    for o in range(3):
        value = value + tiles[o].astype(full)
    result_o[...] = value.astype(result_o.dtype)
    pltpu.make_async_copy(full_v, full_v, sems.at[4]).wait()


def finish_call(ctx_size, hidden_units, per, fin, fin_two, key, resid, r_part, r_in, hidden, query, outw):
    rows, model = resid.shape
    shard = key.shape[0]
    kv_width = KV_HEADS * HD
    low, full = jnp.bfloat16, jnp.float32
    vmem = pl.BlockSpec(memory_space=pltpu.VMEM)
    anywhere = pl.BlockSpec(memory_space=pl.ANY)
    shapes = (
        ((rows, model), low, vmem),
        ((rows, model), full, vmem),
        ((1, shard), full, vmem),
        (query.shape, full, vmem),
        ((1, shard), full, vmem),
        ((shard, kv_width), full, vmem),
        ((1, per), full, vmem),
        ((shard, kv_width), full, vmem),
        ((1, per), full, vmem),
        (outw.shape, full, vmem),
        ((1, shard), full, vmem),
        ((shard, hidden_units), full, anywhere),
        ((shard, hidden_units), full, anywhere),
        ((shard, hidden_units), full, anywhere),
    )
    return pl.pallas_call(
        functools.partial(finish_kernel, ctx_size),
        out_shape=tuple(jax.ShapeDtypeStruct(shape, kind) for shape, kind, _ in shapes),
        in_specs=[anywhere, anywhere, vmem, vmem, anywhere, anywhere] + [vmem] * 3,
        out_specs=tuple(spec for _, _, spec in shapes),
        scratch_shapes=[
            pltpu.VMEM(fin.shape, low),
            pltpu.VMEM(fin_two.shape, low),
            pltpu.VMEM((3, rows, model), low),
            pltpu.VMEM((3, shard, hidden_units), full),
            pltpu.SemaphoreType.DMA((5,)),
        ],
        compiler_params=pltpu.CompilerParams(vmem_limit_bytes=63 << 20),
        name="finish",
    )(fin, fin_two, key, resid, r_part, r_in, hidden, query, outw)


def fits(mesh):
    return mesh.shape["dp"] == 8 and mesh.shape["ctx"] == 4


def fast_device(
    hidden,
    cotangent,
    span_order,
    attn_gain,
    w_query,
    b_query,
    w_key,
    b_key,
    w_value,
    b_value,
    w_out,
    ffn_gain,
    w_gate,
    w_up,
    w_down,
):
    ctx_size = lax.axis_size("ctx")
    batches = hidden.shape[0]
    length = hidden.shape[1]
    row_count = batches * length
    shard_rows = w_query.shape[0]
    kv_width = KV_HEADS * HD
    q_width = HEADS * HD

    grad_out = cotangent.reshape(row_count, D)
    per = b_key.shape[0]
    pair = jnp.pad(jnp.concatenate([b_key, b_value]), (0, shard_rows - 2 * per))
    sides = jnp.pad(jnp.stack([attn_gain, b_query, ffn_gain, pair]), ((0, HD - 4), (0, 0))).T
    source = hidden.reshape(row_count, D)
    normed, query_heads, key_value, log_total, mixed, resid, normed_two, small, proj_full, out_full, big, big_two, go_all, _, spread, norm_y, *turns = front_call(
        ctx_size, span_order, source, sides, w_query, w_key, w_value, w_out, w_gate, w_up, w_down, grad_out
    )
    grad_two, r_part, grads, grads_two, near, zin, *_ = ffn_call(ctx_size, shard_rows, normed_two, norm_y, go_all, big, big_two)
    hidden_back, query_sum, kv_sum, out_sum, fin, fin_two, r_in, *_ = back_call(
        ctx_size, grad_two, resid, source, grad_out, normed, mixed, query_heads, key_value, log_total,
        turns[0], turns[1], turns[3], turns[2], small, spread,
        proj_full, out_full, grads, grads_two, near, zin, r_part,
    )
    (
        result, hidden_grad, attn_gain_grad, w_query_grad, b_query_grad, w_key_grad, b_key_grad, w_value_grad,
        b_value_grad, w_out_grad, ffn_gain_grad, w_gate_grad, w_up_grad, w_down_grad,
    ) = finish_call(
        ctx_size, w_gate.shape[1], per, fin, fin_two, kv_sum, resid, r_part, r_in, hidden_back, query_sum, out_sum
    )
    return (
        result.reshape(batches, length, D),
        hidden_grad.reshape(batches, length, D),
        attn_gain_grad.reshape(shard_rows),
        w_query_grad,
        b_query_grad.reshape(shard_rows),
        w_key_grad,
        b_key_grad.reshape(per),
        w_value_grad,
        b_value_grad.reshape(per),
        w_out_grad,
        ffn_gain_grad.reshape(shard_rows),
        w_gate_grad,
        w_up_grad,
        w_down_grad,
    )


def general_device(
    hidden,
    cotangent,
    span_order,
    attn_gain,
    w_query,
    b_query,
    w_key,
    b_key,
    w_value,
    b_value,
    w_out,
    ffn_gain,
    w_gate,
    w_up,
    w_down,
):
    ctx_size = lax.axis_size("ctx")
    ctx_rank = lax.axis_index("ctx")
    batches = hidden.shape[0]
    length = hidden.shape[1]
    span_len = length // 2
    seq_len = length * ctx_size
    row_count = batches * length
    groups = HEADS // KV_HEADS
    shard_rows = w_query.shape[0]
    head_scale = HD ** (-0.5)
    kv_width = KV_HEADS * HD
    q_width = HEADS * HD
    places = jnp.arange(seq_len, dtype=jnp.int32)
    every_pos = jnp.repeat(span_order, span_len, axis=1) * span_len + places[None, :] % span_len
    local_pos = lax.dynamic_slice_in_dim(every_pos, ctx_rank * length, length, 1)
    cosine, sine = angles_for(local_pos.reshape(row_count), HD)
    allowed = (every_pos[:, None, :] <= local_pos[:, :, None])[:, None, None]
    attn_full = (
        lax.all_gather(attn_gain, ("dp", "ctx"), axis=0, tiled=True),
        lax.all_gather(w_query, ("dp", "ctx"), axis=0, tiled=True),
        lax.all_gather(w_key, ("dp", "ctx"), axis=0, tiled=True),
        lax.all_gather(w_value, ("dp", "ctx"), axis=0, tiled=True),
        lax.all_gather(w_out, ("dp", "ctx"), axis=0, tiled=True),
        lax.all_gather(b_query, ("dp", "ctx"), axis=0, tiled=True),
        lax.all_gather(b_key, ("dp", "ctx"), axis=0, tiled=True),
        lax.all_gather(b_value, ("dp", "ctx"), axis=0, tiled=True),
    )
    gain_one = attn_full[0].astype(jnp.float32)
    source = hidden.reshape(row_count, D).astype(jnp.float32)
    attn_factor, normed = norm_forward(source, gain_one)
    query_raw = plain_dot(normed, attn_full[1]) + attn_full[5].astype(jnp.float32)
    key_raw = plain_dot(normed, attn_full[2]) + attn_full[6].astype(jnp.float32)
    value_low = (plain_dot(normed, attn_full[3]) + attn_full[7].astype(jnp.float32)).astype(
        jnp.bfloat16
    )
    query_rot = rotate(query_raw.reshape(row_count, HEADS, HD), cosine, sine).astype(jnp.bfloat16)
    query_rot = query_rot.reshape(batches, length, KV_HEADS, groups, HD)
    key_rot = rotate(key_raw.reshape(row_count, KV_HEADS, HD), cosine, sine).astype(jnp.bfloat16)
    key_rot = key_rot.reshape(batches, length, kv_width)
    key_all, value_all = (
        lax.all_gather(key_rot, "ctx", axis=1, tiled=True),
        lax.all_gather(value_low.reshape(batches, length, kv_width), "ctx", axis=1, tiled=True),
    )
    key_all = key_all.reshape(batches, seq_len, KV_HEADS, HD)
    value_all = value_all.reshape(batches, seq_len, KV_HEADS, HD)
    scores = (
        jnp.einsum("bqkgd,bskd->bkgqs", query_rot, key_all, preferred_element_type=jnp.float32)
        * head_scale
    )
    masked = jnp.where(allowed, scores, masked_fill)
    row_max = jnp.max(masked, axis=-1, keepdims=True)
    expo = jnp.exp(masked - row_max)
    expo_sum = jnp.sum(expo, axis=-1, keepdims=True)
    log_total = row_max + jnp.log(expo_sum)
    attend = (expo / expo_sum).astype(jnp.bfloat16)
    mixed = jnp.einsum("bkgqs,bskd->bqkgd", attend, value_all, preferred_element_type=jnp.float32)
    mixed = mixed.reshape(row_count, q_width).astype(jnp.bfloat16)
    resid = source + right_dot(mixed, attn_full[4])
    ffn_full = (
        lax.all_gather(ffn_gain, ("dp", "ctx"), axis=0, tiled=True),
        lax.all_gather(w_gate, ("dp", "ctx"), axis=0, tiled=True),
        lax.all_gather(w_up, ("dp", "ctx"), axis=0, tiled=True),
        lax.all_gather(w_down, ("dp", "ctx"), axis=0, tiled=True),
    )
    gain_two = ffn_full[0].astype(jnp.float32)
    ffn_factor, normed_two = norm_forward(resid, gain_two)
    gate_pre = plain_dot(normed_two, ffn_full[1])
    up_pre = plain_dot(normed_two, ffn_full[2])
    sigmoid_gate = jax.nn.sigmoid(gate_pre)
    silu_gate = gate_pre * sigmoid_gate
    act = (silu_gate * up_pre).astype(jnp.bfloat16)
    output = resid + right_dot(act, ffn_full[3])
    result = output.astype(jnp.bfloat16).reshape(batches, length, D)
    ffn_back = (
        lax.all_gather(ffn_gain, ("dp", "ctx"), axis=0, tiled=True),
        lax.all_gather(w_gate, ("dp", "ctx"), axis=0, tiled=True),
        lax.all_gather(w_up, ("dp", "ctx"), axis=0, tiled=True),
        lax.all_gather(w_down, ("dp", "ctx"), axis=0, tiled=True),
    )
    grad_out = cotangent.reshape(row_count, D)
    grad_plain = grad_out.astype(jnp.float32)
    grad_act = plain_dot(grad_out, ffn_back[3])
    grad_gate = (grad_act * up_pre * sigmoid_gate * (1.0 + gate_pre * (1.0 - sigmoid_gate))).astype(
        jnp.bfloat16
    )
    grad_up = (grad_act * silu_gate).astype(jnp.bfloat16)
    pieces = (
        lax.all_gather(normed_two, "ctx", axis=0, tiled=True),
        lax.all_gather(grad_gate, "ctx", axis=0, tiled=True),
        lax.all_gather(grad_up, "ctx", axis=0, tiled=True),
        lax.all_gather(act, "ctx", axis=0, tiled=True),
        lax.all_gather(grad_out, "ctx", axis=0, tiled=True),
    )
    picked_in = owned_columns(pieces[0], ctx_size, ctx_rank, shard_rows)
    picked_out = owned_columns(pieces[4], ctx_size, ctx_rank, shard_rows)
    w_gate_grad, w_up_grad, w_down_grad = (
        lax.psum_scatter(
            outer_add(picked_in, pieces[1]).astype(jnp.bfloat16),
            "dp",
            scatter_dimension=0,
            tiled=True,
        ).astype(jnp.float32),
        lax.psum_scatter(
            outer_add(picked_in, pieces[2]).astype(jnp.bfloat16),
            "dp",
            scatter_dimension=0,
            tiled=True,
        ).astype(jnp.float32),
        lax.psum_scatter(
            outer_add(picked_out, pieces[3]).astype(jnp.bfloat16),
            "dp",
            scatter_dimension=0,
            tiled=True,
        ).astype(jnp.float32),
    )
    grad_norm_two = right_dot(grad_gate, ffn_back[1]) + right_dot(grad_up, ffn_back[2])
    resid_back, ffn_gain_part = norm_backward(resid, ffn_factor, gain_two, grad_norm_two)
    grad_resid = grad_plain + resid_back
    attn_back = (
        lax.all_gather(attn_gain, ("dp", "ctx"), axis=0, tiled=True),
        lax.all_gather(w_query, ("dp", "ctx"), axis=0, tiled=True),
        lax.all_gather(w_key, ("dp", "ctx"), axis=0, tiled=True),
        lax.all_gather(w_value, ("dp", "ctx"), axis=0, tiled=True),
        lax.all_gather(w_out, ("dp", "ctx"), axis=0, tiled=True),
        lax.all_gather(b_query, ("dp", "ctx"), axis=0, tiled=True),
        lax.all_gather(b_key, ("dp", "ctx"), axis=0, tiled=True),
        lax.all_gather(b_value, ("dp", "ctx"), axis=0, tiled=True),
    )
    grad_attn = grad_resid.astype(jnp.bfloat16)
    grad_mixed = plain_dot(grad_attn, attn_back[4]).astype(jnp.bfloat16)
    grad_mixed = grad_mixed.reshape(batches, length, KV_HEADS, groups, HD)
    scores = (
        jnp.einsum("bqkgd,bskd->bkgqs", query_rot, key_all, preferred_element_type=jnp.float32)
        * head_scale
    )
    masked = jnp.where(allowed, scores, masked_fill)
    attend_full = jnp.exp(masked - log_total)
    attend = attend_full.astype(jnp.bfloat16)
    grad_attend = jnp.einsum(
        "bqkgd,bskd->bkgqs", grad_mixed, value_all, preferred_element_type=jnp.float32
    )
    value_grad_all = jnp.einsum(
        "bkgqs,bqkgd->bskd", attend, grad_mixed, preferred_element_type=jnp.float32
    )
    delta = jnp.sum(grad_attend * attend_full, axis=-1, keepdims=True)
    grad_scores = (attend_full * (grad_attend - delta)).astype(jnp.bfloat16)
    query_grad_rot = (
        jnp.einsum("bkgqs,bskd->bqkgd", grad_scores, key_all, preferred_element_type=jnp.float32)
        * head_scale
    )
    key_grad_all = (
        jnp.einsum("bkgqs,bqkgd->bskd", grad_scores, query_rot, preferred_element_type=jnp.float32)
        * head_scale
    )
    key_grad_rot, value_grad = (
        lax.psum_scatter(
            key_grad_all.reshape(batches, seq_len, kv_width), "ctx", scatter_dimension=1, tiled=True
        ),
        lax.psum_scatter(
            value_grad_all.reshape(batches, seq_len, kv_width),
            "ctx",
            scatter_dimension=1,
            tiled=True,
        ),
    )
    query_grad = (
        rotate_back(query_grad_rot.reshape(row_count, HEADS, HD), cosine, sine)
        .reshape(row_count, q_width)
        .astype(jnp.bfloat16)
    )
    key_grad = (
        rotate_back(key_grad_rot.reshape(row_count, KV_HEADS, HD), cosine, sine)
        .reshape(row_count, kv_width)
        .astype(jnp.bfloat16)
    )
    value_grad = value_grad.reshape(row_count, kv_width).astype(jnp.bfloat16)
    proj_grad = jnp.concatenate([query_grad, key_grad, value_grad], axis=1)
    pieces = (
        lax.all_gather(normed, "ctx", axis=0, tiled=True),
        lax.all_gather(proj_grad, "ctx", axis=0, tiled=True),
        lax.all_gather(grad_attn, "ctx", axis=0, tiled=True),
        lax.all_gather(mixed, "ctx", axis=0, tiled=True),
    )
    picked_in = owned_columns(pieces[0], ctx_size, ctx_rank, shard_rows)
    picked_out = owned_columns(pieces[2], ctx_size, ctx_rank, shard_rows)
    proj_sum, w_out_grad = (
        lax.psum_scatter(
            outer_add(picked_in, pieces[1]).astype(jnp.bfloat16),
            "dp",
            scatter_dimension=0,
            tiled=True,
        ).astype(jnp.float32),
        lax.psum_scatter(
            outer_add(picked_out, pieces[3]).astype(jnp.bfloat16),
            "dp",
            scatter_dimension=0,
            tiled=True,
        ).astype(jnp.float32),
    )
    grad_norm_one = (
        right_dot(query_grad, attn_back[1])
        + right_dot(key_grad, attn_back[2])
        + right_dot(value_grad, attn_back[3])
    )
    source_back, attn_gain_part = norm_backward(source, attn_factor, gain_one, grad_norm_one)
    hidden_grad = (grad_resid + source_back).reshape(batches, length, D)
    query_bias_part = jnp.sum(query_grad.astype(jnp.float32), axis=0)
    key_bias_part = jnp.sum(key_grad.astype(jnp.float32), axis=0)
    value_bias_part = jnp.sum(value_grad.astype(jnp.float32), axis=0)
    small_sums = (
        lax.psum_scatter(attn_gain_part, ("dp", "ctx"), scatter_dimension=0, tiled=True),
        lax.psum_scatter(query_bias_part, ("dp", "ctx"), scatter_dimension=0, tiled=True),
        lax.psum_scatter(key_bias_part, ("dp", "ctx"), scatter_dimension=0, tiled=True),
        lax.psum_scatter(value_bias_part, ("dp", "ctx"), scatter_dimension=0, tiled=True),
        lax.psum_scatter(ffn_gain_part, ("dp", "ctx"), scatter_dimension=0, tiled=True),
    )
    w_query_grad = proj_sum[:, :q_width]
    w_key_grad = proj_sum[:, q_width : q_width + kv_width]
    w_value_grad = proj_sum[:, q_width + kv_width :]
    return (
        result,
        hidden_grad,
        small_sums[0],
        w_query_grad,
        small_sums[1],
        w_key_grad,
        small_sums[2],
        w_value_grad,
        small_sums[3],
        w_out_grad,
        small_sums[4],
        w_gate_grad,
        w_up_grad,
        w_down_grad,
    )


def solution(mesh):
    placed = (
        P("dp", "ctx", None),
        P("dp", "ctx", None),
        P("dp", None),
        P(("dp", "ctx")),
        P(("dp", "ctx"), None),
        P(("dp", "ctx")),
        P(("dp", "ctx"), None),
        P(("dp", "ctx")),
        P(("dp", "ctx"), None),
        P(("dp", "ctx")),
        P(("dp", "ctx"), None),
        P(("dp", "ctx")),
        P(("dp", "ctx"), None),
        P(("dp", "ctx"), None),
        P(("dp", "ctx"), None),
    )
    return jax.shard_map(
        fast_device if fits(mesh) else general_device,
        mesh=mesh,
        in_specs=placed,
        out_specs=(
            P("dp", "ctx", None),
            P("dp", "ctx", None),
            P(("dp", "ctx")),
            P(("dp", "ctx"), None),
            P(("dp", "ctx")),
            P(("dp", "ctx"), None),
            P(("dp", "ctx")),
            P(("dp", "ctx"), None),
            P(("dp", "ctx")),
            P(("dp", "ctx"), None),
            P(("dp", "ctx")),
            P(("dp", "ctx"), None),
            P(("dp", "ctx"), None),
            P(("dp", "ctx"), None),
        ),
        check_vma=False,
    )
```
